128 devices in a mesh: gx: 8 (over z_lo, x), gy: 16 (over y, z_hi, core).
Axes of the slice: x: 4, y: 4, z: 4 (z_hi: 2, z_lo: 2; z = z_hi * 2 + z_lo), core: 2. Of those that a mesh axis runs over, the one named last changes fastest.
Arguments:
- traces: float32 [4096, 2048], P(('gx', 'gy')), may hold values from -0.09375 to 0.09375
- phase_coef: float32 [2, 4], replicated, may hold values from -0.5 to 0.5
Outputs:
- image: float32 [4096, 2048], P(('gx', 'gy'))
The draws below stay inside these ranges and needn't reach their ends.
All inputs are finite; a program needn't handle non-finite values.
Results may differ from the reference program's by a relative error of at most 0.0003.
Values sent between devices are 32-bit elements; how exact they have to be, the bound alone decides.
A program may use at most 128 MiB of HBM per device.

```python
import jax
import jax.numpy as jnp
from jax import lax

LEVELS = 12
ORDER = 6
TERMS = 4
PANELS = 2048
POINTS = 4096


def shard_levels(stream_key, dims, shards, smallest, top_value):
    factor_of, own = 1.0, jax.random.fold_in(stream_key, 6)
    for axis_at, blocks in shards:
        heights = jnp.exp(jax.random.uniform(jax.random.fold_in(own, axis_at), (blocks,), jnp.float32, smallest / len(shards), top_value / len(shards)))
        factor_of = factor_of * jnp.repeat(heights, dims[axis_at] // blocks).reshape([-1 if axis == axis_at else 1 for axis in range(len(dims))])
    return factor_of


def noise(rng, shape, deviation, reach, shards=(), kind=jnp.bfloat16):
    factor_of = shard_levels(rng, shape, shards, -0.22, 0.18) if shards else 1.0
    values = jax.random.normal(rng, shape, jnp.float32) * deviation * factor_of
    return jnp.minimum(jnp.maximum(values, -reach), reach).astype(kind)


def setup_inputs(seed: int = 0) -> dict:
    key_list = jax.random.split(jax.random.key(seed), 3)
    return {
        "traces": noise(key_list[0], (POINTS, PANELS), (2 ** (0 - LEVELS // 2)), 0.09375, ((0, 128),), jnp.float32),
        "phase_coef": jnp.clip(jax.random.uniform(key_list[1], (2, TERMS), jnp.float32, -0.5, 0.5), -0.5, 0.5),
    }


BEND = 0.015625


def cheb_nodes():
    ticks = jnp.arange(ORDER, dtype=jnp.float32)
    return 0.5 * jnp.cos(jnp.pi * (2.0 * ticks + 1.0) / (2.0 * ORDER))


def lagrange(points):
    nodes = cheb_nodes()
    diagonal = jnp.arange(ORDER)[:, None] == jnp.arange(ORDER)[None, :]
    spread = jnp.where(diagonal, 1.0, nodes[:, None] - nodes[None, :])
    ratios = (points[..., None, None] - nodes[None, :]) / spread
    ratios = jnp.where(diagonal, 1.0, ratios)
    return jnp.prod(ratios, axis=-1)


def profile(position, weights):
    orders = jnp.arange(TERMS, dtype=jnp.float32)
    return jnp.sum(weights * jnp.cos(jnp.pi * orders * position[..., None]), axis=-1)


def cycles(level, target_box, target_off, source_box, source_off, phase_coef):
    quarter = (((2 * target_box + 1) * (2 * source_box + 1)) % 4).astype(jnp.float32) * 0.25
    target_mid = target_box.astype(jnp.float32) + 0.5
    source_mid = source_box.astype(jnp.float32) + 0.5
    first = target_mid * source_off
    second = source_mid * target_off
    first = first - jnp.floor(first)
    second = second - jnp.floor(second)
    where_x = (target_mid + target_off) * (2.0 ** (-level))
    where_k = (source_mid + source_off) * (2.0 ** (level - LEVELS))
    bent = (2.0 ** LEVELS) * BEND * profile(where_x, phase_coef[0]) * profile(where_k, phase_coef[1])
    total = quarter + first + second + target_off * source_off + bent
    return total - jnp.floor(total)


def target_box(word, level):
    total = jnp.zeros_like(word)
    for place in range(level):
        total = total + ((word // 2 ** place) % 2) * 2 ** (level - 1 - place)
    return total


def complex_block(real_part, imag_part, out_axis):
    upper = jnp.concatenate([real_part, -imag_part], axis=-1)
    lower = jnp.concatenate([imag_part, real_part], axis=-1)
    return jnp.concatenate([upper, lower], axis=out_axis)


def step_matrix(word, step, phase_coef):
    level = step + 1
    nodes = cheb_nodes()
    target = target_box(word, level)[..., None, None, None]
    source = (word // 2 ** level)[..., None, None, None]
    sides = jnp.arange(2, dtype=jnp.float32) - 0.5
    offsets = (sides[:, None] + nodes[None, :]) * 0.5
    if level <= LEVELS // 2:
        out_cycles = cycles(level, target, 0.0, source, nodes[:, None, None], phase_coef)
        in_cycles = cycles(level, target, 0.0, source, offsets[None], phase_coef)
        weight = jnp.transpose(lagrange(offsets), (2, 0, 1))
    else:
        bit_value = (word // 2 ** step) % 2
        children = 2 * source + jnp.arange(2, dtype=jnp.int32)[:, None]
        out_cycles = cycles(level, target, nodes[:, None, None], source, 0.0, phase_coef)
        in_cycles = cycles(level - 1, target // 2, nodes[None, None, :], children, 0.0, phase_coef)
        table = lagrange(offsets)
        weight = jnp.where(bit_value[..., None, None] == 0, table[0], table[1])[..., :, None, :]
    angle = 2.0 * jnp.pi * (in_cycles - out_cycles)
    return complex_block(weight * jnp.cos(angle), weight * jnp.sin(angle), -3)


def switch_matrix(word, phase_coef):
    half = LEVELS // 2
    nodes = cheb_nodes()
    target = target_box(word, half)[..., None, None]
    source = (word // 2 ** half)[..., None, None]
    out_cycles = cycles(half, target, nodes[:, None], source, 0.0, phase_coef)
    in_cycles = cycles(half, target, nodes[:, None], source, nodes[None, :], phase_coef)
    angle = 2.0 * jnp.pi * (in_cycles - out_cycles)
    return complex_block(jnp.cos(angle), jnp.sin(angle), -2)


def init_weights(word, phase_coef):
    nodes = cheb_nodes()
    anchor = jnp.zeros_like(word)[..., None]
    source = word[..., None]
    angle = 2.0 * jnp.pi * (cycles(0, anchor, 0.0, source, 0.0, phase_coef) - cycles(0, anchor, 0.0, source, nodes, phase_coef))
    centre = lagrange(jnp.zeros((), jnp.float32))
    return jnp.concatenate([centre * jnp.cos(angle), centre * jnp.sin(angle)], axis=-1)


def final_weights(word, phase_coef):
    target = target_box(word, LEVELS)
    angle = 2.0 * jnp.pi * cycles(LEVELS, target, 0.0, jnp.zeros_like(word), 0.0, phase_coef)
    centre = lagrange(jnp.zeros((), jnp.float32))
    return jnp.concatenate([centre * jnp.cos(angle)[..., None], -centre * jnp.sin(angle)[..., None]], axis=-1)


def reference(traces, phase_coef):
    points = 2 ** LEVELS
    width = 2 * ORDER
    words = jnp.arange(points, dtype=jnp.int32)
    starting = init_weights(words, phase_coef)
    matrices = [step_matrix(words.reshape(points // 2 ** (step + 1), 2, 2 ** step), step, phase_coef) for step in range(LEVELS)]
    switching = switch_matrix(words, phase_coef)
    ending = final_weights(words, phase_coef)
    columns = min(PANELS, 256)
    groups = PANELS // columns

    def run(panel):
        state = starting[:, :, None] * panel[:, None, :]
        for step in range(LEVELS):
            shaped = state.reshape(points // 2 ** (step + 1), 2, 2 ** step, width, columns)
            state = jnp.einsum("halocq,hclqr->halor", matrices[step], shaped, precision=lax.Precision.HIGHEST).reshape(points, width, columns)
            if step + 1 == LEVELS // 2:
                state = jnp.einsum("goq,gqr->gor", switching, state, precision=lax.Precision.HIGHEST)
        return jnp.einsum("gq,gqr->gr", ending, state, precision=lax.Precision.HIGHEST)

    blocks = traces.reshape(points, groups, columns).transpose(1, 0, 2)
    result = lax.map(run, blocks)
    return result.transpose(1, 0, 2).reshape(points, PANELS)
```

```python
import functools

import jax
import jax.numpy as jnp
import numpy as np
from jax import lax
from jax.experimental import pallas as pl
from jax.experimental.pallas import tpu as pltpu
from jax.sharding import PartitionSpec as P

ORDER = 6
MESH = pl.DeviceIdType.MESH
F32 = jnp.float32
BF16 = jnp.bfloat16
AMP = 64.0

NODES = 0.5 * np.cos(np.pi * (2.0 * np.arange(ORDER) + 1.0) / (2.0 * ORDER))


def lagrange(points):
    points = np.asarray(points)[..., None, None]
    same = np.eye(ORDER, dtype=bool)
    spread = np.where(same, 1.0, NODES[:, None] - NODES[None, :])
    return np.where(same, 1.0, (points - NODES[None, :]) / spread).prod(-1)


CENTRE = lagrange(0.0)
HALVES = np.stack([((side - 0.5) + NODES) * 0.5 for side in (0, 1)])
TABLE = lagrange(HALVES)
WEIGHT = np.transpose(TABLE, (0, 2, 1))


def tail_table():
    out = np.zeros((64, ORDER, ORDER))
    for high in range(64):
        total = np.eye(ORDER)
        for place in range(6):
            total = TABLE[(high >> place) & 1] @ total
        out[high] = total
    flat = out.transpose(1, 2, 0).reshape(36, 64)
    return np.pad(np.concatenate([flat, flat], axis=1), ((0, 4), (0, 0))).astype(np.float32)


def fit(function, terms):
    u = 0.125 + 0.125 * np.cos(np.pi * (np.arange(200) + 0.5) / 200)
    poly = np.polynomial.chebyshev.Chebyshev.fit(u, function(np.sqrt(u)), terms - 1, domain=[0, 0.25])
    return [float(c) for c in poly.convert(kind=np.polynomial.Polynomial).coef]


SIN = fit(lambda r: np.sin(np.pi * r) / r, 5)
SIN2 = [2.0 * c for c in fit(lambda r: np.sin(np.pi * r) / r, 4)]
COS = fit(lambda r: np.cos(np.pi * r), 5)


def horner(coefs, u):
    total = coefs[-1]
    for c in coefs[-2::-1]:
        total = total * u + c
    return total


def turn(c):
    r = c - jnp.floor(c + 0.5)
    u = r * r
    twice = r * horner(SIN2, u)
    half_cos = horner(COS, u)
    return 1.0 - (0.5 * twice) * twice, twice * half_cos


def half_turn(y):
    r = 0.5 - y
    u = r * r
    return r * horner(SIN, u), horner(COS, u)


def bend_value(coef, row, y):
    cosine = (0.5 - y) * horner(SIN, (0.5 - y) * (0.5 - y))
    c0, c1, c2, c3 = (coef[row, m] for m in range(4))
    return (c0 - c2) + cosine * ((c1 - 3.0 * c3) + cosine * (2.0 * c2 + cosine * (4.0 * c3)))


def bend_step(coef, middle, size):
    e1, e2, e3 = (coef[0, m] * float(-2.0 * AMP * np.sin(np.pi * m * size / 2.0)) for m in (1, 2, 3))
    cosine, sine = half_turn(middle)
    return sine * ((e1 - e3) + cosine * (2.0 * e2 + cosine * (4.0 * e3)))


def apply_real(weights, values):
    out = []
    for t in range(ORDER):
        total = weights[t][0] * values[0]
        for s in range(1, ORDER):
            total = total + weights[t][s] * values[s]
        out.append(total)
    return out


def iota(axis):
    return lax.broadcasted_iota(jnp.int32, (8, 128), axis)


def asf(value):
    return value.astype(F32)


def position():
    gx, gy = lax.axis_index("gx"), lax.axis_index("gy")
    return gx % 4, gy // 4, ((gy // 2) % 2) * 2 + gx // 4, gy % 2


def device(x, y, z, core):
    return {"gx": (z % 2) * 4 + x, "gy": y * 4 + (z // 2) * 2 + core}


def lane_parts(x, y, z):
    lane = iota(1)
    place = lane // 16
    box = (place % 2) + 4 * ((place // 2) % 2) + 16 * (place // 4)
    box = box + (2 * (y % 2) + 8 * (x % 2) + 32 * (z % 2))
    top = lane % 16
    return box, top


def early_levels(coef, box, top, v_ref):
    sub = iota(0)
    bits = [asf(sub % 2), asf((sub // 2) % 2), asf(sub // 4)]
    sign = [2.0 * bit - 1.0 for bit in bits]
    x0 = jnp.full((8, 128), 0.5, F32)
    x1 = x0 + sign[0] * 0.25
    x2 = x1 + sign[1] * 0.125
    word4 = asf(box * 16 + top)
    steps = bend_step(coef, x0 + sign[0] * 0.125, 0.25)
    p0_mid = coef[0, 0] - coef[0, 2]
    first = {}
    for j0 in range(2):
        outs = []
        for j1 in range(2):
            j = j0 + 2 * j1
            word = word4 * 4.0 + j
            start = 0.5 * (j0 + 0.5) + AMP * p0_mid * bend_value(coef, 1, (word + 0.5) * 2.0**-12)
            cosines, sines = [], []
            for s in range(ORDER):
                node = float(NODES[s])
                p1 = bend_value(coef, 1, (word + (0.5 + node)) * 2.0**-12)
                c, d = turn(start + sign[0] * ((j + 0.5 + node) * 0.25 + steps * p1))
                cosines.append(c)
                sines.append(d)
            outs.append((cosines, sines))
        weights = [[float(WEIGHT[j0][t][s] * CENTRE[s]) for s in range(ORDER)] for t in range(ORDER)]
        joined = [[jnp.stack([outs[0][c][s], outs[1][c][s]]) for s in range(ORDER)] for c in range(2)]
        first[j0] = [apply_real(weights, joined[c]) for c in range(2)]
    steps = bend_step(coef, x1 + sign[1] * 0.0625, 0.125)
    second = {}
    for j1 in range(2):
        word = word4 * 2.0 + j1
        linear = j1 + 2.0 * asf(top % 2) + 0.5
        real, imag = [], []
        for s in range(ORDER):
            node = float(NODES[s])
            p1 = bend_value(coef, 1, (word + (0.5 + node)) * 2.0**-11)
            c, d = turn(sign[1] * ((linear + node) * 0.25 + steps * p1))
            a = jnp.stack([first[0][0][s][j1], first[1][0][s][j1]])
            b = jnp.stack([first[0][1][s][j1], first[1][1][s][j1]])
            real.append(a * c - b * d)
            imag.append(a * d + b * c)
        weights = [[float(WEIGHT[j1][t][s]) for s in range(ORDER)] for t in range(ORDER)]
        second[j1] = (apply_real(weights, real), apply_real(weights, imag))
    steps = bend_step(coef, x2 + sign[2] * 0.03125, 0.0625)
    linear = asf(top % 4) + 0.5
    real, imag = [], []
    for s in range(ORDER):
        node = float(NODES[s])
        p1 = bend_value(coef, 1, (word4 + (0.5 + node)) * 2.0**-10)
        c, d = turn(sign[2] * ((linear + node) * 0.25 + steps * p1))
        a = jnp.concatenate([second[0][0][s], second[1][0][s]])
        b = jnp.concatenate([second[0][1][s], second[1][1][s]])
        real.append(a * c - b * d)
        imag.append(a * d + b * c)
    weights = lane_weights(top % 2)
    for c, values in enumerate((real, imag)):
        for t, value in enumerate(apply_real(weights, values)):
            v_ref[2 * t + c] = value


def lane_weights(bit):
    pick = bit == 1
    return [
        [jnp.where(pick, float(WEIGHT[1][t][s]), float(WEIGHT[0][t][s])) for s in range(ORDER)]
        for t in range(ORDER)
    ]


def late_setup(coef, box, top, w_ref, p_ref):
    for i, level in enumerate((4, 5, 6)):
        weights = lane_weights((top // 2 ** (level - 3)) % 2)
        for t in range(ORDER):
            for s in range(ORDER):
                w_ref[i, ORDER * t + s] = weights[t][s]
        word = asf(box * 2 ** (7 - level) + top // 2 ** (level - 3))
        for s in range(ORDER):
            p_ref[i, s] = bend_value(coef, 1, (word + float(0.5 + NODES[s])) * 2.0 ** (level - 13))
    for s in range(ORDER):
        p_ref[3, s] = bend_value(coef, 1, (asf(box) + float(0.5 + NODES[s])) * 2.0**-6)


def late_levels(coef, box, top, w_ref, p_ref, v3, v4, v5, v6, hi_ref, lo_ref):
    sub = iota(0)
    x3 = asf(4 * (sub % 2) + 2 * ((sub // 2) % 2) + sub // 4) * 0.125 + 0.0625
    full = box * 16 + top
    states = {3: v3, 4: v4, 5: v5, 6: v6}

    def level_step(level, parent, bit):
        i = level - 4
        sign = (2 * bit - 1).astype(F32)
        steps = bend_step(coef, parent + sign * 2.0 ** -(level + 2), 2.0 ** -(level + 1))
        linear = asf((full // 2 ** (level - 3)) % 4) + 0.5
        source, target = states[level - 1], states[level]
        real, imag = [], []
        for s in range(ORDER):
            c, d = turn(sign * ((linear + float(NODES[s])) * 0.25 + steps * p_ref[i, s]))
            a, b = source[2 * s], source[2 * s + 1]
            real.append(a * c - b * d)
            imag.append(a * d + b * c)
        weights = [[w_ref[i, ORDER * t + s] for s in range(ORDER)] for t in range(ORDER)]
        for c, values in enumerate((real, imag)):
            for t, value in enumerate(apply_real(weights, values)):
                target[2 * t + c] = value
        return parent + sign * 2.0 ** -(level + 1)

    def switch(centre, group):
        states6 = [(v6[2 * s], v6[2 * s + 1]) for s in range(ORDER)]
        mid = asf(box) + 0.5
        for t in range(ORDER):
            node = float(NODES[t])
            steps = bend_step(coef, centre + node / 128.0, node / 64.0)
            linear = mid * node
            real = imag = None
            for s in range(ORDER):
                c, d = turn((linear + float(node * NODES[s])) + steps * p_ref[3, s])
                a, b = states6[s]
                real = a * c - b * d if real is None else real + (a * c - b * d)
                imag = a * d + b * c if imag is None else imag + (a * d + b * c)
            rows = pl.ds(pl.multiple_of(group * 96 + 16 * t, 16), 16)
            for j in range(4):
                both = jnp.concatenate([real[j], imag[j]], axis=0)
                high = both.astype(BF16)
                hi_ref[rows, 128 * j : 128 * (j + 1)] = high
                lo_ref[rows, 128 * j : 128 * (j + 1)] = (both - high.astype(F32)).astype(BF16)

    def over3(q3, _):
        x4 = level_step(4, x3, q3)

        def over4(q4, _):
            x5 = level_step(5, x4, q4)

            def over5(q5, _):
                x6 = level_step(6, x5, q5)
                switch(x6, q3 + 2 * q4 + 4 * q5)
                return 0

            return lax.fori_loop(0, 2, over5, 0)

        return lax.fori_loop(0, 2, over4, 0)

    lax.fori_loop(0, 2, over3, 0)


def last_weights(coef, group, tail_ref, h_ref):
    sub, lane = iota(0), iota(1)
    box6 = 32 * (sub % 2) + 16 * ((sub // 2) % 2) + 8 * (sub // 4)
    box6 = box6 + (4 * (group % 2) + 2 * ((group // 2) % 2) + group // 4)
    inner = 0
    for place in range(6):
        inner = inner + ((lane // 2**place) % 2) * 2 ** (5 - place)
    centre = (asf(box6 * 64 + inner) + 0.5) * 2.0**-12
    p1_mid = coef[1, 0] - coef[1, 2]
    real = [None] * ORDER
    imag = [None] * ORDER
    for t in range(ORDER):
        node = float(NODES[t])
        steps = bend_step(coef, centre + node / 8192.0, node / 4096.0)
        c, d = turn(-0.5 * node - steps * p1_mid)
        c, d = c * float(CENTRE[t]), d * float(CENTRE[t])
        for s in range(ORDER):
            row = tail_ref[ORDER * t + s : ORDER * t + s + 1, :]
            real[s] = c * row if t == 0 else real[s] + c * row
            imag[s] = d * row if t == 0 else imag[s] + d * row
    for s in range(ORDER):
        h_ref[2 * s] = real[s]
        h_ref[2 * s + 1] = -imag[s]


def kernel(
    x_ref,
    coef_ref,
    tail_ref,
    out_ref,
    w_ref,
    p_ref,
    v3,
    v4,
    v5,
    v6,
    hi_ref,
    lo_ref,
    h_ref,
    xr_ref,
    xs_ref,
    part_ref,
    rr_ref,
    tile_ref,
    send_sems,
    recv_sems,
):
    x, y, z, core = position()
    px, py, pz = x % 2, y % 2, z % 2
    group = px + 2 * py + 4 * pz
    spin = 1 - 2 * core
    cx, cy, cz = ((x + core) // 2) % 2, ((y + core) // 2) % 2, ((z + core) // 2) % 2
    block = cx + 2 * cy + 4 * cz + 8 * core
    slot = 2 * (z // 2 + 2 * (y // 2) + 4 * (x // 2)) + core

    def same_parity(i):
        return device(px + 2 * (i // 8), py + 2 * ((i // 4) % 2), pz + 2 * ((i // 2) % 2), i % 2)

    def in_cube(g):
        a = (2 * cx + spin * (g % 2) + 4) % 4
        b = (2 * cy + spin * ((g // 2) % 2) + 4) % 4
        c = (2 * cz + spin * (g // 4) + 4) % 4
        return device(a, b, c, core)

    barrier = pltpu.get_barrier_semaphore()

    def greet_class(i, _):
        @pl.when(i != slot_of_me)
        def _():
            pl.semaphore_signal(barrier, inc=1, device_id=same_parity(i), device_id_type=MESH)

        return 0

    slot_of_me = 8 * (x // 2) + 4 * (y // 2) + 2 * (z // 2) + core
    lax.fori_loop(0, 16, greet_class, 0)

    def greet_cube(step, _):
        other = (group + step) % 8
        pl.semaphore_signal(barrier, inc=1, device_id=in_cube(other), device_id_type=MESH)
        return 0

    lax.fori_loop(1, 8, greet_cube, 0)

    box, top = lane_parts(x, y, z)
    early_levels(coef_ref, box, top, v3)
    pl.semaphore_wait(barrier, 22)

    def scatter(step, _):
        m = (block + step) % 16
        turned = 1 - 2 * (m // 8)
        a = (2 * (m % 2) + turned * px + 4) % 4
        b = (2 * ((m // 2) % 2) + turned * py + 4) % 4
        c = (2 * ((m // 4) % 2) + turned * pz + 4) % 4
        pltpu.make_async_remote_copy(
            src_ref=x_ref.at[:, pl.ds(pl.multiple_of(m * 128, 128), 128)],
            dst_ref=xr_ref.at[slot],
            send_sem=send_sems.at[0],
            recv_sem=recv_sems.at[0],
            device_id=device(a, b, c, m // 8),
            device_id_type=MESH,
        ).start()
        return 0

    lax.fori_loop(1, 16, scatter, 0)
    pltpu.make_async_copy(
        x_ref.at[:, pl.ds(pl.multiple_of(block * 128, 128), 128)], xr_ref.at[slot], recv_sems.at[0]
    ).start()

    late_setup(coef_ref, box, top, w_ref, p_ref)
    late_levels(coef_ref, box, top, w_ref, p_ref, v3, v4, v5, v6, hi_ref, lo_ref)
    last_weights(coef_ref, group, tail_ref, h_ref)

    pltpu.make_async_copy(xr_ref, xr_ref, recv_sems.at[0]).wait()
    for i in range(8):
        for j in range(4):
            piece = jnp.concatenate([xr_ref[2 * i + s, pl.ds(j, 8, stride=4), :] for s in range(2)], axis=0)
            high = piece.astype(BF16)
            rows = slice(128 * j + 16 * i, 128 * j + 16 * i + 16)
            xs_ref[rows, 0:128] = high
            xs_ref[rows, 128:256] = (piece - high.astype(F32)).astype(BF16)

    def product(g):
        rows = pl.ds(pl.multiple_of(g * 96, 16), 96)
        wide = jnp.dot(hi_ref[rows, :], xs_ref[...], preferred_element_type=F32)
        small = jnp.dot(lo_ref[rows, :], xs_ref[:, 0:128], preferred_element_type=F32)
        return wide[:, 0:128] + (wide[:, 128:256] + small)

    def reduce(step, _):
        other = (group + step) % 8
        part_ref[step] = product(other)
        pltpu.make_async_remote_copy(
            src_ref=part_ref.at[step],
            dst_ref=rr_ref.at[step - 1],
            send_sem=send_sems.at[1],
            recv_sem=recv_sems.at[1],
            device_id=in_cube(other),
            device_id_type=MESH,
        ).start()
        return 0

    lax.fori_loop(1, 8, reduce, 0)
    part_ref[0] = product(group)
    pltpu.make_async_copy(rr_ref, rr_ref, recv_sems.at[1]).wait()
    for i in range(12):
        rows = slice(8 * i, 8 * i + 8)
        total = part_ref[0, rows, :]
        for k in range(7):
            total = total + rr_ref[k, rows, :]
        part_ref[0, rows, :] = total

    sums = [part_ref[0, 8 * i : 8 * i + 8, :] for i in range(12)]
    for high in range(64):
        total = None
        for i in range(12):
            term = h_ref[i, :, high : high + 1] * sums[i]
            total = term if total is None else total + term
        tile_ref[high] = total

    mine = z // 2 + 2 * y + 8 * x + 32 * pz
    here = out_ref.at[
        pl.ds(pl.multiple_of((px + 2 * py) * 8, 8), 8), pl.ds(pl.multiple_of(block * 128, 128), 128)
    ]
    own = core == pz

    def deliver(step, _):
        high = (mine + step) % 64

        @pl.when(jnp.logical_or(step != 0, jnp.logical_not(own)))
        def _():
            pltpu.make_async_remote_copy(
                src_ref=tile_ref.at[high],
                dst_ref=here,
                send_sem=send_sems.at[2],
                recv_sem=recv_sems.at[2],
                device_id=device((high // 8) % 4, (high // 2) % 4, 2 * (high % 2) + high // 32, pz),
                device_id_type=MESH,
            ).start()

        return 0

    lax.fori_loop(0, 64, deliver, 0)

    @pl.when(own)
    def _():
        pltpu.make_async_copy(tile_ref.at[mine], here, recv_sems.at[2]).start()

    pltpu.make_async_copy(xr_ref.at[0:15], xr_ref.at[0:15], send_sems.at[0]).wait()
    pltpu.make_async_copy(rr_ref, rr_ref, send_sems.at[1]).wait()

    @pl.when(own)
    def _():
        pltpu.make_async_copy(tile_ref.at[0:63], tile_ref.at[0:63], send_sems.at[2]).wait()

    @pl.when(jnp.logical_not(own))
    def _():
        pltpu.make_async_copy(tile_ref, tile_ref, send_sems.at[2]).wait()

    pltpu.make_async_copy(out_ref, out_ref, recv_sems.at[2]).wait()


def shards(traces, phase_coef):
    return pl.pallas_call(
        kernel,
        out_shape=jax.ShapeDtypeStruct((32, 2048), F32),
        in_specs=[
            pl.BlockSpec(memory_space=pl.ANY),
            pl.BlockSpec(memory_space=pltpu.SMEM),
            pl.BlockSpec(memory_space=pltpu.VMEM),
        ],
        out_specs=pl.BlockSpec(memory_space=pltpu.VMEM),
        scratch_shapes=[
            pltpu.VMEM((3, 36, 8, 128), F32),
            pltpu.VMEM((4, 6, 8, 128), F32),
            pltpu.VMEM((12, 4, 8, 128), F32),
            pltpu.VMEM((12, 4, 8, 128), F32),
            pltpu.VMEM((12, 4, 8, 128), F32),
            pltpu.VMEM((12, 4, 8, 128), F32),
            pltpu.VMEM((768, 512), BF16),
            pltpu.VMEM((768, 512), BF16),
            pltpu.VMEM((12, 8, 128), F32),
            pltpu.VMEM((16, 32, 128), F32),
            pltpu.VMEM((512, 256), BF16),
            pltpu.VMEM((8, 96, 128), F32),
            pltpu.VMEM((7, 96, 128), F32),
            pltpu.VMEM((64, 8, 128), F32),
            pltpu.SemaphoreType.DMA((3,)),
            pltpu.SemaphoreType.DMA((3,)),
        ],
        compiler_params=pltpu.CompilerParams(
            collective_id=0, has_side_effects=True, vmem_limit_bytes=32 * 2**20
        ),
    )(traces, phase_coef, jnp.asarray(tail_table()))


def solution(mesh):
    placed = (P(("gx", "gy"), None), P())
    return jax.shard_map(
        shards, mesh=mesh, in_specs=placed, out_specs=P(("gx", "gy"), None), check_vma=False
    )
```

```python
import functools

import jax
import jax.numpy as jnp
import numpy as np
from jax import lax
from jax.experimental import pallas as pl
from jax.experimental.pallas import tpu as pltpu
from jax.sharding import PartitionSpec as P

ORDER = 6
MESH = pl.DeviceIdType.MESH
F32 = jnp.float32
BF16 = jnp.bfloat16
AMP = 64.0

NODES = 0.5 * np.cos(np.pi * (2.0 * np.arange(ORDER) + 1.0) / (2.0 * ORDER))


def lagrange(points):
    points = np.asarray(points)[..., None, None]
    same = np.eye(ORDER, dtype=bool)
    spread = np.where(same, 1.0, NODES[:, None] - NODES[None, :])
    return np.where(same, 1.0, (points - NODES[None, :]) / spread).prod(-1)


CENTRE = lagrange(0.0)
HALVES = np.stack([((side - 0.5) + NODES) * 0.5 for side in (0, 1)])
TABLE = lagrange(HALVES)
WEIGHT = np.transpose(TABLE, (0, 2, 1))


def tail_table():
    out = np.zeros((64, ORDER, ORDER))
    for high in range(64):
        total = np.eye(ORDER)
        for place in range(6):
            total = TABLE[(high >> place) & 1] @ total
        out[high] = total
    flat = out.transpose(1, 2, 0).reshape(36, 64)
    return np.pad(np.concatenate([flat, flat], axis=1), ((0, 4), (0, 0))).astype(np.float32)


def fit(function, terms):
    u = 0.125 + 0.125 * np.cos(np.pi * (np.arange(200) + 0.5) / 200)
    poly = np.polynomial.chebyshev.Chebyshev.fit(u, function(np.sqrt(u)), terms - 1, domain=[0, 0.25])
    return [float(c) for c in poly.convert(kind=np.polynomial.Polynomial).coef]


SIN = fit(lambda r: np.sin(np.pi * r) / r, 5)
SIN2 = [2.0 * c for c in fit(lambda r: np.sin(np.pi * r) / r, 4)]
COS = fit(lambda r: np.cos(np.pi * r), 5)


def horner(coefs, u):
    total = coefs[-1]
    for c in coefs[-2::-1]:
        total = total * u + c
    return total


def turn(c):
    r = c - jnp.floor(c + 0.5)
    u = r * r
    twice = r * horner(SIN2, u)
    half_cos = horner(COS, u)
    return 1.0 - (0.5 * twice) * twice, twice * half_cos


def half_turn(y):
    r = 0.5 - y
    u = r * r
    return r * horner(SIN, u), horner(COS, u)


def bend_value(coef, row, y):
    cosine = (0.5 - y) * horner(SIN, (0.5 - y) * (0.5 - y))
    c0, c1, c2, c3 = (coef[row, m] for m in range(4))
    return (c0 - c2) + cosine * ((c1 - 3.0 * c3) + cosine * (2.0 * c2 + cosine * (4.0 * c3)))


def bend_step(coef, middle, size):
    e1, e2, e3 = (coef[0, m] * float(-2.0 * AMP * np.sin(np.pi * m * size / 2.0)) for m in (1, 2, 3))
    cosine, sine = half_turn(middle)
    return sine * ((e1 - e3) + cosine * (2.0 * e2 + cosine * (4.0 * e3)))


def apply_real(weights, values):
    out = []
    for t in range(ORDER):
        total = weights[t][0] * values[0]
        for s in range(1, ORDER):
            total = total + weights[t][s] * values[s]
        out.append(total)
    return out


def iota(axis):
    return lax.broadcasted_iota(jnp.int32, (8, 128), axis)


def asf(value):
    return value.astype(F32)


def position():
    gx, gy = lax.axis_index("gx"), lax.axis_index("gy")
    return gx % 4, gy // 4, ((gy // 2) % 2) * 2 + gx // 4, gy % 2


def device(x, y, z, core):
    return {"gx": (z % 2) * 4 + x, "gy": y * 4 + (z // 2) * 2 + core}


def lane_parts(x, y, z):
    lane = iota(1)
    place = lane // 16
    box = (place % 2) + 4 * ((place // 2) % 2) + 16 * (place // 4)
    box = box + (2 * (y % 2) + 8 * (x % 2) + 32 * (z % 2))
    top = lane % 16
    return box, top


def early_levels(coef, box, top, v_ref):
    sub = iota(0)
    bits = [asf(sub % 2), asf((sub // 2) % 2), asf(sub // 4)]
    sign = [2.0 * bit - 1.0 for bit in bits]
    x0 = jnp.full((8, 128), 0.5, F32)
    x1 = x0 + sign[0] * 0.25
    x2 = x1 + sign[1] * 0.125
    word4 = asf(box * 16 + top)
    steps = bend_step(coef, x0 + sign[0] * 0.125, 0.25)
    p0_mid = coef[0, 0] - coef[0, 2]
    first = {}
    for j0 in range(2):
        outs = []
        for j1 in range(2):
            j = j0 + 2 * j1
            word = word4 * 4.0 + j
            start = 0.5 * (j0 + 0.5) + AMP * p0_mid * bend_value(coef, 1, (word + 0.5) * 2.0**-12)
            cosines, sines = [], []
            for s in range(ORDER):
                node = float(NODES[s])
                p1 = bend_value(coef, 1, (word + (0.5 + node)) * 2.0**-12)
                c, d = turn(start + sign[0] * ((j + 0.5 + node) * 0.25 + steps * p1))
                cosines.append(c)
                sines.append(d)
            outs.append((cosines, sines))
        weights = [[float(WEIGHT[j0][t][s] * CENTRE[s]) for s in range(ORDER)] for t in range(ORDER)]
        joined = [[jnp.stack([outs[0][c][s], outs[1][c][s]]) for s in range(ORDER)] for c in range(2)]
        first[j0] = [apply_real(weights, joined[c]) for c in range(2)]
    steps = bend_step(coef, x1 + sign[1] * 0.0625, 0.125)
    second = {}
    for j1 in range(2):
        word = word4 * 2.0 + j1
        linear = j1 + 2.0 * asf(top % 2) + 0.5
        real, imag = [], []
        for s in range(ORDER):
            node = float(NODES[s])
            p1 = bend_value(coef, 1, (word + (0.5 + node)) * 2.0**-11)
            c, d = turn(sign[1] * ((linear + node) * 0.25 + steps * p1))
            a = jnp.stack([first[0][0][s][j1], first[1][0][s][j1]])
            b = jnp.stack([first[0][1][s][j1], first[1][1][s][j1]])
            real.append(a * c - b * d)
            imag.append(a * d + b * c)
        weights = [[float(WEIGHT[j1][t][s]) for s in range(ORDER)] for t in range(ORDER)]
        second[j1] = (apply_real(weights, real), apply_real(weights, imag))
    steps = bend_step(coef, x2 + sign[2] * 0.03125, 0.0625)
    linear = asf(top % 4) + 0.5
    real, imag = [], []
    for s in range(ORDER):
        node = float(NODES[s])
        p1 = bend_value(coef, 1, (word4 + (0.5 + node)) * 2.0**-10)
        c, d = turn(sign[2] * ((linear + node) * 0.25 + steps * p1))
        a = jnp.concatenate([second[0][0][s], second[1][0][s]])
        b = jnp.concatenate([second[0][1][s], second[1][1][s]])
        real.append(a * c - b * d)
        imag.append(a * d + b * c)
    weights = lane_weights(top % 2)
    for c, values in enumerate((real, imag)):
        for t, value in enumerate(apply_real(weights, values)):
            v_ref[2 * t + c] = value


def lane_weights(bit):
    pick = bit == 1
    return [
        [jnp.where(pick, float(WEIGHT[1][t][s]), float(WEIGHT[0][t][s])) for s in range(ORDER)]
        for t in range(ORDER)
    ]


def late_setup(coef, box, top, w_ref, p_ref):
    for i, level in enumerate((4, 5, 6)):
        weights = lane_weights((top // 2 ** (level - 3)) % 2)
        for t in range(ORDER):
            for s in range(ORDER):
                w_ref[i, ORDER * t + s] = weights[t][s]
        word = asf(box * 2 ** (7 - level) + top // 2 ** (level - 3))
        for s in range(ORDER):
            p_ref[i, s] = bend_value(coef, 1, (word + float(0.5 + NODES[s])) * 2.0 ** (level - 13))
    for s in range(ORDER):
        p_ref[3, s] = bend_value(coef, 1, (asf(box) + float(0.5 + NODES[s])) * 2.0**-6)


def late_levels(coef, box, top, w_ref, p_ref, v3, v4, v5, v6, g_ref):
    sub = iota(0)
    x3 = asf(4 * (sub % 2) + 2 * ((sub // 2) % 2) + sub // 4) * 0.125 + 0.0625
    full = box * 16 + top
    states = {3: v3, 4: v4, 5: v5, 6: v6}

    def level_step(level, parent, bit):
        i = level - 4
        sign = (2 * bit - 1).astype(F32)
        steps = bend_step(coef, parent + sign * 2.0 ** -(level + 2), 2.0 ** -(level + 1))
        linear = asf((full // 2 ** (level - 3)) % 4) + 0.5
        source, target = states[level - 1], states[level]
        real, imag = [], []
        for s in range(ORDER):
            c, d = turn(sign * ((linear + float(NODES[s])) * 0.25 + steps * p_ref[i, s]))
            a, b = source[2 * s], source[2 * s + 1]
            real.append(a * c - b * d)
            imag.append(a * d + b * c)
        weights = [[w_ref[i, ORDER * t + s] for s in range(ORDER)] for t in range(ORDER)]
        for c, values in enumerate((real, imag)):
            for t, value in enumerate(apply_real(weights, values)):
                target[2 * t + c] = value
        return parent + sign * 2.0 ** -(level + 1)

    def switch(centre, group):
        states6 = [(v6[2 * s], v6[2 * s + 1]) for s in range(ORDER)]
        mid = asf(box) + 0.5
        for t in range(ORDER):
            node = float(NODES[t])
            steps = bend_step(coef, centre + node / 128.0, node / 64.0)
            linear = mid * node
            real = imag = None
            for s in range(ORDER):
                c, d = turn((linear + float(node * NODES[s])) + steps * p_ref[3, s])
                a, b = states6[s]
                real = a * c - b * d if real is None else real + (a * c - b * d)
                imag = a * d + b * c if imag is None else imag + (a * d + b * c)
            rows = pl.ds(pl.multiple_of(group * 192 + 16 * t, 16), 16)
            rows_low = pl.ds(pl.multiple_of(group * 192 + 96 + 16 * t, 16), 16)
            for j in range(4):
                both = jnp.concatenate([real[j], imag[j]], axis=0)
                high = both.astype(BF16)
                g_ref[rows, 128 * j : 128 * (j + 1)] = high
                g_ref[rows_low, 128 * j : 128 * (j + 1)] = (both - high.astype(F32)).astype(BF16)

    def over3(q3, _):
        x4 = level_step(4, x3, q3)

        def over4(q4, _):
            x5 = level_step(5, x4, q4)

            def over5(q5, _):
                x6 = level_step(6, x5, q5)
                switch(x6, q3 + 2 * q4 + 4 * q5)
                return 0

            return lax.fori_loop(0, 2, over5, 0)

        return lax.fori_loop(0, 2, over4, 0)

    lax.fori_loop(0, 2, over3, 0)


def last_weights(coef, group, tail_ref, h_ref):
    sub, lane = iota(0), iota(1)
    box6 = 32 * (sub % 2) + 16 * ((sub // 2) % 2) + 8 * (sub // 4)
    box6 = box6 + (4 * (group % 2) + 2 * ((group // 2) % 2) + group // 4)
    inner = 0
    for place in range(6):
        inner = inner + ((lane // 2**place) % 2) * 2 ** (5 - place)
    centre = (asf(box6 * 64 + inner) + 0.5) * 2.0**-12
    p1_mid = coef[1, 0] - coef[1, 2]
    real = [None] * ORDER
    imag = [None] * ORDER
    for t in range(ORDER):
        node = float(NODES[t])
        steps = bend_step(coef, centre + node / 8192.0, node / 4096.0)
        c, d = turn(-0.5 * node - steps * p1_mid)
        c, d = c * float(CENTRE[t]), d * float(CENTRE[t])
        for s in range(ORDER):
            row = tail_ref[ORDER * t + s : ORDER * t + s + 1, :]
            real[s] = c * row if t == 0 else real[s] + c * row
            imag[s] = d * row if t == 0 else imag[s] + d * row
    for s in range(ORDER):
        h_ref[2 * s] = real[s]
        h_ref[2 * s + 1] = -imag[s]


def kernel(
    x_ref,
    coef_hbm,
    tail_hbm,
    out_ref,
    coef_ref,
    tail_ref,
    w_ref,
    p_ref,
    v3,
    v4,
    v5,
    v6,
    g_ref,
    h_ref,
    xr_ref,
    xs_ref,
    wide_ref,
    part_ref,
    rr_ref,
    sum_ref,
    tile_ref,
    send_sems,
    recv_sems,
):
    fetch_coef = pltpu.make_async_copy(coef_hbm, coef_ref, recv_sems.at[3])
    fetch_tail = pltpu.make_async_copy(tail_hbm, tail_ref, recv_sems.at[4])
    fetch_coef.start()
    fetch_tail.start()
    x, y, z, core = position()
    px, py, pz = x % 2, y % 2, z % 2
    group = px + 2 * py + 4 * pz
    spin = 1 - 2 * core
    cx, cy, cz = ((x + core) // 2) % 2, ((y + core) // 2) % 2, ((z + core) // 2) % 2
    block = cx + 2 * cy + 4 * cz + 8 * core
    slot = 2 * (z // 2 + 2 * (y // 2) + 4 * (x // 2)) + core

    def same_parity(i):
        return device(px + 2 * (i // 8), py + 2 * ((i // 4) % 2), pz + 2 * ((i // 2) % 2), i % 2)

    def in_cube(g):
        a = (2 * cx + spin * (g % 2) + 4) % 4
        b = (2 * cy + spin * ((g // 2) % 2) + 4) % 4
        c = (2 * cz + spin * (g // 4) + 4) % 4
        return device(a, b, c, core)

    barrier = pltpu.get_barrier_semaphore()

    def greet_class(i, _):
        @pl.when(i != slot_of_me)
        def _():
            pl.semaphore_signal(barrier, inc=1, device_id=same_parity(i), device_id_type=MESH)

        return 0

    slot_of_me = 8 * (x // 2) + 4 * (y // 2) + 2 * (z // 2) + core
    lax.fori_loop(0, 16, greet_class, 0)

    def greet_cube(step, _):
        other = (group + step) % 8
        pl.semaphore_signal(barrier, inc=1, device_id=in_cube(other), device_id_type=MESH)
        return 0

    lax.fori_loop(1, 8, greet_cube, 0)

    box, top = lane_parts(x, y, z)
    fetch_coef.wait()
    early_levels(coef_ref, box, top, v3)
    pl.semaphore_wait(barrier, 22)

    def scatter(step, _):
        m = (block + step) % 16
        turned = 1 - 2 * (m // 8)
        a = (2 * (m % 2) + turned * px + 4) % 4
        b = (2 * ((m // 2) % 2) + turned * py + 4) % 4
        c = (2 * ((m // 4) % 2) + turned * pz + 4) % 4
        pltpu.make_async_remote_copy(
            src_ref=x_ref.at[:, pl.ds(pl.multiple_of(m * 128, 128), 128)],
            dst_ref=xr_ref.at[slot],
            send_sem=send_sems.at[0],
            recv_sem=recv_sems.at[0],
            device_id=device(a, b, c, m // 8),
            device_id_type=MESH,
        ).start()
        return 0

    lax.fori_loop(1, 16, scatter, 0)
    pltpu.make_async_copy(
        x_ref.at[:, pl.ds(pl.multiple_of(block * 128, 128), 128)], xr_ref.at[slot], recv_sems.at[0]
    ).start()

    late_setup(coef_ref, box, top, w_ref, p_ref)
    late_levels(coef_ref, box, top, w_ref, p_ref, v3, v4, v5, v6, g_ref)
    fetch_tail.wait()
    last_weights(coef_ref, group, tail_ref, h_ref)

    pltpu.make_async_copy(xr_ref, xr_ref, recv_sems.at[0]).wait()
    for i in range(8):
        for j in range(4):
            piece = jnp.concatenate([xr_ref[2 * i + s, pl.ds(j, 8, stride=4), :] for s in range(2)], axis=0)
            high = piece.astype(BF16)
            rows = slice(128 * j + 16 * i, 128 * j + 16 * i + 16)
            xs_ref[rows, 0:128] = high
            xs_ref[rows, 128:256] = (piece - high.astype(F32)).astype(BF16)

    def products(half):
        rows = pl.ds(pl.multiple_of(half * 768, 16), 768)
        wide_ref[...] = jnp.dot(g_ref[rows, :], xs_ref[...], preferred_element_type=F32)

    def part(i):
        high = pl.ds(pl.multiple_of(i * 192, 8), 96)
        low = pl.ds(pl.multiple_of(i * 192 + 96, 8), 96)
        return wide_ref[high, 0:128] + (wide_ref[high, 128:256] + wide_ref[low, 0:128])

    def reduce(half, i):
        other = half * 4 + i
        part_ref[other] = part(i)
        pltpu.make_async_remote_copy(
            src_ref=part_ref.at[other],
            dst_ref=rr_ref.at[group],
            send_sem=send_sems.at[1],
            recv_sem=recv_sems.at[1],
            device_id=in_cube(other),
            device_id_type=MESH,
        ).start()

    def reduce_far(i, _):
        reduce(1 - pz, (px + 2 * py + i) % 4)
        return 0

    def reduce_near(i, _):
        reduce(pz, (px + 2 * py + i) % 4)
        return 0

    products(1 - pz)
    lax.fori_loop(0, 4, reduce_far, 0)
    products(pz)
    lax.fori_loop(1, 4, reduce_near, 0)
    rr_ref[group] = part(px + 2 * py)
    pltpu.make_async_copy(rr_ref.at[0:7], rr_ref.at[0:7], recv_sems.at[1]).wait()
    for i in range(12):
        rows = slice(8 * i, 8 * i + 8)
        total = rr_ref[0, rows, :]
        for k in range(1, 8):
            total = total + rr_ref[k, rows, :]
        sum_ref[i] = total

    sums = [sum_ref[i] for i in range(12)]
    for high in range(64):
        total = None
        for i in range(12):
            term = h_ref[i, :, high : high + 1] * sums[i]
            total = term if total is None else total + term
        tile_ref[high] = total

    mine = z // 2 + 2 * y + 8 * x + 32 * pz
    here = out_ref.at[
        pl.ds(pl.multiple_of((px + 2 * py) * 8, 8), 8), pl.ds(pl.multiple_of(block * 128, 128), 128)
    ]
    own = core == pz

    def deliver(step, _):
        high = (mine + step) % 64

        @pl.when(jnp.logical_or(step != 0, jnp.logical_not(own)))
        def _():
            pltpu.make_async_remote_copy(
                src_ref=tile_ref.at[high],
                dst_ref=here,
                send_sem=send_sems.at[2],
                recv_sem=recv_sems.at[2],
                device_id=device((high // 8) % 4, (high // 2) % 4, 2 * (high % 2) + high // 32, pz),
                device_id_type=MESH,
            ).start()

        return 0

    lax.fori_loop(0, 64, deliver, 0)

    @pl.when(own)
    def _():
        pltpu.make_async_copy(tile_ref.at[mine], here, recv_sems.at[2]).start()

    pltpu.make_async_copy(xr_ref.at[0:15], xr_ref.at[0:15], send_sems.at[0]).wait()
    pltpu.make_async_copy(part_ref.at[0:7], part_ref.at[0:7], send_sems.at[1]).wait()

    @pl.when(own)
    def _():
        pltpu.make_async_copy(tile_ref.at[0:63], tile_ref.at[0:63], send_sems.at[2]).wait()

    @pl.when(jnp.logical_not(own))
    def _():
        pltpu.make_async_copy(tile_ref, tile_ref, send_sems.at[2]).wait()

    pltpu.make_async_copy(out_ref, out_ref, recv_sems.at[2]).wait()


def shards(traces, phase_coef):
    return pl.pallas_call(
        kernel,
        out_shape=jax.ShapeDtypeStruct((32, 2048), F32),
        in_specs=[
            pl.BlockSpec(memory_space=pl.ANY),
            pl.BlockSpec(memory_space=pl.ANY),
            pl.BlockSpec(memory_space=pl.ANY),
        ],
        out_specs=pl.BlockSpec(memory_space=pltpu.VMEM),
        scratch_shapes=[
            pltpu.SMEM((2, 4), F32),
            pltpu.VMEM((40, 128), F32),
            pltpu.VMEM((3, 36, 8, 128), F32),
            pltpu.VMEM((4, 6, 8, 128), F32),
            pltpu.VMEM((12, 4, 8, 128), F32),
            pltpu.VMEM((12, 4, 8, 128), F32),
            pltpu.VMEM((12, 4, 8, 128), F32),
            pltpu.VMEM((12, 4, 8, 128), F32),
            pltpu.VMEM((1536, 512), BF16),
            pltpu.VMEM((12, 8, 128), F32),
            pltpu.VMEM((16, 32, 128), F32),
            pltpu.VMEM((512, 256), BF16),
            pltpu.VMEM((768, 256), F32),
            pltpu.VMEM((8, 96, 128), F32),
            pltpu.VMEM((8, 96, 128), F32),
            pltpu.VMEM((12, 8, 128), F32),
            pltpu.VMEM((64, 8, 128), F32),
            pltpu.SemaphoreType.DMA((3,)),
            pltpu.SemaphoreType.DMA((5,)),
        ],
        compiler_params=pltpu.CompilerParams(
            collective_id=0, has_side_effects=True, vmem_limit_bytes=60 * 2**20
        ),
    )(traces, phase_coef, jnp.asarray(tail_table()))


def solution(mesh):
    placed = (P(("gx", "gy"), None), P())
    return jax.shard_map(
        shards, mesh=mesh, in_specs=placed, out_specs=P(("gx", "gy"), None), check_vma=False
    )
```

```python
import functools

import jax
import jax.numpy as jnp
import numpy as np
from jax import lax
from jax.experimental import pallas as pl
from jax.experimental.pallas import tpu as pltpu
from jax.sharding import PartitionSpec as P

ORDER = 6
MESH = pl.DeviceIdType.MESH
F32 = jnp.float32
BF16 = jnp.bfloat16
AMP = 64.0

NODES = 0.5 * np.cos(np.pi * (2.0 * np.arange(ORDER) + 1.0) / (2.0 * ORDER))


def lagrange(points):
    points = np.asarray(points)[..., None, None]
    same = np.eye(ORDER, dtype=bool)
    spread = np.where(same, 1.0, NODES[:, None] - NODES[None, :])
    return np.where(same, 1.0, (points - NODES[None, :]) / spread).prod(-1)


CENTRE = lagrange(0.0)
HALVES = np.stack([((side - 0.5) + NODES) * 0.5 for side in (0, 1)])
TABLE = lagrange(HALVES)
WEIGHT = np.transpose(TABLE, (0, 2, 1))


def tail_table():
    out = np.zeros((64, ORDER, ORDER))
    for high in range(64):
        total = np.eye(ORDER)
        for place in range(6):
            total = TABLE[(high >> place) & 1] @ total
        out[high] = total
    flat = out.transpose(1, 2, 0).reshape(36, 64)
    return np.pad(np.concatenate([flat, flat], axis=1), ((0, 4), (0, 0))).astype(np.float32)


def fit(function, terms):
    u = 0.125 + 0.125 * np.cos(np.pi * (np.arange(200) + 0.5) / 200)
    poly = np.polynomial.chebyshev.Chebyshev.fit(u, function(np.sqrt(u)), terms - 1, domain=[0, 0.25])
    return [float(c) for c in poly.convert(kind=np.polynomial.Polynomial).coef]


SIN = fit(lambda r: np.sin(np.pi * r) / r, 5)
SIN2 = [2.0 * c for c in fit(lambda r: np.sin(np.pi * r) / r, 4)]
COS = fit(lambda r: np.cos(np.pi * r), 5)


def horner(coefs, u):
    total = coefs[-1]
    for c in coefs[-2::-1]:
        total = total * u + c
    return total


def turn(c):
    r = c - jnp.floor(c + 0.5)
    u = r * r
    twice = r * horner(SIN2, u)
    half_cos = horner(COS, u)
    return 1.0 - (0.5 * twice) * twice, twice * half_cos


def half_turn(y):
    r = 0.5 - y
    u = r * r
    return r * horner(SIN, u), horner(COS, u)


def bend_value(coef, row, y):
    cosine = (0.5 - y) * horner(SIN, (0.5 - y) * (0.5 - y))
    c0, c1, c2, c3 = (coef[row, m] for m in range(4))
    return (c0 - c2) + cosine * ((c1 - 3.0 * c3) + cosine * (2.0 * c2 + cosine * (4.0 * c3)))


def bend_step(coef, middle, size):
    e1, e2, e3 = (coef[0, m] * float(-2.0 * AMP * np.sin(np.pi * m * size / 2.0)) for m in (1, 2, 3))
    cosine, sine = half_turn(middle)
    return sine * ((e1 - e3) + cosine * (2.0 * e2 + cosine * (4.0 * e3)))


def apply_real(weights, values):
    out = []
    for t in range(ORDER):
        total = weights[t][0] * values[0]
        for s in range(1, ORDER):
            total = total + weights[t][s] * values[s]
        out.append(total)
    return out


def iota(axis):
    return lax.broadcasted_iota(jnp.int32, (8, 128), axis)


def asf(value):
    return value.astype(F32)


def position():
    gx, gy = lax.axis_index("gx"), lax.axis_index("gy")
    return gx % 4, gy // 4, ((gy // 2) % 2) * 2 + gx // 4, gy % 2


def device(x, y, z, core):
    return {"gx": (z % 2) * 4 + x, "gy": y * 4 + (z // 2) * 2 + core}


def lane_parts(x, y, z):
    lane = iota(1)
    place = lane // 16
    box = (place % 2) + 4 * ((place // 2) % 2) + 16 * (place // 4)
    box = box + (2 * (y % 2) + 8 * (x % 2) + 32 * (z % 2))
    top = lane % 16
    return box, top


def early_levels(coef, box, top, v_ref):
    sub = iota(0)
    bits = [asf(sub % 2), asf((sub // 2) % 2), asf(sub // 4)]
    sign = [2.0 * bit - 1.0 for bit in bits]
    x0 = jnp.full((8, 128), 0.5, F32)
    x1 = x0 + sign[0] * 0.25
    x2 = x1 + sign[1] * 0.125
    word4 = asf(box * 16 + top)
    steps = bend_step(coef, x0 + sign[0] * 0.125, 0.25)
    p0_mid = coef[0, 0] - coef[0, 2]
    first = {}
    for j0 in range(2):
        outs = []
        for j1 in range(2):
            j = j0 + 2 * j1
            word = word4 * 4.0 + j
            start = 0.5 * (j0 + 0.5) + AMP * p0_mid * bend_value(coef, 1, (word + 0.5) * 2.0**-12)
            cosines, sines = [], []
            for s in range(ORDER):
                node = float(NODES[s])
                p1 = bend_value(coef, 1, (word + (0.5 + node)) * 2.0**-12)
                c, d = turn(start + sign[0] * ((j + 0.5 + node) * 0.25 + steps * p1))
                cosines.append(c)
                sines.append(d)
            outs.append((cosines, sines))
        weights = [[float(WEIGHT[j0][t][s] * CENTRE[s]) for s in range(ORDER)] for t in range(ORDER)]
        joined = [[jnp.stack([outs[0][c][s], outs[1][c][s]]) for s in range(ORDER)] for c in range(2)]
        first[j0] = [apply_real(weights, joined[c]) for c in range(2)]
    steps = bend_step(coef, x1 + sign[1] * 0.0625, 0.125)
    second = {}
    for j1 in range(2):
        word = word4 * 2.0 + j1
        linear = j1 + 2.0 * asf(top % 2) + 0.5
        real, imag = [], []
        for s in range(ORDER):
            node = float(NODES[s])
            p1 = bend_value(coef, 1, (word + (0.5 + node)) * 2.0**-11)
            c, d = turn(sign[1] * ((linear + node) * 0.25 + steps * p1))
            a = jnp.stack([first[0][0][s][j1], first[1][0][s][j1]])
            b = jnp.stack([first[0][1][s][j1], first[1][1][s][j1]])
            real.append(a * c - b * d)
            imag.append(a * d + b * c)
        weights = [[float(WEIGHT[j1][t][s]) for s in range(ORDER)] for t in range(ORDER)]
        second[j1] = (apply_real(weights, real), apply_real(weights, imag))
    steps = bend_step(coef, x2 + sign[2] * 0.03125, 0.0625)
    linear = asf(top % 4) + 0.5
    real, imag = [], []
    for s in range(ORDER):
        node = float(NODES[s])
        p1 = bend_value(coef, 1, (word4 + (0.5 + node)) * 2.0**-10)
        c, d = turn(sign[2] * ((linear + node) * 0.25 + steps * p1))
        a = jnp.concatenate([second[0][0][s], second[1][0][s]])
        b = jnp.concatenate([second[0][1][s], second[1][1][s]])
        real.append(a * c - b * d)
        imag.append(a * d + b * c)
    weights = lane_weights(top % 2)
    for c, values in enumerate((real, imag)):
        for t, value in enumerate(apply_real(weights, values)):
            v_ref[2 * t + c] = value


def lane_weights(bit):
    pick = bit == 1
    return [
        [jnp.where(pick, float(WEIGHT[1][t][s]), float(WEIGHT[0][t][s])) for s in range(ORDER)]
        for t in range(ORDER)
    ]


def late_setup(coef, box, top, w_ref, p_ref, c_ref):
    for i, level in enumerate((4, 5, 6)):
        weights = lane_weights((top // 2 ** (level - 3)) % 2)
        for t in range(ORDER):
            for s in range(ORDER):
                w_ref[i, ORDER * t + s] = weights[t][s]
        word = asf(box * 2 ** (7 - level) + top // 2 ** (level - 3))
        for s in range(ORDER):
            p_ref[i, s] = bend_value(coef, 1, (word + float(0.5 + NODES[s])) * 2.0 ** (level - 13))
    for s in range(ORDER):
        p_ref[3, s] = bend_value(coef, 1, (asf(box) + float(0.5 + NODES[s])) * 2.0**-6)
    turn_of = top % 8

    def by_lane(values):
        out = jnp.full((8, 128), float(values[ORDER - 1]), F32)
        for t in range(ORDER - 1):
            out = jnp.where(turn_of == t, float(values[t]), out)
        return out

    e1, e2, e3 = (coef[0, m] * by_lane(-2.0 * AMP * np.sin(np.pi * m * NODES / 128.0)) for m in (1, 2, 3))
    node = by_lane(NODES)
    c_ref[0] = node
    c_ref[1] = e1 - e3
    c_ref[2] = 2.0 * e2
    c_ref[3] = 4.0 * e3
    c_ref[4] = node * (asf(box) + 0.5)


def spread(value, t):
    return jnp.take_along_axis(value, (iota(1) // 8) * 8 + t, axis=1)


def late_levels(coef, box, top, side, w_ref, p_ref, c_ref, v3, v4, v5, g_ref, between):
    sub = iota(0)
    x3 = asf(4 * (sub % 2) + 2 * ((sub // 2) % 2) + sub // 4) * 0.125 + 0.0625
    full = box * 16 + top
    states = {3: v3, 4: v4, 5: v5}

    def turns(level, parent, sign):
        i = level - 4
        steps = bend_step(coef, parent + sign * 2.0 ** -(level + 2), 2.0 ** -(level + 1))
        linear = asf((full // 2 ** (level - 3)) % 4) + 0.5
        return [turn(sign * ((linear + float(NODES[s])) * 0.25 + steps * p_ref[i, s])) for s in range(ORDER)]

    def level_step(level, parent, bit):
        i = level - 4
        sign = (2 * bit - 1).astype(F32)
        source, target = states[level - 1], states[level]
        real, imag = [], []
        for s, (c, d) in enumerate(turns(level, parent, sign)):
            a, b = source[2 * s], source[2 * s + 1]
            real.append(a * c - b * d)
            imag.append(a * d + b * c)
        weights = [[w_ref[i, ORDER * t + s] for s in range(ORDER)] for t in range(ORDER)]
        for c, values in enumerate((real, imag)):
            for t, value in enumerate(apply_real(weights, values)):
                target[2 * t + c] = value
        return parent + sign * 2.0 ** -(level + 1)

    def last_step(parent, bit, place):
        sign = (2 * bit - 1).astype(F32)
        middle = parent + sign * 2.0**-7 + c_ref[0] * (1.0 / 128.0)
        cosine, sine = half_turn(middle)
        steps = sine * (c_ref[1] + cosine * (c_ref[2] + cosine * c_ref[3]))
        switch = [turn((c_ref[4] + c_ref[0] * float(NODES[u])) + steps * p_ref[3, u]) for u in range(ORDER)]
        merged = []
        for s, (c, d) in enumerate(turns(6, parent, sign)):
            a = b = None
            for u in range(ORDER):
                weight = w_ref[2, ORDER * u + s]
                a = switch[u][0] * weight if a is None else a + switch[u][0] * weight
                b = switch[u][1] * weight if b is None else b + switch[u][1] * weight
            merged.append((a * c - b * d, a * d + b * c))
        for t in range(ORDER):
            real = imag = None
            for s in range(ORDER):
                c, d = spread(merged[s][0], t), spread(merged[s][1], t)
                a, b = v5[2 * s], v5[2 * s + 1]
                real = a * c - b * d if real is None else real + (a * c - b * d)
                imag = a * d + b * c if imag is None else imag + (a * d + b * c)
            rows = pl.ds(pl.multiple_of(place * 192 + 16 * t, 16), 16)
            rows_low = pl.ds(pl.multiple_of(place * 192 + 96 + 16 * t, 16), 16)
            for j in range(4):
                both = jnp.concatenate([real[j], imag[j]], axis=0)
                high = both.astype(BF16)
                g_ref[rows, 128 * j : 128 * (j + 1)] = high
                g_ref[rows_low, 128 * j : 128 * (j + 1)] = (both - high.astype(F32)).astype(BF16)

    x4 = level_step(4, x3, side)

    def over4(q4, _):
        pl.when(q4 == 1)(between)
        x5 = level_step(5, x4, q4)

        def over5(q5, _):
            last_step(x5, q5, q4 + 2 * q5)
            return 0

        return lax.fori_loop(0, 2, over5, 0)

    lax.fori_loop(0, 2, over4, 0)


def last_weights(coef, group, tail_ref, h_ref):
    sub, lane = iota(0), iota(1)
    box6 = 32 * (sub % 2) + 16 * ((sub // 2) % 2) + 8 * (sub // 4)
    box6 = box6 + (4 * (group % 2) + 2 * ((group // 2) % 2) + group // 4)
    inner = 0
    for place in range(6):
        inner = inner + ((lane // 2**place) % 2) * 2 ** (5 - place)
    centre = (asf(box6 * 64 + inner) + 0.5) * 2.0**-12
    p1_mid = coef[1, 0] - coef[1, 2]
    real = [None] * ORDER
    imag = [None] * ORDER
    for t in range(ORDER):
        node = float(NODES[t])
        steps = bend_step(coef, centre + node / 8192.0, node / 4096.0)
        c, d = turn(-0.5 * node - steps * p1_mid)
        c, d = c * float(CENTRE[t]), d * float(CENTRE[t])
        for s in range(ORDER):
            row = tail_ref[ORDER * t + s : ORDER * t + s + 1, :]
            real[s] = c * row if t == 0 else real[s] + c * row
            imag[s] = d * row if t == 0 else imag[s] + d * row
    for s in range(ORDER):
        h_ref[2 * s] = real[s]
        h_ref[2 * s + 1] = -imag[s]


def kernel(
    x_ref,
    coef_hbm,
    tail_hbm,
    out_ref,
    coef_ref,
    tail_ref,
    w_ref,
    p_ref,
    c_ref,
    v3,
    v4,
    v5,
    g_ref,
    h_ref,
    xr_ref,
    xf_ref,
    xs_ref,
    wide_ref,
    part_ref,
    rr_ref,
    sum_ref,
    tile_ref,
    send_sems,
    recv_sems,
):
    fetch_coef = pltpu.make_async_copy(coef_hbm, coef_ref, recv_sems.at[3])
    fetch_tail = pltpu.make_async_copy(tail_hbm, tail_ref, recv_sems.at[4])
    fetch_coef.start()
    fetch_tail.start()
    x, y, z, core = position()
    px, py, pz = x % 2, y % 2, z % 2
    group = px + 2 * py + 4 * pz
    block = ((x + core) // 2) % 2 + 2 * (((y + core) // 2) % 2) + 4 * (((z + core) // 2) % 2) + 8 * core
    slot = 2 * (z // 2 + 2 * (y // 2) + 4 * (x // 2)) + core
    lone = core == px

    def same_parity(i):
        return device(px + 2 * (i // 8), py + 2 * ((i // 4) % 2), pz + 2 * ((i // 2) % 2), i % 2)

    def in_cube(tiling, g, on):
        spin = 1 - 2 * tiling
        a = (2 * ((x + tiling) // 2) + spin * (g % 2) + 4) % 4
        b = (2 * ((y + tiling) // 2) + spin * ((g // 2) % 2) + 4) % 4
        c = (2 * ((z + tiling) // 2) + spin * (g // 4) + 4) % 4
        return device(a, b, c, on)

    barrier = pltpu.get_barrier_semaphore()
    own_place = 8 * (x // 2) + 4 * (y // 2) + 2 * (z // 2) + core

    def greet_class(i, _):
        other = (own_place + i) % 16
        pl.semaphore_signal(barrier, inc=1, device_id=same_parity(other), device_id_type=MESH)
        return 0

    lax.fori_loop(1, 16, greet_class, 0)

    def greet_cube(step, _):
        other = (group + step) % 8
        pl.semaphore_signal(barrier, inc=1, device_id=in_cube(core, other, px), device_id_type=MESH)
        return 0

    lax.fori_loop(1, 8, greet_cube, 0)

    @pl.when(jnp.logical_not(lone))
    def _():
        pl.semaphore_signal(barrier, inc=1, device_id=in_cube(core, group, px), device_id_type=MESH)
        pl.semaphore_wait(barrier, 23)

    @pl.when(lone)
    def _():
        pl.semaphore_wait(barrier, 22)

    def scatter(step, _):
        m = (block + step) % 16
        turned = 1 - 2 * (m // 8)
        a = (2 * (m % 2) + turned * px + 4) % 4
        b = (2 * ((m // 2) % 2) + turned * py + 4) % 4
        c = (2 * ((m // 4) % 2) + turned * pz + 4) % 4
        pltpu.make_async_remote_copy(
            src_ref=x_ref.at[:, pl.ds(pl.multiple_of(m * 128, 128), 128)],
            dst_ref=xr_ref.at[slot],
            send_sem=send_sems.at[0],
            recv_sem=recv_sems.at[0],
            device_id=device(a, b, c, m // 8),
            device_id_type=MESH,
        ).start()
        return 0

    lax.fori_loop(1, 16, scatter, 0)
    pltpu.make_async_copy(
        x_ref.at[:, pl.ds(pl.multiple_of(block * 128, 128), 128)], xr_ref.at[slot], recv_sems.at[0]
    ).start()

    forward = pltpu.make_async_remote_copy(
        src_ref=xr_ref,
        dst_ref=xf_ref,
        send_sem=send_sems.at[3],
        recv_sem=recv_sems.at[5],
        device_id=device(x, y, z, 1 - core),
        device_id_type=MESH,
    )

    def hand_over():
        pltpu.make_async_copy(xr_ref, xr_ref, recv_sems.at[0]).wait()
        forward.start()

    box, top = lane_parts(x, y, z)
    fetch_coef.wait()
    early_levels(coef_ref, box, top, v3)
    late_setup(coef_ref, box, top, w_ref, p_ref, c_ref)
    late_levels(coef_ref, box, top, core, w_ref, p_ref, c_ref, v3, v4, v5, g_ref, hand_over)
    fetch_tail.wait()
    last_weights(coef_ref, group, tail_ref, h_ref)

    def split(source, start):
        for i in range(8):
            for j in range(4):
                piece = jnp.concatenate([source[2 * i + s, pl.ds(j, 8, stride=4), :] for s in range(2)], axis=0)
                high = piece.astype(BF16)
                rows = slice(128 * j + 16 * i, 128 * j + 16 * i + 16)
                xs_ref[rows, start : start + 128] = high
                xs_ref[rows, start + 128 : start + 256] = (piece - high.astype(F32)).astype(BF16)

    split(xr_ref, 0)
    forward.wait_recv()
    split(xf_ref, 256)

    def products(half):
        rows = pl.ds(pl.multiple_of(half * 384, 16), 384)
        wide_ref[...] = jnp.dot(g_ref[rows, :], xs_ref[...], preferred_element_type=F32)

    def part(i, start):
        high = pl.ds(pl.multiple_of(i * 192, 8), 96)
        low = pl.ds(pl.multiple_of(i * 192 + 96, 8), 96)
        return wide_ref[high, start : start + 128] + (
            wide_ref[high, start + 128 : start + 256] + wide_ref[low, start : start + 128]
        )

    def reduce(half, i):
        other = core + 2 * i + 4 * half
        for flip in range(2):
            tiling = core if flip == 0 else 1 - core
            here = part_ref.at[4 * flip + 2 * half + i]
            here[...] = part(i, 256 * flip)

            def send():
                pltpu.make_async_remote_copy(
                    src_ref=here,
                    dst_ref=rr_ref.at[group],
                    send_sem=send_sems.at[1],
                    recv_sem=recv_sems.at[1],
                    device_id=in_cube(tiling, other, tiling),
                    device_id_type=MESH,
                ).start()

            if flip == 0:
                pl.when(other != group)(send)
            else:
                send()

    def reduce_half(half):
        products(half)

        def body(i, _):
            reduce(half, (py + 1 + i) % 2)
            return 0

        lax.fori_loop(0, 2, body, 0)

    reduce_half(1 - pz)
    reduce_half(pz)

    @pl.when(lone)
    def _():
        rr_ref[group] = part_ref[2 * pz + py]
        pltpu.make_async_copy(rr_ref.at[0:7], rr_ref.at[0:7], recv_sems.at[1]).wait()

    @pl.when(jnp.logical_not(lone))
    def _():
        pltpu.make_async_copy(rr_ref, rr_ref, recv_sems.at[1]).wait()

    for i in range(12):
        rows = slice(8 * i, 8 * i + 8)
        total = rr_ref[0, rows, :]
        for k in range(1, 8):
            total = total + rr_ref[k, rows, :]
        sum_ref[i] = total

    sums = [sum_ref[i] for i in range(12)]
    for high in range(64):
        total = None
        for i in range(12):
            term = h_ref[i, :, high : high + 1] * sums[i]
            total = term if total is None else total + term
        tile_ref[high] = total

    mine = z // 2 + 2 * y + 8 * x + 32 * pz
    here = out_ref.at[
        pl.ds(pl.multiple_of((px + 2 * py) * 8, 8), 8), pl.ds(pl.multiple_of(block * 128, 128), 128)
    ]
    own = core == pz

    def deliver(step, _):
        high = (mine + step) % 64

        @pl.when(jnp.logical_or(step != 0, jnp.logical_not(own)))
        def _():
            pltpu.make_async_remote_copy(
                src_ref=tile_ref.at[high],
                dst_ref=here,
                send_sem=send_sems.at[2],
                recv_sem=recv_sems.at[2],
                device_id=device((high // 8) % 4, (high // 2) % 4, 2 * (high % 2) + high // 32, pz),
                device_id_type=MESH,
            ).start()

        return 0

    lax.fori_loop(0, 64, deliver, 0)

    @pl.when(own)
    def _():
        pltpu.make_async_copy(tile_ref.at[mine], here, recv_sems.at[2]).start()

    pltpu.make_async_copy(xr_ref.at[0:15], xr_ref.at[0:15], send_sems.at[0]).wait()
    forward.wait_send()

    @pl.when(lone)
    def _():
        pltpu.make_async_copy(part_ref.at[0:7], part_ref.at[0:7], send_sems.at[1]).wait()

    @pl.when(jnp.logical_not(lone))
    def _():
        pltpu.make_async_copy(part_ref, part_ref, send_sems.at[1]).wait()


    @pl.when(own)
    def _():
        pltpu.make_async_copy(tile_ref.at[0:63], tile_ref.at[0:63], send_sems.at[2]).wait()

    @pl.when(jnp.logical_not(own))
    def _():
        pltpu.make_async_copy(tile_ref, tile_ref, send_sems.at[2]).wait()

    pltpu.make_async_copy(out_ref, out_ref, recv_sems.at[2]).wait()


def shards(traces, phase_coef):
    return pl.pallas_call(
        kernel,
        out_shape=jax.ShapeDtypeStruct((32, 2048), F32),
        in_specs=[
            pl.BlockSpec(memory_space=pl.ANY),
            pl.BlockSpec(memory_space=pl.ANY),
            pl.BlockSpec(memory_space=pl.ANY),
        ],
        out_specs=pl.BlockSpec(memory_space=pltpu.VMEM),
        scratch_shapes=[
            pltpu.SMEM((2, 4), F32),
            pltpu.VMEM((40, 128), F32),
            pltpu.VMEM((3, 36, 8, 128), F32),
            pltpu.VMEM((4, 6, 8, 128), F32),
            pltpu.VMEM((5, 8, 128), F32),
            pltpu.VMEM((12, 4, 8, 128), F32),
            pltpu.VMEM((12, 4, 8, 128), F32),
            pltpu.VMEM((12, 4, 8, 128), F32),
            pltpu.VMEM((768, 512), BF16),
            pltpu.VMEM((12, 8, 128), F32),
            pltpu.VMEM((16, 32, 128), F32),
            pltpu.VMEM((16, 32, 128), F32),
            pltpu.VMEM((512, 512), BF16),
            pltpu.VMEM((384, 512), F32),
            pltpu.VMEM((8, 96, 128), F32),
            pltpu.VMEM((8, 96, 128), F32),
            pltpu.VMEM((12, 8, 128), F32),
            pltpu.VMEM((64, 8, 128), F32),
            pltpu.SemaphoreType.DMA((4,)),
            pltpu.SemaphoreType.DMA((6,)),
        ],
        compiler_params=pltpu.CompilerParams(
            collective_id=0, has_side_effects=True, vmem_limit_bytes=60 * 2**20
        ),
    )(traces, phase_coef, jnp.asarray(tail_table()))


def solution(mesh):
    placed = (P(("gx", "gy"), None), P())
    return jax.shard_map(
        shards, mesh=mesh, in_specs=placed, out_specs=P(("gx", "gy"), None), check_vma=False
    )
```

```python
import functools

import jax
import jax.numpy as jnp
import numpy as np
from jax import lax
from jax.experimental import pallas as pl
from jax.experimental.pallas import tpu as pltpu
from jax.sharding import PartitionSpec as P

ORDER = 6
MESH = pl.DeviceIdType.MESH
F32 = jnp.float32
BF16 = jnp.bfloat16
AMP = 64.0

NODES = 0.5 * np.cos(np.pi * (2.0 * np.arange(ORDER) + 1.0) / (2.0 * ORDER))


def lagrange(points):
    points = np.asarray(points)[..., None, None]
    same = np.eye(ORDER, dtype=bool)
    spread = np.where(same, 1.0, NODES[:, None] - NODES[None, :])
    return np.where(same, 1.0, (points - NODES[None, :]) / spread).prod(-1)


CENTRE = lagrange(0.0)
HALVES = np.stack([((side - 0.5) + NODES) * 0.5 for side in (0, 1)])
TABLE = lagrange(HALVES)
WEIGHT = np.transpose(TABLE, (0, 2, 1))


def tail_table():
    out = np.zeros((ORDER, 64, 128))
    for high in range(64):
        total = np.eye(ORDER)
        for place in range(6):
            total = TABLE[(high >> place) & 1] @ total
        out[:, high, :96] = np.repeat(CENTRE[:, None] * total, 16, axis=1)
    return out.astype(np.float32)


def fit(function, terms):
    u = 0.125 + 0.125 * np.cos(np.pi * (np.arange(200) + 0.5) / 200)
    poly = np.polynomial.chebyshev.Chebyshev.fit(u, function(np.sqrt(u)), terms - 1, domain=[0, 0.25])
    return [float(c) for c in poly.convert(kind=np.polynomial.Polynomial).coef]


SIN = fit(lambda r: np.sin(np.pi * r) / r, 5)
SIN2 = [2.0 * c for c in fit(lambda r: np.sin(np.pi * r) / r, 4)]
COS = fit(lambda r: np.cos(np.pi * r), 5)


def horner(coefs, u):
    total = coefs[-1]
    for c in coefs[-2::-1]:
        total = total * u + c
    return total


def turn(c):
    r = c - jnp.floor(c + 0.5)
    u = r * r
    twice = r * horner(SIN2, u)
    half_cos = horner(COS, u)
    return 1.0 - (0.5 * twice) * twice, twice * half_cos


def turn_cos(c):
    r = c - jnp.floor(c + 0.5)
    twice = r * horner(SIN2, r * r)
    return 1.0 - (0.5 * twice) * twice


def half_turn(y):
    r = 0.5 - y
    u = r * r
    return r * horner(SIN, u), horner(COS, u)


def bend_value(coef, row, y):
    cosine = (0.5 - y) * horner(SIN, (0.5 - y) * (0.5 - y))
    c0, c1, c2, c3 = (coef[row, m] for m in range(4))
    return (c0 - c2) + cosine * ((c1 - 3.0 * c3) + cosine * (2.0 * c2 + cosine * (4.0 * c3)))


def bend_step(coef, middle, size):
    e1, e2, e3 = (coef[0, m] * float(-2.0 * AMP * np.sin(np.pi * m * size / 2.0)) for m in (1, 2, 3))
    cosine, sine = half_turn(middle)
    return sine * ((e1 - e3) + cosine * (2.0 * e2 + cosine * (4.0 * e3)))


def apply_real(weights, values):
    out = []
    for t in range(ORDER):
        total = weights[t][0] * values[0]
        for s in range(1, ORDER):
            total = total + weights[t][s] * values[s]
        out.append(total)
    return out


def iota(axis):
    return lax.broadcasted_iota(jnp.int32, (8, 128), axis)


def asf(value):
    return value.astype(F32)


def position():
    gx, gy = lax.axis_index("gx"), lax.axis_index("gy")
    return gx % 4, gy // 4, ((gy // 2) % 2) * 2 + gx // 4, gy % 2


def device(x, y, z, core):
    return {"gx": (z % 2) * 4 + x, "gy": y * 4 + (z // 2) * 2 + core}


def lane_parts(classes, core):
    lane = iota(1)
    place = lane // 16
    x, y, z = (
        (2 * c + e + core) & 3 for c, e in zip(classes, (place // 4, (place // 2) % 2, place % 2))
    )
    return (z // 2) + 2 * y + 8 * x + 32 * (z % 2), lane % 16


def early_levels(coef, box, top, v_ref):
    sub = iota(0)
    bits = [asf(sub % 2), asf((sub // 2) % 2), asf(sub // 4)]
    sign = [2.0 * bit - 1.0 for bit in bits]
    x0 = jnp.full((8, 128), 0.5, F32)
    x1 = x0 + sign[0] * 0.25
    x2 = x1 + sign[1] * 0.125
    word4 = asf(box * 16 + top)
    steps = bend_step(coef, x0 + sign[0] * 0.125, 0.25)
    p0_mid = coef[0, 0] - coef[0, 2]
    first = {}
    for j0 in range(2):
        outs = []
        for j1 in range(2):
            j = j0 + 2 * j1
            word = word4 * 4.0 + j
            start = 0.5 * (j0 + 0.5) + AMP * p0_mid * bend_value(coef, 1, (word + 0.5) * 2.0**-12)
            cosines, sines = [], []
            for s in range(ORDER):
                node = float(NODES[s])
                p1 = bend_value(coef, 1, (word + (0.5 + node)) * 2.0**-12)
                c, d = turn(start + sign[0] * ((j + 0.5 + node) * 0.25 + steps * p1))
                cosines.append(c)
                sines.append(d)
            outs.append((cosines, sines))
        weights = [[float(WEIGHT[j0][t][s] * CENTRE[s]) for s in range(ORDER)] for t in range(ORDER)]
        joined = [[jnp.stack([outs[0][c][s], outs[1][c][s]]) for s in range(ORDER)] for c in range(2)]
        first[j0] = [apply_real(weights, joined[c]) for c in range(2)]
    steps = bend_step(coef, x1 + sign[1] * 0.0625, 0.125)
    second = {}
    for j1 in range(2):
        word = word4 * 2.0 + j1
        linear = j1 + 2.0 * asf(top % 2) + 0.5
        real, imag = [], []
        for s in range(ORDER):
            node = float(NODES[s])
            p1 = bend_value(coef, 1, (word + (0.5 + node)) * 2.0**-11)
            c, d = turn(sign[1] * ((linear + node) * 0.25 + steps * p1))
            a = jnp.stack([first[0][0][s][j1], first[1][0][s][j1]])
            b = jnp.stack([first[0][1][s][j1], first[1][1][s][j1]])
            real.append(a * c - b * d)
            imag.append(a * d + b * c)
        weights = [[float(WEIGHT[j1][t][s]) for s in range(ORDER)] for t in range(ORDER)]
        second[j1] = (apply_real(weights, real), apply_real(weights, imag))
    steps = bend_step(coef, x2 + sign[2] * 0.03125, 0.0625)
    linear = asf(top % 4) + 0.5
    real, imag = [], []
    for s in range(ORDER):
        node = float(NODES[s])
        p1 = bend_value(coef, 1, (word4 + (0.5 + node)) * 2.0**-10)
        c, d = turn(sign[2] * ((linear + node) * 0.25 + steps * p1))
        a = jnp.concatenate([second[0][0][s], second[1][0][s]])
        b = jnp.concatenate([second[0][1][s], second[1][1][s]])
        real.append(a * c - b * d)
        imag.append(a * d + b * c)
    weights = lane_weights(top % 2)
    for c, values in enumerate((real, imag)):
        for t, value in enumerate(apply_real(weights, values)):
            v_ref[2 * t + c] = value


def lane_weights(bit):
    pick = bit == 1
    return [
        [jnp.where(pick, float(WEIGHT[1][t][s]), float(WEIGHT[0][t][s])) for s in range(ORDER)]
        for t in range(ORDER)
    ]


def late_setup(coef, box, top, w_ref, p_ref, c_ref):
    for i, level in enumerate((4, 5, 6)):
        weights = lane_weights((top // 2 ** (level - 3)) % 2)
        for t in range(ORDER):
            for s in range(ORDER):
                w_ref[i, ORDER * t + s] = weights[t][s]
        word = asf(box * 2 ** (7 - level) + top // 2 ** (level - 3))
        for s in range(ORDER):
            p_ref[i, s] = bend_value(coef, 1, (word + float(0.5 + NODES[s])) * 2.0 ** (level - 13))
    for s in range(ORDER):
        p_ref[3, s] = bend_value(coef, 1, (asf(box) + float(0.5 + NODES[s])) * 2.0**-6)
    turn_of = top % 8

    def by_lane(values):
        out = jnp.full((8, 128), float(values[ORDER - 1]), F32)
        for t in range(ORDER - 1):
            out = jnp.where(turn_of == t, float(values[t]), out)
        return out

    e1, e2, e3 = (coef[0, m] * by_lane(-2.0 * AMP * np.sin(np.pi * m * NODES / 128.0)) for m in (1, 2, 3))
    node = by_lane(NODES)
    c_ref[0] = node
    c_ref[1] = e1 - e3
    c_ref[2] = 2.0 * e2
    c_ref[3] = 4.0 * e3
    c_ref[4] = node * (asf(box) + 0.5)


def spread(value, t):
    return jnp.take_along_axis(value, (iota(1) // 8) * 8 + t, axis=1)


def late_levels(coef, box, top, w_ref, p_ref, c_ref, v3, v4, v5, g_ref):
    sub = iota(0)
    x3 = asf(4 * (sub % 2) + 2 * ((sub // 2) % 2) + sub // 4) * 0.125 + 0.0625
    full = box * 16 + top
    states = {3: v3, 4: v4, 5: v5}

    def turns(level, parent, sign):
        i = level - 4
        steps = bend_step(coef, parent + sign * 2.0 ** -(level + 2), 2.0 ** -(level + 1))
        linear = asf((full // 2 ** (level - 3)) % 4) + 0.5
        return [turn(sign * ((linear + float(NODES[s])) * 0.25 + steps * p_ref[i, s])) for s in range(ORDER)]

    def level_step(level, parent, bit):
        i = level - 4
        sign = (2 * bit - 1).astype(F32)
        source, target = states[level - 1], states[level]
        real, imag = [], []
        for s, (c, d) in enumerate(turns(level, parent, sign)):
            a, b = source[2 * s], source[2 * s + 1]
            real.append(a * c - b * d)
            imag.append(a * d + b * c)
        weights = [[w_ref[i, ORDER * t + s] for s in range(ORDER)] for t in range(ORDER)]
        for c, values in enumerate((real, imag)):
            for t, value in enumerate(apply_real(weights, values)):
                target[2 * t + c] = value
        return parent + sign * 2.0 ** -(level + 1)

    def last_step(parent, bit, place):
        sign = (2 * bit - 1).astype(F32)
        middle = parent + sign * 2.0**-7 + c_ref[0] * (1.0 / 128.0)
        cosine, sine = half_turn(middle)
        steps = sine * (c_ref[1] + cosine * (c_ref[2] + cosine * c_ref[3]))
        switch = [turn((c_ref[4] + c_ref[0] * float(NODES[u])) + steps * p_ref[3, u]) for u in range(ORDER)]
        merged = []
        for s, (c, d) in enumerate(turns(6, parent, sign)):
            a = b = None
            for u in range(ORDER):
                weight = w_ref[2, ORDER * u + s]
                a = switch[u][0] * weight if a is None else a + switch[u][0] * weight
                b = switch[u][1] * weight if b is None else b + switch[u][1] * weight
            merged.append((a * c - b * d, a * d + b * c))
        for t in range(ORDER):
            real = imag = None
            for s in range(ORDER):
                c, d = spread(merged[s][0], t), spread(merged[s][1], t)
                a, b = v5[2 * s], v5[2 * s + 1]
                real = a * c - b * d if real is None else real + (a * c - b * d)
                imag = a * d + b * c if imag is None else imag + (a * d + b * c)
            rows = pl.ds(pl.multiple_of(place * 192 + 16 * t, 16), 16)
            rows_low = pl.ds(pl.multiple_of(place * 192 + 96 + 16 * t, 16), 16)
            for j in range(4):
                both = jnp.concatenate([real[j], imag[j]], axis=0)
                high = both.astype(BF16)
                g_ref[rows, 128 * j : 128 * (j + 1)] = high
                g_ref[rows_low, 128 * j : 128 * (j + 1)] = (both - high.astype(F32)).astype(BF16)

    def over3(q3, _):
        x4 = level_step(4, x3, q3)

        def over4(q4, _):
            x5 = level_step(5, x4, q4)

            def over5(q5, _):
                last_step(x5, q5, q3 + 2 * q4 + 4 * q5)
                return 0

            return lax.fori_loop(0, 2, over5, 0)

        return lax.fori_loop(0, 2, over4, 0)

    lax.fori_loop(0, 2, over3, 0)


def last_weights(coef, group, tail_ref, h_ref):
    sub, lane = iota(0), iota(1)
    own = lane % 8
    same = sub == own
    box6 = 32 * (own % 2) + 16 * ((own // 2) % 2) + 8 * (own // 4)
    box6 = box6 + (4 * (group % 2) + 2 * ((group // 2) % 2) + group // 4)
    inner = 32 * (sub % 2) + 16 * ((sub // 2) % 2) + 8 * (sub // 4)
    base = box6 * 64 + inner
    quarter = 0.25 * asf((lane // 8) % 2)
    p1_mid = coef[1, 0] - coef[1, 2]

    def rows_of(r):
        centre = (asf(base + (4 * (r % 2) + 2 * ((r // 2) % 2) + r // 4)) + 0.5) * 2.0**-12
        total = None
        for t in range(ORDER):
            node = float(NODES[t])
            steps = bend_step(coef, centre + node / 8192.0, node / 4096.0)
            term = turn_cos((quarter - 0.5 * node) - steps * p1_mid)
            term = term * tail_ref[t, pl.ds(pl.multiple_of(8 * r, 8), 8), :]
            total = term if total is None else total + term
        return total

    def body(i, _):
        for half in range(2):
            total = rows_of(2 * i + half)
            for k in range(0, 8, 2):
                both = jnp.concatenate(
                    [jnp.where(same, jnp.broadcast_to(total[k + n : k + n + 1], (8, 128)), 0.0) for n in range(2)], axis=0
                )
                high = both.astype(BF16)
                row = 64 * half + 8 * k
                h_ref[pl.ds(pl.multiple_of(256 * i + row, 16), 16), :] = high
                h_ref[pl.ds(pl.multiple_of(256 * i + 128 + row, 16), 16), :] = (both - high.astype(F32)).astype(BF16)
        return 0

    lax.fori_loop(0, 4, body, 0)


def kernel(
    x_ref,
    coef_hbm,
    tail_hbm,
    out_ref,
    coef_ref,
    tail_ref,
    w_ref,
    p_ref,
    c_ref,
    v3,
    v4,
    v5,
    g_ref,
    h_ref,
    xr_ref,
    xs_ref,
    wide_ref,
    part_ref,
    rr_ref,
    sum_ref,
    last_ref,
    tile_ref,
    send_sems,
    recv_sems,
):
    fetch_coef = pltpu.make_async_copy(coef_hbm, coef_ref, recv_sems.at[3])
    fetch_tail = pltpu.make_async_copy(tail_hbm, tail_ref, recv_sems.at[4])
    fetch_coef.start()
    fetch_tail.start()
    chip = position()
    core = chip[3]
    own_u = [(p + 3 * core) % 4 for p in chip[:3]]
    classes = [u // 2 for u in own_u]
    groups = [((u + 3) % 4) // 2 for u in own_u]
    target = classes[0] + 2 * classes[1] + 4 * classes[2]
    block = groups[0] + 2 * groups[1] + 4 * groups[2] + 8 * core

    def bits(i):
        return i % 2, (i // 2) % 2, (i // 4) % 2

    def member(tiling, cs, gs):
        return device(*((2 * c + (g + 1 + c) % 2 + tiling) % 4 for c, g in zip(cs, gs)), tiling)

    barrier = pltpu.get_barrier_semaphore()
    own_e = (own_u[0] % 2) + 2 * (own_u[1] % 2) + 4 * (own_u[2] % 2) + 8 * core

    def greet_class(step, _):
        i = (own_e + step) % 16
        source = device(*((2 * c + e + core) % 4 for c, e in zip(classes, bits(i))), i // 8)
        pl.semaphore_signal(barrier, inc=1, device_id=source, device_id_type=MESH)
        return 0

    lax.fori_loop(1, 16, greet_class, 0)

    def greet_group(step, _):
        other = (target + step) % 8
        pl.semaphore_signal(barrier, inc=1, device_id=member(core, bits(other), groups), device_id_type=MESH)
        return 0

    lax.fori_loop(1, 8, greet_group, 0)
    pl.semaphore_wait(barrier, 22)

    def scatter(step, _):
        m = (block + step) % 16
        tiling = m // 8
        us = [(p + 3 * tiling) % 4 for p in chip[:3]]
        slot = 2 * (us[2] % 2 + 2 * (us[1] % 2) + 4 * (us[0] % 2)) + core
        pltpu.make_async_remote_copy(
            src_ref=x_ref.at[:, pl.ds(pl.multiple_of(m * 128, 128), 128)],
            dst_ref=xr_ref.at[slot],
            send_sem=send_sems.at[0],
            recv_sem=recv_sems.at[0],
            device_id=member(tiling, [u // 2 for u in us], bits(m)),
            device_id_type=MESH,
        ).start()
        return 0

    lax.fori_loop(1, 16, scatter, 0)
    slot = 2 * (own_u[2] % 2 + 2 * (own_u[1] % 2) + 4 * (own_u[0] % 2)) + core
    pltpu.make_async_copy(
        x_ref.at[:, pl.ds(pl.multiple_of(block * 128, 128), 128)], xr_ref.at[slot], recv_sems.at[0]
    ).start()

    box, top = lane_parts(classes, core)
    fetch_coef.wait()
    early_levels(coef_ref, box, top, v3)
    late_setup(coef_ref, box, top, w_ref, p_ref, c_ref)
    late_levels(coef_ref, box, top, w_ref, p_ref, c_ref, v3, v4, v5, g_ref)
    fetch_tail.wait()
    last_weights(coef_ref, target, tail_ref, h_ref)

    pltpu.make_async_copy(xr_ref, xr_ref, recv_sems.at[0]).wait()
    for i in range(8):
        for j in range(4):
            piece = jnp.concatenate([xr_ref[2 * i + s, pl.ds(j, 8, stride=4), :] for s in range(2)], axis=0)
            high = piece.astype(BF16)
            rows = slice(128 * j + 16 * i, 128 * j + 16 * i + 16)
            xs_ref[rows, 0:128] = high
            xs_ref[rows, 128:256] = (piece - high.astype(F32)).astype(BF16)

    def products(half):
        rows = pl.ds(pl.multiple_of(half * 768, 16), 768)
        wide_ref[...] = jnp.dot(g_ref[rows, :], xs_ref[...], preferred_element_type=F32)

    def part(i):
        high = pl.ds(pl.multiple_of(i * 192, 8), 96)
        low = pl.ds(pl.multiple_of(i * 192 + 96, 8), 96)
        return wide_ref[high, 0:128] + (wide_ref[high, 128:256] + wide_ref[low, 0:128])

    near = target % 4

    def reduce(half, i):
        other = half * 4 + i
        part_ref[other] = part(i)
        pltpu.make_async_remote_copy(
            src_ref=part_ref.at[other],
            dst_ref=rr_ref.at[target],
            send_sem=send_sems.at[1],
            recv_sem=recv_sems.at[1],
            device_id=member(core, bits(other), groups),
            device_id_type=MESH,
        ).start()

    def reduce_far(i, _):
        reduce(1 - classes[2], (near + i) % 4)
        return 0

    def reduce_near(i, _):
        reduce(classes[2], (near + i) % 4)
        return 0

    products(1 - classes[2])
    lax.fori_loop(0, 4, reduce_far, 0)
    products(classes[2])
    lax.fori_loop(1, 4, reduce_near, 0)
    rr_ref[target] = part(near)
    pltpu.make_async_copy(rr_ref.at[0:7], rr_ref.at[0:7], recv_sems.at[1]).wait()
    for i in range(0, 12, 2):
        rows = slice(8 * i, 8 * i + 16)
        total = rr_ref[0, rows, :]
        for k in range(1, 8):
            total = total + rr_ref[k, rows, :]
        high = total.astype(BF16)
        sum_ref[rows, 0:128] = high
        sum_ref[rows, 128:256] = (total - high.astype(F32)).astype(BF16)
    sum_ref[96:128, :] = jnp.zeros((32, 256), BF16)

    mine = chip[2] // 2 + 2 * chip[1] + 8 * chip[0] + 32 * (chip[2] % 2)
    own = core == classes[2]
    here = out_ref.at[pl.ds(pl.multiple_of(near * 8, 8), 8), pl.ds(pl.multiple_of(block * 128, 128), 128)]

    def deliver_some(step, _):
        quarter = (mine // 16 + step) % 4
        rows = pl.ds(pl.multiple_of(quarter * 256, 16), 256)
        last_ref[...] = jnp.dot(h_ref[rows, :], sum_ref[...], preferred_element_type=F32)
        tiles = last_ref[0:128, 0:128] + (last_ref[0:128, 128:256] + last_ref[128:256, 0:128])
        tile_ref[pl.ds(quarter * 16, 16)] = tiles.reshape(16, 8, 128)

        def deliver(i, _):
            place = (mine + i) % 16
            high = quarter * 16 + place

            @pl.when(jnp.logical_or(high != mine, jnp.logical_not(own)))
            def _():
                pltpu.make_async_remote_copy(
                    src_ref=tile_ref.at[high],
                    dst_ref=here,
                    send_sem=send_sems.at[2],
                    recv_sem=recv_sems.at[2],
                    device_id=device((high // 8) % 4, (high // 2) % 4, 2 * (high % 2) + high // 32, classes[2]),
                    device_id_type=MESH,
                ).start()

            return 0

        return lax.fori_loop(0, 16, deliver, 0)

    lax.fori_loop(0, 4, deliver_some, 0)

    @pl.when(own)
    def _():
        pltpu.make_async_copy(tile_ref.at[mine], here, recv_sems.at[2]).start()

    pltpu.make_async_copy(xr_ref.at[0:15], xr_ref.at[0:15], send_sems.at[0]).wait()
    pltpu.make_async_copy(part_ref.at[0:7], part_ref.at[0:7], send_sems.at[1]).wait()

    @pl.when(own)
    def _():
        pltpu.make_async_copy(tile_ref.at[0:63], tile_ref.at[0:63], send_sems.at[2]).wait()

    @pl.when(jnp.logical_not(own))
    def _():
        pltpu.make_async_copy(tile_ref, tile_ref, send_sems.at[2]).wait()

    pltpu.make_async_copy(out_ref, out_ref, recv_sems.at[2]).wait()


def write_out(in_ref, out_ref, sems):
    copies = [
        pltpu.make_async_copy(in_ref.at[8 * i : 8 * i + 8], out_ref.at[8 * i : 8 * i + 8], sems.at[i]) for i in range(4)
    ]
    for copy in copies:
        copy.start()
    for copy in copies:
        copy.wait()


def shards(traces, phase_coef):
    image = pl.pallas_call(
        kernel,
        out_shape=jax.ShapeDtypeStruct((32, 2048), F32),
        in_specs=[
            pl.BlockSpec(memory_space=pl.ANY),
            pl.BlockSpec(memory_space=pl.ANY),
            pl.BlockSpec(memory_space=pl.ANY),
        ],
        out_specs=pl.BlockSpec(memory_space=pltpu.VMEM),
        scratch_shapes=[
            pltpu.SMEM((2, 4), F32),
            pltpu.VMEM((6, 64, 128), F32),
            pltpu.VMEM((3, 36, 8, 128), F32),
            pltpu.VMEM((4, 6, 8, 128), F32),
            pltpu.VMEM((5, 8, 128), F32),
            pltpu.VMEM((12, 4, 8, 128), F32),
            pltpu.VMEM((12, 4, 8, 128), F32),
            pltpu.VMEM((12, 4, 8, 128), F32),
            pltpu.VMEM((1536, 512), BF16),
            pltpu.VMEM((1024, 128), BF16),
            pltpu.VMEM((16, 32, 128), F32),
            pltpu.VMEM((512, 256), BF16),
            pltpu.VMEM((768, 256), F32),
            pltpu.VMEM((8, 96, 128), F32),
            pltpu.VMEM((8, 96, 128), F32),
            pltpu.VMEM((128, 256), BF16),
            pltpu.VMEM((256, 256), F32),
            pltpu.VMEM((64, 8, 128), F32),
            pltpu.SemaphoreType.DMA((3,)),
            pltpu.SemaphoreType.DMA((5,)),
        ],
        compiler_params=pltpu.CompilerParams(
            collective_id=0, has_side_effects=True, vmem_limit_bytes=60 * 2**20
        ),
    )(traces, phase_coef, jnp.asarray(tail_table()))
    return pl.pallas_call(
        write_out,
        out_shape=jax.ShapeDtypeStruct((32, 2048), F32),
        in_specs=[pl.BlockSpec(memory_space=pl.ANY)],
        out_specs=pl.BlockSpec(memory_space=pl.ANY),
        scratch_shapes=[pltpu.SemaphoreType.DMA((4,))],
    )(image)


def solution(mesh):
    placed = (P(("gx", "gy"), None), P())
    return jax.shard_map(
        shards, mesh=mesh, in_specs=placed, out_specs=P(("gx", "gy"), None), check_vma=False
    )
```

```python
import functools

import jax
import jax.numpy as jnp
import numpy as np
from jax import lax
from jax.experimental import pallas as pl
from jax.experimental.pallas import tpu as pltpu
from jax.sharding import PartitionSpec as P

ORDER = 6
MESH = pl.DeviceIdType.MESH
F32 = jnp.float32
BF16 = jnp.bfloat16
AMP = 64.0

NODES = 0.5 * np.cos(np.pi * (2.0 * np.arange(ORDER) + 1.0) / (2.0 * ORDER))


def lagrange(points):
    points = np.asarray(points)[..., None, None]
    same = np.eye(ORDER, dtype=bool)
    spread = np.where(same, 1.0, NODES[:, None] - NODES[None, :])
    return np.where(same, 1.0, (points - NODES[None, :]) / spread).prod(-1)


CENTRE = lagrange(0.0)
HALVES = np.stack([((side - 0.5) + NODES) * 0.5 for side in (0, 1)])
TABLE = lagrange(HALVES)
WEIGHT = np.transpose(TABLE, (0, 2, 1))


def tail_table():
    out = np.zeros((ORDER, 64, 128))
    for high in range(64):
        total = np.eye(ORDER)
        for place in range(6):
            total = TABLE[(high >> place) & 1] @ total
        out[:, high, :96] = np.repeat(CENTRE[:, None] * total, 16, axis=1)
    return out.astype(np.float32)


def fit(function, terms):
    u = 0.125 + 0.125 * np.cos(np.pi * (np.arange(200) + 0.5) / 200)
    poly = np.polynomial.chebyshev.Chebyshev.fit(u, function(np.sqrt(u)), terms - 1, domain=[0, 0.25])
    return [float(c) for c in poly.convert(kind=np.polynomial.Polynomial).coef]


SIN = fit(lambda r: np.sin(np.pi * r) / r, 5)
SIN2 = [2.0 * c for c in fit(lambda r: np.sin(np.pi * r) / r, 4)]
COS = fit(lambda r: np.cos(np.pi * r), 5)


def horner(coefs, u):
    total = coefs[-1]
    for c in coefs[-2::-1]:
        total = total * u + c
    return total


def turn(c):
    r = c - jnp.floor(c + 0.5)
    u = r * r
    twice = r * horner(SIN2, u)
    half_cos = horner(COS, u)
    return 1.0 - (0.5 * twice) * twice, twice * half_cos


def turn_cos(c):
    r = c - jnp.floor(c + 0.5)
    twice = r * horner(SIN2, r * r)
    return 1.0 - (0.5 * twice) * twice


def half_turn(y):
    r = 0.5 - y
    u = r * r
    return r * horner(SIN, u), horner(COS, u)


def bend_value(coef, row, y):
    cosine = (0.5 - y) * horner(SIN, (0.5 - y) * (0.5 - y))
    c0, c1, c2, c3 = (coef[row, m] for m in range(4))
    return (c0 - c2) + cosine * ((c1 - 3.0 * c3) + cosine * (2.0 * c2 + cosine * (4.0 * c3)))


def bend_step(coef, middle, size):
    e1, e2, e3 = (coef[0, m] * float(-2.0 * AMP * np.sin(np.pi * m * size / 2.0)) for m in (1, 2, 3))
    cosine, sine = half_turn(middle)
    return sine * ((e1 - e3) + cosine * (2.0 * e2 + cosine * (4.0 * e3)))


def apply_real(weights, values):
    out = []
    for t in range(ORDER):
        total = weights[t][0] * values[0]
        for s in range(1, ORDER):
            total = total + weights[t][s] * values[s]
        out.append(total)
    return out


def iota(axis):
    return lax.broadcasted_iota(jnp.int32, (8, 128), axis)


def asf(value):
    return value.astype(F32)


def div(a, b):
    return lax.div(a, jnp.int32(b))


def rem(a, b):
    return lax.rem(a, jnp.int32(b))


def position():
    gx, gy = lax.axis_index("gx"), lax.axis_index("gy")
    return rem(gx, 4), div(gy, 4), rem(div(gy, 2), 2) * 2 + div(gx, 4), rem(gy, 2)


def device(x, y, z, core):
    return {"gx": rem(z, 2) * 4 + x, "gy": y * 4 + div(z, 2) * 2 + core}


def lane_parts(classes, core):
    lane = iota(1)
    place = lane // 16
    x, y, z = (
        (2 * c + e + core) & 3 for c, e in zip(classes, (place // 4, (place // 2) % 2, place % 2))
    )
    return (z // 2) + 2 * y + 8 * x + 32 * (z % 2), lane % 16


def early_levels(coef, box, top, v_ref):
    sub = iota(0)
    bits = [asf(sub % 2), asf((sub // 2) % 2), asf(sub // 4)]
    sign = [2.0 * bit - 1.0 for bit in bits]
    x0 = jnp.full((8, 128), 0.5, F32)
    x1 = x0 + sign[0] * 0.25
    x2 = x1 + sign[1] * 0.125
    word4 = asf(box * 16 + top)
    steps = bend_step(coef, x0 + sign[0] * 0.125, 0.25)
    p0_mid = coef[0, 0] - coef[0, 2]
    first = {}
    for j0 in range(2):
        outs = []
        for j1 in range(2):
            j = j0 + 2 * j1
            word = word4 * 4.0 + j
            start = 0.5 * (j0 + 0.5) + AMP * p0_mid * bend_value(coef, 1, (word + 0.5) * 2.0**-12)
            cosines, sines = [], []
            for s in range(ORDER):
                node = float(NODES[s])
                p1 = bend_value(coef, 1, (word + (0.5 + node)) * 2.0**-12)
                c, d = turn(start + sign[0] * ((j + 0.5 + node) * 0.25 + steps * p1))
                cosines.append(c)
                sines.append(d)
            outs.append((cosines, sines))
        weights = [[float(WEIGHT[j0][t][s] * CENTRE[s]) for s in range(ORDER)] for t in range(ORDER)]
        joined = [[jnp.stack([outs[0][c][s], outs[1][c][s]]) for s in range(ORDER)] for c in range(2)]
        first[j0] = [apply_real(weights, joined[c]) for c in range(2)]
    steps = bend_step(coef, x1 + sign[1] * 0.0625, 0.125)
    second = {}
    for j1 in range(2):
        word = word4 * 2.0 + j1
        linear = j1 + 2.0 * asf(top % 2) + 0.5
        real, imag = [], []
        for s in range(ORDER):
            node = float(NODES[s])
            p1 = bend_value(coef, 1, (word + (0.5 + node)) * 2.0**-11)
            c, d = turn(sign[1] * ((linear + node) * 0.25 + steps * p1))
            a = jnp.stack([first[0][0][s][j1], first[1][0][s][j1]])
            b = jnp.stack([first[0][1][s][j1], first[1][1][s][j1]])
            real.append(a * c - b * d)
            imag.append(a * d + b * c)
        weights = [[float(WEIGHT[j1][t][s]) for s in range(ORDER)] for t in range(ORDER)]
        second[j1] = (apply_real(weights, real), apply_real(weights, imag))
    steps = bend_step(coef, x2 + sign[2] * 0.03125, 0.0625)
    linear = asf(top % 4) + 0.5
    real, imag = [], []
    for s in range(ORDER):
        node = float(NODES[s])
        p1 = bend_value(coef, 1, (word4 + (0.5 + node)) * 2.0**-10)
        c, d = turn(sign[2] * ((linear + node) * 0.25 + steps * p1))
        a = jnp.concatenate([second[0][0][s], second[1][0][s]])
        b = jnp.concatenate([second[0][1][s], second[1][1][s]])
        real.append(a * c - b * d)
        imag.append(a * d + b * c)
    weights = lane_weights(top % 2)
    for c, values in enumerate((real, imag)):
        for t, value in enumerate(apply_real(weights, values)):
            v_ref[2 * t + c] = value


def lane_weights(bit):
    pick = bit == 1
    return [
        [jnp.where(pick, float(WEIGHT[1][t][s]), float(WEIGHT[0][t][s])) for s in range(ORDER)]
        for t in range(ORDER)
    ]


def late_setup(coef, box, top, w_ref, p_ref, c_ref):
    for i, level in enumerate((4, 5, 6)):
        weights = lane_weights((top // 2 ** (level - 3)) % 2)
        for t in range(ORDER):
            for s in range(ORDER):
                w_ref[i, ORDER * t + s] = weights[t][s]
        word = asf(box * 2 ** (7 - level) + top // 2 ** (level - 3))
        for s in range(ORDER):
            p_ref[i, s] = bend_value(coef, 1, (word + float(0.5 + NODES[s])) * 2.0 ** (level - 13))
    for s in range(ORDER):
        p_ref[3, s] = bend_value(coef, 1, (asf(box) + float(0.5 + NODES[s])) * 2.0**-6)
    turn_of = top % 8

    def by_lane(values):
        out = jnp.full((8, 128), float(values[ORDER - 1]), F32)
        for t in range(ORDER - 1):
            out = jnp.where(turn_of == t, float(values[t]), out)
        return out

    e1, e2, e3 = (coef[0, m] * by_lane(-2.0 * AMP * np.sin(np.pi * m * NODES / 128.0)) for m in (1, 2, 3))
    node = by_lane(NODES)
    c_ref[0] = node
    c_ref[1] = e1 - e3
    c_ref[2] = 2.0 * e2
    c_ref[3] = 4.0 * e3
    c_ref[4] = node * (asf(box) + 0.5)


def spread(value, t):
    return jnp.take_along_axis(value, (iota(1) // 8) * 8 + t, axis=1)


def late_levels(coef, box, top, w_ref, p_ref, c_ref, v3, v4, v5, g_ref):
    sub = iota(0)
    x3 = asf(4 * (sub % 2) + 2 * ((sub // 2) % 2) + sub // 4) * 0.125 + 0.0625
    full = box * 16 + top
    states = {3: v3, 4: v4, 5: v5}

    def turns(level, parent, sign):
        i = level - 4
        steps = bend_step(coef, parent + sign * 2.0 ** -(level + 2), 2.0 ** -(level + 1))
        linear = asf((full // 2 ** (level - 3)) % 4) + 0.5
        return [turn(sign * ((linear + float(NODES[s])) * 0.25 + steps * p_ref[i, s])) for s in range(ORDER)]

    def level_step(level, parent, bit):
        i = level - 4
        sign = (2 * bit - 1).astype(F32)
        source, target = states[level - 1], states[level]
        real, imag = [], []
        for s, (c, d) in enumerate(turns(level, parent, sign)):
            a, b = source[2 * s], source[2 * s + 1]
            real.append(a * c - b * d)
            imag.append(a * d + b * c)
        weights = [[w_ref[i, ORDER * t + s] for s in range(ORDER)] for t in range(ORDER)]
        for c, values in enumerate((real, imag)):
            for t, value in enumerate(apply_real(weights, values)):
                target[2 * t + c] = value
        return parent + sign * 2.0 ** -(level + 1)

    def last_step(parent, bit, place):
        sign = (2 * bit - 1).astype(F32)
        middle = parent + sign * 2.0**-7 + c_ref[0] * (1.0 / 128.0)
        cosine, sine = half_turn(middle)
        steps = sine * (c_ref[1] + cosine * (c_ref[2] + cosine * c_ref[3]))
        switch = [turn((c_ref[4] + c_ref[0] * float(NODES[u])) + steps * p_ref[3, u]) for u in range(ORDER)]
        merged = []
        for s, (c, d) in enumerate(turns(6, parent, sign)):
            a = b = None
            for u in range(ORDER):
                weight = w_ref[2, ORDER * u + s]
                a = switch[u][0] * weight if a is None else a + switch[u][0] * weight
                b = switch[u][1] * weight if b is None else b + switch[u][1] * weight
            merged.append((a * c - b * d, a * d + b * c))
        for t in range(ORDER):
            real = imag = None
            for s in range(ORDER):
                c, d = spread(merged[s][0], t), spread(merged[s][1], t)
                a, b = v5[2 * s], v5[2 * s + 1]
                real = a * c - b * d if real is None else real + (a * c - b * d)
                imag = a * d + b * c if imag is None else imag + (a * d + b * c)
            rows = pl.ds(pl.multiple_of(place * 192 + 16 * t, 16), 16)
            rows_low = pl.ds(pl.multiple_of(place * 192 + 96 + 16 * t, 16), 16)
            for j in range(4):
                both = jnp.concatenate([real[j], imag[j]], axis=0)
                high = both.astype(BF16)
                g_ref[rows, 128 * j : 128 * (j + 1)] = high
                g_ref[rows_low, 128 * j : 128 * (j + 1)] = (both - high.astype(F32)).astype(BF16)

    def over3(q3, _):
        x4 = level_step(4, x3, q3)

        def over4(q4, _):
            x5 = level_step(5, x4, q4)

            def over5(q5, _):
                last_step(x5, q5, q3 + 2 * q4 + 4 * q5)
                return 0

            return lax.fori_loop(0, 2, over5, 0)

        return lax.fori_loop(0, 2, over4, 0)

    lax.fori_loop(0, 2, over3, 0)


def last_weights(coef, group, tail_ref, h_ref):
    sub, lane = iota(0), iota(1)
    own = lane % 8
    same = sub == own
    box6 = 32 * (own % 2) + 16 * ((own // 2) % 2) + 8 * (own // 4)
    box6 = box6 + (4 * (group % 2) + 2 * ((group // 2) % 2) + group // 4)
    inner = 32 * (sub % 2) + 16 * ((sub // 2) % 2) + 8 * (sub // 4)
    base = box6 * 64 + inner
    quarter = 0.25 * asf((lane // 8) % 2)
    p1_mid = coef[1, 0] - coef[1, 2]

    def rows_of(r):
        centre = (asf(base + (4 * (r % 2) + 2 * ((r // 2) % 2) + r // 4)) + 0.5) * 2.0**-12
        total = None
        for t in range(ORDER):
            node = float(NODES[t])
            steps = bend_step(coef, centre + node / 8192.0, node / 4096.0)
            term = turn_cos((quarter - 0.5 * node) - steps * p1_mid)
            term = term * tail_ref[t, pl.ds(pl.multiple_of(8 * r, 8), 8), :]
            total = term if total is None else total + term
        return total

    def body(i, _):
        for half in range(2):
            total = rows_of(2 * i + half)
            for k in range(0, 8, 2):
                both = jnp.concatenate(
                    [jnp.where(same, jnp.broadcast_to(total[k + n : k + n + 1], (8, 128)), 0.0) for n in range(2)], axis=0
                )
                high = both.astype(BF16)
                row = 64 * half + 8 * k
                h_ref[pl.ds(pl.multiple_of(256 * i + row, 16), 16), :] = high
                h_ref[pl.ds(pl.multiple_of(256 * i + 128 + row, 16), 16), :] = (both - high.astype(F32)).astype(BF16)
        return 0

    lax.fori_loop(0, 4, body, 0)


def kernel(
    x_ref,
    coef_hbm,
    tail_hbm,
    out_ref,
    coef_ref,
    tail_ref,
    w_ref,
    p_ref,
    c_ref,
    v3,
    v4,
    v5,
    g_ref,
    h_ref,
    xr_ref,
    xs_ref,
    wide_ref,
    part_ref,
    rr_ref,
    sum_ref,
    last_ref,
    tile_ref,
    send_sems,
    recv_sems,
):
    fetch_coef = pltpu.make_async_copy(coef_hbm, coef_ref, recv_sems.at[3])
    fetch_tail = pltpu.make_async_copy(tail_hbm, tail_ref, recv_sems.at[4])
    fetch_coef.start()
    fetch_tail.start()
    chip = position()
    core = chip[3]
    own_u = [rem(p + 3 * core, 4) for p in chip[:3]]
    other_u = [rem(p + 3 * (1 - core), 4) for p in chip[:3]]
    classes = [div(u, 2) for u in own_u]
    groups = [div(rem(u + 3, 4), 2) for u in own_u]
    ends = [rem(u, 2) for u in own_u]
    target = classes[0] + 2 * classes[1] + 4 * classes[2]
    block = groups[0] + 2 * groups[1] + 4 * groups[2] + 8 * core

    def bits(i):
        return rem(i, 2), rem(div(i, 2), 2), div(i, 4)

    def member(tiling, cs, gs):
        return device(*(rem(2 * c + rem(g + 1 + c, 2) + tiling, 4) for c, g in zip(cs, gs)), tiling)

    barrier = pltpu.get_barrier_semaphore()

    def greet_class(step, _):
        es = [rem(e + b, 2) for e, b in zip(ends, bits(rem(step, 8)))]
        source = device(
            *(rem(2 * c + e + core, 4) for c, e in zip(classes, es)), rem(core + div(step, 8), 2)
        )
        pl.semaphore_signal(barrier, inc=1, device_id=source, device_id_type=MESH)
        return 0

    lax.fori_loop(1, 16, greet_class, 0, unroll=True)

    def greet_group(step, _):
        cs = [rem(c + b, 2) for c, b in zip(classes, bits(step))]
        pl.semaphore_signal(barrier, inc=1, device_id=member(core, cs, groups), device_id_type=MESH)
        return 0

    lax.fori_loop(1, 8, greet_group, 0, unroll=True)

    box, top = lane_parts(classes, core)
    fetch_coef.wait()
    early_levels(coef_ref, box, top, v3)
    late_setup(coef_ref, box, top, w_ref, p_ref, c_ref)
    pl.semaphore_wait(barrier, 22)

    def slot_of(us):
        return 2 * (rem(us[2], 2) + 2 * rem(us[1], 2) + 4 * rem(us[0], 2)) + core

    def scatter(tiling, us):
        slot = slot_of(us)
        cs = [div(u, 2) for u in us]

        def body(step, _):
            gs = [rem(g + b, 2) for g, b in zip(groups, bits(step))]
            m = gs[0] + 2 * gs[1] + 4 * gs[2] + 8 * tiling
            pltpu.make_async_remote_copy(
                src_ref=x_ref.at[:, pl.ds(pl.multiple_of(m * 128, 128), 128)],
                dst_ref=xr_ref.at[slot],
                send_sem=send_sems.at[0],
                recv_sem=recv_sems.at[0],
                device_id=member(tiling, cs, gs),
                device_id_type=MESH,
            ).start()
            return 0

        return body

    lax.fori_loop(1, 8, scatter(core, own_u), 0, unroll=True)
    lax.fori_loop(0, 8, scatter(1 - core, other_u), 0, unroll=True)
    pltpu.make_async_copy(
        x_ref.at[:, pl.ds(pl.multiple_of(block * 128, 128), 128)], xr_ref.at[slot_of(own_u)], recv_sems.at[0]
    ).start()

    late_levels(coef_ref, box, top, w_ref, p_ref, c_ref, v3, v4, v5, g_ref)
    fetch_tail.wait()
    last_weights(coef_ref, target, tail_ref, h_ref)

    pltpu.make_async_copy(xr_ref, xr_ref, recv_sems.at[0]).wait()
    for i in range(8):
        for j in range(4):
            piece = jnp.concatenate([xr_ref[2 * i + s, pl.ds(j, 8, stride=4), :] for s in range(2)], axis=0)
            high = piece.astype(BF16)
            rows = slice(128 * j + 16 * i, 128 * j + 16 * i + 16)
            xs_ref[rows, 0:128] = high
            xs_ref[rows, 128:256] = (piece - high.astype(F32)).astype(BF16)

    def products(half):
        rows = pl.ds(pl.multiple_of(half * 768, 16), 768)
        wide_ref[...] = jnp.dot(g_ref[rows, :], xs_ref[...], preferred_element_type=F32)

    def part(i):
        high = pl.ds(pl.multiple_of(i * 192, 8), 96)
        low = pl.ds(pl.multiple_of(i * 192 + 96, 8), 96)
        return wide_ref[high, 0:128] + (wide_ref[high, 128:256] + wide_ref[low, 0:128])

    near = rem(target, 4)

    def reduce(half, i):
        other = half * 4 + i
        part_ref[other] = part(i)
        pltpu.make_async_remote_copy(
            src_ref=part_ref.at[other],
            dst_ref=rr_ref.at[target],
            send_sem=send_sems.at[1],
            recv_sem=recv_sems.at[1],
            device_id=member(core, bits(other), groups),
            device_id_type=MESH,
        ).start()

    def reduce_far(i, _):
        reduce(1 - classes[2], rem(near + i, 4))
        return 0

    def reduce_near(i, _):
        reduce(classes[2], rem(near + i, 4))
        return 0

    products(1 - classes[2])
    lax.fori_loop(0, 4, reduce_far, 0, unroll=True)
    products(classes[2])
    lax.fori_loop(1, 4, reduce_near, 0, unroll=True)
    rr_ref[target] = part(near)
    pltpu.make_async_copy(rr_ref.at[0:7], rr_ref.at[0:7], recv_sems.at[1]).wait()
    for i in range(0, 12, 2):
        rows = slice(8 * i, 8 * i + 16)
        total = rr_ref[0, rows, :]
        for k in range(1, 8):
            total = total + rr_ref[k, rows, :]
        high = total.astype(BF16)
        sum_ref[rows, 0:128] = high
        sum_ref[rows, 128:256] = (total - high.astype(F32)).astype(BF16)
    sum_ref[96:128, :] = jnp.zeros((32, 256), BF16)

    mine = div(chip[2], 2) + 2 * chip[1] + 8 * chip[0] + 32 * rem(chip[2], 2)
    own = core == classes[2]
    here = out_ref.at[pl.ds(pl.multiple_of(near * 8, 8), 8), pl.ds(pl.multiple_of(block * 128, 128), 128)]
    mine_high, mine_low = div(mine, 16), rem(mine, 16)

    def deliver_some(step, _):
        quarter = rem(mine_high + step, 4)
        rows = pl.ds(pl.multiple_of(quarter * 256, 16), 256)
        last_ref[...] = jnp.dot(h_ref[rows, :], sum_ref[...], preferred_element_type=F32)
        tiles = last_ref[0:128, 0:128] + (last_ref[0:128, 128:256] + last_ref[128:256, 0:128])
        tile_ref[pl.ds(quarter * 16, 16)] = tiles.reshape(16, 8, 128)

        def deliver(i, _):
            place = rem(mine_low + i, 16)
            high = quarter * 16 + place

            @pl.when(jnp.logical_or(high != mine, jnp.logical_not(own)))
            def _():
                x_to = div(place, 8) + 2 * rem(quarter, 2)
                z_to = 2 * rem(place, 2) + div(quarter, 2)
                pltpu.make_async_remote_copy(
                    src_ref=tile_ref.at[high],
                    dst_ref=here,
                    send_sem=send_sems.at[2],
                    recv_sem=recv_sems.at[2],
                    device_id=device(x_to, rem(div(place, 2), 4), z_to, classes[2]),
                    device_id_type=MESH,
                ).start()

            return 0

        return lax.fori_loop(0, 16, deliver, 0, unroll=4)

    lax.fori_loop(0, 4, deliver_some, 0)

    @pl.when(own)
    def _():
        pltpu.make_async_copy(tile_ref.at[mine], here, recv_sems.at[2]).start()

    pltpu.make_async_copy(xr_ref.at[0:15], xr_ref.at[0:15], send_sems.at[0]).wait()
    pltpu.make_async_copy(part_ref.at[0:7], part_ref.at[0:7], send_sems.at[1]).wait()

    @pl.when(own)
    def _():
        pltpu.make_async_copy(tile_ref.at[0:63], tile_ref.at[0:63], send_sems.at[2]).wait()

    @pl.when(jnp.logical_not(own))
    def _():
        pltpu.make_async_copy(tile_ref, tile_ref, send_sems.at[2]).wait()

    pltpu.make_async_copy(out_ref, out_ref, recv_sems.at[2]).wait()


def shards(traces, phase_coef):
    return pl.pallas_call(
        kernel,
        out_shape=jax.ShapeDtypeStruct((32, 2048), F32),
        in_specs=[
            pl.BlockSpec(memory_space=pl.ANY),
            pl.BlockSpec(memory_space=pl.ANY),
            pl.BlockSpec(memory_space=pl.ANY),
        ],
        out_specs=pl.BlockSpec(memory_space=pl.ANY),
        scratch_shapes=[
            pltpu.SMEM((2, 4), F32),
            pltpu.VMEM((6, 64, 128), F32),
            pltpu.VMEM((3, 36, 8, 128), F32),
            pltpu.VMEM((4, 6, 8, 128), F32),
            pltpu.VMEM((5, 8, 128), F32),
            pltpu.VMEM((12, 4, 8, 128), F32),
            pltpu.VMEM((12, 4, 8, 128), F32),
            pltpu.VMEM((12, 4, 8, 128), F32),
            pltpu.VMEM((1536, 512), BF16),
            pltpu.VMEM((1024, 128), BF16),
            pltpu.VMEM((16, 32, 128), F32),
            pltpu.VMEM((512, 256), BF16),
            pltpu.VMEM((768, 256), F32),
            pltpu.VMEM((8, 96, 128), F32),
            pltpu.VMEM((8, 96, 128), F32),
            pltpu.VMEM((128, 256), BF16),
            pltpu.VMEM((256, 256), F32),
            pltpu.VMEM((64, 8, 128), F32),
            pltpu.SemaphoreType.DMA((3,)),
            pltpu.SemaphoreType.DMA((5,)),
        ],
        compiler_params=pltpu.CompilerParams(
            collective_id=0, has_side_effects=True, vmem_limit_bytes=60 * 2**20
        ),
    )(traces, phase_coef, jnp.asarray(tail_table()))


def solution(mesh):
    placed = (P(("gx", "gy"), None), P())
    return jax.shard_map(
        shards, mesh=mesh, in_specs=placed, out_specs=P(("gx", "gy"), None), check_vma=False
    )
```

```python
import functools

import jax
import jax.numpy as jnp
import numpy as np
from jax import lax
from jax.experimental import pallas as pl
from jax.experimental.pallas import tpu as pltpu
from jax.sharding import PartitionSpec as P

ORDER = 6
MESH = pl.DeviceIdType.MESH
F32 = jnp.float32
BF16 = jnp.bfloat16
AMP = 64.0

NODES = 0.5 * np.cos(np.pi * (2.0 * np.arange(ORDER) + 1.0) / (2.0 * ORDER))


def lagrange(points):
    points = np.asarray(points)[..., None, None]
    same = np.eye(ORDER, dtype=bool)
    spread = np.where(same, 1.0, NODES[:, None] - NODES[None, :])
    return np.where(same, 1.0, (points - NODES[None, :]) / spread).prod(-1)


CENTRE = lagrange(0.0)
HALVES = np.stack([((side - 0.5) + NODES) * 0.5 for side in (0, 1)])
TABLE = lagrange(HALVES)
WEIGHT = np.transpose(TABLE, (0, 2, 1))


def tail_table():
    out = np.zeros((ORDER, 64, 128))
    for high in range(64):
        total = np.eye(ORDER)
        for place in range(6):
            total = TABLE[(high >> place) & 1] @ total
        out[:, high, :96] = np.repeat(CENTRE[:, None] * total, 16, axis=1)
    return out.astype(np.float32)


def fit(function, terms):
    u = 0.125 + 0.125 * np.cos(np.pi * (np.arange(200) + 0.5) / 200)
    poly = np.polynomial.chebyshev.Chebyshev.fit(u, function(np.sqrt(u)), terms - 1, domain=[0, 0.25])
    return [float(c) for c in poly.convert(kind=np.polynomial.Polynomial).coef]


SIN = fit(lambda r: np.sin(np.pi * r) / r, 5)
SIN2 = [2.0 * c for c in fit(lambda r: np.sin(np.pi * r) / r, 4)]
COS = fit(lambda r: np.cos(np.pi * r), 5)


def horner(coefs, u):
    total = coefs[-1]
    for c in coefs[-2::-1]:
        total = total * u + c
    return total


def turn(c):
    r = c - jnp.floor(c + 0.5)
    u = r * r
    twice = r * horner(SIN2, u)
    half_cos = horner(COS, u)
    return 1.0 - (0.5 * twice) * twice, twice * half_cos


def turn_cos(c):
    r = c - jnp.floor(c + 0.5)
    twice = r * horner(SIN2, r * r)
    return 1.0 - (0.5 * twice) * twice


def half_turn(y):
    r = 0.5 - y
    u = r * r
    return r * horner(SIN, u), horner(COS, u)


def bend_value(coef, row, y):
    cosine = (0.5 - y) * horner(SIN, (0.5 - y) * (0.5 - y))
    c0, c1, c2, c3 = (coef[row, m] for m in range(4))
    return (c0 - c2) + cosine * ((c1 - 3.0 * c3) + cosine * (2.0 * c2 + cosine * (4.0 * c3)))


def bend_step(coef, middle, size):
    e1, e2, e3 = (coef[0, m] * float(-2.0 * AMP * np.sin(np.pi * m * size / 2.0)) for m in (1, 2, 3))
    cosine, sine = half_turn(middle)
    return sine * ((e1 - e3) + cosine * (2.0 * e2 + cosine * (4.0 * e3)))


def apply_real(weights, values):
    out = []
    for t in range(ORDER):
        total = weights[t][0] * values[0]
        for s in range(1, ORDER):
            total = total + weights[t][s] * values[s]
        out.append(total)
    return out


def iota(axis):
    return lax.broadcasted_iota(jnp.int32, (8, 128), axis)


def asf(value):
    return value.astype(F32)


def div(a, b):
    return lax.div(a, jnp.int32(b))


def rem(a, b):
    return lax.rem(a, jnp.int32(b))


def position():
    gx, gy = lax.axis_index("gx"), lax.axis_index("gy")
    return rem(gx, 4), div(gy, 4), rem(div(gy, 2), 2) * 2 + div(gx, 4), rem(gy, 2)


def device(x, y, z, core):
    return {"gx": rem(z, 2) * 4 + x, "gy": y * 4 + div(z, 2) * 2 + core}


def lane_parts(classes, core):
    lane = iota(1)
    place = lane >> 4
    x, y, z = (
        (2 * c + e + core) & 3 for c, e in zip(classes, (place >> 2, (place >> 1) & 1, place & 1))
    )
    return (z >> 1) + 2 * y + 8 * x + 32 * (z & 1), lane & 15


def early_levels(coef, box, top, v_ref):
    sub = iota(0)
    bits = [asf(sub & 1), asf((sub >> 1) & 1), asf(sub >> 2)]
    sign = [2.0 * bit - 1.0 for bit in bits]
    x0 = jnp.full((8, 128), 0.5, F32)
    x1 = x0 + sign[0] * 0.25
    x2 = x1 + sign[1] * 0.125
    word4 = asf(box * 16 + top)
    steps = bend_step(coef, x0 + sign[0] * 0.125, 0.25)
    p0_mid = coef[0, 0] - coef[0, 2]
    first = {}
    for j0 in range(2):
        outs = []
        for j1 in range(2):
            j = j0 + 2 * j1
            word = word4 * 4.0 + j
            start = 0.5 * (j0 + 0.5) + AMP * p0_mid * bend_value(coef, 1, (word + 0.5) * 2.0**-12)
            cosines, sines = [], []
            for s in range(ORDER):
                node = float(NODES[s])
                p1 = bend_value(coef, 1, (word + (0.5 + node)) * 2.0**-12)
                c, d = turn(start + sign[0] * ((j + 0.5 + node) * 0.25 + steps * p1))
                cosines.append(c)
                sines.append(d)
            outs.append((cosines, sines))
        weights = [[float(WEIGHT[j0][t][s] * CENTRE[s]) for s in range(ORDER)] for t in range(ORDER)]
        joined = [[jnp.stack([outs[0][c][s], outs[1][c][s]]) for s in range(ORDER)] for c in range(2)]
        first[j0] = [apply_real(weights, joined[c]) for c in range(2)]
    steps = bend_step(coef, x1 + sign[1] * 0.0625, 0.125)
    second = {}
    for j1 in range(2):
        word = word4 * 2.0 + j1
        linear = j1 + 2.0 * asf(top & 1) + 0.5
        real, imag = [], []
        for s in range(ORDER):
            node = float(NODES[s])
            p1 = bend_value(coef, 1, (word + (0.5 + node)) * 2.0**-11)
            c, d = turn(sign[1] * ((linear + node) * 0.25 + steps * p1))
            a = jnp.stack([first[0][0][s][j1], first[1][0][s][j1]])
            b = jnp.stack([first[0][1][s][j1], first[1][1][s][j1]])
            real.append(a * c - b * d)
            imag.append(a * d + b * c)
        weights = [[float(WEIGHT[j1][t][s]) for s in range(ORDER)] for t in range(ORDER)]
        second[j1] = (apply_real(weights, real), apply_real(weights, imag))
    steps = bend_step(coef, x2 + sign[2] * 0.03125, 0.0625)
    linear = asf(top & 3) + 0.5
    real, imag = [], []
    for s in range(ORDER):
        node = float(NODES[s])
        p1 = bend_value(coef, 1, (word4 + (0.5 + node)) * 2.0**-10)
        c, d = turn(sign[2] * ((linear + node) * 0.25 + steps * p1))
        a = jnp.concatenate([second[0][0][s], second[1][0][s]])
        b = jnp.concatenate([second[0][1][s], second[1][1][s]])
        real.append(a * c - b * d)
        imag.append(a * d + b * c)
    weights = lane_weights(top & 1)
    for c, values in enumerate((real, imag)):
        for t, value in enumerate(apply_real(weights, values)):
            v_ref[2 * t + c] = value


def lane_weights(bit):
    pick = bit == 1
    return [
        [jnp.where(pick, float(WEIGHT[1][t][s]), float(WEIGHT[0][t][s])) for s in range(ORDER)]
        for t in range(ORDER)
    ]


def late_setup(coef, box, top, w_ref, p_ref, c_ref):
    for i, level in enumerate((4, 5, 6)):
        weights = lane_weights((top >> (level - 3)) & 1)
        for t in range(ORDER):
            for s in range(ORDER):
                w_ref[i, ORDER * t + s] = weights[t][s]
        word = asf(box * 2 ** (7 - level) + (top >> (level - 3)))
        for s in range(ORDER):
            p_ref[i, s] = bend_value(coef, 1, (word + float(0.5 + NODES[s])) * 2.0 ** (level - 13))
    for s in range(ORDER):
        p_ref[3, s] = bend_value(coef, 1, (asf(box) + float(0.5 + NODES[s])) * 2.0**-6)
    turn_of = top & 7

    def by_lane(values):
        out = jnp.full((8, 128), float(values[ORDER - 1]), F32)
        for t in range(ORDER - 1):
            out = jnp.where(turn_of == t, float(values[t]), out)
        return out

    e1, e2, e3 = (coef[0, m] * by_lane(-2.0 * AMP * np.sin(np.pi * m * NODES / 128.0)) for m in (1, 2, 3))
    node = by_lane(NODES)
    c_ref[0] = node
    c_ref[1] = e1 - e3
    c_ref[2] = 2.0 * e2
    c_ref[3] = 4.0 * e3
    c_ref[4] = node * (asf(box) + 0.5)


def spread(value, t):
    return jnp.take_along_axis(value, (iota(1) & 120) + t, axis=1)


def late_levels(coef, box, top, q3, w_ref, p_ref, c_ref, v3, v4, v5, g_ref):
    sub = iota(0)
    x3 = asf(4 * (sub & 1) + (sub & 2) + (sub >> 2)) * 0.125 + 0.0625
    full = box * 16 + top
    states = {3: v3, 4: v4, 5: v5}

    def turns(level, parent, sign):
        i = level - 4
        steps = bend_step(coef, parent + sign * 2.0 ** -(level + 2), 2.0 ** -(level + 1))
        linear = asf((full >> (level - 3)) & 3) + 0.5
        return [turn(sign * ((linear + float(NODES[s])) * 0.25 + steps * p_ref[i, s])) for s in range(ORDER)]

    def level_step(level, parent, bit):
        i = level - 4
        sign = (2 * bit - 1).astype(F32)
        source, target = states[level - 1], states[level]
        real, imag = [], []
        for s, (c, d) in enumerate(turns(level, parent, sign)):
            a, b = source[2 * s], source[2 * s + 1]
            real.append(a * c - b * d)
            imag.append(a * d + b * c)
        weights = [[w_ref[i, ORDER * t + s] for s in range(ORDER)] for t in range(ORDER)]
        for c, values in enumerate((real, imag)):
            for t, value in enumerate(apply_real(weights, values)):
                target[2 * t + c] = value
        return parent + sign * 2.0 ** -(level + 1)

    def last_step(parent, bit, place):
        sign = (2 * bit - 1).astype(F32)
        middle = parent + sign * 2.0**-7 + c_ref[0] * (1.0 / 128.0)
        cosine, sine = half_turn(middle)
        steps = sine * (c_ref[1] + cosine * (c_ref[2] + cosine * c_ref[3]))
        switch = [turn((c_ref[4] + c_ref[0] * float(NODES[u])) + steps * p_ref[3, u]) for u in range(ORDER)]
        merged = []
        for s, (c, d) in enumerate(turns(6, parent, sign)):
            a = b = None
            for u in range(ORDER):
                weight = w_ref[2, ORDER * u + s]
                a = switch[u][0] * weight if a is None else a + switch[u][0] * weight
                b = switch[u][1] * weight if b is None else b + switch[u][1] * weight
            c, d = a * c - b * d, a * d + b * c
            merged.append((c, d - c, c + d))
        parts = [v5[2 * s] + v5[2 * s + 1] for s in range(ORDER)]
        for t in range(ORDER):
            k1 = k2 = k3 = None
            for s in range(ORDER):
                c, up, down = (spread(value, t) for value in merged[s])
                m1, m2, m3 = parts[s] * c, v5[2 * s] * up, v5[2 * s + 1] * down
                k1 = m1 if k1 is None else k1 + m1
                k2 = m2 if k2 is None else k2 + m2
                k3 = m3 if k3 is None else k3 + m3
            real, imag = k1 - k3, k1 + k2
            rows = pl.ds(pl.multiple_of(place * 192 + 16 * t, 16), 16)
            rows_low = pl.ds(pl.multiple_of(place * 192 + 96 + 16 * t, 16), 16)
            for j in range(4):
                both = jnp.concatenate([real[j], imag[j]], axis=0)
                high = both.astype(BF16)
                g_ref[rows, 128 * j : 128 * (j + 1)] = high
                g_ref[rows_low, 128 * j : 128 * (j + 1)] = (both - high.astype(F32)).astype(BF16)

    x4 = level_step(4, x3, q3)

    def over4(q4, _):
        x5 = level_step(5, x4, q4)

        def over5(q5, _):
            last_step(x5, q5, 4 * q3 + q4 + 2 * q5)
            return 0

        return lax.fori_loop(0, 2, over5, 0)

    lax.fori_loop(0, 2, over4, 0)


def last_weights(coef, group, tail_ref, h_ref):
    sub, lane = iota(0), iota(1)
    own = lane & 7
    same = sub == own
    box6 = 32 * (own & 1) + 8 * (own & 2) + 2 * (own & 4)
    box6 = box6 + (4 * rem(group, 2) + 2 * rem(div(group, 2), 2) + div(group, 4))
    inner = 32 * (sub & 1) + 8 * (sub & 2) + 2 * (sub & 4)
    base = box6 * 64 + inner
    quarter = 0.25 * asf((lane >> 3) & 1)
    p1_mid = coef[1, 0] - coef[1, 2]

    def rows_of(r):
        centre = (asf(base + (4 * rem(r, 2) + 2 * rem(div(r, 2), 2) + div(r, 4))) + 0.5) * 2.0**-12
        total = None
        for t in range(ORDER):
            node = float(NODES[t])
            steps = bend_step(coef, centre + node / 8192.0, node / 4096.0)
            term = turn_cos((quarter - 0.5 * node) - steps * p1_mid)
            term = term * tail_ref[t, pl.ds(pl.multiple_of(8 * r, 8), 8), :]
            total = term if total is None else total + term
        return total

    def body(i, _):
        for half in range(2):
            total = rows_of(2 * i + half)
            for k in range(0, 8, 2):
                both = jnp.concatenate(
                    [jnp.where(same, jnp.broadcast_to(total[k + n : k + n + 1], (8, 128)), 0.0) for n in range(2)], axis=0
                )
                high = both.astype(BF16)
                row = 64 * half + 8 * k
                h_ref[pl.ds(pl.multiple_of(256 * i + row, 16), 16), :] = high
                h_ref[pl.ds(pl.multiple_of(256 * i + 128 + row, 16), 16), :] = (both - high.astype(F32)).astype(BF16)
        return 0

    lax.fori_loop(0, 4, body, 0)


def kernel(
    x_ref,
    coef_hbm,
    tail_hbm,
    out_ref,
    coef_ref,
    tail_ref,
    w_ref,
    p_ref,
    c_ref,
    v3,
    v4,
    v5,
    g_ref,
    h_ref,
    xr_ref,
    xs_ref,
    wide_ref,
    part_ref,
    rr_ref,
    sum_ref,
    last_ref,
    tile_ref,
    send_sems,
    recv_sems,
):
    fetch_coef = pltpu.make_async_copy(coef_hbm, coef_ref, recv_sems.at[3])
    fetch_tail = pltpu.make_async_copy(tail_hbm, tail_ref, recv_sems.at[4])
    fetch_coef.start()
    fetch_tail.start()
    chip = position()
    core = chip[3]
    own_u = [rem(p + 3 * core, 4) for p in chip[:3]]
    other_u = [rem(p + 3 * (1 - core), 4) for p in chip[:3]]
    classes = [div(u, 2) for u in own_u]
    groups = [div(rem(u + 3, 4), 2) for u in own_u]
    ends = [rem(u, 2) for u in own_u]
    target = classes[0] + 2 * classes[1] + 4 * classes[2]
    block = groups[0] + 2 * groups[1] + 4 * groups[2] + 8 * core

    def bits(i):
        return rem(i, 2), rem(div(i, 2), 2), div(i, 4)

    def member(tiling, cs, gs):
        return device(*(rem(2 * c + rem(g + 1 + c, 2) + tiling, 4) for c, g in zip(cs, gs)), tiling)

    barrier = pltpu.get_barrier_semaphore()

    def greet_class(step, _):
        es = [rem(e + b, 2) for e, b in zip(ends, bits(rem(step, 8)))]
        source = device(
            *(rem(2 * c + e + core, 4) for c, e in zip(classes, es)), rem(core + div(step, 8), 2)
        )
        pl.semaphore_signal(barrier, inc=1, device_id=source, device_id_type=MESH)
        return 0

    lax.fori_loop(1, 16, greet_class, 0, unroll=True)

    def greet_group(step, _):
        cs = [rem(c + b, 2) for c, b in zip(classes, bits(step))]
        pl.semaphore_signal(barrier, inc=1, device_id=member(core, cs, groups), device_id_type=MESH)
        return 0

    lax.fori_loop(1, 8, greet_group, 0, unroll=True)

    box, top = lane_parts(classes, core)
    fetch_coef.wait()
    early_levels(coef_ref, box, top, v3)
    late_setup(coef_ref, box, top, w_ref, p_ref, c_ref)
    pl.semaphore_wait(barrier, 22)

    def slot_of(us):
        return 2 * (rem(us[2], 2) + 2 * rem(us[1], 2) + 4 * rem(us[0], 2)) + core

    def scatter(tiling, us):
        slot = slot_of(us)
        cs = [div(u, 2) for u in us]

        def body(step, _):
            gs = [rem(g + b, 2) for g, b in zip(groups, bits(step))]
            m = gs[0] + 2 * gs[1] + 4 * gs[2] + 8 * tiling
            pltpu.make_async_remote_copy(
                src_ref=x_ref.at[:, pl.ds(pl.multiple_of(m * 128, 128), 128)],
                dst_ref=xr_ref.at[slot],
                send_sem=send_sems.at[0],
                recv_sem=recv_sems.at[0],
                device_id=member(tiling, cs, gs),
                device_id_type=MESH,
            ).start()
            return 0

        return body

    lax.fori_loop(1, 8, scatter(core, own_u), 0, unroll=True)
    lax.fori_loop(0, 8, scatter(1 - core, other_u), 0, unroll=True)
    pltpu.make_async_copy(
        x_ref.at[:, pl.ds(pl.multiple_of(block * 128, 128), 128)], xr_ref.at[slot_of(own_u)], recv_sems.at[0]
    ).start()

    def boxes(q3):
        late_levels(coef_ref, box, top, q3, w_ref, p_ref, c_ref, v3, v4, v5, g_ref)

    def products(q3):
        rows = pl.ds(pl.multiple_of(q3 * 768, 16), 768)
        wide_ref[...] = jnp.dot(g_ref[rows, :], xs_ref[...], preferred_element_type=F32)

    def part(i):
        high = pl.ds(pl.multiple_of(i * 192, 8), 96)
        low = pl.ds(pl.multiple_of(i * 192 + 96, 8), 96)
        return wide_ref[high, 0:128] + (wide_ref[high, 128:256] + wide_ref[low, 0:128])

    def reduce(q3):
        def body(step, _):
            other = [q3, rem(classes[1] + rem(step, 2), 2), rem(classes[2] + div(step, 2), 2)]
            i = other[1] + 2 * other[2]
            part_ref[4 * q3 + i] = part(i)
            pltpu.make_async_remote_copy(
                src_ref=part_ref.at[4 * q3 + i],
                dst_ref=rr_ref.at[target],
                send_sem=send_sems.at[1],
                recv_sem=recv_sems.at[1],
                device_id=member(core, other, groups),
                device_id_type=MESH,
            ).start()
            return 0

        return body

    far, near = 1 - classes[0], classes[0]
    boxes(far)
    fetch_tail.wait()
    last_weights(coef_ref, target, tail_ref, h_ref)
    pltpu.make_async_copy(xr_ref, xr_ref, recv_sems.at[0]).wait()
    for i in range(8):
        for j in range(4):
            piece = jnp.concatenate([xr_ref[2 * i + s, pl.ds(j, 8, stride=4), :] for s in range(2)], axis=0)
            high = piece.astype(BF16)
            rows = slice(128 * j + 16 * i, 128 * j + 16 * i + 16)
            xs_ref[rows, 0:128] = high
            xs_ref[rows, 128:256] = (piece - high.astype(F32)).astype(BF16)
    products(far)
    lax.fori_loop(0, 4, reduce(far), 0, unroll=True)
    boxes(near)
    products(near)
    lax.fori_loop(1, 4, reduce(near), 0, unroll=True)
    rr_ref[target] = part(classes[1] + 2 * classes[2])
    pltpu.make_async_copy(rr_ref.at[0:7], rr_ref.at[0:7], recv_sems.at[1]).wait()
    for i in range(0, 12, 2):
        rows = slice(8 * i, 8 * i + 16)
        total = rr_ref[0, rows, :]
        for k in range(1, 8):
            total = total + rr_ref[k, rows, :]
        high = total.astype(BF16)
        sum_ref[rows, 0:128] = high
        sum_ref[rows, 128:256] = (total - high.astype(F32)).astype(BF16)
    sum_ref[96:128, :] = jnp.zeros((32, 256), BF16)

    mine = div(chip[2], 2) + 2 * chip[1] + 8 * chip[0] + 32 * rem(chip[2], 2)
    own = core == classes[2]
    row = pl.multiple_of((classes[0] + 2 * classes[1]) * 8, 8)
    here = out_ref.at[pl.ds(row, 8), pl.ds(pl.multiple_of(block * 128, 128), 128)]

    def flip(a, b):
        return rem(a + b, 2)

    def deliver(quarter, step):
        z_hi = flip(div(chip[2], 2), rem(step, 2))
        y_to = flip(rem(chip[1], 2), rem(div(step, 4), 2)) + 2 * flip(div(chip[1], 2), rem(div(step, 2), 2))
        x_lo = flip(rem(chip[0], 2), div(step, 8))
        x_to, z_to = x_lo + 2 * rem(quarter, 2), 2 * z_hi + div(quarter, 2)
        pltpu.make_async_remote_copy(
            src_ref=tile_ref.at[quarter * 16 + z_hi + 2 * y_to + 8 * x_lo],
            dst_ref=here,
            send_sem=send_sems.at[2],
            recv_sem=recv_sems.at[2],
            device_id=device(x_to, y_to, z_to, classes[2]),
            device_id_type=MESH,
        ).start()

    def deliver_some(step, _):
        other = 3 - step
        quarter = flip(div(chip[0], 2), rem(other, 2)) + 2 * flip(rem(chip[2], 2), div(other, 2))
        rows = pl.ds(pl.multiple_of(quarter * 256, 16), 256)
        last_ref[...] = jnp.dot(h_ref[rows, :], sum_ref[...], preferred_element_type=F32)
        tiles = last_ref[0:128, 0:128] + (last_ref[0:128, 128:256] + last_ref[128:256, 0:128])
        tile_ref[pl.ds(quarter * 16, 16)] = tiles.reshape(16, 8, 128)

        def body(i, _):
            deliver(quarter, 15 - i)
            return 0

        lax.fori_loop(0, 15, body, 0, unroll=5)

        @pl.when(jnp.logical_or(step != 3, jnp.logical_not(own)))
        def _():
            deliver(quarter, 0)

        return 0

    lax.fori_loop(0, 4, deliver_some, 0)

    @pl.when(own)
    def _():
        pltpu.make_async_copy(tile_ref.at[mine], here, recv_sems.at[2]).start()

    pltpu.make_async_copy(xr_ref.at[0:15], xr_ref.at[0:15], send_sems.at[0]).wait()
    pltpu.make_async_copy(part_ref.at[0:7], part_ref.at[0:7], send_sems.at[1]).wait()

    @pl.when(own)
    def _():
        pltpu.make_async_copy(tile_ref.at[0:63], tile_ref.at[0:63], send_sems.at[2]).wait()

    @pl.when(jnp.logical_not(own))
    def _():
        pltpu.make_async_copy(tile_ref, tile_ref, send_sems.at[2]).wait()

    pltpu.make_async_copy(out_ref, out_ref, recv_sems.at[2]).wait()


def shards(traces, phase_coef):
    return pl.pallas_call(
        kernel,
        out_shape=jax.ShapeDtypeStruct((32, 2048), F32),
        in_specs=[
            pl.BlockSpec(memory_space=pl.ANY),
            pl.BlockSpec(memory_space=pl.ANY),
            pl.BlockSpec(memory_space=pl.ANY),
        ],
        out_specs=pl.BlockSpec(memory_space=pl.ANY),
        scratch_shapes=[
            pltpu.SMEM((2, 4), F32),
            pltpu.VMEM((6, 64, 128), F32),
            pltpu.VMEM((3, 36, 8, 128), F32),
            pltpu.VMEM((4, 6, 8, 128), F32),
            pltpu.VMEM((5, 8, 128), F32),
            pltpu.VMEM((12, 4, 8, 128), F32),
            pltpu.VMEM((12, 4, 8, 128), F32),
            pltpu.VMEM((12, 4, 8, 128), F32),
            pltpu.VMEM((1536, 512), BF16),
            pltpu.VMEM((1024, 128), BF16),
            pltpu.VMEM((16, 32, 128), F32),
            pltpu.VMEM((512, 256), BF16),
            pltpu.VMEM((768, 256), F32),
            pltpu.VMEM((8, 96, 128), F32),
            pltpu.VMEM((8, 96, 128), F32),
            pltpu.VMEM((128, 256), BF16),
            pltpu.VMEM((256, 256), F32),
            pltpu.VMEM((64, 8, 128), F32),
            pltpu.SemaphoreType.DMA((3,)),
            pltpu.SemaphoreType.DMA((5,)),
        ],
        compiler_params=pltpu.CompilerParams(
            collective_id=0, has_side_effects=True, vmem_limit_bytes=60 * 2**20
        ),
    )(traces, phase_coef, jnp.asarray(tail_table()))


def solution(mesh):
    placed = (P(("gx", "gy"), None), P())
    return jax.shard_map(
        shards, mesh=mesh, in_specs=placed, out_specs=P(("gx", "gy"), None), check_vma=False
    )
```

```python
import functools

import jax
import jax.numpy as jnp
import numpy as np
from jax import lax
from jax.experimental import pallas as pl
from jax.experimental.pallas import tpu as pltpu
from jax.sharding import PartitionSpec as P

ORDER = 6
MESH = pl.DeviceIdType.MESH
F32 = jnp.float32
BF16 = jnp.bfloat16
AMP = 64.0

NODES = 0.5 * np.cos(np.pi * (2.0 * np.arange(ORDER) + 1.0) / (2.0 * ORDER))


def lagrange(points):
    points = np.asarray(points)[..., None, None]
    same = np.eye(ORDER, dtype=bool)
    spread = np.where(same, 1.0, NODES[:, None] - NODES[None, :])
    return np.where(same, 1.0, (points - NODES[None, :]) / spread).prod(-1)


CENTRE = lagrange(0.0)
HALVES = np.stack([((side - 0.5) + NODES) * 0.5 for side in (0, 1)])
TABLE = lagrange(HALVES)
WEIGHT = np.transpose(TABLE, (0, 2, 1))


def tail_table():
    out = np.zeros((ORDER, 64, 128))
    for high in range(64):
        total = np.eye(ORDER)
        for place in range(6):
            total = TABLE[(high >> place) & 1] @ total
        out[:, high, :96] = np.repeat(CENTRE[:, None] * total, 16, axis=1)
    return out.astype(np.float32)


def fit(function, terms):
    u = 0.125 + 0.125 * np.cos(np.pi * (np.arange(200) + 0.5) / 200)
    poly = np.polynomial.chebyshev.Chebyshev.fit(u, function(np.sqrt(u)), terms - 1, domain=[0, 0.25])
    return [float(c) for c in poly.convert(kind=np.polynomial.Polynomial).coef]


SIN = fit(lambda r: np.sin(np.pi * r) / r, 5)
SIN2 = [2.0 * c for c in fit(lambda r: np.sin(np.pi * r) / r, 4)]
COS = fit(lambda r: np.cos(np.pi * r), 5)


def horner(coefs, u):
    total = coefs[-1]
    for c in coefs[-2::-1]:
        total = total * u + c
    return total


def turn(c):
    r = c - jnp.floor(c + 0.5)
    u = r * r
    twice = r * horner(SIN2, u)
    half_cos = horner(COS, u)
    return 1.0 - (0.5 * twice) * twice, twice * half_cos


def turn_cos(c):
    r = c - jnp.floor(c + 0.5)
    twice = r * horner(SIN2, r * r)
    return 1.0 - (0.5 * twice) * twice


def half_turn(y):
    r = 0.5 - y
    u = r * r
    return r * horner(SIN, u), horner(COS, u)


def bend_value(coef, row, y):
    cosine = (0.5 - y) * horner(SIN, (0.5 - y) * (0.5 - y))
    c0, c1, c2, c3 = (coef[row, m] for m in range(4))
    return (c0 - c2) + cosine * ((c1 - 3.0 * c3) + cosine * (2.0 * c2 + cosine * (4.0 * c3)))


def bend_step(coef, middle, size):
    e1, e2, e3 = (coef[0, m] * float(-2.0 * AMP * np.sin(np.pi * m * size / 2.0)) for m in (1, 2, 3))
    cosine, sine = half_turn(middle)
    return sine * ((e1 - e3) + cosine * (2.0 * e2 + cosine * (4.0 * e3)))


def apply_real(weights, values):
    out = []
    for t in range(ORDER):
        total = weights[t][0] * values[0]
        for s in range(1, ORDER):
            total = total + weights[t][s] * values[s]
        out.append(total)
    return out


def iota(axis):
    return lax.broadcasted_iota(jnp.int32, (8, 128), axis)


def asf(value):
    return value.astype(F32)


def div(a, b):
    return lax.div(a, jnp.int32(b))


def rem(a, b):
    return lax.rem(a, jnp.int32(b))


def position():
    gx, gy = lax.axis_index("gx"), lax.axis_index("gy")
    return rem(gx, 4), div(gy, 4), rem(div(gy, 2), 2) * 2 + div(gx, 4), rem(gy, 2)


def device(x, y, z, core):
    return {"gx": rem(z, 2) * 4 + x, "gy": y * 4 + div(z, 2) * 2 + core}


def lane_parts(classes, core):
    lane = iota(1)
    place = lane >> 4
    x, y, z = (
        (2 * c + e + core) & 3 for c, e in zip(classes, (place >> 2, (place >> 1) & 1, place & 1))
    )
    return (z >> 1) + 2 * y + 8 * x + 32 * (z & 1), lane & 15


def early_levels(coef, box, top, v_ref):
    sub = iota(0)
    bits = [asf(sub & 1), asf((sub >> 1) & 1), asf(sub >> 2)]
    sign = [2.0 * bit - 1.0 for bit in bits]
    x0 = jnp.full((8, 128), 0.5, F32)
    x1 = x0 + sign[0] * 0.25
    x2 = x1 + sign[1] * 0.125
    word4 = asf(box * 16 + top)
    steps = bend_step(coef, x0 + sign[0] * 0.125, 0.25)
    p0_mid = coef[0, 0] - coef[0, 2]
    first = {}
    for j0 in range(2):
        outs = []
        for j1 in range(2):
            j = j0 + 2 * j1
            word = word4 * 4.0 + j
            start = 0.5 * (j0 + 0.5) + AMP * p0_mid * bend_value(coef, 1, (word + 0.5) * 2.0**-12)
            cosines, sines = [], []
            for s in range(ORDER):
                node = float(NODES[s])
                p1 = bend_value(coef, 1, (word + (0.5 + node)) * 2.0**-12)
                c, d = turn(start + sign[0] * ((j + 0.5 + node) * 0.25 + steps * p1))
                cosines.append(c)
                sines.append(d)
            outs.append((cosines, sines))
        weights = [[float(WEIGHT[j0][t][s] * CENTRE[s]) for s in range(ORDER)] for t in range(ORDER)]
        joined = [[jnp.stack([outs[0][c][s], outs[1][c][s]]) for s in range(ORDER)] for c in range(2)]
        first[j0] = [apply_real(weights, joined[c]) for c in range(2)]
    steps = bend_step(coef, x1 + sign[1] * 0.0625, 0.125)
    second = {}
    for j1 in range(2):
        word = word4 * 2.0 + j1
        linear = j1 + 2.0 * asf(top & 1) + 0.5
        real, imag = [], []
        for s in range(ORDER):
            node = float(NODES[s])
            p1 = bend_value(coef, 1, (word + (0.5 + node)) * 2.0**-11)
            c, d = turn(sign[1] * ((linear + node) * 0.25 + steps * p1))
            a = jnp.stack([first[0][0][s][j1], first[1][0][s][j1]])
            b = jnp.stack([first[0][1][s][j1], first[1][1][s][j1]])
            real.append(a * c - b * d)
            imag.append(a * d + b * c)
        weights = [[float(WEIGHT[j1][t][s]) for s in range(ORDER)] for t in range(ORDER)]
        second[j1] = (apply_real(weights, real), apply_real(weights, imag))
    steps = bend_step(coef, x2 + sign[2] * 0.03125, 0.0625)
    linear = asf(top & 3) + 0.5
    real, imag = [], []
    for s in range(ORDER):
        node = float(NODES[s])
        p1 = bend_value(coef, 1, (word4 + (0.5 + node)) * 2.0**-10)
        c, d = turn(sign[2] * ((linear + node) * 0.25 + steps * p1))
        a = jnp.concatenate([second[0][0][s], second[1][0][s]])
        b = jnp.concatenate([second[0][1][s], second[1][1][s]])
        real.append(a * c - b * d)
        imag.append(a * d + b * c)
    weights = lane_weights(top & 1)
    for c, values in enumerate((real, imag)):
        for t, value in enumerate(apply_real(weights, values)):
            v_ref[2 * t + c] = value


def lane_weights(bit):
    pick = bit == 1
    return [
        [jnp.where(pick, float(WEIGHT[1][t][s]), float(WEIGHT[0][t][s])) for s in range(ORDER)]
        for t in range(ORDER)
    ]


def late_setup(coef, box, top, w_ref, p_ref, c_ref):
    for i, level in enumerate((4, 5, 6)):
        weights = lane_weights((top >> (level - 3)) & 1)
        for t in range(ORDER):
            for s in range(ORDER):
                w_ref[i, ORDER * t + s] = weights[t][s]
        word = asf(box * 2 ** (7 - level) + (top >> (level - 3)))
        for s in range(ORDER):
            p_ref[i, s] = bend_value(coef, 1, (word + float(0.5 + NODES[s])) * 2.0 ** (level - 13))
    for s in range(ORDER):
        p_ref[3, s] = bend_value(coef, 1, (asf(box) + float(0.5 + NODES[s])) * 2.0**-6)
    turn_of = top & 7

    def by_lane(values):
        out = jnp.full((8, 128), float(values[ORDER - 1]), F32)
        for t in range(ORDER - 1):
            out = jnp.where(turn_of == t, float(values[t]), out)
        return out

    e1, e2, e3 = (coef[0, m] * by_lane(-2.0 * AMP * np.sin(np.pi * m * NODES / 128.0)) for m in (1, 2, 3))
    node = by_lane(NODES)
    c_ref[0] = node
    c_ref[1] = e1 - e3
    c_ref[2] = 2.0 * e2
    c_ref[3] = 4.0 * e3
    c_ref[4] = node * (asf(box) + 0.5)


def spread(value, t):
    return jnp.take_along_axis(value, (iota(1) & 120) + t, axis=1)


def late_levels(coef, box, top, q3, w_ref, p_ref, c_ref, v3, v4, v5, g_ref):
    sub = iota(0)
    x3 = asf(4 * (sub & 1) + (sub & 2) + (sub >> 2)) * 0.125 + 0.0625
    full = box * 16 + top
    states = {3: v3, 4: v4, 5: v5}

    def turns(level, parent, sign):
        i = level - 4
        steps = bend_step(coef, parent + sign * 2.0 ** -(level + 2), 2.0 ** -(level + 1))
        linear = asf((full >> (level - 3)) & 3) + 0.5
        return [turn(sign * ((linear + float(NODES[s])) * 0.25 + steps * p_ref[i, s])) for s in range(ORDER)]

    def level_step(level, parent, bit):
        i = level - 4
        sign = (2 * bit - 1).astype(F32)
        source, target = states[level - 1], states[level]
        real, imag = [], []
        for s, (c, d) in enumerate(turns(level, parent, sign)):
            a, b = source[2 * s], source[2 * s + 1]
            real.append(a * c - b * d)
            imag.append(a * d + b * c)
        weights = [[w_ref[i, ORDER * t + s] for s in range(ORDER)] for t in range(ORDER)]
        for c, values in enumerate((real, imag)):
            for t, value in enumerate(apply_real(weights, values)):
                target[2 * t + c] = value
        return parent + sign * 2.0 ** -(level + 1)

    def last_step(parent, bit, place):
        sign = (2 * bit - 1).astype(F32)
        middle = parent + sign * 2.0**-7 + c_ref[0] * (1.0 / 128.0)
        cosine, sine = half_turn(middle)
        steps = sine * (c_ref[1] + cosine * (c_ref[2] + cosine * c_ref[3]))
        switch = [turn((c_ref[4] + c_ref[0] * float(NODES[u])) + steps * p_ref[3, u]) for u in range(ORDER)]
        merged = []
        for s, (c, d) in enumerate(turns(6, parent, sign)):
            a = b = None
            for u in range(ORDER):
                weight = w_ref[2, ORDER * u + s]
                a = switch[u][0] * weight if a is None else a + switch[u][0] * weight
                b = switch[u][1] * weight if b is None else b + switch[u][1] * weight
            c, d = a * c - b * d, a * d + b * c
            merged.append((c, d - c, c + d))
        parts = [v5[2 * s] + v5[2 * s + 1] for s in range(ORDER)]
        for t in range(ORDER):
            k1 = k2 = k3 = None
            for s in range(ORDER):
                c, up, down = (spread(value, t) for value in merged[s])
                m1, m2, m3 = parts[s] * c, v5[2 * s] * up, v5[2 * s + 1] * down
                k1 = m1 if k1 is None else k1 + m1
                k2 = m2 if k2 is None else k2 + m2
                k3 = m3 if k3 is None else k3 + m3
            real, imag = k1 - k3, k1 + k2
            rows = pl.ds(pl.multiple_of(place * 192 + 16 * t, 16), 16)
            rows_low = pl.ds(pl.multiple_of(place * 192 + 96 + 16 * t, 16), 16)
            for j in range(4):
                both = jnp.concatenate([real[j], imag[j]], axis=0)
                high = both.astype(BF16)
                g_ref[rows, 128 * j : 128 * (j + 1)] = high
                g_ref[rows_low, 128 * j : 128 * (j + 1)] = (both - high.astype(F32)).astype(BF16)

    x4 = level_step(4, x3, q3)

    def over4(q4, _):
        x5 = level_step(5, x4, q4)

        def over5(q5, _):
            last_step(x5, q5, 4 * q3 + q4 + 2 * q5)
            return 0

        return lax.fori_loop(0, 2, over5, 0)

    lax.fori_loop(0, 2, over4, 0)


def last_weights(coef, group, tail_ref, h_ref):
    sub, lane = iota(0), iota(1)
    own = lane & 7
    same = sub == own
    box6 = 32 * (own & 1) + 8 * (own & 2) + 2 * (own & 4)
    box6 = box6 + (4 * rem(group, 2) + 2 * rem(div(group, 2), 2) + div(group, 4))
    inner = 32 * (sub & 1) + 8 * (sub & 2) + 2 * (sub & 4)
    base = box6 * 64 + inner
    quarter = 0.25 * asf((lane >> 3) & 1)
    p1_mid = coef[1, 0] - coef[1, 2]

    def rows_of(r):
        centre = (asf(base + (4 * rem(r, 2) + 2 * rem(div(r, 2), 2) + div(r, 4))) + 0.5) * 2.0**-12
        total = None
        for t in range(ORDER):
            node = float(NODES[t])
            steps = bend_step(coef, centre + node / 8192.0, node / 4096.0)
            term = turn_cos((quarter - 0.5 * node) - steps * p1_mid)
            term = term * tail_ref[t, pl.ds(pl.multiple_of(8 * r, 8), 8), :]
            total = term if total is None else total + term
        return total

    def body(i, _):
        for half in range(2):
            total = rows_of(2 * i + half)
            for k in range(0, 8, 2):
                both = jnp.concatenate(
                    [jnp.where(same, jnp.broadcast_to(total[k + n : k + n + 1], (8, 128)), 0.0) for n in range(2)], axis=0
                )
                high = both.astype(BF16)
                row = 64 * half + 8 * k
                h_ref[pl.ds(pl.multiple_of(256 * i + row, 16), 16), :] = high
                h_ref[pl.ds(pl.multiple_of(256 * i + 128 + row, 16), 16), :] = (both - high.astype(F32)).astype(BF16)
        return 0

    lax.fori_loop(0, 4, body, 0)


def kernel(
    x_ref,
    coef_hbm,
    tail_hbm,
    out_ref,
    coef_ref,
    tail_ref,
    w_ref,
    p_ref,
    c_ref,
    v3,
    v4,
    v5,
    g_ref,
    h_ref,
    xr_ref,
    xs_ref,
    wide_ref,
    part_ref,
    rr_ref,
    sum_ref,
    last_ref,
    tile_ref,
    send_sems,
    recv_sems,
):
    fetch_coef = pltpu.make_async_copy(coef_hbm, coef_ref, recv_sems.at[3])
    fetch_tail = pltpu.make_async_copy(tail_hbm, tail_ref, recv_sems.at[4])
    fetch_coef.start()
    fetch_tail.start()
    chip = position()
    core = chip[3]
    own_u = [rem(p + 3 * core, 4) for p in chip[:3]]
    other_u = [rem(p + 3 * (1 - core), 4) for p in chip[:3]]
    classes = [div(u, 2) for u in own_u]
    groups = [div(rem(u + 3, 4), 2) for u in own_u]
    ends = [rem(u, 2) for u in own_u]
    target = classes[0] + 2 * classes[1] + 4 * classes[2]
    block = groups[0] + 2 * groups[1] + 4 * groups[2] + 8 * core

    def bits(i):
        return rem(i, 2), rem(div(i, 2), 2), div(i, 4)

    def member(tiling, cs, gs):
        return device(*(rem(2 * c + rem(g + 1 + c, 2) + tiling, 4) for c, g in zip(cs, gs)), tiling)

    barrier = pltpu.get_barrier_semaphore()

    def greet_class(step, _):
        es = [rem(e + b, 2) for e, b in zip(ends, bits(rem(step, 8)))]
        source = device(
            *(rem(2 * c + e + core, 4) for c, e in zip(classes, es)), rem(core + div(step, 8), 2)
        )
        pl.semaphore_signal(barrier, inc=1, device_id=source, device_id_type=MESH)
        return 0

    lax.fori_loop(1, 16, greet_class, 0, unroll=True)

    def greet_group(step, _):
        cs = [rem(c + b, 2) for c, b in zip(classes, bits(step))]
        pl.semaphore_signal(barrier, inc=1, device_id=member(core, cs, groups), device_id_type=MESH)
        return 0

    lax.fori_loop(1, 8, greet_group, 0, unroll=True)

    pl.semaphore_wait(barrier, 22)

    def slot_of(us):
        return 2 * (rem(us[2], 2) + 2 * rem(us[1], 2) + 4 * rem(us[0], 2)) + core

    def scatter(tiling, us):
        slot = slot_of(us)
        cs = [div(u, 2) for u in us]

        def body(step, _):
            gs = [rem(g + b, 2) for g, b in zip(groups, bits(step))]
            m = gs[0] + 2 * gs[1] + 4 * gs[2] + 8 * tiling
            pltpu.make_async_remote_copy(
                src_ref=x_ref.at[:, pl.ds(pl.multiple_of(m * 128, 128), 128)],
                dst_ref=xr_ref.at[slot],
                send_sem=send_sems.at[0],
                recv_sem=recv_sems.at[0],
                device_id=member(tiling, cs, gs),
                device_id_type=MESH,
            ).start()
            return 0

        return body

    lax.fori_loop(1, 8, scatter(core, own_u), 0, unroll=True)
    lax.fori_loop(0, 8, scatter(1 - core, other_u), 0, unroll=True)
    pltpu.make_async_copy(
        x_ref.at[:, pl.ds(pl.multiple_of(block * 128, 128), 128)], xr_ref.at[slot_of(own_u)], recv_sems.at[0]
    ).start()

    box, top = lane_parts(classes, core)
    fetch_coef.wait()
    early_levels(coef_ref, box, top, v3)
    late_setup(coef_ref, box, top, w_ref, p_ref, c_ref)

    def boxes(q3, _):
        late_levels(coef_ref, box, top, q3, w_ref, p_ref, c_ref, v3, v4, v5, g_ref)
        return 0

    def products(q3):
        rows = pl.ds(pl.multiple_of(q3 * 768, 16), 768)
        wide_ref[...] = jnp.dot(g_ref[rows, :], xs_ref[...], preferred_element_type=F32)

    def part(i):
        high = pl.ds(pl.multiple_of(i * 192, 8), 96)
        low = pl.ds(pl.multiple_of(i * 192 + 96, 8), 96)
        return wide_ref[high, 0:128] + (wide_ref[high, 128:256] + wide_ref[low, 0:128])

    def reduce(q3):
        def body(step, _):
            other = [q3, rem(classes[1] + rem(step, 2), 2), rem(classes[2] + div(step, 2), 2)]
            i = other[1] + 2 * other[2]
            part_ref[4 * q3 + i] = part(i)
            pltpu.make_async_remote_copy(
                src_ref=part_ref.at[4 * q3 + i],
                dst_ref=rr_ref.at[target],
                send_sem=send_sems.at[1],
                recv_sem=recv_sems.at[1],
                device_id=member(core, other, groups),
                device_id_type=MESH,
            ).start()
            return 0

        return body

    far, near = 1 - classes[0], classes[0]
    lax.fori_loop(0, 2, boxes, 0)
    fetch_tail.wait()
    last_weights(coef_ref, target, tail_ref, h_ref)
    pltpu.make_async_copy(xr_ref, xr_ref, recv_sems.at[0]).wait()
    for i in range(8):
        for j in range(4):
            piece = jnp.concatenate([xr_ref[2 * i + s, pl.ds(j, 8, stride=4), :] for s in range(2)], axis=0)
            high = piece.astype(BF16)
            rows = slice(128 * j + 16 * i, 128 * j + 16 * i + 16)
            xs_ref[rows, 0:128] = high
            xs_ref[rows, 128:256] = (piece - high.astype(F32)).astype(BF16)
    products(far)
    lax.fori_loop(0, 4, reduce(far), 0, unroll=True)
    products(near)
    lax.fori_loop(1, 4, reduce(near), 0, unroll=True)
    rr_ref[target] = part(classes[1] + 2 * classes[2])
    pltpu.make_async_copy(rr_ref.at[0:7], rr_ref.at[0:7], recv_sems.at[1]).wait()
    for i in range(0, 12, 2):
        rows = slice(8 * i, 8 * i + 16)
        total = rr_ref[0, rows, :]
        for k in range(1, 8):
            total = total + rr_ref[k, rows, :]
        high = total.astype(BF16)
        sum_ref[rows, 0:128] = high
        sum_ref[rows, 128:256] = (total - high.astype(F32)).astype(BF16)
    sum_ref[96:128, :] = jnp.zeros((32, 256), BF16)

    mine = div(chip[2], 2) + 2 * chip[1] + 8 * chip[0] + 32 * rem(chip[2], 2)
    own = core == classes[2]
    row = pl.multiple_of((classes[0] + 2 * classes[1]) * 8, 8)
    here = out_ref.at[pl.ds(row, 8), pl.ds(pl.multiple_of(block * 128, 128), 128)]

    def flip(a, b):
        return rem(a + b, 2)

    def deliver(quarter, step):
        z_hi = flip(div(chip[2], 2), rem(step, 2))
        y_to = flip(rem(chip[1], 2), rem(div(step, 4), 2)) + 2 * flip(div(chip[1], 2), rem(div(step, 2), 2))
        x_lo = flip(rem(chip[0], 2), div(step, 8))
        x_to, z_to = x_lo + 2 * rem(quarter, 2), 2 * z_hi + div(quarter, 2)
        pltpu.make_async_remote_copy(
            src_ref=tile_ref.at[quarter * 16 + z_hi + 2 * y_to + 8 * x_lo],
            dst_ref=here,
            send_sem=send_sems.at[2],
            recv_sem=recv_sems.at[2],
            device_id=device(x_to, y_to, z_to, classes[2]),
            device_id_type=MESH,
        ).start()

    def deliver_some(step, _):
        other = 3 - step
        quarter = flip(div(chip[0], 2), rem(other, 2)) + 2 * flip(rem(chip[2], 2), div(other, 2))
        rows = pl.ds(pl.multiple_of(quarter * 256, 16), 256)
        last_ref[...] = jnp.dot(h_ref[rows, :], sum_ref[...], preferred_element_type=F32)
        tiles = last_ref[0:128, 0:128] + (last_ref[0:128, 128:256] + last_ref[128:256, 0:128])
        tile_ref[pl.ds(quarter * 16, 16)] = tiles.reshape(16, 8, 128)

        def body(i, _):
            deliver(quarter, 15 - i)
            return 0

        lax.fori_loop(0, 15, body, 0, unroll=5)

        @pl.when(jnp.logical_or(step != 3, jnp.logical_not(own)))
        def _():
            deliver(quarter, 0)

        return 0

    lax.fori_loop(0, 4, deliver_some, 0)

    @pl.when(own)
    def _():
        pltpu.make_async_copy(tile_ref.at[mine], here, recv_sems.at[2]).start()

    pltpu.make_async_copy(xr_ref.at[0:15], xr_ref.at[0:15], send_sems.at[0]).wait()
    pltpu.make_async_copy(part_ref.at[0:7], part_ref.at[0:7], send_sems.at[1]).wait()

    @pl.when(own)
    def _():
        pltpu.make_async_copy(tile_ref.at[0:63], tile_ref.at[0:63], send_sems.at[2]).wait()

    @pl.when(jnp.logical_not(own))
    def _():
        pltpu.make_async_copy(tile_ref, tile_ref, send_sems.at[2]).wait()

    pltpu.make_async_copy(out_ref, out_ref, recv_sems.at[2]).wait()


def shards(traces, phase_coef):
    return pl.pallas_call(
        kernel,
        out_shape=jax.ShapeDtypeStruct((32, 2048), F32),
        in_specs=[
            pl.BlockSpec(memory_space=pl.ANY),
            pl.BlockSpec(memory_space=pl.ANY),
            pl.BlockSpec(memory_space=pl.ANY),
        ],
        out_specs=pl.BlockSpec(memory_space=pl.ANY),
        scratch_shapes=[
            pltpu.SMEM((2, 4), F32),
            pltpu.VMEM((6, 64, 128), F32),
            pltpu.VMEM((3, 36, 8, 128), F32),
            pltpu.VMEM((4, 6, 8, 128), F32),
            pltpu.VMEM((5, 8, 128), F32),
            pltpu.VMEM((12, 4, 8, 128), F32),
            pltpu.VMEM((12, 4, 8, 128), F32),
            pltpu.VMEM((12, 4, 8, 128), F32),
            pltpu.VMEM((1536, 512), BF16),
            pltpu.VMEM((1024, 128), BF16),
            pltpu.VMEM((16, 32, 128), F32),
            pltpu.VMEM((512, 256), BF16),
            pltpu.VMEM((768, 256), F32),
            pltpu.VMEM((8, 96, 128), F32),
            pltpu.VMEM((8, 96, 128), F32),
            pltpu.VMEM((128, 256), BF16),
            pltpu.VMEM((256, 256), F32),
            pltpu.VMEM((64, 8, 128), F32),
            pltpu.SemaphoreType.DMA((3,)),
            pltpu.SemaphoreType.DMA((5,)),
        ],
        compiler_params=pltpu.CompilerParams(
            collective_id=0, has_side_effects=True, vmem_limit_bytes=60 * 2**20
        ),
    )(traces, phase_coef, jnp.asarray(tail_table()))


def solution(mesh):
    placed = (P(("gx", "gy"), None), P())
    return jax.shard_map(
        shards, mesh=mesh, in_specs=placed, out_specs=P(("gx", "gy"), None), check_vma=False
    )
```

```python
import functools

import jax
import jax.numpy as jnp
import numpy as np
from jax import lax
from jax.experimental import pallas as pl
from jax.experimental.pallas import tpu as pltpu
from jax.sharding import PartitionSpec as P

ORDER = 6
MESH = pl.DeviceIdType.MESH
F32 = jnp.float32
BF16 = jnp.bfloat16
AMP = 64.0

NODES = 0.5 * np.cos(np.pi * (2.0 * np.arange(ORDER) + 1.0) / (2.0 * ORDER))


def lagrange(points):
    points = np.asarray(points)[..., None, None]
    same = np.eye(ORDER, dtype=bool)
    spread = np.where(same, 1.0, NODES[:, None] - NODES[None, :])
    return np.where(same, 1.0, (points - NODES[None, :]) / spread).prod(-1)


CENTRE = lagrange(0.0)
HALVES = np.stack([((side - 0.5) + NODES) * 0.5 for side in (0, 1)])
TABLE = lagrange(HALVES)
WEIGHT = np.transpose(TABLE, (0, 2, 1))


def tail_table():
    out = np.zeros((ORDER, 64, 128))
    for high in range(64):
        total = np.eye(ORDER)
        for place in range(6):
            total = TABLE[(high >> place) & 1] @ total
        out[:, high, :96] = np.repeat(CENTRE[:, None] * total, 16, axis=1)
    return out.astype(np.float32)


def fit(function, terms):
    u = 0.125 + 0.125 * np.cos(np.pi * (np.arange(200) + 0.5) / 200)
    poly = np.polynomial.chebyshev.Chebyshev.fit(u, function(np.sqrt(u)), terms - 1, domain=[0, 0.25])
    return [float(c) for c in poly.convert(kind=np.polynomial.Polynomial).coef]


SIN = fit(lambda r: np.sin(np.pi * r) / r, 5)
SIN2 = [2.0 * c for c in fit(lambda r: np.sin(np.pi * r) / r, 4)]
COS = fit(lambda r: np.cos(np.pi * r), 5)


def horner(coefs, u):
    total = coefs[-1]
    for c in coefs[-2::-1]:
        total = total * u + c
    return total


def turn(c):
    r = c - jnp.floor(c + 0.5)
    u = r * r
    twice = r * horner(SIN2, u)
    half_cos = horner(COS, u)
    return 1.0 - (0.5 * twice) * twice, twice * half_cos


def turn_cos(c):
    r = c - jnp.floor(c + 0.5)
    twice = r * horner(SIN2, r * r)
    return 1.0 - (0.5 * twice) * twice


def half_turn(y):
    r = 0.5 - y
    u = r * r
    return r * horner(SIN, u), horner(COS, u)


def bend_value(coef, row, y):
    cosine = (0.5 - y) * horner(SIN, (0.5 - y) * (0.5 - y))
    c0, c1, c2, c3 = (coef[row, m] for m in range(4))
    return (c0 - c2) + cosine * ((c1 - 3.0 * c3) + cosine * (2.0 * c2 + cosine * (4.0 * c3)))


def bend_terms(coef, size):
    e1, e2, e3 = (coef[0, m] * float(-2.0 * AMP * np.sin(np.pi * m * size / 2.0)) for m in (1, 2, 3))
    return e1 - e3, 2.0 * e2, 4.0 * e3


def bend_step(terms, middle):
    cosine, sine = half_turn(middle)
    return sine * (terms[0] + cosine * (terms[1] + cosine * terms[2]))


def apply_real(weights, values):
    out = []
    for t in range(ORDER):
        total = weights[t][0] * values[0]
        for s in range(1, ORDER):
            total = total + weights[t][s] * values[s]
        out.append(total)
    return out


def iota(axis):
    return lax.broadcasted_iota(jnp.int32, (8, 128), axis)


def asf(value):
    return value.astype(F32)


def div(a, b):
    return lax.div(a, jnp.int32(b))


def rem(a, b):
    return lax.rem(a, jnp.int32(b))


def position():
    gx, gy = lax.axis_index("gx"), lax.axis_index("gy")
    return rem(gx, 4), div(gy, 4), rem(div(gy, 2), 2) * 2 + div(gx, 4), rem(gy, 2)


def device(x, y, z, core):
    return {"gx": rem(z, 2) * 4 + x, "gy": y * 4 + div(z, 2) * 2 + core}


def lane_parts(classes, core):
    lane = iota(1)
    place = lane >> 4
    x, y, z = (
        (2 * c + e + core) & 3 for c, e in zip(classes, (place >> 2, (place >> 1) & 1, place & 1))
    )
    return (z >> 1) + 2 * y + 8 * x + 32 * (z & 1), lane & 15


def early_levels(coef, box, top, w_ref, p_ref, v_ref):
    sub = iota(0)
    bits = [asf(sub & 1), asf((sub >> 1) & 1), asf(sub >> 2)]
    sign = [2.0 * bit - 1.0 for bit in bits]
    x0 = jnp.full((8, 128), 0.5, F32)
    x1 = x0 + sign[0] * 0.25
    x2 = x1 + sign[1] * 0.125
    word4 = asf(box * 16 + top)
    steps = [
        bend_step(bend_terms(coef, 2.0 ** -(level + 1)), x + sign[level - 1] * 2.0 ** -(level + 2))
        for level, x in ((1, x0), (2, x1), (3, x2))
    ]
    p0_mid = coef[0, 0] - coef[0, 2]
    linear2 = 2.0 * asf(top & 1) + 0.5
    linear3 = asf(top & 3) + 0.5
    third = [turn(sign[2] * ((linear3 + float(NODES[s])) * 0.25 + steps[2] * p_ref[0, s])) for s in range(ORDER)]

    def side_weights(side):
        return [
            [jnp.where(side == 1, float(WEIGHT[1][t][s]), float(WEIGHT[0][t][s])) for s in range(ORDER)]
            for t in range(ORDER)
        ]

    def turned(values, angles):
        pairs = [(a * c - b * d, a * d + b * c) for (a, b), (c, d) in zip(values, angles)]
        return [a for a, _ in pairs], [b for _, b in pairs]

    def body(group, _):
        j0, j1 = rem(group, 2), div(group, 2)
        j0f, j1f, groupf = asf(j0), asf(j1), asf(group)
        word = word4 * 4.0 + groupf
        start = 0.5 * (j0f + 0.5) + AMP * p0_mid * bend_value(coef, 1, (word + 0.5) * 2.0**-12)
        real, imag = [], []
        for s in range(ORDER):
            node = float(NODES[s])
            p1 = bend_value(coef, 1, (word + (0.5 + node)) * 2.0**-12)
            c, d = turn(start + sign[0] * ((groupf + (0.5 + node)) * 0.25 + steps[0] * p1))
            real.append(c * float(CENTRE[s]))
            imag.append(d * float(CENTRE[s]))
        weights = side_weights(j0)
        values = list(zip(apply_real(weights, real), apply_real(weights, imag)))
        word = word4 * 2.0 + j1f
        angles = []
        for s in range(ORDER):
            node = float(NODES[s])
            p1 = bend_value(coef, 1, (word + (0.5 + node)) * 2.0**-11)
            angles.append(turn(sign[1] * (((linear2 + j1f) + node) * 0.25 + steps[1] * p1)))
        weights = side_weights(j1)
        real, imag = turned(values, angles)
        values = list(zip(apply_real(weights, real), apply_real(weights, imag)))
        weights = [[w_ref[0, ORDER * t + s] for s in range(ORDER)] for t in range(ORDER)]
        for c, parts in enumerate(turned(values, third)):
            for t, value in enumerate(apply_real(weights, parts)):
                v_ref[0, 2 * t + c, group] = value
        return 0

    lax.fori_loop(0, 4, body, 0)


def late_setup(coef, box, top, w_ref, p_ref, c_ref):
    full = box * 16 + top

    def body(i, scale):
        word = full >> i
        pick = (word & 1) == 1
        for t in range(ORDER):
            for s in range(ORDER):
                w_ref[i, ORDER * t + s] = jnp.where(pick, float(WEIGHT[1][t][s]), float(WEIGHT[0][t][s]))
        for s in range(ORDER):
            p_ref[i, s] = bend_value(coef, 1, (asf(word) + float(0.5 + NODES[s])) * scale)
        return scale * 2.0

    lax.fori_loop(0, 5, body, jnp.float32(2.0**-10))
    turn_of = top & 7

    def by_lane(values):
        out = jnp.full((8, 128), float(values[ORDER - 1]), F32)
        for t in range(ORDER - 1):
            out = jnp.where(turn_of == t, float(values[t]), out)
        return out

    e1, e2, e3 = (coef[0, m] * by_lane(-2.0 * AMP * np.sin(np.pi * m * NODES / 128.0)) for m in (1, 2, 3))
    node = by_lane(NODES)
    c_ref[0] = node
    c_ref[1] = e1 - e3
    c_ref[2] = 2.0 * e2
    c_ref[3] = 4.0 * e3
    c_ref[4] = node * (asf(box) + 0.5)


def spread(value, t):
    return jnp.take_along_axis(value, (iota(1) & 120) + t, axis=1)


def late_levels(coef, box, top, order, w_ref, p_ref, c_ref, v_ref, g_ref):
    sub = iota(0)
    x3 = asf(4 * (sub & 1) + (sub & 2) + (sub >> 2)) * 0.125 + 0.0625
    full = box * 16 + top
    terms = [bend_terms(coef, 2.0 ** -(level + 1)) for level in (4, 5, 6)]

    def sign_of(bit):
        return (2 * bit - 1).astype(F32)

    def turns(i, level_terms, shift, parent, sign):
        steps = bend_step(level_terms, parent + sign * shift)
        linear = asf((full >> i) & 3) + 0.5
        return [turn(sign * ((linear + float(NODES[s])) * 0.25 + steps * p_ref[i, s])) for s in range(ORDER)]

    def level_step(level, q3, q4):
        first = level == 4
        i = level - 3
        parent = x3 + jnp.where(first, 0.0, sign_of(q3) * 2.0**-5)
        sign = jnp.where(first, sign_of(q3), sign_of(q4))
        level_terms = [jnp.where(first, a, b) for a, b in zip(terms[0], terms[1])]
        real, imag = [], []
        for s, (c, d) in enumerate(turns(i, level_terms, jnp.where(first, 2.0**-6, 2.0**-7), parent, sign)):
            a, b = v_ref[i - 1, 2 * s], v_ref[i - 1, 2 * s + 1]
            real.append(a * c - b * d)
            imag.append(a * d + b * c)
        weights = [[w_ref[i, ORDER * t + s] for s in range(ORDER)] for t in range(ORDER)]
        for c, values in enumerate((real, imag)):
            for t, value in enumerate(apply_real(weights, values)):
                v_ref[i, 2 * t + c] = value

    def last_step(parent, bit, place):
        sign = sign_of(bit)
        middle = parent + sign * 2.0**-7 + c_ref[0] * (1.0 / 128.0)
        steps = bend_step((c_ref[1], c_ref[2], c_ref[3]), middle)
        switch = [turn((c_ref[4] + c_ref[0] * float(NODES[u])) + steps * p_ref[4, u]) for u in range(ORDER)]
        merged = []
        for s, (c, d) in enumerate(turns(3, terms[2], 2.0**-8, parent, sign)):
            a = b = None
            for u in range(ORDER):
                weight = w_ref[3, ORDER * u + s]
                a = switch[u][0] * weight if a is None else a + switch[u][0] * weight
                b = switch[u][1] * weight if b is None else b + switch[u][1] * weight
            c, d = a * c - b * d, a * d + b * c
            merged.append((c, d - c, c + d))
        parts = [v_ref[2, 2 * s] + v_ref[2, 2 * s + 1] for s in range(ORDER)]
        for t in range(ORDER):
            k1 = k2 = k3 = None
            for s in range(ORDER):
                c, up, down = (spread(value, t) for value in merged[s])
                m1, m2, m3 = parts[s] * c, v_ref[2, 2 * s] * up, v_ref[2, 2 * s + 1] * down
                k1 = m1 if k1 is None else k1 + m1
                k2 = m2 if k2 is None else k2 + m2
                k3 = m3 if k3 is None else k3 + m3
            real, imag = k1 - k3, k1 + k2
            rows = pl.ds(pl.multiple_of(place * 192 + 16 * t, 16), 16)
            rows_low = pl.ds(pl.multiple_of(place * 192 + 96 + 16 * t, 16), 16)
            for j in range(4):
                both = jnp.concatenate([real[j], imag[j]], axis=0)
                high = both.astype(BF16)
                g_ref[rows, 128 * j : 128 * (j + 1)] = high
                g_ref[rows_low, 128 * j : 128 * (j + 1)] = (both - high.astype(F32)).astype(BF16)

    def over(n, _):
        q3, q4 = order(div(n, 2)), rem(n, 2)

        def levels(level, _):
            level_step(level, q3, q4)
            return 0

        lax.fori_loop(4 + q4, 6, levels, 0)
        x5 = x3 + (sign_of(q3) * 2.0**-5 + sign_of(q4) * 2.0**-6)

        def over5(q5, _):
            last_step(x5, q5, 4 * q3 + q4 + 2 * q5)
            return 0

        return lax.fori_loop(0, 2, over5, 0)

    lax.fori_loop(0, 4, over, 0)


def last_weights(coef, group, tail_ref, h_ref):
    sub, lane = iota(0), iota(1)
    own = lane & 7
    same = sub == own
    box6 = 32 * (own & 1) + 8 * (own & 2) + 2 * (own & 4)
    box6 = box6 + (4 * rem(group, 2) + 2 * rem(div(group, 2), 2) + div(group, 4))
    inner = 32 * (sub & 1) + 8 * (sub & 2) + 2 * (sub & 4)
    base = box6 * 64 + inner
    quarter = 0.25 * asf((lane >> 3) & 1)
    p1_mid = coef[1, 0] - coef[1, 2]

    def rows_of(r):
        centre = (asf(base + (4 * rem(r, 2) + 2 * rem(div(r, 2), 2) + div(r, 4))) + 0.5) * 2.0**-12
        total = None
        for t in range(ORDER):
            node = float(NODES[t])
            steps = bend_step(bend_terms(coef, node / 4096.0), centre + node / 8192.0)
            term = turn_cos((quarter - 0.5 * node) - steps * p1_mid)
            term = term * tail_ref[t, pl.ds(pl.multiple_of(8 * r, 8), 8), :]
            total = term if total is None else total + term
        return total

    def body(r, _):
        total = rows_of(r)
        start = 256 * div(r, 2) + 64 * rem(r, 2)
        for k in range(0, 8, 2):
            both = jnp.concatenate(
                [jnp.where(same, jnp.broadcast_to(total[k + n : k + n + 1], (8, 128)), 0.0) for n in range(2)], axis=0
            )
            high = both.astype(BF16)
            h_ref[pl.ds(pl.multiple_of(start + 8 * k, 16), 16), :] = high
            h_ref[pl.ds(pl.multiple_of(start + 128 + 8 * k, 16), 16), :] = (both - high.astype(F32)).astype(BF16)
        return 0

    lax.fori_loop(0, 8, body, 0)


def kernel(
    x_ref,
    coef_hbm,
    tail_hbm,
    out_ref,
    coef_ref,
    tail_ref,
    w_ref,
    p_ref,
    c_ref,
    v_ref,
    g_ref,
    h_ref,
    xr_ref,
    xs_ref,
    wide_ref,
    part_ref,
    rr_ref,
    sum_ref,
    last_ref,
    tile_ref,
    send_sems,
    recv_sems,
):
    fetch_coef = pltpu.make_async_copy(coef_hbm, coef_ref, recv_sems.at[3])
    fetch_tail = pltpu.make_async_copy(tail_hbm, tail_ref, recv_sems.at[4])
    fetch_coef.start()
    fetch_tail.start()
    chip = position()
    core = chip[3]
    own_u = [rem(p + 3 * core, 4) for p in chip[:3]]
    other_u = [rem(p + 3 * (1 - core), 4) for p in chip[:3]]
    classes = [div(u, 2) for u in own_u]
    groups = [div(rem(u + 3, 4), 2) for u in own_u]
    ends = [rem(u, 2) for u in own_u]
    target = classes[0] + 2 * classes[1] + 4 * classes[2]
    block = groups[0] + 2 * groups[1] + 4 * groups[2] + 8 * core

    def bits(i):
        return rem(i, 2), rem(div(i, 2), 2), div(i, 4)

    def member(tiling, cs, gs):
        return device(*(rem(2 * c + rem(g + 1 + c, 2) + tiling, 4) for c, g in zip(cs, gs)), tiling)

    barrier = pltpu.get_barrier_semaphore()

    def greet_class(step, _):
        es = [rem(e + b, 2) for e, b in zip(ends, bits(rem(step, 8)))]
        source = device(
            *(rem(2 * c + e + core, 4) for c, e in zip(classes, es)), rem(core + div(step, 8), 2)
        )
        pl.semaphore_signal(barrier, inc=1, device_id=source, device_id_type=MESH)
        return 0

    lax.fori_loop(1, 16, greet_class, 0)

    def greet_group(step, _):
        cs = [rem(c + b, 2) for c, b in zip(classes, bits(step))]
        pl.semaphore_signal(barrier, inc=1, device_id=member(core, cs, groups), device_id_type=MESH)
        return 0

    lax.fori_loop(1, 8, greet_group, 0)

    pl.semaphore_wait(barrier, 22)

    def slot_of(us):
        return 2 * (rem(us[2], 2) + 2 * rem(us[1], 2) + 4 * rem(us[0], 2)) + core

    def scatter(tiling, us):
        slot = slot_of(us)
        cs = [div(u, 2) for u in us]

        def body(step, _):
            gs = [rem(g + b, 2) for g, b in zip(groups, bits(step))]
            m = gs[0] + 2 * gs[1] + 4 * gs[2] + 8 * tiling
            pltpu.make_async_remote_copy(
                src_ref=x_ref.at[:, pl.ds(pl.multiple_of(m * 128, 128), 128)],
                dst_ref=xr_ref.at[slot],
                send_sem=send_sems.at[0],
                recv_sem=recv_sems.at[0],
                device_id=member(tiling, cs, gs),
                device_id_type=MESH,
            ).start()
            return 0

        return body

    lax.fori_loop(1, 8, scatter(core, own_u), 0)
    lax.fori_loop(0, 8, scatter(1 - core, other_u), 0)
    pltpu.make_async_copy(
        x_ref.at[:, pl.ds(pl.multiple_of(block * 128, 128), 128)], xr_ref.at[slot_of(own_u)], recv_sems.at[0]
    ).start()

    box, top = lane_parts(classes, core)
    fetch_coef.wait()
    late_setup(coef_ref, box, top, w_ref, p_ref, c_ref)
    early_levels(coef_ref, box, top, w_ref, p_ref, v_ref)

    def order(h):
        return rem(classes[0] + 1 + h, 2)

    late_levels(coef_ref, box, top, order, w_ref, p_ref, c_ref, v_ref, g_ref)
    fetch_tail.wait()
    last_weights(coef_ref, target, tail_ref, h_ref)
    pltpu.make_async_copy(xr_ref, xr_ref, recv_sems.at[0]).wait()

    def split(i, _):
        for j in range(4):
            piece = jnp.concatenate([xr_ref[2 * i + s, pl.ds(j, 8, stride=4), :] for s in range(2)], axis=0)
            high = piece.astype(BF16)
            rows = pl.ds(pl.multiple_of(128 * j + 16 * i, 16), 16)
            xs_ref[rows, 0:128] = high
            xs_ref[rows, 128:256] = (piece - high.astype(F32)).astype(BF16)
        return 0

    lax.fori_loop(0, 8, split, 0)

    def half(h, _):
        q3 = order(h)
        rows = pl.ds(pl.multiple_of(q3 * 768, 16), 768)
        wide_ref[...] = jnp.dot(g_ref[rows, :], xs_ref[...], preferred_element_type=F32)

        def reduce(step, _):
            other = [q3, rem(classes[1] + rem(step, 2), 2), rem(classes[2] + div(step, 2), 2)]
            i = other[1] + 2 * other[2]
            high = pl.ds(pl.multiple_of(i * 192, 8), 96)
            low = pl.ds(pl.multiple_of(i * 192 + 96, 8), 96)
            part = wide_ref[high, 0:128] + (wide_ref[high, 128:256] + wide_ref[low, 0:128])
            away = jnp.logical_or(h == 0, step > 0)

            @pl.when(away)
            def _():
                part_ref[4 * q3 + i] = part
                pltpu.make_async_remote_copy(
                    src_ref=part_ref.at[4 * q3 + i],
                    dst_ref=rr_ref.at[target],
                    send_sem=send_sems.at[1],
                    recv_sem=recv_sems.at[1],
                    device_id=member(core, other, groups),
                    device_id_type=MESH,
                ).start()

            @pl.when(jnp.logical_not(away))
            def _():
                rr_ref[target] = part

            return 0

        return lax.fori_loop(0, 4, reduce, 0)

    lax.fori_loop(0, 2, half, 0)
    pltpu.make_async_copy(rr_ref.at[0:7], rr_ref.at[0:7], recv_sems.at[1]).wait()

    def add(i, _):
        rows = pl.ds(pl.multiple_of(16 * i, 16), 16)
        total = rr_ref[0, rows, :]
        for k in range(1, 8):
            total = total + rr_ref[k, rows, :]
        high = total.astype(BF16)
        sum_ref[rows, 0:128] = high
        sum_ref[rows, 128:256] = (total - high.astype(F32)).astype(BF16)
        return 0

    lax.fori_loop(0, 6, add, 0)
    sum_ref[96:128, :] = jnp.zeros((32, 256), BF16)

    mine = div(chip[2], 2) + 2 * chip[1] + 8 * chip[0] + 32 * rem(chip[2], 2)
    own = core == classes[2]
    row = pl.multiple_of((classes[0] + 2 * classes[1]) * 8, 8)
    here = out_ref.at[pl.ds(row, 8), pl.ds(pl.multiple_of(block * 128, 128), 128)]

    def flip(a, b):
        return rem(a + b, 2)

    def deliver(quarter, step):
        z_hi = flip(div(chip[2], 2), rem(step, 2))
        y_to = flip(rem(chip[1], 2), rem(div(step, 4), 2)) + 2 * flip(div(chip[1], 2), rem(div(step, 2), 2))
        x_lo = flip(rem(chip[0], 2), div(step, 8))
        x_to, z_to = x_lo + 2 * rem(quarter, 2), 2 * z_hi + div(quarter, 2)
        pltpu.make_async_remote_copy(
            src_ref=tile_ref.at[quarter * 16 + z_hi + 2 * y_to + 8 * x_lo],
            dst_ref=here,
            send_sem=send_sems.at[2],
            recv_sem=recv_sems.at[2],
            device_id=device(x_to, y_to, z_to, classes[2]),
            device_id_type=MESH,
        ).start()

    def deliver_some(step, _):
        other = 3 - step
        quarter = flip(div(chip[0], 2), rem(other, 2)) + 2 * flip(rem(chip[2], 2), div(other, 2))
        rows = pl.ds(pl.multiple_of(quarter * 256, 16), 256)
        last_ref[...] = jnp.dot(h_ref[rows, :], sum_ref[...], preferred_element_type=F32)
        tiles = last_ref[0:128, 0:128] + (last_ref[0:128, 128:256] + last_ref[128:256, 0:128])
        tile_ref[pl.ds(quarter * 16, 16)] = tiles.reshape(16, 8, 128)

        def body(i, _):
            deliver(quarter, 15 - i)
            return 0

        lax.fori_loop(0, 15, body, 0, unroll=5)

        @pl.when(jnp.logical_or(step != 3, jnp.logical_not(own)))
        def _():
            deliver(quarter, 0)

        return 0

    lax.fori_loop(0, 4, deliver_some, 0)

    @pl.when(own)
    def _():
        pltpu.make_async_copy(tile_ref.at[mine], here, recv_sems.at[2]).start()

    pltpu.make_async_copy(xr_ref.at[0:15], xr_ref.at[0:15], send_sems.at[0]).wait()
    pltpu.make_async_copy(part_ref.at[0:7], part_ref.at[0:7], send_sems.at[1]).wait()

    @pl.when(own)
    def _():
        pltpu.make_async_copy(tile_ref.at[0:63], tile_ref.at[0:63], send_sems.at[2]).wait()

    @pl.when(jnp.logical_not(own))
    def _():
        pltpu.make_async_copy(tile_ref, tile_ref, send_sems.at[2]).wait()

    pltpu.make_async_copy(out_ref, out_ref, recv_sems.at[2]).wait()


def shards(traces, phase_coef):
    return pl.pallas_call(
        kernel,
        out_shape=jax.ShapeDtypeStruct((32, 2048), F32),
        in_specs=[
            pl.BlockSpec(memory_space=pl.ANY),
            pl.BlockSpec(memory_space=pl.ANY),
            pl.BlockSpec(memory_space=pl.ANY),
        ],
        out_specs=pl.BlockSpec(memory_space=pl.ANY),
        scratch_shapes=[
            pltpu.SMEM((2, 4), F32),
            pltpu.VMEM((6, 64, 128), F32),
            pltpu.VMEM((5, 36, 8, 128), F32),
            pltpu.VMEM((5, 6, 8, 128), F32),
            pltpu.VMEM((5, 8, 128), F32),
            pltpu.VMEM((3, 12, 4, 8, 128), F32),
            pltpu.VMEM((1536, 512), BF16),
            pltpu.VMEM((1024, 128), BF16),
            pltpu.VMEM((16, 32, 128), F32),
            pltpu.VMEM((512, 256), BF16),
            pltpu.VMEM((768, 256), F32),
            pltpu.VMEM((8, 96, 128), F32),
            pltpu.VMEM((8, 96, 128), F32),
            pltpu.VMEM((128, 256), BF16),
            pltpu.VMEM((256, 256), F32),
            pltpu.VMEM((64, 8, 128), F32),
            pltpu.SemaphoreType.DMA((3,)),
            pltpu.SemaphoreType.DMA((5,)),
        ],
        compiler_params=pltpu.CompilerParams(
            collective_id=0, has_side_effects=True, vmem_limit_bytes=60 * 2**20
        ),
    )(traces, phase_coef, jnp.asarray(tail_table()))


def solution(mesh):
    placed = (P(("gx", "gy"), None), P())
    return jax.shard_map(
        shards, mesh=mesh, in_specs=placed, out_specs=P(("gx", "gy"), None), check_vma=False
    )
```

```python
import functools

import jax
import jax.numpy as jnp
import numpy as np
from jax import lax
from jax.experimental import pallas as pl
from jax.experimental.pallas import tpu as pltpu
from jax.sharding import PartitionSpec as P

ORDER = 6
LOGICAL = pl.DeviceIdType.LOGICAL
F32 = jnp.float32
BF16 = jnp.bfloat16
AMP = 64.0

NODES = 0.5 * np.cos(np.pi * (2.0 * np.arange(ORDER) + 1.0) / (2.0 * ORDER))


def lagrange(points):
    points = np.asarray(points)[..., None, None]
    same = np.eye(ORDER, dtype=bool)
    spread = np.where(same, 1.0, NODES[:, None] - NODES[None, :])
    return np.where(same, 1.0, (points - NODES[None, :]) / spread).prod(-1)


CENTRE = lagrange(0.0)
HALVES = np.stack([((side - 0.5) + NODES) * 0.5 for side in (0, 1)])
TABLE = lagrange(HALVES)
WEIGHT = np.transpose(TABLE, (0, 2, 1))


def tail_table():
    out = np.zeros((ORDER, 64, 128))
    for high in range(64):
        total = np.eye(ORDER)
        for place in range(6):
            total = TABLE[(high >> place) & 1] @ total
        out[:, high, :96] = np.repeat(CENTRE[:, None] * total, 16, axis=1)
    return out.astype(np.float32)


def fit(function, terms):
    u = 0.125 + 0.125 * np.cos(np.pi * (np.arange(200) + 0.5) / 200)
    poly = np.polynomial.chebyshev.Chebyshev.fit(u, function(np.sqrt(u)), terms - 1, domain=[0, 0.25])
    return [float(c) for c in poly.convert(kind=np.polynomial.Polynomial).coef]


SIN = fit(lambda r: np.sin(np.pi * r) / r, 5)
SIN2 = [2.0 * c for c in fit(lambda r: np.sin(np.pi * r) / r, 4)]
COS = fit(lambda r: np.cos(np.pi * r), 5)


def horner(coefs, u):
    total = coefs[-1]
    for c in coefs[-2::-1]:
        total = total * u + c
    return total


def turn(c):
    r = c - jnp.floor(c + 0.5)
    u = r * r
    twice = r * horner(SIN2, u)
    half_cos = horner(COS, u)
    return 1.0 - (0.5 * twice) * twice, twice * half_cos


def turn_cos(c):
    r = c - jnp.floor(c + 0.5)
    twice = r * horner(SIN2, r * r)
    return 1.0 - (0.5 * twice) * twice


def half_turn(y):
    r = 0.5 - y
    u = r * r
    return r * horner(SIN, u), horner(COS, u)


def bend_value(coef, row, y):
    cosine = (0.5 - y) * horner(SIN, (0.5 - y) * (0.5 - y))
    c0, c1, c2, c3 = (coef[row, m] for m in range(4))
    return (c0 - c2) + cosine * ((c1 - 3.0 * c3) + cosine * (2.0 * c2 + cosine * (4.0 * c3)))


def bend_terms(coef, size):
    e1, e2, e3 = (coef[0, m] * float(-2.0 * AMP * np.sin(np.pi * m * size / 2.0)) for m in (1, 2, 3))
    return e1 - e3, 2.0 * e2, 4.0 * e3


def bend_step(terms, middle):
    cosine, sine = half_turn(middle)
    return sine * (terms[0] + cosine * (terms[1] + cosine * terms[2]))


def apply_real(weights, values):
    out = []
    for t in range(ORDER):
        total = weights[t][0] * values[0]
        for s in range(1, ORDER):
            total = total + weights[t][s] * values[s]
        out.append(total)
    return out


def iota(axis):
    return lax.broadcasted_iota(jnp.int32, (8, 128), axis)


def asf(value):
    return value.astype(F32)


def div(a, b):
    return lax.div(a, jnp.int32(b))


def rem(a, b):
    return lax.rem(a, jnp.int32(b))


def subset(deltas, mask):
    total = None
    for k, delta in enumerate(deltas):
        if (mask >> k) & 1:
            total = delta if total is None else total + delta
    return 0 if total is None else total


def flips(bits, weights):
    return [weight * (1 - 2 * bit) for bit, weight in zip(bits, weights)]


def lane_parts(classes, core):
    lane = iota(1)
    place = lane >> 4
    x, y, z = (
        (2 * c + e + core) & 3 for c, e in zip(classes, (place >> 2, (place >> 1) & 1, place & 1))
    )
    return (z >> 1) + 2 * y + 8 * x + 32 * (z & 1), lane & 15


def early_levels(coef, box, top, w_ref, p_ref, v_ref):
    sub = iota(0)
    bits = [asf(sub & 1), asf((sub >> 1) & 1), asf(sub >> 2)]
    sign = [2.0 * bit - 1.0 for bit in bits]
    x0 = jnp.full((8, 128), 0.5, F32)
    x1 = x0 + sign[0] * 0.25
    x2 = x1 + sign[1] * 0.125
    word4 = asf(box * 16 + top)
    steps = [
        bend_step(bend_terms(coef, 2.0 ** -(level + 1)), x + sign[level - 1] * 2.0 ** -(level + 2))
        for level, x in ((1, x0), (2, x1), (3, x2))
    ]
    p0_mid = coef[0, 0] - coef[0, 2]
    linear2 = 2.0 * asf(top & 1) + 0.5
    linear3 = asf(top & 3) + 0.5
    third = [turn(sign[2] * ((linear3 + float(NODES[s])) * 0.25 + steps[2] * p_ref[0, s])) for s in range(ORDER)]

    def side_weights(side):
        return [
            [jnp.where(side == 1, float(WEIGHT[1][t][s]), float(WEIGHT[0][t][s])) for s in range(ORDER)]
            for t in range(ORDER)
        ]

    def turned(values, angles):
        pairs = [(a * c - b * d, a * d + b * c) for (a, b), (c, d) in zip(values, angles)]
        return [a for a, _ in pairs], [b for _, b in pairs]

    def body(group, _):
        j0, j1 = rem(group, 2), div(group, 2)
        j0f, j1f, groupf = asf(j0), asf(j1), asf(group)
        word = word4 * 4.0 + groupf
        start = 0.5 * (j0f + 0.5) + AMP * p0_mid * bend_value(coef, 1, (word + 0.5) * 2.0**-12)
        real, imag = [], []
        for s in range(ORDER):
            node = float(NODES[s])
            p1 = bend_value(coef, 1, (word + (0.5 + node)) * 2.0**-12)
            c, d = turn(start + sign[0] * ((groupf + (0.5 + node)) * 0.25 + steps[0] * p1))
            real.append(c * float(CENTRE[s]))
            imag.append(d * float(CENTRE[s]))
        weights = side_weights(j0)
        values = list(zip(apply_real(weights, real), apply_real(weights, imag)))
        word = word4 * 2.0 + j1f
        angles = []
        for s in range(ORDER):
            node = float(NODES[s])
            p1 = bend_value(coef, 1, (word + (0.5 + node)) * 2.0**-11)
            angles.append(turn(sign[1] * (((linear2 + j1f) + node) * 0.25 + steps[1] * p1)))
        weights = side_weights(j1)
        real, imag = turned(values, angles)
        values = list(zip(apply_real(weights, real), apply_real(weights, imag)))
        weights = [[w_ref[0, ORDER * t + s] for s in range(ORDER)] for t in range(ORDER)]
        for c, parts in enumerate(turned(values, third)):
            for t, value in enumerate(apply_real(weights, parts)):
                v_ref[0, 2 * t + c, group] = value
        return 0

    lax.fori_loop(0, 4, body, 0)


def late_setup(coef, box, top, w_ref, p_ref, c_ref):
    full = box * 16 + top

    def body(i, scale):
        word = full >> i
        pick = (word & 1) == 1
        for t in range(ORDER):
            for s in range(ORDER):
                w_ref[i, ORDER * t + s] = jnp.where(pick, float(WEIGHT[1][t][s]), float(WEIGHT[0][t][s]))
        for s in range(ORDER):
            p_ref[i, s] = bend_value(coef, 1, (asf(word) + float(0.5 + NODES[s])) * scale)
        return scale * 2.0

    lax.fori_loop(0, 5, body, jnp.float32(2.0**-10))
    turn_of = top & 7

    def by_lane(values):
        out = jnp.full((8, 128), float(values[ORDER - 1]), F32)
        for t in range(ORDER - 1):
            out = jnp.where(turn_of == t, float(values[t]), out)
        return out

    e1, e2, e3 = (coef[0, m] * by_lane(-2.0 * AMP * np.sin(np.pi * m * NODES / 128.0)) for m in (1, 2, 3))
    node = by_lane(NODES)
    c_ref[0] = node
    c_ref[1] = e1 - e3
    c_ref[2] = 2.0 * e2
    c_ref[3] = 4.0 * e3
    c_ref[4] = node * (asf(box) + 0.5)


def spread(value, t):
    return jnp.take_along_axis(value, (iota(1) & 120) + t, axis=1)


def late_levels(coef, box, top, order, w_ref, p_ref, c_ref, v_ref, g_ref):
    sub = iota(0)
    x3 = asf(4 * (sub & 1) + (sub & 2) + (sub >> 2)) * 0.125 + 0.0625
    full = box * 16 + top
    terms = [bend_terms(coef, 2.0 ** -(level + 1)) for level in (4, 5, 6)]

    def sign_of(bit):
        return (2 * bit - 1).astype(F32)

    def turns(i, level_terms, shift, parent, sign):
        steps = bend_step(level_terms, parent + sign * shift)
        linear = asf((full >> i) & 3) + 0.5
        return [turn(sign * ((linear + float(NODES[s])) * 0.25 + steps * p_ref[i, s])) for s in range(ORDER)]

    def level_step(level, q3, q4):
        first = level == 4
        i = level - 3
        parent = x3 + jnp.where(first, 0.0, sign_of(q3) * 2.0**-5)
        sign = jnp.where(first, sign_of(q3), sign_of(q4))
        level_terms = [jnp.where(first, a, b) for a, b in zip(terms[0], terms[1])]
        real, imag = [], []
        for s, (c, d) in enumerate(turns(i, level_terms, jnp.where(first, 2.0**-6, 2.0**-7), parent, sign)):
            a, b = v_ref[i - 1, 2 * s], v_ref[i - 1, 2 * s + 1]
            real.append(a * c - b * d)
            imag.append(a * d + b * c)
        weights = [[w_ref[i, ORDER * t + s] for s in range(ORDER)] for t in range(ORDER)]
        for c, values in enumerate((real, imag)):
            for t, value in enumerate(apply_real(weights, values)):
                v_ref[i, 2 * t + c] = value

    def last_step(parent, bit, place):
        sign = sign_of(bit)
        middle = parent + sign * 2.0**-7 + c_ref[0] * (1.0 / 128.0)
        steps = bend_step((c_ref[1], c_ref[2], c_ref[3]), middle)
        switch = [turn((c_ref[4] + c_ref[0] * float(NODES[u])) + steps * p_ref[4, u]) for u in range(ORDER)]
        merged = []
        for s, (c, d) in enumerate(turns(3, terms[2], 2.0**-8, parent, sign)):
            a = b = None
            for u in range(ORDER):
                weight = w_ref[3, ORDER * u + s]
                a = switch[u][0] * weight if a is None else a + switch[u][0] * weight
                b = switch[u][1] * weight if b is None else b + switch[u][1] * weight
            c, d = a * c - b * d, a * d + b * c
            merged.append((c, d - c, c + d))
        parts = [v_ref[2, 2 * s] + v_ref[2, 2 * s + 1] for s in range(ORDER)]
        for t in range(ORDER):
            k1 = k2 = k3 = None
            for s in range(ORDER):
                c, up, down = (spread(value, t) for value in merged[s])
                m1, m2, m3 = parts[s] * c, v_ref[2, 2 * s] * up, v_ref[2, 2 * s + 1] * down
                k1 = m1 if k1 is None else k1 + m1
                k2 = m2 if k2 is None else k2 + m2
                k3 = m3 if k3 is None else k3 + m3
            real, imag = k1 - k3, k1 + k2
            rows = pl.ds(pl.multiple_of(place * 192 + 16 * t, 16), 16)
            rows_low = pl.ds(pl.multiple_of(place * 192 + 96 + 16 * t, 16), 16)
            for j in range(4):
                both = jnp.concatenate([real[j], imag[j]], axis=0)
                high = both.astype(BF16)
                g_ref[rows, 128 * j : 128 * (j + 1)] = high
                g_ref[rows_low, 128 * j : 128 * (j + 1)] = (both - high.astype(F32)).astype(BF16)

    def over(n, _):
        q3, q4 = order(div(n, 2)), rem(n, 2)

        def levels(level, _):
            level_step(level, q3, q4)
            return 0

        lax.fori_loop(4 + q4, 6, levels, 0)
        x5 = x3 + (sign_of(q3) * 2.0**-5 + sign_of(q4) * 2.0**-6)

        def over5(q5, _):
            last_step(x5, q5, 4 * q3 + q4 + 2 * q5)
            return 0

        return lax.fori_loop(0, 2, over5, 0)

    lax.fori_loop(0, 4, over, 0)


def last_weights(coef, group, tail_ref, h_ref):
    sub, lane = iota(0), iota(1)
    own = lane & 7
    same = sub == own
    box6 = 32 * (own & 1) + 8 * (own & 2) + 2 * (own & 4)
    box6 = box6 + (4 * rem(group, 2) + 2 * rem(div(group, 2), 2) + div(group, 4))
    inner = 32 * (sub & 1) + 8 * (sub & 2) + 2 * (sub & 4)
    base = box6 * 64 + inner
    quarter = 0.25 * asf((lane >> 3) & 1)
    p1_mid = coef[1, 0] - coef[1, 2]

    def rows_of(r):
        centre = (asf(base + (4 * rem(r, 2) + 2 * rem(div(r, 2), 2) + div(r, 4))) + 0.5) * 2.0**-12
        total = None
        for t in range(ORDER):
            node = float(NODES[t])
            steps = bend_step(bend_terms(coef, node / 4096.0), centre + node / 8192.0)
            term = turn_cos((quarter - 0.5 * node) - steps * p1_mid)
            term = term * tail_ref[t, pl.ds(pl.multiple_of(8 * r, 8), 8), :]
            total = term if total is None else total + term
        return total

    def body(r, _):
        total = rows_of(r)
        start = 256 * div(r, 2) + 64 * rem(r, 2)
        for k in range(0, 8, 2):
            both = jnp.concatenate(
                [jnp.where(same, jnp.broadcast_to(total[k + n : k + n + 1], (8, 128)), 0.0) for n in range(2)], axis=0
            )
            high = both.astype(BF16)
            h_ref[pl.ds(pl.multiple_of(start + 8 * k, 16), 16), :] = high
            h_ref[pl.ds(pl.multiple_of(start + 128 + 8 * k, 16), 16), :] = (both - high.astype(F32)).astype(BF16)
        return 0

    lax.fori_loop(0, 8, body, 0)


def kernel(
    x_ref,
    coef_hbm,
    tail_hbm,
    out_ref,
    coef_ref,
    tail_ref,
    w_ref,
    p_ref,
    c_ref,
    v_ref,
    g_ref,
    h_ref,
    xr_ref,
    xs_ref,
    wide_ref,
    part_ref,
    rr_ref,
    sum_ref,
    last_ref,
    tile_ref,
    send_sems,
    recv_sems,
):
    fetch_coef = pltpu.make_async_copy(coef_hbm, coef_ref, recv_sems.at[3])
    fetch_tail = pltpu.make_async_copy(tail_hbm, tail_ref, recv_sems.at[4])
    fetch_coef.start()
    fetch_tail.start()
    gx, gy = lax.axis_index("gx"), lax.axis_index("gy")
    core = rem(gy, 2)
    zl, xs = div(gx, 4), rem(gx, 4)
    xh, xl = div(xs, 2), rem(xs, 2)
    yh, yl, zh = div(gy, 8), rem(div(gy, 4), 2), rem(div(gy, 2), 2)
    me = gx * 16 + gy
    highs, lows = (xh, yh, zh), (xl, yl, zl)
    unlike = [h + l - 2 * h * l for h, l in zip(highs, lows)]
    to_a = [16 * (1 - 2 * xl), 4 * (1 - 2 * yl), 64 * (1 - 2 * zl)]
    to_b = [16 * (3 - 2 * xs), 4 * (3 - 2 * (2 * yh + yl)), 2 * (1 - 2 * zh) + 64 * (1 - 2 * zl)]
    to_class = [a + core * (b - a) for a, b in zip(to_a, to_b)]
    to_group = [b + core * (a - b) for a, b in zip(to_a, to_b)]
    to_core = 1 - 2 * core
    class_a, class_b = highs, [1 - d for d in unlike]
    place_a, place_b = lows, [1 - l for l in lows]
    group_a, group_b = [1 - d for d in unlike], [1 - h for h in highs]

    def mine(for_a, for_b):
        return [a + core * (b - a) for a, b in zip(for_a, for_b)]

    def others(for_a, for_b):
        return [b + core * (a - b) for a, b in zip(for_a, for_b)]

    def number(values):
        return values[0] + 2 * values[1] + 4 * values[2]

    classes, groups = mine(class_a, class_b), mine(group_a, group_b)
    target = number(classes)
    block = number(groups) + 8 * core

    barrier = pltpu.get_barrier_semaphore()
    for mask in range(1, 16):
        source = me + subset(to_class + [to_core], mask)
        pl.semaphore_signal(barrier, inc=1, device_id=source, device_id_type=LOGICAL)
    for mask in range(1, 8):
        pl.semaphore_signal(barrier, inc=1, device_id=me + subset(to_group, mask), device_id_type=LOGICAL)
    pl.semaphore_wait(barrier, 22)

    def columns(m):
        return x_ref.at[:, pl.ds(pl.multiple_of(m * 128, 128), 128)]

    own_slot = 2 * number(mine(place_a, place_b)[::-1]) + core
    other_slot = 2 * number(others(place_a, place_b)[::-1]) + core
    other_groups = others(group_a, group_b)
    other_block = number(other_groups) + 8 * (1 - core)
    for mask in range(7, -1, -1):
        routes = [(other_block, other_groups, other_slot, me + to_core + subset(to_group, mask))]
        if mask:
            routes.append((block, groups, own_slot, me + subset(to_class, mask)))
        for first, group_bits, slot, device in routes:
            pltpu.make_async_remote_copy(
                src_ref=columns(first + subset(flips(group_bits, (1, 2, 4)), mask)),
                dst_ref=xr_ref.at[slot],
                send_sem=send_sems.at[0],
                recv_sem=recv_sems.at[0],
                device_id=device,
                device_id_type=LOGICAL,
            ).start()
    pltpu.make_async_copy(columns(block), xr_ref.at[own_slot], recv_sems.at[0]).start()

    box, top = lane_parts(classes, core)
    fetch_coef.wait()
    late_setup(coef_ref, box, top, w_ref, p_ref, c_ref)
    early_levels(coef_ref, box, top, w_ref, p_ref, v_ref)

    def order(h):
        return classes[0] + (1 - h) * (1 - 2 * classes[0])

    late_levels(coef_ref, box, top, order, w_ref, p_ref, c_ref, v_ref, g_ref)
    fetch_tail.wait()
    last_weights(coef_ref, target, tail_ref, h_ref)
    pltpu.make_async_copy(xr_ref, xr_ref, recv_sems.at[0]).wait()

    def split(i, _):
        for j in range(4):
            piece = jnp.concatenate([xr_ref[2 * i + s, pl.ds(j, 8, stride=4), :] for s in range(2)], axis=0)
            high = piece.astype(BF16)
            rows = pl.ds(pl.multiple_of(128 * j + 16 * i, 16), 16)
            xs_ref[rows, 0:128] = high
            xs_ref[rows, 128:256] = (piece - high.astype(F32)).astype(BF16)
        return 0

    lax.fori_loop(0, 8, split, 0)

    def half(h, _):
        q3 = order(h)
        rows = pl.ds(pl.multiple_of(q3 * 768, 16), 768)
        wide_ref[...] = jnp.dot(g_ref[rows, :], xs_ref[...], preferred_element_type=F32)

        far = (1 - h) * to_group[0]
        for mask in range(3, -1, -1):
            i = classes[1] + 2 * classes[2] + subset(flips(classes[1:], (1, 2)), mask)
            high = pl.ds(pl.multiple_of(i * 192, 8), 96)
            low = pl.ds(pl.multiple_of(i * 192 + 96, 8), 96)
            part = wide_ref[high, 0:128] + (wide_ref[high, 128:256] + wide_ref[low, 0:128])

            def send():
                part_ref[4 * q3 + i] = part
                pltpu.make_async_remote_copy(
                    src_ref=part_ref.at[4 * q3 + i],
                    dst_ref=rr_ref.at[target],
                    send_sem=send_sems.at[1],
                    recv_sem=recv_sems.at[1],
                    device_id=me + far + subset(to_group[1:], mask),
                    device_id_type=LOGICAL,
                ).start()

            if mask:
                send()
            else:
                pl.when(h == 0)(send)

                @pl.when(h == 1)
                def _():
                    rr_ref[target] = part

        return 0

    lax.fori_loop(0, 2, half, 0)
    pltpu.make_async_copy(rr_ref.at[0:7], rr_ref.at[0:7], recv_sems.at[1]).wait()

    def add(i, _):
        rows = pl.ds(pl.multiple_of(16 * i, 16), 16)
        total = rr_ref[0, rows, :]
        for k in range(1, 8):
            total = total + rr_ref[k, rows, :]
        high = total.astype(BF16)
        sum_ref[rows, 0:128] = high
        sum_ref[rows, 128:256] = (total - high.astype(F32)).astype(BF16)
        return 0

    lax.fori_loop(0, 6, add, 0)
    sum_ref[96:128, :] = jnp.zeros((32, 256), BF16)

    home = zh + 2 * yl + 4 * yh + 8 * xl
    own = core == classes[2]
    row = pl.multiple_of((classes[0] + 2 * classes[1]) * 8, 8)
    here = out_ref.at[pl.ds(row, 8), pl.ds(pl.multiple_of(block * 128, 128), 128)]
    turns = flips((zh, yl, xl, yh), (1, 2, 8, 4))

    def deliver(high):
        pltpu.make_async_remote_copy(
            src_ref=tile_ref.at[high],
            dst_ref=here,
            send_sem=send_sems.at[2],
            recv_sem=recv_sems.at[2],
            device_id=2 * high + classes[2],
            device_id_type=LOGICAL,
        ).start()

    def deliver_some(step, _):
        same_x, same_z = rem(step, 2), div(step, 2)
        x_to = (1 - xh) + same_x * (2 * xh - 1)
        z_to = (1 - zl) + same_z * (2 * zl - 1)
        quarter = x_to + 2 * z_to
        rows = pl.ds(pl.multiple_of(quarter * 256, 16), 256)
        last_ref[...] = jnp.dot(h_ref[rows, :], sum_ref[...], preferred_element_type=F32)
        tiles = last_ref[0:128, 0:128] + (last_ref[0:128, 128:256] + last_ref[128:256, 0:128])
        tile_ref[pl.ds(quarter * 16, 16)] = tiles.reshape(16, 8, 128)
        first = quarter * 16 + home
        for mask in range(15, 0, -1):
            deliver(first + subset(turns, mask))

        @pl.when(jnp.logical_or(step != 3, jnp.logical_not(own)))
        def _():
            deliver(first)

        return 0

    lax.fori_loop(0, 4, deliver_some, 0)

    @pl.when(own)
    def _():
        pltpu.make_async_copy(tile_ref.at[home + 16 * xh + 32 * zl], here, recv_sems.at[2]).start()

    pltpu.make_async_copy(xr_ref.at[0:15], xr_ref.at[0:15], send_sems.at[0]).wait()
    pltpu.make_async_copy(part_ref.at[0:7], part_ref.at[0:7], send_sems.at[1]).wait()

    @pl.when(own)
    def _():
        pltpu.make_async_copy(tile_ref.at[0:63], tile_ref.at[0:63], send_sems.at[2]).wait()

    @pl.when(jnp.logical_not(own))
    def _():
        pltpu.make_async_copy(tile_ref, tile_ref, send_sems.at[2]).wait()

    pltpu.make_async_copy(out_ref, out_ref, recv_sems.at[2]).wait()


def shards(traces, phase_coef):
    return pl.pallas_call(
        kernel,
        out_shape=jax.ShapeDtypeStruct((32, 2048), F32),
        in_specs=[
            pl.BlockSpec(memory_space=pl.ANY),
            pl.BlockSpec(memory_space=pl.ANY),
            pl.BlockSpec(memory_space=pl.ANY),
        ],
        out_specs=pl.BlockSpec(memory_space=pl.ANY),
        scratch_shapes=[
            pltpu.SMEM((2, 4), F32),
            pltpu.VMEM((6, 64, 128), F32),
            pltpu.VMEM((5, 36, 8, 128), F32),
            pltpu.VMEM((5, 6, 8, 128), F32),
            pltpu.VMEM((5, 8, 128), F32),
            pltpu.VMEM((3, 12, 4, 8, 128), F32),
            pltpu.VMEM((1536, 512), BF16),
            pltpu.VMEM((1024, 128), BF16),
            pltpu.VMEM((16, 32, 128), F32),
            pltpu.VMEM((512, 256), BF16),
            pltpu.VMEM((768, 256), F32),
            pltpu.VMEM((8, 96, 128), F32),
            pltpu.VMEM((8, 96, 128), F32),
            pltpu.VMEM((128, 256), BF16),
            pltpu.VMEM((256, 256), F32),
            pltpu.VMEM((64, 8, 128), F32),
            pltpu.SemaphoreType.DMA((3,)),
            pltpu.SemaphoreType.DMA((5,)),
        ],
        compiler_params=pltpu.CompilerParams(
            collective_id=0, has_side_effects=True, vmem_limit_bytes=60 * 2**20
        ),
    )(traces, phase_coef, jnp.asarray(tail_table()))


def solution(mesh):
    placed = (P(("gx", "gy"), None), P())
    return jax.shard_map(
        shards, mesh=mesh, in_specs=placed, out_specs=P(("gx", "gy"), None), check_vma=False
    )
```

```python
import functools

import jax
import jax.numpy as jnp
import numpy as np
from jax import lax
from jax.experimental import pallas as pl
from jax.experimental.pallas import tpu as pltpu
from jax.sharding import PartitionSpec as P

ORDER = 6
LOGICAL = pl.DeviceIdType.LOGICAL
F32 = jnp.float32
BF16 = jnp.bfloat16
AMP = 64.0

NODES = 0.5 * np.cos(np.pi * (2.0 * np.arange(ORDER) + 1.0) / (2.0 * ORDER))


def lagrange(points):
    points = np.asarray(points)[..., None, None]
    same = np.eye(ORDER, dtype=bool)
    spread = np.where(same, 1.0, NODES[:, None] - NODES[None, :])
    return np.where(same, 1.0, (points - NODES[None, :]) / spread).prod(-1)


CENTRE = lagrange(0.0)
HALVES = np.stack([((side - 0.5) + NODES) * 0.5 for side in (0, 1)])
TABLE = lagrange(HALVES)
WEIGHT = np.transpose(TABLE, (0, 2, 1))


def tail_table():
    out = np.zeros((ORDER, 64, 128))
    for high in range(64):
        total = np.eye(ORDER)
        for place in range(6):
            total = TABLE[(high >> place) & 1] @ total
        out[:, high, :96] = np.repeat(CENTRE[:, None] * total, 16, axis=1)
    return out.astype(np.float32)


def fit(function, terms):
    u = 0.125 + 0.125 * np.cos(np.pi * (np.arange(200) + 0.5) / 200)
    poly = np.polynomial.chebyshev.Chebyshev.fit(u, function(np.sqrt(u)), terms - 1, domain=[0, 0.25])
    return [float(c) for c in poly.convert(kind=np.polynomial.Polynomial).coef]


SIN = fit(lambda r: np.sin(np.pi * r) / r, 5)
SIN2 = [2.0 * c for c in fit(lambda r: np.sin(np.pi * r) / r, 4)]
COS = fit(lambda r: np.cos(np.pi * r), 5)


def horner(coefs, u):
    total = coefs[-1]
    for c in coefs[-2::-1]:
        total = total * u + c
    return total


def turn(c):
    r = c - jnp.floor(c + 0.5)
    u = r * r
    twice = r * horner(SIN2, u)
    half_cos = horner(COS, u)
    return 1.0 - (0.5 * twice) * twice, twice * half_cos


def turn_cos(c):
    r = c - jnp.floor(c + 0.5)
    twice = r * horner(SIN2, r * r)
    return 1.0 - (0.5 * twice) * twice


def half_turn(y):
    r = 0.5 - y
    u = r * r
    return r * horner(SIN, u), horner(COS, u)


def bend_value(coef, row, y):
    cosine = (0.5 - y) * horner(SIN, (0.5 - y) * (0.5 - y))
    c0, c1, c2, c3 = (coef[row, m] for m in range(4))
    return (c0 - c2) + cosine * ((c1 - 3.0 * c3) + cosine * (2.0 * c2 + cosine * (4.0 * c3)))


def bend_terms(coef, size):
    e1, e2, e3 = (coef[0, m] * float(-2.0 * AMP * np.sin(np.pi * m * size / 2.0)) for m in (1, 2, 3))
    return e1 - e3, 2.0 * e2, 4.0 * e3


def bend_step(terms, middle):
    cosine, sine = half_turn(middle)
    return sine * (terms[0] + cosine * (terms[1] + cosine * terms[2]))


def apply_real(weights, values):
    out = []
    for t in range(ORDER):
        total = weights[t][0] * values[0]
        for s in range(1, ORDER):
            total = total + weights[t][s] * values[s]
        out.append(total)
    return out


def iota(axis):
    return lax.broadcasted_iota(jnp.int32, (8, 128), axis)


def asf(value):
    return value.astype(F32)


def div(a, b):
    return lax.div(a, jnp.int32(b))


def rem(a, b):
    return lax.rem(a, jnp.int32(b))


def subset(deltas, mask):
    total = None
    for k, delta in enumerate(deltas):
        if (mask >> k) & 1:
            total = delta if total is None else total + delta
    return 0 if total is None else total


def flips(bits, weights):
    return [weight * (1 - 2 * bit) for bit, weight in zip(bits, weights)]


def lane_parts(classes, core):
    lane = iota(1)
    place = lane >> 4
    x, y, z = (
        (2 * c + e + core) & 3 for c, e in zip(classes, (place >> 2, (place >> 1) & 1, place & 1))
    )
    return (z >> 1) + 2 * y + 8 * x + 32 * (z & 1), lane & 15


def early_levels(coef, box, top, w_ref, p_ref, v_ref):
    sub = iota(0)
    bits = [asf(sub & 1), asf((sub >> 1) & 1), asf(sub >> 2)]
    sign = [2.0 * bit - 1.0 for bit in bits]
    x0 = jnp.full((8, 128), 0.5, F32)
    x1 = x0 + sign[0] * 0.25
    x2 = x1 + sign[1] * 0.125
    word4 = asf(box * 16 + top)
    steps = [
        bend_step(bend_terms(coef, 2.0 ** -(level + 1)), x + sign[level - 1] * 2.0 ** -(level + 2))
        for level, x in ((1, x0), (2, x1), (3, x2))
    ]
    p0_mid = coef[0, 0] - coef[0, 2]
    linear2 = 2.0 * asf(top & 1) + 0.5
    linear3 = asf(top & 3) + 0.5
    third = [turn(sign[2] * ((linear3 + float(NODES[s])) * 0.25 + steps[2] * p_ref[0, s])) for s in range(ORDER)]

    def side_weights(side):
        return [
            [jnp.where(side == 1, float(WEIGHT[1][t][s]), float(WEIGHT[0][t][s])) for s in range(ORDER)]
            for t in range(ORDER)
        ]

    def turned(values, angles):
        pairs = [(a * c - b * d, a * d + b * c) for (a, b), (c, d) in zip(values, angles)]
        return [a for a, _ in pairs], [b for _, b in pairs]

    def body(group, _):
        j0, j1 = rem(group, 2), div(group, 2)
        j0f, j1f, groupf = asf(j0), asf(j1), asf(group)
        word = word4 * 4.0 + groupf
        start = 0.5 * (j0f + 0.5) + AMP * p0_mid * bend_value(coef, 1, (word + 0.5) * 2.0**-12)
        real, imag = [], []
        for s in range(ORDER):
            node = float(NODES[s])
            p1 = bend_value(coef, 1, (word + (0.5 + node)) * 2.0**-12)
            c, d = turn(start + sign[0] * ((groupf + (0.5 + node)) * 0.25 + steps[0] * p1))
            real.append(c * float(CENTRE[s]))
            imag.append(d * float(CENTRE[s]))
        weights = side_weights(j0)
        values = list(zip(apply_real(weights, real), apply_real(weights, imag)))
        word = word4 * 2.0 + j1f
        angles = []
        for s in range(ORDER):
            node = float(NODES[s])
            p1 = bend_value(coef, 1, (word + (0.5 + node)) * 2.0**-11)
            angles.append(turn(sign[1] * (((linear2 + j1f) + node) * 0.25 + steps[1] * p1)))
        weights = side_weights(j1)
        real, imag = turned(values, angles)
        values = list(zip(apply_real(weights, real), apply_real(weights, imag)))
        weights = [[w_ref[0, ORDER * t + s] for s in range(ORDER)] for t in range(ORDER)]
        for c, parts in enumerate(turned(values, third)):
            for t, value in enumerate(apply_real(weights, parts)):
                v_ref[0, 2 * t + c, group] = value
        return 0

    lax.fori_loop(0, 4, body, 0)


def late_setup(coef, box, top, w_ref, p_ref, c_ref):
    full = box * 16 + top

    def body(i, scale):
        word = full >> i
        pick = (word & 1) == 1
        for t in range(ORDER):
            for s in range(ORDER):
                w_ref[i, ORDER * t + s] = jnp.where(pick, float(WEIGHT[1][t][s]), float(WEIGHT[0][t][s]))
        for s in range(ORDER):
            p_ref[i, s] = bend_value(coef, 1, (asf(word) + float(0.5 + NODES[s])) * scale)
        return scale * 2.0

    lax.fori_loop(0, 5, body, jnp.float32(2.0**-10))
    turn_of = top & 7

    def by_lane(values):
        out = jnp.full((8, 128), float(values[ORDER - 1]), F32)
        for t in range(ORDER - 1):
            out = jnp.where(turn_of == t, float(values[t]), out)
        return out

    e1, e2, e3 = (coef[0, m] * by_lane(-2.0 * AMP * np.sin(np.pi * m * NODES / 128.0)) for m in (1, 2, 3))
    node = by_lane(NODES)
    c_ref[0] = node
    c_ref[1] = e1 - e3
    c_ref[2] = 2.0 * e2
    c_ref[3] = 4.0 * e3
    c_ref[4] = node * (asf(box) + 0.5)


def spread(value, t):
    return jnp.take_along_axis(value, (iota(1) & 120) + t, axis=1)


def late_levels(coef, box, top, order, w_ref, p_ref, c_ref, v_ref, g_ref):
    sub = iota(0)
    x3 = asf(4 * (sub & 1) + (sub & 2) + (sub >> 2)) * 0.125 + 0.0625
    full = box * 16 + top
    terms = [bend_terms(coef, 2.0 ** -(level + 1)) for level in (4, 5, 6)]

    def sign_of(bit):
        return (2 * bit - 1).astype(F32)

    def turns(i, level_terms, shift, parent, sign):
        steps = bend_step(level_terms, parent + sign * shift)
        linear = asf((full >> i) & 3) + 0.5
        return [turn(sign * ((linear + float(NODES[s])) * 0.25 + steps * p_ref[i, s])) for s in range(ORDER)]

    def level_step(level, q3, q4):
        first = level == 4
        i = level - 3
        parent = x3 + jnp.where(first, 0.0, sign_of(q3) * 2.0**-5)
        sign = jnp.where(first, sign_of(q3), sign_of(q4))
        level_terms = [jnp.where(first, a, b) for a, b in zip(terms[0], terms[1])]
        real, imag = [], []
        for s, (c, d) in enumerate(turns(i, level_terms, jnp.where(first, 2.0**-6, 2.0**-7), parent, sign)):
            a, b = v_ref[i - 1, 2 * s], v_ref[i - 1, 2 * s + 1]
            real.append(a * c - b * d)
            imag.append(a * d + b * c)
        weights = [[w_ref[i, ORDER * t + s] for s in range(ORDER)] for t in range(ORDER)]
        for c, values in enumerate((real, imag)):
            for t, value in enumerate(apply_real(weights, values)):
                v_ref[i, 2 * t + c] = value

    def last_step(parent, bit, place):
        sign = sign_of(bit)
        middle = parent + sign * 2.0**-7 + c_ref[0] * (1.0 / 128.0)
        steps = bend_step((c_ref[1], c_ref[2], c_ref[3]), middle)
        switch = [turn((c_ref[4] + c_ref[0] * float(NODES[u])) + steps * p_ref[4, u]) for u in range(ORDER)]
        merged = []
        for s, (c, d) in enumerate(turns(3, terms[2], 2.0**-8, parent, sign)):
            a = b = None
            for u in range(ORDER):
                weight = w_ref[3, ORDER * u + s]
                a = switch[u][0] * weight if a is None else a + switch[u][0] * weight
                b = switch[u][1] * weight if b is None else b + switch[u][1] * weight
            merged.append((a * c - b * d, a * d + b * c))
        parts = [v_ref[2, 2 * s] + v_ref[2, 2 * s + 1] for s in range(ORDER)]
        for t in range(ORDER):
            k1 = k2 = k3 = None
            for s in range(ORDER):
                c, d = spread(merged[s][0], t), spread(merged[s][1], t)
                m1, m2, m3 = parts[s] * c, v_ref[2, 2 * s] * (d - c), v_ref[2, 2 * s + 1] * (c + d)
                k1 = m1 if k1 is None else k1 + m1
                k2 = m2 if k2 is None else k2 + m2
                k3 = m3 if k3 is None else k3 + m3
            real, imag = k1 - k3, k1 + k2
            rows = pl.ds(pl.multiple_of(place * 192 + 16 * t, 16), 16)
            rows_low = pl.ds(pl.multiple_of(place * 192 + 96 + 16 * t, 16), 16)
            for j in range(4):
                both = jnp.concatenate([real[j], imag[j]], axis=0)
                high = both.astype(BF16)
                g_ref[rows, 128 * j : 128 * (j + 1)] = high
                g_ref[rows_low, 128 * j : 128 * (j + 1)] = (both - high.astype(F32)).astype(BF16)

    def over(n, _):
        q3, q4 = order(div(n, 2)), rem(n, 2)

        def levels(level, _):
            level_step(level, q3, q4)
            return 0

        lax.fori_loop(4 + q4, 6, levels, 0)
        x5 = x3 + (sign_of(q3) * 2.0**-5 + sign_of(q4) * 2.0**-6)

        def over5(q5, _):
            last_step(x5, q5, 4 * q3 + q4 + 2 * q5)
            return 0

        return lax.fori_loop(0, 2, over5, 0)

    lax.fori_loop(0, 4, over, 0)


def last_weights(coef, group, tail_ref, h_ref):
    sub, lane = iota(0), iota(1)
    own = lane & 7
    same = sub == own
    box6 = 32 * (own & 1) + 8 * (own & 2) + 2 * (own & 4)
    box6 = box6 + (4 * rem(group, 2) + 2 * rem(div(group, 2), 2) + div(group, 4))
    inner = 32 * (sub & 1) + 8 * (sub & 2) + 2 * (sub & 4)
    base = box6 * 64 + inner
    quarter = 0.25 * asf((lane >> 3) & 1)
    p1_mid = coef[1, 0] - coef[1, 2]

    def rows_of(r):
        centre = (asf(base + (4 * rem(r, 2) + 2 * rem(div(r, 2), 2) + div(r, 4))) + 0.5) * 2.0**-12
        total = None
        for t in range(ORDER):
            node = float(NODES[t])
            steps = bend_step(bend_terms(coef, node / 4096.0), centre + node / 8192.0)
            term = turn_cos((quarter - 0.5 * node) - steps * p1_mid)
            term = term * tail_ref[t, pl.ds(pl.multiple_of(8 * r, 8), 8), :]
            total = term if total is None else total + term
        return total

    def body(r, _):
        total = rows_of(r)
        start = 256 * div(r, 2) + 64 * rem(r, 2)
        for k in range(0, 8, 2):
            both = jnp.concatenate(
                [jnp.where(same, jnp.broadcast_to(total[k + n : k + n + 1], (8, 128)), 0.0) for n in range(2)], axis=0
            )
            high = both.astype(BF16)
            h_ref[pl.ds(pl.multiple_of(start + 8 * k, 16), 16), :] = high
            h_ref[pl.ds(pl.multiple_of(start + 128 + 8 * k, 16), 16), :] = (both - high.astype(F32)).astype(BF16)
        return 0

    lax.fori_loop(0, 8, body, 0)


def kernel(
    x_ref,
    coef_hbm,
    tail_hbm,
    out_ref,
    coef_ref,
    tail_ref,
    w_ref,
    p_ref,
    c_ref,
    v_ref,
    g_ref,
    h_ref,
    xr_ref,
    xs_ref,
    wide_ref,
    part_ref,
    rr_ref,
    sum_ref,
    last_ref,
    tile_ref,
    send_sems,
    recv_sems,
):
    fetch_coef = pltpu.make_async_copy(coef_hbm, coef_ref, recv_sems.at[3])
    fetch_tail = pltpu.make_async_copy(tail_hbm, tail_ref, recv_sems.at[4])
    fetch_coef.start()
    fetch_tail.start()
    gx, gy = lax.axis_index("gx"), lax.axis_index("gy")
    core = rem(gy, 2)
    zl, xs = div(gx, 4), rem(gx, 4)
    xh, xl = div(xs, 2), rem(xs, 2)
    yh, yl, zh = div(gy, 8), rem(div(gy, 4), 2), rem(div(gy, 2), 2)
    me = gx * 16 + gy
    highs, lows = (xh, yh, zh), (xl, yl, zl)
    unlike = [h + l - 2 * h * l for h, l in zip(highs, lows)]
    to_a = [16 * (1 - 2 * xl), 4 * (1 - 2 * yl), 64 * (1 - 2 * zl)]
    to_b = [16 * (3 - 2 * xs), 4 * (3 - 2 * (2 * yh + yl)), 2 * (1 - 2 * zh) + 64 * (1 - 2 * zl)]
    to_class = [a + core * (b - a) for a, b in zip(to_a, to_b)]
    to_group = [b + core * (a - b) for a, b in zip(to_a, to_b)]
    to_core = 1 - 2 * core
    class_a, class_b = highs, [1 - d for d in unlike]
    place_a, place_b = lows, [1 - l for l in lows]
    group_a, group_b = [1 - d for d in unlike], [1 - h for h in highs]

    def mine(for_a, for_b):
        return [a + core * (b - a) for a, b in zip(for_a, for_b)]

    def others(for_a, for_b):
        return [b + core * (a - b) for a, b in zip(for_a, for_b)]

    def number(values):
        return values[0] + 2 * values[1] + 4 * values[2]

    classes, groups = mine(class_a, class_b), mine(group_a, group_b)
    target = number(classes)
    block = number(groups) + 8 * core

    barrier = pltpu.get_barrier_semaphore()
    for mask in range(1, 16):
        source = me + subset(to_class + [to_core], mask)
        pl.semaphore_signal(barrier, inc=1, device_id=source, device_id_type=LOGICAL)
    for mask in range(1, 8):
        pl.semaphore_signal(barrier, inc=1, device_id=me + subset(to_group, mask), device_id_type=LOGICAL)
    pl.semaphore_wait(barrier, 22)

    def columns(m):
        return x_ref.at[:, pl.ds(pl.multiple_of(m * 128, 128), 128)]

    own_slot = 2 * number(mine(place_a, place_b)[::-1]) + core
    other_slot = 2 * number(others(place_a, place_b)[::-1]) + core
    other_groups = others(group_a, group_b)
    other_block = number(other_groups) + 8 * (1 - core)
    for mask in range(7, -1, -1):
        routes = [(other_block, other_groups, other_slot, me + to_core + subset(to_group, mask))]
        if mask:
            routes.append((block, groups, own_slot, me + subset(to_class, mask)))
        for first, group_bits, slot, device in routes:
            pltpu.make_async_remote_copy(
                src_ref=columns(first + subset(flips(group_bits, (1, 2, 4)), mask)),
                dst_ref=xr_ref.at[slot],
                send_sem=send_sems.at[0],
                recv_sem=recv_sems.at[0],
                device_id=device,
                device_id_type=LOGICAL,
            ).start()
    pltpu.make_async_copy(columns(block), xr_ref.at[own_slot], recv_sems.at[0]).start()

    box, top = lane_parts(classes, core)
    fetch_coef.wait()
    late_setup(coef_ref, box, top, w_ref, p_ref, c_ref)
    early_levels(coef_ref, box, top, w_ref, p_ref, v_ref)

    def order(h):
        return classes[0] + (1 - h) * (1 - 2 * classes[0])

    late_levels(coef_ref, box, top, order, w_ref, p_ref, c_ref, v_ref, g_ref)
    pltpu.make_async_copy(xr_ref, xr_ref, recv_sems.at[0]).wait()

    def split(i, _):
        for j in range(4):
            piece = jnp.concatenate([xr_ref[2 * i + s, pl.ds(j, 8, stride=4), :] for s in range(2)], axis=0)
            high = piece.astype(BF16)
            rows = pl.ds(pl.multiple_of(128 * j + 16 * i, 16), 16)
            xs_ref[rows, 0:128] = high
            xs_ref[rows, 128:256] = (piece - high.astype(F32)).astype(BF16)
        return 0

    lax.fori_loop(0, 8, split, 0)

    def half(h, _):
        q3 = order(h)
        rows = pl.ds(pl.multiple_of(q3 * 768, 16), 768)
        wide_ref[...] = jnp.dot(g_ref[rows, :], xs_ref[...], preferred_element_type=F32)

        far = (1 - h) * to_group[0]
        for mask in range(3, -1, -1):
            i = classes[1] + 2 * classes[2] + subset(flips(classes[1:], (1, 2)), mask)
            high = pl.ds(pl.multiple_of(i * 192, 8), 96)
            low = pl.ds(pl.multiple_of(i * 192 + 96, 8), 96)
            part = wide_ref[high, 0:128] + (wide_ref[high, 128:256] + wide_ref[low, 0:128])

            def send():
                part_ref[4 * q3 + i] = part
                pltpu.make_async_remote_copy(
                    src_ref=part_ref.at[4 * q3 + i],
                    dst_ref=rr_ref.at[target],
                    send_sem=send_sems.at[1],
                    recv_sem=recv_sems.at[1],
                    device_id=me + far + subset(to_group[1:], mask),
                    device_id_type=LOGICAL,
                ).start()

            if mask:
                send()
            else:
                pl.when(h == 0)(send)

                @pl.when(h == 1)
                def _():
                    rr_ref[target] = part

        return 0

    lax.fori_loop(0, 2, half, 0)
    fetch_tail.wait()
    last_weights(coef_ref, target, tail_ref, h_ref)
    pltpu.make_async_copy(rr_ref.at[0:7], rr_ref.at[0:7], recv_sems.at[1]).wait()

    def add(i, _):
        rows = pl.ds(pl.multiple_of(16 * i, 16), 16)
        total = rr_ref[0, rows, :]
        for k in range(1, 8):
            total = total + rr_ref[k, rows, :]
        high = total.astype(BF16)
        sum_ref[rows, 0:128] = high
        sum_ref[rows, 128:256] = (total - high.astype(F32)).astype(BF16)
        return 0

    lax.fori_loop(0, 6, add, 0)
    sum_ref[96:128, :] = jnp.zeros((32, 256), BF16)

    home = zh + 2 * yl + 4 * yh + 8 * xl
    own = core == classes[2]
    row = pl.multiple_of((classes[0] + 2 * classes[1]) * 8, 8)
    here = out_ref.at[pl.ds(row, 8), pl.ds(pl.multiple_of(block * 128, 128), 128)]
    turns = flips((zh, yl, xl, yh), (1, 2, 8, 4))

    def deliver(high):
        pltpu.make_async_remote_copy(
            src_ref=tile_ref.at[high],
            dst_ref=here,
            send_sem=send_sems.at[2],
            recv_sem=recv_sems.at[2],
            device_id=2 * high + classes[2],
            device_id_type=LOGICAL,
        ).start()

    def deliver_some(step, _):
        same_x, same_z = rem(step, 2), div(step, 2)
        x_to = (1 - xh) + same_x * (2 * xh - 1)
        z_to = (1 - zl) + same_z * (2 * zl - 1)
        quarter = x_to + 2 * z_to
        rows = pl.ds(pl.multiple_of(quarter * 256, 16), 256)
        last_ref[...] = jnp.dot(h_ref[rows, :], sum_ref[...], preferred_element_type=F32)
        tiles = last_ref[0:128, 0:128] + (last_ref[0:128, 128:256] + last_ref[128:256, 0:128])
        tile_ref[pl.ds(quarter * 16, 16)] = tiles.reshape(16, 8, 128)
        first = quarter * 16 + home
        for mask in range(15, 0, -1):
            deliver(first + subset(turns, mask))

        @pl.when(jnp.logical_or(step != 3, jnp.logical_not(own)))
        def _():
            deliver(first)

        return 0

    lax.fori_loop(0, 4, deliver_some, 0)

    @pl.when(own)
    def _():
        pltpu.make_async_copy(tile_ref.at[home + 16 * xh + 32 * zl], here, recv_sems.at[2]).start()

    pltpu.make_async_copy(xr_ref.at[0:15], xr_ref.at[0:15], send_sems.at[0]).wait()
    pltpu.make_async_copy(part_ref.at[0:7], part_ref.at[0:7], send_sems.at[1]).wait()

    @pl.when(own)
    def _():
        pltpu.make_async_copy(tile_ref.at[0:63], tile_ref.at[0:63], send_sems.at[2]).wait()

    @pl.when(jnp.logical_not(own))
    def _():
        pltpu.make_async_copy(tile_ref, tile_ref, send_sems.at[2]).wait()

    pltpu.make_async_copy(out_ref, out_ref, recv_sems.at[2]).wait()


def shards(traces, phase_coef):
    return pl.pallas_call(
        kernel,
        out_shape=jax.ShapeDtypeStruct((32, 2048), F32),
        in_specs=[
            pl.BlockSpec(memory_space=pl.ANY),
            pl.BlockSpec(memory_space=pl.ANY),
            pl.BlockSpec(memory_space=pl.ANY),
        ],
        out_specs=pl.BlockSpec(memory_space=pl.ANY),
        scratch_shapes=[
            pltpu.SMEM((2, 4), F32),
            pltpu.VMEM((6, 64, 128), F32),
            pltpu.VMEM((5, 36, 8, 128), F32),
            pltpu.VMEM((5, 6, 8, 128), F32),
            pltpu.VMEM((5, 8, 128), F32),
            pltpu.VMEM((3, 12, 4, 8, 128), F32),
            pltpu.VMEM((1536, 512), BF16),
            pltpu.VMEM((1024, 128), BF16),
            pltpu.VMEM((16, 32, 128), F32),
            pltpu.VMEM((512, 256), BF16),
            pltpu.VMEM((768, 256), F32),
            pltpu.VMEM((8, 96, 128), F32),
            pltpu.VMEM((8, 96, 128), F32),
            pltpu.VMEM((128, 256), BF16),
            pltpu.VMEM((256, 256), F32),
            pltpu.VMEM((64, 8, 128), F32),
            pltpu.SemaphoreType.DMA((3,)),
            pltpu.SemaphoreType.DMA((5,)),
        ],
        compiler_params=pltpu.CompilerParams(
            collective_id=0, has_side_effects=True, vmem_limit_bytes=60 * 2**20
        ),
    )(traces, phase_coef, jnp.asarray(tail_table()))


def solution(mesh):
    placed = (P(("gx", "gy"), None), P())
    return jax.shard_map(
        shards, mesh=mesh, in_specs=placed, out_specs=P(("gx", "gy"), None), check_vma=False
    )
```

```python
import functools

import jax
import jax.numpy as jnp
import numpy as np
from jax import lax
from jax.experimental import pallas as pl
from jax.experimental.pallas import tpu as pltpu
from jax.sharding import PartitionSpec as P

ORDER = 6
LOGICAL = pl.DeviceIdType.LOGICAL
F32 = jnp.float32
BF16 = jnp.bfloat16
AMP = 64.0

NODES = 0.5 * np.cos(np.pi * (2.0 * np.arange(ORDER) + 1.0) / (2.0 * ORDER))


def lagrange(points):
    points = np.asarray(points)[..., None, None]
    same = np.eye(ORDER, dtype=bool)
    spread = np.where(same, 1.0, NODES[:, None] - NODES[None, :])
    return np.where(same, 1.0, (points - NODES[None, :]) / spread).prod(-1)


CENTRE = lagrange(0.0)
HALVES = np.stack([((side - 0.5) + NODES) * 0.5 for side in (0, 1)])
TABLE = lagrange(HALVES)
WEIGHT = np.transpose(TABLE, (0, 2, 1))


def tail_table():
    out = np.zeros((ORDER, 64, 128))
    for high in range(64):
        total = np.eye(ORDER)
        for place in range(6):
            total = TABLE[(high >> place) & 1] @ total
        out[:, high, :96] = np.repeat(CENTRE[:, None] * total, 16, axis=1)
    return out.astype(np.float32)


def fit(function, terms):
    u = 0.125 + 0.125 * np.cos(np.pi * (np.arange(200) + 0.5) / 200)
    poly = np.polynomial.chebyshev.Chebyshev.fit(u, function(np.sqrt(u)), terms - 1, domain=[0, 0.25])
    return [float(c) for c in poly.convert(kind=np.polynomial.Polynomial).coef]


SIN = fit(lambda r: np.sin(np.pi * r) / r, 5)
SIN2 = [2.0 * c for c in fit(lambda r: np.sin(np.pi * r) / r, 4)]
COS = fit(lambda r: np.cos(np.pi * r), 5)


def horner(coefs, u):
    total = coefs[-1]
    for c in coefs[-2::-1]:
        total = total * u + c
    return total


def turn(c):
    r = c - jnp.floor(c + 0.5)
    u = r * r
    twice = r * horner(SIN2, u)
    half_cos = horner(COS, u)
    return 1.0 - (0.5 * twice) * twice, twice * half_cos


def turn_cos(c):
    r = c - jnp.floor(c + 0.5)
    twice = r * horner(SIN2, r * r)
    return 1.0 - (0.5 * twice) * twice


def half_turn(y):
    r = 0.5 - y
    u = r * r
    return r * horner(SIN, u), horner(COS, u)


def bend_value(coef, row, y):
    cosine = (0.5 - y) * horner(SIN, (0.5 - y) * (0.5 - y))
    c0, c1, c2, c3 = (coef[row, m] for m in range(4))
    return (c0 - c2) + cosine * ((c1 - 3.0 * c3) + cosine * (2.0 * c2 + cosine * (4.0 * c3)))


def bend_terms(coef, size):
    e1, e2, e3 = (coef[0, m] * float(-2.0 * AMP * np.sin(np.pi * m * size / 2.0)) for m in (1, 2, 3))
    return e1 - e3, 2.0 * e2, 4.0 * e3


def bend_step(terms, middle):
    cosine, sine = half_turn(middle)
    return sine * (terms[0] + cosine * (terms[1] + cosine * terms[2]))


def apply_real(weights, values):
    out = []
    for t in range(ORDER):
        total = weights[t][0] * values[0]
        for s in range(1, ORDER):
            total = total + weights[t][s] * values[s]
        out.append(total)
    return out


def iota(axis):
    return lax.broadcasted_iota(jnp.int32, (8, 128), axis)


def asf(value):
    return value.astype(F32)


def div(a, b):
    return lax.div(a, jnp.int32(b))


def rem(a, b):
    return lax.rem(a, jnp.int32(b))


def subset(deltas, mask):
    total = None
    for k, delta in enumerate(deltas):
        if (mask >> k) & 1:
            total = delta if total is None else total + delta
    return 0 if total is None else total


def flips(bits, weights):
    return [weight * (1 - 2 * bit) for bit, weight in zip(bits, weights)]


def lane_parts(classes, core):
    lane = iota(1)
    place = lane >> 4
    x, y, z = (
        (2 * c + e + core) & 3 for c, e in zip(classes, (place >> 2, (place >> 1) & 1, place & 1))
    )
    return (z >> 1) + 2 * y + 8 * x + 32 * (z & 1), lane & 15


def early_levels(coef, box, top, w_ref, p_ref, v_ref):
    sub = iota(0)
    bits = [asf(sub & 1), asf((sub >> 1) & 1), asf(sub >> 2)]
    sign = [2.0 * bit - 1.0 for bit in bits]
    x0 = jnp.full((8, 128), 0.5, F32)
    x1 = x0 + sign[0] * 0.25
    x2 = x1 + sign[1] * 0.125
    word4 = asf(box * 16 + top)
    steps = [
        bend_step(bend_terms(coef, 2.0 ** -(level + 1)), x + sign[level - 1] * 2.0 ** -(level + 2))
        for level, x in ((1, x0), (2, x1), (3, x2))
    ]
    p0_mid = coef[0, 0] - coef[0, 2]

    def turned(values, angles):
        pairs = [(a * c - b * d, a * d + b * c) for (a, b), (c, d) in zip(values, angles)]
        return [a for a, _ in pairs], [b for _, b in pairs]

    def constants(side):
        return [[float(WEIGHT[side][t][s]) for s in range(ORDER)] for t in range(ORDER)]

    first = []
    for j0 in range(2):
        outs = []
        for j1 in range(2):
            j = j0 + 2 * j1
            word = word4 * 4.0 + float(j)
            start = 0.5 * (j0 + 0.5) + AMP * p0_mid * bend_value(coef, 1, (word + 0.5) * 2.0**-12)
            pairs = []
            for s in range(ORDER):
                node = float(NODES[s])
                p1 = bend_value(coef, 1, (word + (0.5 + node)) * 2.0**-12)
                c, d = turn(start + sign[0] * ((j + 0.5 + node) * 0.25 + steps[0] * p1))
                pairs.append((c * float(CENTRE[s]), d * float(CENTRE[s])))
            outs.append(pairs)
        joined = [[jnp.stack([outs[0][s][c], outs[1][s][c]]) for s in range(ORDER)] for c in range(2)]
        first.append([apply_real(constants(j0), joined[c]) for c in range(2)])
    linear2 = 2.0 * asf(top & 1) + 0.5
    second = []
    for j1 in range(2):
        word = word4 * 2.0 + float(j1)
        angles = []
        for s in range(ORDER):
            node = float(NODES[s])
            p1 = bend_value(coef, 1, (word + (0.5 + node)) * 2.0**-11)
            angles.append(turn(sign[1] * ((linear2 + (j1 + node)) * 0.25 + steps[1] * p1)))
        values = [[jnp.stack([first[0][c][s][j1], first[1][c][s][j1]]) for c in range(2)] for s in range(ORDER)]
        second.append([apply_real(constants(j1), part) for part in turned(values, angles)])
    linear3 = asf(top & 3) + 0.5
    angles = [turn(sign[2] * ((linear3 + float(NODES[s])) * 0.25 + steps[2] * p_ref[0, s])) for s in range(ORDER)]
    values = [[jnp.concatenate([second[0][c][s], second[1][c][s]]) for c in range(2)] for s in range(ORDER)]
    weights = [[w_ref[0, ORDER * t + s] for s in range(ORDER)] for t in range(ORDER)]
    for c, part in enumerate(turned(values, angles)):
        for t, value in enumerate(apply_real(weights, part)):
            v_ref[0, 2 * t + c] = value


def late_setup(coef, box, top, w_ref, p_ref, c_ref):
    full = box * 16 + top

    def body(i, scale):
        word = full >> i
        pick = (word & 1) == 1
        for t in range(ORDER):
            for s in range(ORDER):
                w_ref[i, ORDER * t + s] = jnp.where(pick, float(WEIGHT[1][t][s]), float(WEIGHT[0][t][s]))
        for s in range(ORDER):
            p_ref[i, s] = bend_value(coef, 1, (asf(word) + float(0.5 + NODES[s])) * scale)
        return scale * 2.0

    lax.fori_loop(0, 5, body, jnp.float32(2.0**-10))
    turn_of = top & 7

    def by_lane(values):
        out = jnp.full((8, 128), float(values[ORDER - 1]), F32)
        for t in range(ORDER - 1):
            out = jnp.where(turn_of == t, float(values[t]), out)
        return out

    e1, e2, e3 = (coef[0, m] * by_lane(-2.0 * AMP * np.sin(np.pi * m * NODES / 128.0)) for m in (1, 2, 3))
    node = by_lane(NODES)
    c_ref[0] = node
    c_ref[1] = e1 - e3
    c_ref[2] = 2.0 * e2
    c_ref[3] = 4.0 * e3
    c_ref[4] = node * (asf(box) + 0.5)


def spread(value, t):
    return jnp.take_along_axis(value, (iota(1) & 120) + t, axis=1)


def late_levels(coef, box, top, order, w_ref, p_ref, c_ref, v_ref, g_ref, between):
    sub = iota(0)
    x3 = asf(4 * (sub & 1) + (sub & 2) + (sub >> 2)) * 0.125 + 0.0625
    full = box * 16 + top
    terms = [bend_terms(coef, 2.0 ** -(level + 1)) for level in (4, 5, 6)]

    def sign_of(bit):
        return (2 * bit - 1).astype(F32)

    def turns(i, level_terms, shift, parent, sign):
        steps = bend_step(level_terms, parent + sign * shift)
        linear = asf((full >> i) & 3) + 0.5
        return [turn(sign * ((linear + float(NODES[s])) * 0.25 + steps * p_ref[i, s])) for s in range(ORDER)]

    def level_step(level, q3, q4):
        first = level == 4
        i = level - 3
        parent = x3 + jnp.where(first, 0.0, sign_of(q3) * 2.0**-5)
        sign = jnp.where(first, sign_of(q3), sign_of(q4))
        level_terms = [jnp.where(first, a, b) for a, b in zip(terms[0], terms[1])]
        real, imag = [], []
        for s, (c, d) in enumerate(turns(i, level_terms, jnp.where(first, 2.0**-6, 2.0**-7), parent, sign)):
            a, b = v_ref[i - 1, 2 * s], v_ref[i - 1, 2 * s + 1]
            real.append(a * c - b * d)
            imag.append(a * d + b * c)
        weights = [[w_ref[i, ORDER * t + s] for s in range(ORDER)] for t in range(ORDER)]
        for c, values in enumerate((real, imag)):
            for t, value in enumerate(apply_real(weights, values)):
                v_ref[i, 2 * t + c] = value

    def last_step(parent, bit, place):
        sign = sign_of(bit)
        middle = parent + sign * 2.0**-7 + c_ref[0] * (1.0 / 128.0)
        steps = bend_step((c_ref[1], c_ref[2], c_ref[3]), middle)
        switch = [turn((c_ref[4] + c_ref[0] * float(NODES[u])) + steps * p_ref[4, u]) for u in range(ORDER)]
        merged = []
        for s, (c, d) in enumerate(turns(3, terms[2], 2.0**-8, parent, sign)):
            a = b = None
            for u in range(ORDER):
                weight = w_ref[3, ORDER * u + s]
                a = switch[u][0] * weight if a is None else a + switch[u][0] * weight
                b = switch[u][1] * weight if b is None else b + switch[u][1] * weight
            merged.append((a * c - b * d, a * d + b * c))
        parts = [v_ref[2, 2 * s] + v_ref[2, 2 * s + 1] for s in range(ORDER)]
        for t in range(ORDER):
            k1 = k2 = k3 = None
            for s in range(ORDER):
                c, d = spread(merged[s][0], t), spread(merged[s][1], t)
                m1, m2, m3 = parts[s] * c, v_ref[2, 2 * s] * (d - c), v_ref[2, 2 * s + 1] * (c + d)
                k1 = m1 if k1 is None else k1 + m1
                k2 = m2 if k2 is None else k2 + m2
                k3 = m3 if k3 is None else k3 + m3
            real, imag = k1 - k3, k1 + k2
            rows = pl.ds(pl.multiple_of(place * 192 + 16 * t, 16), 16)
            rows_low = pl.ds(pl.multiple_of(place * 192 + 96 + 16 * t, 16), 16)
            for j in range(4):
                both = jnp.concatenate([real[j], imag[j]], axis=0)
                high = both.astype(BF16)
                g_ref[rows, 128 * j : 128 * (j + 1)] = high
                g_ref[rows_low, 128 * j : 128 * (j + 1)] = (both - high.astype(F32)).astype(BF16)

    def over(n, _):
        pl.when(n == 3)(between)
        q3, q4 = order(div(n, 2)), rem(n, 2)

        def levels(level, _):
            level_step(level, q3, q4)
            return 0

        lax.fori_loop(4 + q4, 6, levels, 0)
        x5 = x3 + (sign_of(q3) * 2.0**-5 + sign_of(q4) * 2.0**-6)

        def over5(q5, _):
            last_step(x5, q5, 4 * q3 + q4 + 2 * q5)
            return 0

        return lax.fori_loop(0, 2, over5, 0)

    lax.fori_loop(0, 4, over, 0)


def last_weights(coef, group, tail_ref, h_ref):
    sub, lane = iota(0), iota(1)
    own = lane & 7
    same = sub == own
    box6 = 32 * (own & 1) + 8 * (own & 2) + 2 * (own & 4)
    box6 = box6 + (4 * rem(group, 2) + 2 * rem(div(group, 2), 2) + div(group, 4))
    inner = 32 * (sub & 1) + 8 * (sub & 2) + 2 * (sub & 4)
    base = box6 * 64 + inner
    quarter = 0.25 * asf((lane >> 3) & 1)
    p1_mid = coef[1, 0] - coef[1, 2]

    def rows_of(r):
        centre = (asf(base + (4 * rem(r, 2) + 2 * rem(div(r, 2), 2) + div(r, 4))) + 0.5) * 2.0**-12
        total = None
        for t in range(ORDER):
            node = float(NODES[t])
            steps = bend_step(bend_terms(coef, node / 4096.0), centre + node / 8192.0)
            term = turn_cos((quarter - 0.5 * node) - steps * p1_mid)
            term = term * tail_ref[t, pl.ds(pl.multiple_of(8 * r, 8), 8), :]
            total = term if total is None else total + term
        return total

    def body(r, _):
        total = rows_of(r)
        start = 256 * div(r, 2) + 64 * rem(r, 2)
        for k in range(0, 8, 2):
            both = jnp.concatenate(
                [jnp.where(same, jnp.broadcast_to(total[k + n : k + n + 1], (8, 128)), 0.0) for n in range(2)], axis=0
            )
            high = both.astype(BF16)
            h_ref[pl.ds(pl.multiple_of(start + 8 * k, 16), 16), :] = high
            h_ref[pl.ds(pl.multiple_of(start + 128 + 8 * k, 16), 16), :] = (both - high.astype(F32)).astype(BF16)
        return 0

    lax.fori_loop(0, 8, body, 0)


def kernel(
    x_ref,
    coef_hbm,
    tail_hbm,
    out_ref,
    coef_ref,
    tail_ref,
    w_ref,
    p_ref,
    c_ref,
    v_ref,
    g_ref,
    h_ref,
    xr_ref,
    xs_ref,
    wide_ref,
    part_ref,
    rr_ref,
    sum_ref,
    last_ref,
    tile_ref,
    send_sems,
    recv_sems,
):
    fetch_coef = pltpu.make_async_copy(coef_hbm, coef_ref, recv_sems.at[3])
    fetch_tail = pltpu.make_async_copy(tail_hbm, tail_ref, recv_sems.at[4])
    fetch_coef.start()
    fetch_tail.start()
    gx, gy = lax.axis_index("gx"), lax.axis_index("gy")
    core = rem(gy, 2)
    zl, xs = div(gx, 4), rem(gx, 4)
    xh, xl = div(xs, 2), rem(xs, 2)
    yh, yl, zh = div(gy, 8), rem(div(gy, 4), 2), rem(div(gy, 2), 2)
    me = gx * 16 + gy
    highs, lows = (xh, yh, zh), (xl, yl, zl)
    unlike = [h + l - 2 * h * l for h, l in zip(highs, lows)]
    to_a = [16 * (1 - 2 * xl), 4 * (1 - 2 * yl), 64 * (1 - 2 * zl)]
    to_b = [16 * (3 - 2 * xs), 4 * (3 - 2 * (2 * yh + yl)), 2 * (1 - 2 * zh) + 64 * (1 - 2 * zl)]
    to_class = [a + core * (b - a) for a, b in zip(to_a, to_b)]
    to_group = [b + core * (a - b) for a, b in zip(to_a, to_b)]
    to_core = 1 - 2 * core
    class_a, class_b = highs, [1 - d for d in unlike]
    place_a, place_b = lows, [1 - l for l in lows]
    group_a, group_b = [1 - d for d in unlike], [1 - h for h in highs]

    def mine(for_a, for_b):
        return [a + core * (b - a) for a, b in zip(for_a, for_b)]

    def others(for_a, for_b):
        return [b + core * (a - b) for a, b in zip(for_a, for_b)]

    def number(values):
        return values[0] + 2 * values[1] + 4 * values[2]

    classes, groups = mine(class_a, class_b), mine(group_a, group_b)
    target = number(classes)
    block = number(groups) + 8 * core

    barrier = pltpu.get_barrier_semaphore()
    for mask in range(1, 16):
        source = me + subset(to_class + [to_core], mask)
        pl.semaphore_signal(barrier, inc=1, device_id=source, device_id_type=LOGICAL)
    for mask in range(1, 8):
        pl.semaphore_signal(barrier, inc=1, device_id=me + subset(to_group, mask), device_id_type=LOGICAL)
    pl.semaphore_wait(barrier, 22)

    def columns(m):
        return x_ref.at[:, pl.ds(pl.multiple_of(m * 128, 128), 128)]

    own_slot = 2 * number(mine(place_a, place_b)[::-1]) + core
    other_slot = 2 * number(others(place_a, place_b)[::-1]) + core
    other_groups = others(group_a, group_b)
    other_block = number(other_groups) + 8 * (1 - core)
    for mask in range(7, -1, -1):
        routes = [(other_block, other_groups, other_slot, me + to_core + subset(to_group, mask))]
        if mask:
            routes.append((block, groups, own_slot, me + subset(to_class, mask)))
        for first, group_bits, slot, device in routes:
            pltpu.make_async_remote_copy(
                src_ref=columns(first + subset(flips(group_bits, (1, 2, 4)), mask)),
                dst_ref=xr_ref.at[slot],
                send_sem=send_sems.at[0],
                recv_sem=recv_sems.at[0],
                device_id=device,
                device_id_type=LOGICAL,
            ).start()
    pltpu.make_async_copy(columns(block), xr_ref.at[own_slot], recv_sems.at[0]).start()

    box, top = lane_parts(classes, core)
    fetch_coef.wait()
    late_setup(coef_ref, box, top, w_ref, p_ref, c_ref)
    early_levels(coef_ref, box, top, w_ref, p_ref, v_ref)

    def order(h):
        return classes[0] + (1 - h) * (1 - 2 * classes[0])

    def split(i, _):
        for j in range(4):
            piece = jnp.concatenate([xr_ref[2 * i + s, pl.ds(j, 8, stride=4), :] for s in range(2)], axis=0)
            high = piece.astype(BF16)
            rows = pl.ds(pl.multiple_of(128 * j + 16 * i, 16), 16)
            xs_ref[rows, 0:128] = high
            xs_ref[rows, 128:256] = (piece - high.astype(F32)).astype(BF16)
        return 0

    def half(h):
        q3 = order(h)
        rows = pl.ds(pl.multiple_of(q3 * 768, 16), 768)
        wide_ref[...] = jnp.dot(g_ref[rows, :], xs_ref[...], preferred_element_type=F32)

        far = to_group[0] if h == 0 else 0
        for mask in range(3, -1, -1):
            i = classes[1] + 2 * classes[2] + subset(flips(classes[1:], (1, 2)), mask)
            high = pl.ds(pl.multiple_of(i * 192, 8), 96)
            low = pl.ds(pl.multiple_of(i * 192 + 96, 8), 96)
            part = wide_ref[high, 0:128] + (wide_ref[high, 128:256] + wide_ref[low, 0:128])

            def send():
                part_ref[4 * q3 + i] = part
                pltpu.make_async_remote_copy(
                    src_ref=part_ref.at[4 * q3 + i],
                    dst_ref=rr_ref.at[target],
                    send_sem=send_sems.at[1],
                    recv_sem=recv_sems.at[1],
                    device_id=me + far + subset(to_group[1:], mask),
                    device_id_type=LOGICAL,
                ).start()

            if mask or h == 0:
                send()
            else:
                rr_ref[target] = part

    def first_half():
        pltpu.make_async_copy(xr_ref, xr_ref, recv_sems.at[0]).wait()
        lax.fori_loop(0, 8, split, 0)
        half(0)

    late_levels(coef_ref, box, top, order, w_ref, p_ref, c_ref, v_ref, g_ref, first_half)
    half(1)
    fetch_tail.wait()
    last_weights(coef_ref, target, tail_ref, h_ref)
    pltpu.make_async_copy(rr_ref.at[0:7], rr_ref.at[0:7], recv_sems.at[1]).wait()

    def add(i, _):
        rows = pl.ds(pl.multiple_of(16 * i, 16), 16)
        total = rr_ref[0, rows, :]
        for k in range(1, 8):
            total = total + rr_ref[k, rows, :]
        high = total.astype(BF16)
        sum_ref[rows, 0:128] = high
        sum_ref[rows, 128:256] = (total - high.astype(F32)).astype(BF16)
        return 0

    lax.fori_loop(0, 6, add, 0)
    sum_ref[96:128, :] = jnp.zeros((32, 256), BF16)

    home = zh + 2 * yl + 4 * yh + 8 * xl
    own = core == classes[2]
    row = pl.multiple_of((classes[0] + 2 * classes[1]) * 8, 8)
    here = out_ref.at[pl.ds(row, 8), pl.ds(pl.multiple_of(block * 128, 128), 128)]
    turns = flips((zh, yl, xl, yh), (1, 2, 8, 4))

    def deliver(high):
        pltpu.make_async_remote_copy(
            src_ref=tile_ref.at[high],
            dst_ref=here,
            send_sem=send_sems.at[2],
            recv_sem=recv_sems.at[2],
            device_id=2 * high + classes[2],
            device_id_type=LOGICAL,
        ).start()

    def deliver_some(step, _):
        same_x, same_z = rem(step, 2), div(step, 2)
        x_to = (1 - xh) + same_x * (2 * xh - 1)
        z_to = (1 - zl) + same_z * (2 * zl - 1)
        quarter = x_to + 2 * z_to
        rows = pl.ds(pl.multiple_of(quarter * 256, 16), 256)
        last_ref[...] = jnp.dot(h_ref[rows, :], sum_ref[...], preferred_element_type=F32)
        tiles = last_ref[0:128, 0:128] + (last_ref[0:128, 128:256] + last_ref[128:256, 0:128])
        tile_ref[pl.ds(quarter * 16, 16)] = tiles.reshape(16, 8, 128)
        first = quarter * 16 + home
        for mask in range(15, 0, -1):
            deliver(first + subset(turns, mask))

        @pl.when(jnp.logical_or(step != 3, jnp.logical_not(own)))
        def _():
            deliver(first)

        return 0

    lax.fori_loop(0, 4, deliver_some, 0)

    @pl.when(own)
    def _():
        pltpu.make_async_copy(tile_ref.at[home + 16 * xh + 32 * zl], here, recv_sems.at[2]).start()

    pltpu.make_async_copy(xr_ref.at[0:15], xr_ref.at[0:15], send_sems.at[0]).wait()
    pltpu.make_async_copy(part_ref.at[0:7], part_ref.at[0:7], send_sems.at[1]).wait()

    @pl.when(own)
    def _():
        pltpu.make_async_copy(tile_ref.at[0:63], tile_ref.at[0:63], send_sems.at[2]).wait()

    @pl.when(jnp.logical_not(own))
    def _():
        pltpu.make_async_copy(tile_ref, tile_ref, send_sems.at[2]).wait()

    pltpu.make_async_copy(out_ref, out_ref, recv_sems.at[2]).wait()


def shards(traces, phase_coef):
    return pl.pallas_call(
        kernel,
        out_shape=jax.ShapeDtypeStruct((32, 2048), F32),
        in_specs=[
            pl.BlockSpec(memory_space=pl.ANY),
            pl.BlockSpec(memory_space=pl.ANY),
            pl.BlockSpec(memory_space=pl.ANY),
        ],
        out_specs=pl.BlockSpec(memory_space=pl.ANY),
        scratch_shapes=[
            pltpu.SMEM((2, 4), F32),
            pltpu.VMEM((6, 64, 128), F32),
            pltpu.VMEM((5, 36, 8, 128), F32),
            pltpu.VMEM((5, 6, 8, 128), F32),
            pltpu.VMEM((5, 8, 128), F32),
            pltpu.VMEM((3, 12, 4, 8, 128), F32),
            pltpu.VMEM((1536, 512), BF16),
            pltpu.VMEM((1024, 128), BF16),
            pltpu.VMEM((16, 32, 128), F32),
            pltpu.VMEM((512, 256), BF16),
            pltpu.VMEM((768, 256), F32),
            pltpu.VMEM((8, 96, 128), F32),
            pltpu.VMEM((8, 96, 128), F32),
            pltpu.VMEM((128, 256), BF16),
            pltpu.VMEM((256, 256), F32),
            pltpu.VMEM((64, 8, 128), F32),
            pltpu.SemaphoreType.DMA((3,)),
            pltpu.SemaphoreType.DMA((5,)),
        ],
        compiler_params=pltpu.CompilerParams(
            collective_id=0, has_side_effects=True, vmem_limit_bytes=60 * 2**20
        ),
    )(traces, phase_coef, jnp.asarray(tail_table()))


def solution(mesh):
    placed = (P(("gx", "gy"), None), P())
    return jax.shard_map(
        shards, mesh=mesh, in_specs=placed, out_specs=P(("gx", "gy"), None), check_vma=False
    )
```

```python
import functools

import jax
import jax.numpy as jnp
import numpy as np
from jax import lax
from jax.experimental import pallas as pl
from jax.experimental.pallas import tpu as pltpu
from jax.sharding import PartitionSpec as P

ORDER = 6
LOGICAL = pl.DeviceIdType.LOGICAL
F32 = jnp.float32
BF16 = jnp.bfloat16
AMP = 64.0

NODES = 0.5 * np.cos(np.pi * (2.0 * np.arange(ORDER) + 1.0) / (2.0 * ORDER))


def lagrange(points):
    points = np.asarray(points)[..., None, None]
    same = np.eye(ORDER, dtype=bool)
    spread = np.where(same, 1.0, NODES[:, None] - NODES[None, :])
    return np.where(same, 1.0, (points - NODES[None, :]) / spread).prod(-1)


CENTRE = lagrange(0.0)
HALVES = np.stack([((side - 0.5) + NODES) * 0.5 for side in (0, 1)])
TABLE = lagrange(HALVES)
WEIGHT = np.transpose(TABLE, (0, 2, 1))


def tail_table():
    out = np.zeros((ORDER, 64, 128))
    for high in range(64):
        total = np.eye(ORDER)
        for place in range(6):
            total = TABLE[(high >> place) & 1] @ total
        out[:, high, :96] = np.repeat(CENTRE[:, None] * total, 16, axis=1)
    return out.astype(np.float32)


def fit(function, terms):
    u = 0.125 + 0.125 * np.cos(np.pi * (np.arange(200) + 0.5) / 200)
    poly = np.polynomial.chebyshev.Chebyshev.fit(u, function(np.sqrt(u)), terms - 1, domain=[0, 0.25])
    return [float(c) for c in poly.convert(kind=np.polynomial.Polynomial).coef]


SIN = fit(lambda r: np.sin(np.pi * r) / r, 5)
SIN2 = [2.0 * c for c in fit(lambda r: np.sin(np.pi * r) / r, 4)]
COS = fit(lambda r: np.cos(np.pi * r), 5)
COS4 = fit(lambda r: np.cos(np.pi * r), 4)


def horner(coefs, u):
    total = coefs[-1]
    for c in coefs[-2::-1]:
        total = total * u + c
    return total


def turn(c):
    r = c - jnp.floor(c + 0.5)
    u = r * r
    twice = r * horner(SIN2, u)
    half_cos = horner(COS4, u)
    return 1.0 - (0.5 * twice) * twice, twice * half_cos


def turn_cos(c):
    r = c - jnp.floor(c + 0.5)
    twice = r * horner(SIN2, r * r)
    return 1.0 - (0.5 * twice) * twice


def half_turn(y):
    r = 0.5 - y
    u = r * r
    return r * horner(SIN, u), horner(COS, u)


def bend_value(coef, row, y):
    cosine = (0.5 - y) * horner(SIN, (0.5 - y) * (0.5 - y))
    c0, c1, c2, c3 = (coef[row, m] for m in range(4))
    return (c0 - c2) + cosine * ((c1 - 3.0 * c3) + cosine * (2.0 * c2 + cosine * (4.0 * c3)))


def bend_terms(coef, size):
    e1, e2, e3 = (coef[0, m] * float(-2.0 * AMP * np.sin(np.pi * m * size / 2.0)) for m in (1, 2, 3))
    return e1 - e3, 2.0 * e2, 4.0 * e3


def bend_step(terms, middle):
    cosine, sine = half_turn(middle)
    return sine * (terms[0] + cosine * (terms[1] + cosine * terms[2]))


def apply_real(weights, values):
    out = []
    for t in range(ORDER):
        total = weights[t][0] * values[0]
        for s in range(1, ORDER):
            total = total + weights[t][s] * values[s]
        out.append(total)
    return out


def iota(axis):
    return lax.broadcasted_iota(jnp.int32, (8, 128), axis)


def asf(value):
    return value.astype(F32)


def div(a, b):
    return lax.div(a, jnp.int32(b))


def rem(a, b):
    return lax.rem(a, jnp.int32(b))


def subset(deltas, mask):
    total = None
    for k, delta in enumerate(deltas):
        if (mask >> k) & 1:
            total = delta if total is None else total + delta
    return 0 if total is None else total


def abs_flip(bit, turned):
    return 1 - bit if turned else bit


def flips(bits, weights):
    return [weight * (1 - 2 * bit) for bit, weight in zip(bits, weights)]


def lane_parts(classes, core):
    lane = iota(1)
    place = lane >> 4
    x, y, z = (
        (2 * c + e + core) & 3 for c, e in zip(classes, (place >> 2, (place >> 1) & 1, place & 1))
    )
    return (z >> 1) + 2 * y + 8 * x + 32 * (z & 1), lane & 15


def early_levels(coef, box, top, w_ref, p_ref, v_ref):
    sub = iota(0)
    bits = [asf(sub & 1), asf((sub >> 1) & 1), asf(sub >> 2)]
    sign = [2.0 * bit - 1.0 for bit in bits]
    x0 = jnp.full((8, 128), 0.5, F32)
    x1 = x0 + sign[0] * 0.25
    x2 = x1 + sign[1] * 0.125
    word4 = asf(box * 16 + top)
    steps = [
        bend_step(bend_terms(coef, 2.0 ** -(level + 1)), x + sign[level - 1] * 2.0 ** -(level + 2))
        for level, x in ((1, x0), (2, x1), (3, x2))
    ]
    p0_mid = coef[0, 0] - coef[0, 2]

    def turned(values, angles):
        pairs = [(a * c - b * d, a * d + b * c) for (a, b), (c, d) in zip(values, angles)]
        return [a for a, _ in pairs], [b for _, b in pairs]

    def constants(side):
        return [[float(WEIGHT[side][t][s]) for s in range(ORDER)] for t in range(ORDER)]

    first = []
    for j0 in range(2):
        outs = []
        for j1 in range(2):
            j = j0 + 2 * j1
            word = word4 * 4.0 + float(j)
            start = 0.5 * (j0 + 0.5) + AMP * p0_mid * bend_value(coef, 1, (word + 0.5) * 2.0**-12)
            pairs = []
            for s in range(ORDER):
                node = float(NODES[s])
                p1 = bend_value(coef, 1, (word + (0.5 + node)) * 2.0**-12)
                c, d = turn(start + sign[0] * ((j + 0.5 + node) * 0.25 + steps[0] * p1))
                pairs.append((c * float(CENTRE[s]), d * float(CENTRE[s])))
            outs.append(pairs)
        joined = [[jnp.stack([outs[0][s][c], outs[1][s][c]]) for s in range(ORDER)] for c in range(2)]
        first.append([apply_real(constants(j0), joined[c]) for c in range(2)])
    def levels_2_3():
        linear2 = 2.0 * asf(top & 1) + 0.5
        second = []
        for j1 in range(2):
            word = word4 * 2.0 + float(j1)
            angles = []
            for s in range(ORDER):
                node = float(NODES[s])
                p1 = bend_value(coef, 1, (word + (0.5 + node)) * 2.0**-11)
                angles.append(turn(sign[1] * ((linear2 + (j1 + node)) * 0.25 + steps[1] * p1)))
            values = [[jnp.stack([first[0][c][s][j1], first[1][c][s][j1]]) for c in range(2)] for s in range(ORDER)]
            second.append([apply_real(constants(j1), part) for part in turned(values, angles)])
        linear3 = asf(top & 3) + 0.5
        angles = [turn(sign[2] * ((linear3 + float(NODES[s])) * 0.25 + steps[2] * p_ref[0, s])) for s in range(ORDER)]
        values = [[jnp.concatenate([second[0][c][s], second[1][c][s]]) for c in range(2)] for s in range(ORDER)]
        weights = [[w_ref[0, ORDER * t + s] for s in range(ORDER)] for t in range(ORDER)]
        for c, part in enumerate(turned(values, angles)):
            for t, value in enumerate(apply_real(weights, part)):
                v_ref[0, 2 * t + c] = value

    return levels_2_3


def late_setup(coef, box, top, w_ref, p_ref, c_ref):
    full = box * 16 + top

    def body(i, scale):
        word = full >> i
        pick = (word & 1) == 1
        for t in range(ORDER):
            for s in range(ORDER):
                w_ref[i, ORDER * t + s] = jnp.where(pick, float(WEIGHT[1][t][s]), float(WEIGHT[0][t][s]))
        for s in range(ORDER):
            p_ref[i, s] = bend_value(coef, 1, (asf(word) + float(0.5 + NODES[s])) * scale)
        return scale * 2.0

    lax.fori_loop(0, 5, body, jnp.float32(2.0**-10))
    turn_of = top & 7

    def by_lane(values):
        out = jnp.full((8, 128), float(values[ORDER - 1]), F32)
        for t in range(ORDER - 1):
            out = jnp.where(turn_of == t, float(values[t]), out)
        return out

    e1, e2, e3 = (coef[0, m] * by_lane(-2.0 * AMP * np.sin(np.pi * m * NODES / 128.0)) for m in (1, 2, 3))
    node = by_lane(NODES)
    c_ref[0] = node
    c_ref[1] = e1 - e3
    c_ref[2] = 2.0 * e2
    c_ref[3] = 4.0 * e3
    c_ref[4] = node * (asf(box) + 0.5)


def spread(value, t):
    return jnp.take_along_axis(value, (iota(1) & 120) + t, axis=1)


def late_levels(coef, box, top, order, w_ref, p_ref, c_ref, v_ref, g_ref, between):
    sub = iota(0)
    x3 = asf(4 * (sub & 1) + (sub & 2) + (sub >> 2)) * 0.125 + 0.0625
    full = box * 16 + top
    terms = [bend_terms(coef, 2.0 ** -(level + 1)) for level in (4, 5, 6)]

    def sign_of(bit):
        return (2 * bit - 1).astype(F32)

    def turns(i, level_terms, shift, parent, sign):
        steps = bend_step(level_terms, parent + sign * shift)
        linear = asf((full >> i) & 3) + 0.5
        return [turn(sign * ((linear + float(NODES[s])) * 0.25 + steps * p_ref[i, s])) for s in range(ORDER)]

    def level_step(level, q3, q4):
        first = level == 4
        i = level - 3
        parent = x3 + jnp.where(first, 0.0, sign_of(q3) * 2.0**-5)
        sign = jnp.where(first, sign_of(q3), sign_of(q4))
        level_terms = [jnp.where(first, a, b) for a, b in zip(terms[0], terms[1])]
        real, imag = [], []
        for s, (c, d) in enumerate(turns(i, level_terms, jnp.where(first, 2.0**-6, 2.0**-7), parent, sign)):
            a, b = v_ref[i - 1, 2 * s], v_ref[i - 1, 2 * s + 1]
            real.append(a * c - b * d)
            imag.append(a * d + b * c)
        weights = [[w_ref[i, ORDER * t + s] for s in range(ORDER)] for t in range(ORDER)]
        for c, values in enumerate((real, imag)):
            for t, value in enumerate(apply_real(weights, values)):
                v_ref[i, 2 * t + c] = value

    def last_step(parent, bit, place):
        sign = sign_of(bit)
        middle = parent + sign * 2.0**-7 + c_ref[0] * (1.0 / 128.0)
        steps = bend_step((c_ref[1], c_ref[2], c_ref[3]), middle)
        switch = [turn((c_ref[4] + c_ref[0] * float(NODES[u])) + steps * p_ref[4, u]) for u in range(ORDER)]
        merged = []
        for s, (c, d) in enumerate(turns(3, terms[2], 2.0**-8, parent, sign)):
            a = b = None
            for u in range(ORDER):
                weight = w_ref[3, ORDER * u + s]
                a = switch[u][0] * weight if a is None else a + switch[u][0] * weight
                b = switch[u][1] * weight if b is None else b + switch[u][1] * weight
            merged.append((a * c - b * d, a * d + b * c))
        parts = [v_ref[2, 2 * s] + v_ref[2, 2 * s + 1] for s in range(ORDER)]
        for t in range(ORDER):
            k1 = k2 = k3 = None
            for s in range(ORDER):
                c, d = spread(merged[s][0], t), spread(merged[s][1], t)
                m1, m2, m3 = parts[s] * c, v_ref[2, 2 * s] * (d - c), v_ref[2, 2 * s + 1] * (c + d)
                k1 = m1 if k1 is None else k1 + m1
                k2 = m2 if k2 is None else k2 + m2
                k3 = m3 if k3 is None else k3 + m3
            real, imag = k1 - k3, k1 + k2
            rows = pl.ds(pl.multiple_of(place * 192 + 16 * t, 16), 16)
            rows_low = pl.ds(pl.multiple_of(place * 192 + 96 + 16 * t, 16), 16)
            for j in range(4):
                both = jnp.concatenate([real[j], imag[j]], axis=0)
                high = both.astype(BF16)
                g_ref[rows, 128 * j : 128 * (j + 1)] = high
                g_ref[rows_low, 128 * j : 128 * (j + 1)] = (both - high.astype(F32)).astype(BF16)

    def over(n, _):
        pl.when(n == 3)(between)
        q3, q4 = order(div(n, 2)), rem(n, 2)

        def levels(level, _):
            level_step(level, q3, q4)
            return 0

        lax.fori_loop(4 + q4, 6, levels, 0)
        x5 = x3 + (sign_of(q3) * 2.0**-5 + sign_of(q4) * 2.0**-6)

        def over5(q5, _):
            last_step(x5, q5, 4 * q3 + q4 + 2 * q5)
            return 0

        return lax.fori_loop(0, 2, over5, 0)

    lax.fori_loop(0, 4, over, 0)


def last_weights(coef, group, tail_ref, h_ref):
    sub, lane = iota(0), iota(1)
    own = lane & 7
    same = sub == own
    box6 = 32 * (own & 1) + 8 * (own & 2) + 2 * (own & 4)
    box6 = box6 + (4 * rem(group, 2) + 2 * rem(div(group, 2), 2) + div(group, 4))
    inner = 32 * (sub & 1) + 8 * (sub & 2) + 2 * (sub & 4)
    base = box6 * 64 + inner
    quarter = 0.25 * asf((lane >> 3) & 1)
    p1_mid = coef[1, 0] - coef[1, 2]

    def rows_of(r):
        centre = (asf(base + (4 * rem(r, 2) + 2 * rem(div(r, 2), 2) + div(r, 4))) + 0.5) * 2.0**-12
        total = None
        for t in range(ORDER):
            node = float(NODES[t])
            steps = bend_step(bend_terms(coef, node / 4096.0), centre + node / 8192.0)
            term = turn_cos((quarter - 0.5 * node) - steps * p1_mid)
            term = term * tail_ref[t, pl.ds(pl.multiple_of(8 * r, 8), 8), :]
            total = term if total is None else total + term
        return total

    def body(r, _):
        total = rows_of(r)
        start = 256 * div(r, 2) + 64 * rem(r, 2)
        for k in range(0, 8, 2):
            both = jnp.concatenate(
                [jnp.where(same, jnp.broadcast_to(total[k + n : k + n + 1], (8, 128)), 0.0) for n in range(2)], axis=0
            )
            high = both.astype(BF16)
            h_ref[pl.ds(pl.multiple_of(start + 8 * k, 16), 16), :] = high
            h_ref[pl.ds(pl.multiple_of(start + 128 + 8 * k, 16), 16), :] = (both - high.astype(F32)).astype(BF16)
        return 0

    lax.fori_loop(0, 8, body, 0)


def kernel(
    x_ref,
    coef_hbm,
    tail_hbm,
    out_ref,
    coef_ref,
    tail_ref,
    w_ref,
    p_ref,
    c_ref,
    v_ref,
    g_ref,
    h_ref,
    xr_ref,
    xs_ref,
    wide_ref,
    part_ref,
    rr_ref,
    sum_ref,
    tile_ref,
    send_sems,
    recv_sems,
):
    fetch_coef = pltpu.make_async_copy(coef_hbm, coef_ref, recv_sems.at[3])
    fetch_tail = pltpu.make_async_copy(tail_hbm, tail_ref, recv_sems.at[4])
    fetch_coef.start()
    fetch_tail.start()
    gx, gy = lax.axis_index("gx"), lax.axis_index("gy")
    core = rem(gy, 2)
    zl, xs = div(gx, 4), rem(gx, 4)
    xh, xl = div(xs, 2), rem(xs, 2)
    yh, yl, zh = div(gy, 8), rem(div(gy, 4), 2), rem(div(gy, 2), 2)
    me = gx * 16 + gy
    highs, lows = (xh, yh, zh), (xl, yl, zl)
    unlike = [h + l - 2 * h * l for h, l in zip(highs, lows)]
    to_a = [16 * (1 - 2 * xl), 4 * (1 - 2 * yl), 64 * (1 - 2 * zl)]
    to_b = [16 * (3 - 2 * xs), 4 * (3 - 2 * (2 * yh + yl)), 2 * (1 - 2 * zh) + 64 * (1 - 2 * zl)]
    to_class = [a + core * (b - a) for a, b in zip(to_a, to_b)]
    to_group = [b + core * (a - b) for a, b in zip(to_a, to_b)]
    to_core = 1 - 2 * core
    class_a, class_b = highs, [1 - d for d in unlike]
    place_a, place_b = lows, [1 - l for l in lows]
    group_a, group_b = [1 - d for d in unlike], [1 - h for h in highs]

    def mine(for_a, for_b):
        return [a + core * (b - a) for a, b in zip(for_a, for_b)]

    def others(for_a, for_b):
        return [b + core * (a - b) for a, b in zip(for_a, for_b)]

    def number(values):
        return values[0] + 2 * values[1] + 4 * values[2]

    classes, groups = mine(class_a, class_b), mine(group_a, group_b)
    target = number(classes)
    block = number(groups) + 8 * core

    barrier = pltpu.get_barrier_semaphore()
    for mask in range(1, 16):
        source = me + subset(to_class + [to_core], mask)
        pl.semaphore_signal(barrier, inc=1, device_id=source, device_id_type=LOGICAL)
    for mask in range(1, 8):
        pl.semaphore_signal(barrier, inc=1, device_id=me + subset(to_group, mask), device_id_type=LOGICAL)
    box, top = lane_parts(classes, core)
    fetch_coef.wait()
    late_setup(coef_ref, box, top, w_ref, p_ref, c_ref)
    levels_2_3 = early_levels(coef_ref, box, top, w_ref, p_ref, v_ref)
    pl.semaphore_wait(barrier, 22)

    def columns(m):
        return x_ref.at[:, pl.ds(pl.multiple_of(m * 128, 128), 128)]

    own_slot = 2 * number(mine(place_a, place_b)[::-1]) + core
    other_slot = 2 * number(others(place_a, place_b)[::-1]) + core
    other_groups = others(group_a, group_b)
    other_block = number(other_groups) + 8 * (1 - core)
    for mask in range(7, -1, -1):
        routes = [(other_block, other_groups, other_slot, me + to_core + subset(to_group, mask))]
        if mask:
            routes.append((block, groups, own_slot, me + subset(to_class, mask)))
        for first, group_bits, slot, device in routes:
            pltpu.make_async_remote_copy(
                src_ref=columns(first + subset(flips(group_bits, (1, 2, 4)), mask)),
                dst_ref=xr_ref.at[slot],
                send_sem=send_sems.at[0],
                recv_sem=recv_sems.at[0],
                device_id=device,
                device_id_type=LOGICAL,
            ).start()
    pltpu.make_async_copy(columns(block), xr_ref.at[own_slot], recv_sems.at[0]).start()
    levels_2_3()

    def order(h):
        return classes[0] + (1 - h) * (1 - 2 * classes[0])

    def split(i, _):
        for j in range(4):
            piece = jnp.concatenate([xr_ref[2 * i + s, pl.ds(j, 8, stride=4), :] for s in range(2)], axis=0)
            high = piece.astype(BF16)
            rows = pl.ds(pl.multiple_of(128 * j + 16 * i, 16), 16)
            xs_ref[rows, 0:128] = high
            xs_ref[rows, 128:256] = (piece - high.astype(F32)).astype(BF16)
        return 0

    def half(h):
        q3 = order(h)
        rows = pl.ds(pl.multiple_of(q3 * 768, 16), 768)
        wide_ref[...] = jnp.dot(g_ref[rows, :], xs_ref[...], preferred_element_type=F32)

        far = to_group[0] if h == 0 else 0
        for mask in range(3, -1, -1):
            i = classes[1] + 2 * classes[2] + subset(flips(classes[1:], (1, 2)), mask)
            high = pl.ds(pl.multiple_of(i * 192, 8), 96)
            low = pl.ds(pl.multiple_of(i * 192 + 96, 8), 96)
            part = wide_ref[high, 0:128] + (wide_ref[high, 128:256] + wide_ref[low, 0:128])

            def send():
                part_ref[4 * q3 + i] = part
                pltpu.make_async_remote_copy(
                    src_ref=part_ref.at[4 * q3 + i],
                    dst_ref=rr_ref.at[target],
                    send_sem=send_sems.at[1],
                    recv_sem=recv_sems.at[1],
                    device_id=me + far + subset(to_group[1:], mask),
                    device_id_type=LOGICAL,
                ).start()

            if mask or h == 0:
                send()
            else:
                rr_ref[target] = part

    def first_half():
        pltpu.make_async_copy(xr_ref, xr_ref, recv_sems.at[0]).wait()
        lax.fori_loop(0, 8, split, 0)
        half(0)

    late_levels(coef_ref, box, top, order, w_ref, p_ref, c_ref, v_ref, g_ref, first_half)
    half(1)
    fetch_tail.wait()
    last_weights(coef_ref, target, tail_ref, h_ref)
    pltpu.make_async_copy(rr_ref.at[0:7], rr_ref.at[0:7], recv_sems.at[1]).wait()

    def add(i, _):
        rows = pl.ds(pl.multiple_of(16 * i, 16), 16)
        total = rr_ref[0, rows, :]
        for k in range(1, 8):
            total = total + rr_ref[k, rows, :]
        high = total.astype(BF16)
        sum_ref[rows, 0:128] = high
        sum_ref[rows, 128:256] = (total - high.astype(F32)).astype(BF16)
        return 0

    lax.fori_loop(0, 6, add, 0)
    sum_ref[96:128, :] = jnp.zeros((32, 256), BF16)

    home = zh + 2 * yl + 4 * yh + 8 * xl
    own = core == classes[2]
    row = pl.multiple_of((classes[0] + 2 * classes[1]) * 8, 8)
    here = out_ref.at[pl.ds(row, 8), pl.ds(pl.multiple_of(block * 128, 128), 128)]
    turns = flips((zh, yl, xl, yh), (1, 2, 8, 4))

    def deliver(high):
        pltpu.make_async_remote_copy(
            src_ref=tile_ref.at[high],
            dst_ref=here,
            send_sem=send_sems.at[2],
            recv_sem=recv_sems.at[2],
            device_id=2 * high + classes[2],
            device_id_type=LOGICAL,
        ).start()

    quarters = [abs_flip(xh, n % 2) + 2 * abs_flip(zl, n // 2) for n in (3, 2, 1, 0)]

    def make(quarter):
        rows = pl.ds(pl.multiple_of(quarter * 256, 16), 256)
        wide = jnp.dot(h_ref[rows, :], sum_ref[...], preferred_element_type=F32)
        tiles = wide[0:128, 0:128] + (wide[0:128, 128:256] + wide[128:256, 0:128])
        tile_ref[pl.ds(quarter * 16, 16)] = tiles.reshape(16, 8, 128)

    make(quarters[0])
    for n, quarter in enumerate(quarters):
        if n < 3:
            make(quarters[n + 1])
        first = quarter * 16 + home
        for mask in range(15, -1, -1):
            if n < 3 or mask:
                deliver(first + subset(turns, mask))
    pl.when(jnp.logical_not(own))(lambda: deliver(quarters[3] * 16 + home))

    @pl.when(own)
    def _():
        pltpu.make_async_copy(tile_ref.at[home + 16 * xh + 32 * zl], here, recv_sems.at[2]).start()

    pltpu.make_async_copy(xr_ref.at[0:15], xr_ref.at[0:15], send_sems.at[0]).wait()
    pltpu.make_async_copy(part_ref.at[0:7], part_ref.at[0:7], send_sems.at[1]).wait()

    @pl.when(own)
    def _():
        pltpu.make_async_copy(tile_ref.at[0:63], tile_ref.at[0:63], send_sems.at[2]).wait()

    @pl.when(jnp.logical_not(own))
    def _():
        pltpu.make_async_copy(tile_ref, tile_ref, send_sems.at[2]).wait()

    pltpu.make_async_copy(out_ref, out_ref, recv_sems.at[2]).wait()


def shards(traces, phase_coef):
    return pl.pallas_call(
        kernel,
        out_shape=jax.ShapeDtypeStruct((32, 2048), F32),
        in_specs=[
            pl.BlockSpec(memory_space=pl.ANY),
            pl.BlockSpec(memory_space=pl.ANY),
            pl.BlockSpec(memory_space=pl.ANY),
        ],
        out_specs=pl.BlockSpec(memory_space=pl.ANY),
        scratch_shapes=[
            pltpu.SMEM((2, 4), F32),
            pltpu.VMEM((6, 64, 128), F32),
            pltpu.VMEM((5, 36, 8, 128), F32),
            pltpu.VMEM((5, 6, 8, 128), F32),
            pltpu.VMEM((5, 8, 128), F32),
            pltpu.VMEM((3, 12, 4, 8, 128), F32),
            pltpu.VMEM((1536, 512), BF16),
            pltpu.VMEM((1024, 128), BF16),
            pltpu.VMEM((16, 32, 128), F32),
            pltpu.VMEM((512, 256), BF16),
            pltpu.VMEM((768, 256), F32),
            pltpu.VMEM((8, 96, 128), F32),
            pltpu.VMEM((8, 96, 128), F32),
            pltpu.VMEM((128, 256), BF16),
            pltpu.VMEM((64, 8, 128), F32),
            pltpu.SemaphoreType.DMA((3,)),
            pltpu.SemaphoreType.DMA((5,)),
        ],
        compiler_params=pltpu.CompilerParams(
            collective_id=0, has_side_effects=True, vmem_limit_bytes=60 * 2**20
        ),
    )(traces, phase_coef, jnp.asarray(tail_table()))


def solution(mesh):
    placed = (P(("gx", "gy"), None), P())
    return jax.shard_map(
        shards, mesh=mesh, in_specs=placed, out_specs=P(("gx", "gy"), None), check_vma=False
    )
```

```python
import functools

import jax
import jax.numpy as jnp
import numpy as np
from jax import lax
from jax.experimental import pallas as pl
from jax.experimental.pallas import tpu as pltpu
from jax.sharding import PartitionSpec as P

ORDER = 6
LOGICAL = pl.DeviceIdType.LOGICAL
F32 = jnp.float32
BF16 = jnp.bfloat16
AMP = 64.0

NODES = 0.5 * np.cos(np.pi * (2.0 * np.arange(ORDER) + 1.0) / (2.0 * ORDER))


def lagrange(points):
    points = np.asarray(points)[..., None, None]
    same = np.eye(ORDER, dtype=bool)
    spread = np.where(same, 1.0, NODES[:, None] - NODES[None, :])
    return np.where(same, 1.0, (points - NODES[None, :]) / spread).prod(-1)


CENTRE = lagrange(0.0)
HALVES = np.stack([((side - 0.5) + NODES) * 0.5 for side in (0, 1)])
TABLE = lagrange(HALVES)
WEIGHT = np.transpose(TABLE, (0, 2, 1))


def tail_table():
    out = np.zeros((ORDER, 64, 128))
    for high in range(64):
        total = np.eye(ORDER)
        for place in range(6):
            total = TABLE[(high >> place) & 1] @ total
        out[:, high, :96] = np.repeat(CENTRE[:, None] * total, 16, axis=1)
    return out.astype(np.float32)


def fit(function, terms):
    u = 0.125 + 0.125 * np.cos(np.pi * (np.arange(200) + 0.5) / 200)
    poly = np.polynomial.chebyshev.Chebyshev.fit(u, function(np.sqrt(u)), terms - 1, domain=[0, 0.25])
    return [float(c) for c in poly.convert(kind=np.polynomial.Polynomial).coef]


SIN = fit(lambda r: np.sin(np.pi * r) / r, 5)
SIN2 = [2.0 * c for c in fit(lambda r: np.sin(np.pi * r) / r, 4)]
COS = fit(lambda r: np.cos(np.pi * r), 5)
COS4 = fit(lambda r: np.cos(np.pi * r), 4)


def horner(coefs, u):
    total = coefs[-1]
    for c in coefs[-2::-1]:
        total = total * u + c
    return total


def turn(c):
    r = c - jnp.floor(c + 0.5)
    u = r * r
    twice = r * horner(SIN2, u)
    half_cos = horner(COS4, u)
    return 1.0 - (0.5 * twice) * twice, twice * half_cos


def turn_cos(c):
    r = c - jnp.floor(c + 0.5)
    twice = r * horner(SIN2, r * r)
    return 1.0 - (0.5 * twice) * twice


def half_turn(y):
    r = 0.5 - y
    u = r * r
    return r * horner(SIN, u), horner(COS, u)


def bend_value(coef, row, y):
    cosine = (0.5 - y) * horner(SIN, (0.5 - y) * (0.5 - y))
    c0, c1, c2, c3 = (coef[row, m] for m in range(4))
    return (c0 - c2) + cosine * ((c1 - 3.0 * c3) + cosine * (2.0 * c2 + cosine * (4.0 * c3)))


def bend_terms(coef, size):
    e1, e2, e3 = (coef[0, m] * float(-2.0 * AMP * np.sin(np.pi * m * size / 2.0)) for m in (1, 2, 3))
    return e1 - e3, 2.0 * e2, 4.0 * e3


def bend_step(terms, middle):
    cosine, sine = half_turn(middle)
    return sine * (terms[0] + cosine * (terms[1] + cosine * terms[2]))


def apply_real(weights, values):
    out = []
    for t in range(ORDER):
        total = weights[t][0] * values[0]
        for s in range(1, ORDER):
            total = total + weights[t][s] * values[s]
        out.append(total)
    return out


def iota(axis):
    return lax.broadcasted_iota(jnp.int32, (8, 128), axis)


def asf(value):
    return value.astype(F32)


def div(a, b):
    return lax.div(a, jnp.int32(b))


def rem(a, b):
    return lax.rem(a, jnp.int32(b))


def subset(deltas, mask):
    total = None
    for k, delta in enumerate(deltas):
        if (mask >> k) & 1:
            total = delta if total is None else total + delta
    return 0 if total is None else total


def abs_flip(bit, turned):
    return 1 - bit if turned else bit


def flips(bits, weights):
    return [weight * (1 - 2 * bit) for bit, weight in zip(bits, weights)]


def lane_parts(classes, core):
    lane = iota(1)
    place = lane >> 4
    x, y, z = (
        (2 * c + e + core) & 3 for c, e in zip(classes, (place >> 2, (place >> 1) & 1, place & 1))
    )
    return (z >> 1) + 2 * y + 8 * x + 32 * (z & 1), lane & 15


def early_levels(coef, box, top, w_ref, p_ref, v_ref):
    sub = iota(0)
    bits = [asf(sub & 1), asf((sub >> 1) & 1), asf(sub >> 2)]
    sign = [2.0 * bit - 1.0 for bit in bits]
    x0 = jnp.full((8, 128), 0.5, F32)
    x1 = x0 + sign[0] * 0.25
    x2 = x1 + sign[1] * 0.125
    word4 = asf(box * 16 + top)
    steps = [
        bend_step(bend_terms(coef, 2.0 ** -(level + 1)), x + sign[level - 1] * 2.0 ** -(level + 2))
        for level, x in ((1, x0), (2, x1), (3, x2))
    ]
    p0_mid = coef[0, 0] - coef[0, 2]

    def turned(values, angles):
        pairs = [(a * c - b * d, a * d + b * c) for (a, b), (c, d) in zip(values, angles)]
        return [a for a, _ in pairs], [b for _, b in pairs]

    def constants(side):
        return [[float(WEIGHT[side][t][s]) for s in range(ORDER)] for t in range(ORDER)]

    first = []
    for j0 in range(2):
        outs = []
        for j1 in range(2):
            j = j0 + 2 * j1
            word = word4 * 4.0 + float(j)
            start = 0.5 * (j0 + 0.5) + AMP * p0_mid * bend_value(coef, 1, (word + 0.5) * 2.0**-12)
            pairs = []
            for s in range(ORDER):
                node = float(NODES[s])
                p1 = bend_value(coef, 1, (word + (0.5 + node)) * 2.0**-12)
                c, d = turn(start + sign[0] * ((j + 0.5 + node) * 0.25 + steps[0] * p1))
                pairs.append((c * float(CENTRE[s]), d * float(CENTRE[s])))
            outs.append(pairs)
        joined = [[jnp.stack([outs[0][s][c], outs[1][s][c]]) for s in range(ORDER)] for c in range(2)]
        first.append([apply_real(constants(j0), joined[c]) for c in range(2)])
    def levels_2_3():
        linear2 = 2.0 * asf(top & 1) + 0.5
        second = []
        for j1 in range(2):
            word = word4 * 2.0 + float(j1)
            angles = []
            for s in range(ORDER):
                node = float(NODES[s])
                p1 = bend_value(coef, 1, (word + (0.5 + node)) * 2.0**-11)
                angles.append(turn(sign[1] * ((linear2 + (j1 + node)) * 0.25 + steps[1] * p1)))
            values = [[jnp.stack([first[0][c][s][j1], first[1][c][s][j1]]) for c in range(2)] for s in range(ORDER)]
            second.append([apply_real(constants(j1), part) for part in turned(values, angles)])
        linear3 = asf(top & 3) + 0.5
        angles = [turn(sign[2] * ((linear3 + float(NODES[s])) * 0.25 + steps[2] * p_ref[0, s])) for s in range(ORDER)]
        values = [[jnp.concatenate([second[0][c][s], second[1][c][s]]) for c in range(2)] for s in range(ORDER)]
        weights = [[w_ref[0, ORDER * t + s] for s in range(ORDER)] for t in range(ORDER)]
        for c, part in enumerate(turned(values, angles)):
            for t, value in enumerate(apply_real(weights, part)):
                v_ref[0, 2 * t + c] = value

    return levels_2_3


def late_setup(coef, box, top, w_ref, p_ref, c_ref):
    full = box * 16 + top

    def body(i, scale):
        word = full >> i
        pick = (word & 1) == 1
        for t in range(ORDER):
            for s in range(ORDER):
                w_ref[i, ORDER * t + s] = jnp.where(pick, float(WEIGHT[1][t][s]), float(WEIGHT[0][t][s]))
        for s in range(ORDER):
            p_ref[i, s] = bend_value(coef, 1, (asf(word) + float(0.5 + NODES[s])) * scale)
        return scale * 2.0

    lax.fori_loop(0, 5, body, jnp.float32(2.0**-10))
    turn_of = top & 7

    def by_lane(values):
        out = jnp.full((8, 128), float(values[ORDER - 1]), F32)
        for t in range(ORDER - 1):
            out = jnp.where(turn_of == t, float(values[t]), out)
        return out

    e1, e2, e3 = (coef[0, m] * by_lane(-2.0 * AMP * np.sin(np.pi * m * NODES / 128.0)) for m in (1, 2, 3))
    node = by_lane(NODES)
    c_ref[0] = node
    c_ref[1] = e1 - e3
    c_ref[2] = 2.0 * e2
    c_ref[3] = 4.0 * e3
    c_ref[4] = node * (asf(box) + 0.5)


def spread(value, t):
    return jnp.take_along_axis(value, (iota(1) & 120) + t, axis=1)


def late_levels(coef, box, top, order, w_ref, p_ref, c_ref, v_ref, g_ref, between):
    sub = iota(0)
    x3 = asf(4 * (sub & 1) + (sub & 2) + (sub >> 2)) * 0.125 + 0.0625
    full = box * 16 + top
    terms = [bend_terms(coef, 2.0 ** -(level + 1)) for level in (4, 5, 6)]

    def sign_of(bit):
        return (2 * bit - 1).astype(F32)

    def turns(i, level_terms, shift, parent, sign):
        steps = bend_step(level_terms, parent + sign * shift)
        linear = asf((full >> i) & 3) + 0.5
        return [turn(sign * ((linear + float(NODES[s])) * 0.25 + steps * p_ref[i, s])) for s in range(ORDER)]

    def level_step(level, q3, q4):
        first = level == 4
        i = level - 3
        parent = x3 + jnp.where(first, 0.0, sign_of(q3) * 2.0**-5)
        sign = jnp.where(first, sign_of(q3), sign_of(q4))
        level_terms = [jnp.where(first, a, b) for a, b in zip(terms[0], terms[1])]
        real, imag = [], []
        for s, (c, d) in enumerate(turns(i, level_terms, jnp.where(first, 2.0**-6, 2.0**-7), parent, sign)):
            a, b = v_ref[i - 1, 2 * s], v_ref[i - 1, 2 * s + 1]
            real.append(a * c - b * d)
            imag.append(a * d + b * c)
        weights = [[w_ref[i, ORDER * t + s] for s in range(ORDER)] for t in range(ORDER)]
        for c, values in enumerate((real, imag)):
            for t, value in enumerate(apply_real(weights, values)):
                v_ref[i, 2 * t + c] = value

    def last_step(parent, bit, place):
        sign = sign_of(bit)
        middle = parent + sign * 2.0**-7 + c_ref[0] * (1.0 / 128.0)
        steps = bend_step((c_ref[1], c_ref[2], c_ref[3]), middle)
        switch = [turn((c_ref[4] + c_ref[0] * float(NODES[u])) + steps * p_ref[4, u]) for u in range(ORDER)]
        merged = []
        for s, (c, d) in enumerate(turns(3, terms[2], 2.0**-8, parent, sign)):
            a = b = None
            for u in range(ORDER):
                weight = w_ref[3, ORDER * u + s]
                a = switch[u][0] * weight if a is None else a + switch[u][0] * weight
                b = switch[u][1] * weight if b is None else b + switch[u][1] * weight
            merged.append((a * c - b * d, a * d + b * c))
        parts = [v_ref[2, 2 * s] + v_ref[2, 2 * s + 1] for s in range(ORDER)]
        for t in range(ORDER):
            k1 = k2 = k3 = None
            for s in range(ORDER):
                c, d = spread(merged[s][0], t), spread(merged[s][1], t)
                m1, m2, m3 = parts[s] * c, v_ref[2, 2 * s] * (d - c), v_ref[2, 2 * s + 1] * (c + d)
                k1 = m1 if k1 is None else k1 + m1
                k2 = m2 if k2 is None else k2 + m2
                k3 = m3 if k3 is None else k3 + m3
            real, imag = k1 - k3, k1 + k2
            rows = pl.ds(pl.multiple_of(place * 192 + 16 * t, 16), 16)
            rows_low = pl.ds(pl.multiple_of(place * 192 + 96 + 16 * t, 16), 16)
            for j in range(4):
                both = jnp.concatenate([real[j], imag[j]], axis=0)
                high = both.astype(BF16)
                g_ref[rows, 128 * j : 128 * (j + 1)] = high
                g_ref[rows_low, 128 * j : 128 * (j + 1)] = (both - high.astype(F32)).astype(BF16)

    def over(n, _):
        pl.when(n == 3)(between)
        q3, q4 = order(div(n, 2)), rem(n, 2)

        def levels(level, _):
            level_step(level, q3, q4)
            return 0

        lax.fori_loop(4 + q4, 6, levels, 0)
        x5 = x3 + (sign_of(q3) * 2.0**-5 + sign_of(q4) * 2.0**-6)

        def over5(q5, _):
            last_step(x5, q5, 4 * q3 + q4 + 2 * q5)
            return 0

        return lax.fori_loop(0, 2, over5, 0)

    lax.fori_loop(0, 4, over, 0)


def last_weights(coef, group, tail_ref, h_ref):
    sub, lane = iota(0), iota(1)
    own = lane & 7
    same = sub == own
    box6 = 32 * (own & 1) + 8 * (own & 2) + 2 * (own & 4)
    box6 = box6 + (4 * rem(group, 2) + 2 * rem(div(group, 2), 2) + div(group, 4))
    inner = 32 * (sub & 1) + 8 * (sub & 2) + 2 * (sub & 4)
    base = box6 * 64 + inner
    quarter = 0.25 * asf((lane >> 3) & 1)
    p1_mid = coef[1, 0] - coef[1, 2]

    def rows_of(r):
        centre = (asf(base + (4 * rem(r, 2) + 2 * rem(div(r, 2), 2) + div(r, 4))) + 0.5) * 2.0**-12
        total = None
        for t in range(ORDER):
            node = float(NODES[t])
            steps = bend_step(bend_terms(coef, node / 4096.0), centre + node / 8192.0)
            term = turn_cos((quarter - 0.5 * node) - steps * p1_mid)
            term = term * tail_ref[t, pl.ds(pl.multiple_of(8 * r, 8), 8), :]
            total = term if total is None else total + term
        return total

    def body(r, _):
        total = rows_of(r)
        start = 256 * div(r, 2) + 64 * rem(r, 2)
        for k in range(0, 8, 2):
            both = jnp.concatenate(
                [jnp.where(same, jnp.broadcast_to(total[k + n : k + n + 1], (8, 128)), 0.0) for n in range(2)], axis=0
            )
            high = both.astype(BF16)
            h_ref[pl.ds(pl.multiple_of(start + 8 * k, 16), 16), :] = high
            h_ref[pl.ds(pl.multiple_of(start + 128 + 8 * k, 16), 16), :] = (both - high.astype(F32)).astype(BF16)
        return 0

    lax.fori_loop(0, 8, body, 0)


def kernel(
    x_ref,
    coef_hbm,
    tail_hbm,
    out_ref,
    coef_ref,
    tail_ref,
    w_ref,
    p_ref,
    c_ref,
    v_ref,
    g_ref,
    h_ref,
    xr_ref,
    xs_ref,
    wide_ref,
    part_ref,
    rr_ref,
    sum_ref,
    tile_ref,
    send_sems,
    recv_sems,
):
    fetch_coef = pltpu.make_async_copy(coef_hbm, coef_ref, recv_sems.at[3])
    fetch_tail = pltpu.make_async_copy(tail_hbm, tail_ref, recv_sems.at[4])
    fetch_coef.start()
    fetch_tail.start()
    gx, gy = lax.axis_index("gx"), lax.axis_index("gy")
    core = rem(gy, 2)
    zl, xs = div(gx, 4), rem(gx, 4)
    xh, xl = div(xs, 2), rem(xs, 2)
    yh, yl, zh = div(gy, 8), rem(div(gy, 4), 2), rem(div(gy, 2), 2)
    me = gx * 16 + gy
    highs, lows = (xh, yh, zh), (xl, yl, zl)
    unlike = [h + l - 2 * h * l for h, l in zip(highs, lows)]
    to_a = [16 * (1 - 2 * xl), 4 * (1 - 2 * yl), 64 * (1 - 2 * zl)]
    to_b = [16 * (3 - 2 * xs), 4 * (3 - 2 * (2 * yh + yl)), 2 * (1 - 2 * zh) + 64 * (1 - 2 * zl)]
    to_class = [a + core * (b - a) for a, b in zip(to_a, to_b)]
    to_group = [b + core * (a - b) for a, b in zip(to_a, to_b)]
    to_core = 1 - 2 * core
    class_a, class_b = highs, [1 - d for d in unlike]
    place_a, place_b = lows, [1 - l for l in lows]
    group_a, group_b = [1 - d for d in unlike], [1 - h for h in highs]

    def mine(for_a, for_b):
        return [a + core * (b - a) for a, b in zip(for_a, for_b)]

    def others(for_a, for_b):
        return [b + core * (a - b) for a, b in zip(for_a, for_b)]

    def number(values):
        return values[0] + 2 * values[1] + 4 * values[2]

    classes, groups = mine(class_a, class_b), mine(group_a, group_b)
    target = number(classes)
    block = number(groups) + 8 * core

    barrier = pltpu.get_barrier_semaphore()
    for mask in range(1, 16):
        source = me + subset(to_class + [to_core], mask)
        pl.semaphore_signal(barrier, inc=1, device_id=source, device_id_type=LOGICAL)
    for mask in range(1, 8):
        pl.semaphore_signal(barrier, inc=1, device_id=me + subset(to_group, mask), device_id_type=LOGICAL)
    box, top = lane_parts(classes, core)
    fetch_coef.wait()
    late_setup(coef_ref, box, top, w_ref, p_ref, c_ref)
    levels_2_3 = early_levels(coef_ref, box, top, w_ref, p_ref, v_ref)
    pl.semaphore_wait(barrier, 22)

    def columns(m):
        return x_ref.at[:, pl.ds(pl.multiple_of(m * 128, 128), 128)]

    own_slot = 2 * number(mine(place_a, place_b)[::-1]) + core
    other_slot = 2 * number(others(place_a, place_b)[::-1]) + core
    other_groups = others(group_a, group_b)
    other_block = number(other_groups) + 8 * (1 - core)
    for mask in range(7, -1, -1):
        routes = [(other_block, other_groups, other_slot, me + to_core + subset(to_group, mask))]
        if mask:
            routes.append((block, groups, own_slot, me + subset(to_class, mask)))
        for first, group_bits, slot, device in routes:
            pltpu.make_async_remote_copy(
                src_ref=columns(first + subset(flips(group_bits, (1, 2, 4)), mask)),
                dst_ref=xr_ref.at[slot],
                send_sem=send_sems.at[0],
                recv_sem=recv_sems.at[0],
                device_id=device,
                device_id_type=LOGICAL,
            ).start()
    pltpu.make_async_copy(columns(block), xr_ref.at[own_slot], recv_sems.at[0]).start()
    levels_2_3()

    def order(h):
        return classes[0] + (1 - h) * (1 - 2 * classes[0])

    def split(i, _):
        for j in range(4):
            piece = jnp.concatenate([xr_ref[2 * i + s, pl.ds(j, 8, stride=4), :] for s in range(2)], axis=0)
            high = piece.astype(BF16)
            rows = pl.ds(pl.multiple_of(128 * j + 16 * i, 16), 16)
            xs_ref[rows, 0:128] = high
            xs_ref[rows, 128:256] = (piece - high.astype(F32)).astype(BF16)
        return 0

    def half(h):
        q3 = order(h)
        rows = pl.ds(pl.multiple_of(q3 * 768, 16), 768)
        wide_ref[...] = jnp.dot(g_ref[rows, :], xs_ref[...], preferred_element_type=F32)

        far = to_group[0] if h == 0 else 0
        for mask in range(3, -1, -1):
            i = classes[1] + 2 * classes[2] + subset(flips(classes[1:], (1, 2)), mask)
            high = pl.ds(pl.multiple_of(i * 192, 8), 96)
            low = pl.ds(pl.multiple_of(i * 192 + 96, 8), 96)
            part = wide_ref[high, 0:128] + (wide_ref[high, 128:256] + wide_ref[low, 0:128])

            def send():
                part_ref[4 * q3 + i] = part
                pltpu.make_async_remote_copy(
                    src_ref=part_ref.at[4 * q3 + i],
                    dst_ref=rr_ref.at[target],
                    send_sem=send_sems.at[1],
                    recv_sem=recv_sems.at[1],
                    device_id=me + far + subset(to_group[1:], mask),
                    device_id_type=LOGICAL,
                ).start()

            if mask or h == 0:
                send()
            else:
                rr_ref[target] = part

    def first_half():
        pltpu.make_async_copy(xr_ref, xr_ref, recv_sems.at[0]).wait()
        lax.fori_loop(0, 8, split, 0)
        half(0)

    late_levels(coef_ref, box, top, order, w_ref, p_ref, c_ref, v_ref, g_ref, first_half)
    half(1)
    fetch_tail.wait()
    last_weights(coef_ref, target, tail_ref, h_ref)
    pltpu.make_async_copy(rr_ref.at[0:7], rr_ref.at[0:7], recv_sems.at[1]).wait()

    def add(i, _):
        rows = pl.ds(pl.multiple_of(16 * i, 16), 16)
        total = rr_ref[0, rows, :]
        for k in range(1, 8):
            total = total + rr_ref[k, rows, :]
        high = total.astype(BF16)
        sum_ref[rows, 0:128] = high
        sum_ref[rows, 128:256] = (total - high.astype(F32)).astype(BF16)
        return 0

    lax.fori_loop(0, 6, add, 0)
    sum_ref[96:128, :] = jnp.zeros((32, 256), BF16)

    home = zh + 2 * yl + 4 * yh + 8 * xl + 16 * xh + 32 * zl
    own = core == classes[2]
    row = pl.multiple_of((classes[0] + 2 * classes[1]) * 8, 8)
    here = out_ref.at[pl.ds(row, 8), pl.ds(pl.multiple_of(block * 128, 128), 128)]
    turns = flips((zh, yl, xl, yh, xh, zl), (1, 2, 8, 4, 16, 32))

    def deliver(high):
        pltpu.make_async_remote_copy(
            src_ref=tile_ref.at[high],
            dst_ref=here,
            send_sem=send_sems.at[2],
            recv_sem=recv_sems.at[2],
            device_id=2 * high + classes[2],
            device_id_type=LOGICAL,
        ).start()

    for quarter in range(4):
        rows = slice(256 * quarter, 256 * quarter + 256)
        wide = jnp.dot(h_ref[rows, :], sum_ref[...], preferred_element_type=F32)
        tiles = wide[0:128, 0:128] + (wide[0:128, 128:256] + wide[128:256, 0:128])
        tile_ref[16 * quarter : 16 * quarter + 16] = tiles.reshape(16, 8, 128)
        if quarter == 0:
            pl.when(jnp.logical_or(home != 0, jnp.logical_not(own)))(lambda: deliver(0))
    farthest = 63 - home
    for mask in range(62, 0, -1):
        high = home + subset(turns, mask)
        deliver(jnp.where(high == 0, farthest, high))
    pl.when(jnp.logical_or(home == 0, jnp.logical_not(own)))(lambda: deliver(jnp.where(home == 0, farthest, home)))

    @pl.when(own)
    def _():
        pltpu.make_async_copy(tile_ref.at[home], here, recv_sems.at[2]).start()

    pltpu.make_async_copy(xr_ref.at[0:15], xr_ref.at[0:15], send_sems.at[0]).wait()
    pltpu.make_async_copy(part_ref.at[0:7], part_ref.at[0:7], send_sems.at[1]).wait()

    @pl.when(own)
    def _():
        pltpu.make_async_copy(tile_ref.at[0:63], tile_ref.at[0:63], send_sems.at[2]).wait()

    @pl.when(jnp.logical_not(own))
    def _():
        pltpu.make_async_copy(tile_ref, tile_ref, send_sems.at[2]).wait()

    pltpu.make_async_copy(out_ref, out_ref, recv_sems.at[2]).wait()


def shards(traces, phase_coef):
    return pl.pallas_call(
        kernel,
        out_shape=jax.ShapeDtypeStruct((32, 2048), F32),
        in_specs=[
            pl.BlockSpec(memory_space=pl.ANY),
            pl.BlockSpec(memory_space=pl.ANY),
            pl.BlockSpec(memory_space=pl.ANY),
        ],
        out_specs=pl.BlockSpec(memory_space=pl.ANY),
        scratch_shapes=[
            pltpu.SMEM((2, 4), F32),
            pltpu.VMEM((6, 64, 128), F32),
            pltpu.VMEM((5, 36, 8, 128), F32),
            pltpu.VMEM((5, 6, 8, 128), F32),
            pltpu.VMEM((5, 8, 128), F32),
            pltpu.VMEM((3, 12, 4, 8, 128), F32),
            pltpu.VMEM((1536, 512), BF16),
            pltpu.VMEM((1024, 128), BF16),
            pltpu.VMEM((16, 32, 128), F32),
            pltpu.VMEM((512, 256), BF16),
            pltpu.VMEM((768, 256), F32),
            pltpu.VMEM((8, 96, 128), F32),
            pltpu.VMEM((8, 96, 128), F32),
            pltpu.VMEM((128, 256), BF16),
            pltpu.VMEM((64, 8, 128), F32),
            pltpu.SemaphoreType.DMA((3,)),
            pltpu.SemaphoreType.DMA((5,)),
        ],
        compiler_params=pltpu.CompilerParams(
            collective_id=0, has_side_effects=True, vmem_limit_bytes=60 * 2**20
        ),
    )(traces, phase_coef, jnp.asarray(tail_table()))


def solution(mesh):
    placed = (P(("gx", "gy"), None), P())
    return jax.shard_map(
        shards, mesh=mesh, in_specs=placed, out_specs=P(("gx", "gy"), None), check_vma=False
    )
```

```python
import functools

import jax
import jax.numpy as jnp
import numpy as np
from jax import lax
from jax.experimental import pallas as pl
from jax.experimental.pallas import tpu as pltpu
from jax.sharding import PartitionSpec as P

ORDER = 6
LOGICAL = pl.DeviceIdType.LOGICAL
F32 = jnp.float32
BF16 = jnp.bfloat16
AMP = 64.0

NODES = 0.5 * np.cos(np.pi * (2.0 * np.arange(ORDER) + 1.0) / (2.0 * ORDER))


def lagrange(points):
    points = np.asarray(points)[..., None, None]
    same = np.eye(ORDER, dtype=bool)
    spread = np.where(same, 1.0, NODES[:, None] - NODES[None, :])
    return np.where(same, 1.0, (points - NODES[None, :]) / spread).prod(-1)


CENTRE = lagrange(0.0)
HALVES = np.stack([((side - 0.5) + NODES) * 0.5 for side in (0, 1)])
TABLE = lagrange(HALVES)
WEIGHT = np.transpose(TABLE, (0, 2, 1))


def tail_table():
    out = np.zeros((ORDER, 64, 128))
    for high in range(64):
        total = np.eye(ORDER)
        for place in range(6):
            total = TABLE[(high >> place) & 1] @ total
        out[:, high, :96] = np.repeat(CENTRE[:, None] * total, 16, axis=1)
    return out.astype(np.float32)


def fit(function, terms):
    u = 0.125 + 0.125 * np.cos(np.pi * (np.arange(200) + 0.5) / 200)
    poly = np.polynomial.chebyshev.Chebyshev.fit(u, function(np.sqrt(u)), terms - 1, domain=[0, 0.25])
    return [float(c) for c in poly.convert(kind=np.polynomial.Polynomial).coef]


SIN = fit(lambda r: np.sin(np.pi * r) / r, 5)
SIN2 = [2.0 * c for c in fit(lambda r: np.sin(np.pi * r) / r, 4)]
COS = fit(lambda r: np.cos(np.pi * r), 5)
COS4 = fit(lambda r: np.cos(np.pi * r), 4)


def horner(coefs, u):
    total = coefs[-1]
    for c in coefs[-2::-1]:
        total = total * u + c
    return total


def turn(c):
    r = c - jnp.floor(c + 0.5)
    u = r * r
    twice = r * horner(SIN2, u)
    half_cos = horner(COS4, u)
    return 1.0 - (0.5 * twice) * twice, twice * half_cos


def turn_cos(c):
    r = c - jnp.floor(c + 0.5)
    twice = r * horner(SIN2, r * r)
    return 1.0 - (0.5 * twice) * twice


def half_turn(y):
    r = 0.5 - y
    u = r * r
    return r * horner(SIN, u), horner(COS, u)


def bend_value(coef, row, y):
    cosine = (0.5 - y) * horner(SIN, (0.5 - y) * (0.5 - y))
    c0, c1, c2, c3 = (coef[row, m] for m in range(4))
    return (c0 - c2) + cosine * ((c1 - 3.0 * c3) + cosine * (2.0 * c2 + cosine * (4.0 * c3)))


def bend_terms(coef, size):
    e1, e2, e3 = (coef[0, m] * float(-2.0 * AMP * np.sin(np.pi * m * size / 2.0)) for m in (1, 2, 3))
    return e1 - e3, 2.0 * e2, 4.0 * e3


def bend_step(terms, middle):
    cosine, sine = half_turn(middle)
    return sine * (terms[0] + cosine * (terms[1] + cosine * terms[2]))


def apply_real(weights, values):
    out = []
    for t in range(ORDER):
        total = weights[t][0] * values[0]
        for s in range(1, ORDER):
            total = total + weights[t][s] * values[s]
        out.append(total)
    return out


def iota(axis):
    return lax.broadcasted_iota(jnp.int32, (8, 128), axis)


def asf(value):
    return value.astype(F32)


def div(a, b):
    return lax.div(a, jnp.int32(b))


def rem(a, b):
    return lax.rem(a, jnp.int32(b))


def subset(deltas, mask):
    total = None
    for k, delta in enumerate(deltas):
        if (mask >> k) & 1:
            total = delta if total is None else total + delta
    return 0 if total is None else total


def abs_flip(bit, turned):
    return 1 - bit if turned else bit


def flips(bits, weights):
    return [weight * (1 - 2 * bit) for bit, weight in zip(bits, weights)]


def lane_parts(classes, core):
    lane = iota(1)
    place = lane >> 4
    x, y, z = (
        (2 * c + e + core) & 3 for c, e in zip(classes, (place >> 2, (place >> 1) & 1, place & 1))
    )
    return (z >> 1) + 2 * y + 8 * x + 32 * (z & 1), lane & 15


def early_levels(coef, box, top, w_ref, p_ref, v_ref):
    sub = iota(0)
    bits = [asf(sub & 1), asf((sub >> 1) & 1), asf(sub >> 2)]
    sign = [2.0 * bit - 1.0 for bit in bits]
    x0 = jnp.full((8, 128), 0.5, F32)
    x1 = x0 + sign[0] * 0.25
    x2 = x1 + sign[1] * 0.125
    word4 = asf(box * 16 + top)
    steps = [
        bend_step(bend_terms(coef, 2.0 ** -(level + 1)), x + sign[level - 1] * 2.0 ** -(level + 2))
        for level, x in ((1, x0), (2, x1), (3, x2))
    ]
    p0_mid = coef[0, 0] - coef[0, 2]

    def turned(values, angles):
        pairs = [(a * c - b * d, a * d + b * c) for (a, b), (c, d) in zip(values, angles)]
        return [a for a, _ in pairs], [b for _, b in pairs]

    def constants(side):
        return [[float(WEIGHT[side][t][s]) for s in range(ORDER)] for t in range(ORDER)]

    first = []
    for j0 in range(2):
        outs = []
        for j1 in range(2):
            j = j0 + 2 * j1
            word = word4 * 4.0 + float(j)
            start = 0.5 * (j0 + 0.5) + AMP * p0_mid * bend_value(coef, 1, (word + 0.5) * 2.0**-12)
            pairs = []
            for s in range(ORDER):
                node = float(NODES[s])
                p1 = bend_value(coef, 1, (word + (0.5 + node)) * 2.0**-12)
                c, d = turn(start + sign[0] * ((j + 0.5 + node) * 0.25 + steps[0] * p1))
                pairs.append((c * float(CENTRE[s]), d * float(CENTRE[s])))
            outs.append(pairs)
        joined = [[jnp.stack([outs[0][s][c], outs[1][s][c]]) for s in range(ORDER)] for c in range(2)]
        first.append([apply_real(constants(j0), joined[c]) for c in range(2)])
    def levels_2_3():
        linear2 = 2.0 * asf(top & 1) + 0.5
        second = []
        for j1 in range(2):
            word = word4 * 2.0 + float(j1)
            angles = []
            for s in range(ORDER):
                node = float(NODES[s])
                p1 = bend_value(coef, 1, (word + (0.5 + node)) * 2.0**-11)
                angles.append(turn(sign[1] * ((linear2 + (j1 + node)) * 0.25 + steps[1] * p1)))
            values = [[jnp.stack([first[0][c][s][j1], first[1][c][s][j1]]) for c in range(2)] for s in range(ORDER)]
            second.append([apply_real(constants(j1), part) for part in turned(values, angles)])
        linear3 = asf(top & 3) + 0.5
        angles = [turn(sign[2] * ((linear3 + float(NODES[s])) * 0.25 + steps[2] * p_ref[0, s])) for s in range(ORDER)]
        values = [[jnp.concatenate([second[0][c][s], second[1][c][s]]) for c in range(2)] for s in range(ORDER)]
        weights = [[w_ref[0, ORDER * t + s] for s in range(ORDER)] for t in range(ORDER)]
        for c, part in enumerate(turned(values, angles)):
            for t, value in enumerate(apply_real(weights, part)):
                v_ref[0, 2 * t + c] = value

    return levels_2_3


def late_setup(coef, box, top, w_ref, p_ref, c_ref):
    full = box * 16 + top

    def body(i, scale):
        word = full >> i
        pick = (word & 1) == 1
        for t in range(ORDER):
            for s in range(ORDER):
                w_ref[i, ORDER * t + s] = jnp.where(pick, float(WEIGHT[1][t][s]), float(WEIGHT[0][t][s]))
        for s in range(ORDER):
            p_ref[i, s] = bend_value(coef, 1, (asf(word) + float(0.5 + NODES[s])) * scale)
        return scale * 2.0

    lax.fori_loop(0, 5, body, jnp.float32(2.0**-10))
    turn_of = top & 7

    def by_lane(values):
        out = jnp.full((8, 128), float(values[ORDER - 1]), F32)
        for t in range(ORDER - 1):
            out = jnp.where(turn_of == t, float(values[t]), out)
        return out

    e1, e2, e3 = (coef[0, m] * by_lane(-2.0 * AMP * np.sin(np.pi * m * NODES / 128.0)) for m in (1, 2, 3))
    node = by_lane(NODES)
    c_ref[0] = node
    c_ref[1] = e1 - e3
    c_ref[2] = 2.0 * e2
    c_ref[3] = 4.0 * e3
    c_ref[4] = node * (asf(box) + 0.5)


def spread(value, t):
    return jnp.take_along_axis(value, (iota(1) & 120) + t, axis=1)


def late_levels(coef, box, top, order, w_ref, p_ref, c_ref, v_ref, g_ref, between):
    sub = iota(0)
    x3 = asf(4 * (sub & 1) + (sub & 2) + (sub >> 2)) * 0.125 + 0.0625
    full = box * 16 + top
    terms = [bend_terms(coef, 2.0 ** -(level + 1)) for level in (4, 5, 6)]

    def sign_of(bit):
        return (2 * bit - 1).astype(F32)

    def turns(i, level_terms, shift, parent, sign):
        steps = bend_step(level_terms, parent + sign * shift)
        linear = asf((full >> i) & 3) + 0.5
        return [turn(sign * ((linear + float(NODES[s])) * 0.25 + steps * p_ref[i, s])) for s in range(ORDER)]

    def level_step(level, q3, q4):
        first = level == 4
        i = level - 3
        parent = x3 + jnp.where(first, 0.0, sign_of(q3) * 2.0**-5)
        sign = jnp.where(first, sign_of(q3), sign_of(q4))
        level_terms = [jnp.where(first, a, b) for a, b in zip(terms[0], terms[1])]
        real, imag = [], []
        for s, (c, d) in enumerate(turns(i, level_terms, jnp.where(first, 2.0**-6, 2.0**-7), parent, sign)):
            a, b = v_ref[i - 1, 2 * s], v_ref[i - 1, 2 * s + 1]
            real.append(a * c - b * d)
            imag.append(a * d + b * c)
        weights = [[w_ref[i, ORDER * t + s] for s in range(ORDER)] for t in range(ORDER)]
        for c, values in enumerate((real, imag)):
            for t, value in enumerate(apply_real(weights, values)):
                v_ref[i, 2 * t + c] = value

    def last_step(parent, bit, place):
        sign = sign_of(bit)
        middle = parent + sign * 2.0**-7 + c_ref[0] * (1.0 / 128.0)
        steps = bend_step((c_ref[1], c_ref[2], c_ref[3]), middle)
        switch = [turn((c_ref[4] + c_ref[0] * float(NODES[u])) + steps * p_ref[4, u]) for u in range(ORDER)]
        merged = []
        for s, (c, d) in enumerate(turns(3, terms[2], 2.0**-8, parent, sign)):
            a = b = None
            for u in range(ORDER):
                weight = w_ref[3, ORDER * u + s]
                a = switch[u][0] * weight if a is None else a + switch[u][0] * weight
                b = switch[u][1] * weight if b is None else b + switch[u][1] * weight
            merged.append((a * c - b * d, a * d + b * c))
        parts = [v_ref[2, 2 * s] + v_ref[2, 2 * s + 1] for s in range(ORDER)]
        for t in range(ORDER):
            k1 = k2 = k3 = None
            for s in range(ORDER):
                c, d = spread(merged[s][0], t), spread(merged[s][1], t)
                m1, m2, m3 = parts[s] * c, v_ref[2, 2 * s] * (d - c), v_ref[2, 2 * s + 1] * (c + d)
                k1 = m1 if k1 is None else k1 + m1
                k2 = m2 if k2 is None else k2 + m2
                k3 = m3 if k3 is None else k3 + m3
            real, imag = k1 - k3, k1 + k2
            rows = pl.ds(pl.multiple_of(place * 192 + 16 * t, 16), 16)
            rows_low = pl.ds(pl.multiple_of(place * 192 + 96 + 16 * t, 16), 16)
            for j in range(4):
                both = jnp.concatenate([real[j], imag[j]], axis=0)
                high = both.astype(BF16)
                g_ref[rows, 128 * j : 128 * (j + 1)] = high
                g_ref[rows_low, 128 * j : 128 * (j + 1)] = (both - high.astype(F32)).astype(BF16)

    def over(n, _):
        pl.when(n == 3)(between)
        q3, q4 = order(div(n, 2)), rem(n, 2)

        def levels(level, _):
            level_step(level, q3, q4)
            return 0

        lax.fori_loop(4 + q4, 6, levels, 0)
        x5 = x3 + (sign_of(q3) * 2.0**-5 + sign_of(q4) * 2.0**-6)

        def over5(q5, _):
            last_step(x5, q5, 4 * q3 + q4 + 2 * q5)
            return 0

        return lax.fori_loop(0, 2, over5, 0)

    lax.fori_loop(0, 4, over, 0)


def last_weights(coef, group, tail_ref, h_ref):
    sub, lane = iota(0), iota(1)
    own = lane & 7
    same = sub == own
    box6 = 32 * (own & 1) + 8 * (own & 2) + 2 * (own & 4)
    box6 = box6 + (4 * rem(group, 2) + 2 * rem(div(group, 2), 2) + div(group, 4))
    inner = 32 * (sub & 1) + 8 * (sub & 2) + 2 * (sub & 4)
    base = box6 * 64 + inner
    quarter = 0.25 * asf((lane >> 3) & 1)
    p1_mid = coef[1, 0] - coef[1, 2]

    def rows_of(r):
        centre = (asf(base + (4 * rem(r, 2) + 2 * rem(div(r, 2), 2) + div(r, 4))) + 0.5) * 2.0**-12
        total = None
        for t in range(ORDER):
            node = float(NODES[t])
            steps = bend_step(bend_terms(coef, node / 4096.0), centre + node / 8192.0)
            term = turn_cos((quarter - 0.5 * node) - steps * p1_mid)
            term = term * tail_ref[t, pl.ds(pl.multiple_of(8 * r, 8), 8), :]
            total = term if total is None else total + term
        return total

    def body(r, _):
        total = rows_of(r)
        for k in range(0, 8, 2):
            both = jnp.concatenate(
                [jnp.where(same, jnp.broadcast_to(total[k + n : k + n + 1], (8, 128)), 0.0) for n in range(2)], axis=0
            )
            high = both.astype(BF16)
            rows = pl.ds(pl.multiple_of(64 * r + 8 * k, 16), 16)
            h_ref[rows, 0:128] = high
            h_ref[rows, 128:256] = (both - high.astype(F32)).astype(BF16)
            h_ref[rows, 256:384] = high
        return 0

    lax.fori_loop(0, 8, body, 0)


def kernel(
    x_ref,
    coef_hbm,
    tail_hbm,
    out_ref,
    coef_ref,
    tail_ref,
    w_ref,
    p_ref,
    c_ref,
    v_ref,
    g_ref,
    h_ref,
    xr_ref,
    xs_ref,
    wide_ref,
    part_ref,
    rr_ref,
    sum_ref,
    tile_ref,
    send_sems,
    recv_sems,
):
    fetch_coef = pltpu.make_async_copy(coef_hbm, coef_ref, recv_sems.at[3])
    fetch_tail = pltpu.make_async_copy(tail_hbm, tail_ref, recv_sems.at[4])
    fetch_coef.start()
    fetch_tail.start()
    gx, gy = lax.axis_index("gx"), lax.axis_index("gy")
    core = rem(gy, 2)
    zl, xs = div(gx, 4), rem(gx, 4)
    xh, xl = div(xs, 2), rem(xs, 2)
    yh, yl, zh = div(gy, 8), rem(div(gy, 4), 2), rem(div(gy, 2), 2)
    me = gx * 16 + gy
    highs, lows = (xh, yh, zh), (xl, yl, zl)
    unlike = [h + l - 2 * h * l for h, l in zip(highs, lows)]
    to_a = [16 * (1 - 2 * xl), 4 * (1 - 2 * yl), 64 * (1 - 2 * zl)]
    to_b = [16 * (3 - 2 * xs), 4 * (3 - 2 * (2 * yh + yl)), 2 * (1 - 2 * zh) + 64 * (1 - 2 * zl)]
    to_class = [a + core * (b - a) for a, b in zip(to_a, to_b)]
    to_group = [b + core * (a - b) for a, b in zip(to_a, to_b)]
    to_core = 1 - 2 * core
    class_a, class_b = highs, [1 - d for d in unlike]
    place_a, place_b = lows, [1 - l for l in lows]
    group_a, group_b = [1 - d for d in unlike], [1 - h for h in highs]

    def mine(for_a, for_b):
        return [a + core * (b - a) for a, b in zip(for_a, for_b)]

    def others(for_a, for_b):
        return [b + core * (a - b) for a, b in zip(for_a, for_b)]

    def number(values):
        return values[0] + 2 * values[1] + 4 * values[2]

    classes, groups = mine(class_a, class_b), mine(group_a, group_b)
    target = number(classes)
    block = number(groups) + 8 * core

    barrier = pltpu.get_barrier_semaphore()
    for mask in range(1, 16):
        source = me + subset(to_class + [to_core], mask)
        pl.semaphore_signal(barrier, inc=1, device_id=source, device_id_type=LOGICAL)
    for mask in range(1, 8):
        pl.semaphore_signal(barrier, inc=1, device_id=me + subset(to_group, mask), device_id_type=LOGICAL)
    box, top = lane_parts(classes, core)
    fetch_coef.wait()
    late_setup(coef_ref, box, top, w_ref, p_ref, c_ref)
    pl.semaphore_wait(barrier, 22)

    def columns(m):
        return x_ref.at[:, pl.ds(pl.multiple_of(m * 128, 128), 128)]

    own_slot = 2 * number(mine(place_a, place_b)[::-1]) + core
    other_slot = 2 * number(others(place_a, place_b)[::-1]) + core
    other_groups = others(group_a, group_b)
    other_block = number(other_groups) + 8 * (1 - core)
    for mask in range(7, -1, -1):
        routes = [(other_block, other_groups, other_slot, me + to_core + subset(to_group, mask))]
        if mask:
            routes.append((block, groups, own_slot, me + subset(to_class, mask)))
        for first, group_bits, slot, device in routes:
            pltpu.make_async_remote_copy(
                src_ref=columns(first + subset(flips(group_bits, (1, 2, 4)), mask)),
                dst_ref=xr_ref.at[slot],
                send_sem=send_sems.at[0],
                recv_sem=recv_sems.at[0],
                device_id=device,
                device_id_type=LOGICAL,
            ).start()
    pltpu.make_async_copy(columns(block), xr_ref.at[own_slot], recv_sems.at[0]).start()
    early_levels(coef_ref, box, top, w_ref, p_ref, v_ref)()

    def order(h):
        return classes[0] + (1 - h) * (1 - 2 * classes[0])

    def split(i, _):
        for j in range(4):
            piece = jnp.concatenate([xr_ref[2 * i + s, pl.ds(j, 8, stride=4), :] for s in range(2)], axis=0)
            high = piece.astype(BF16)
            rows = pl.ds(pl.multiple_of(128 * j + 16 * i, 16), 16)
            xs_ref[rows, 0:128] = high
            xs_ref[rows, 128:256] = (piece - high.astype(F32)).astype(BF16)
        return 0

    def half(h):
        q3 = order(h)
        rows = pl.ds(pl.multiple_of(q3 * 768, 16), 768)
        wide_ref[...] = jnp.dot(g_ref[rows, :], xs_ref[...], preferred_element_type=F32)

        far = to_group[0] if h == 0 else 0
        for mask in range(3, -1, -1):
            i = classes[1] + 2 * classes[2] + subset(flips(classes[1:], (1, 2)), mask)
            high = pl.ds(pl.multiple_of(i * 192, 8), 96)
            low = pl.ds(pl.multiple_of(i * 192 + 96, 8), 96)
            part = wide_ref[high, 0:128] + (wide_ref[high, 128:256] + wide_ref[low, 0:128])

            def send():
                part_ref[4 * q3 + i] = part
                pltpu.make_async_remote_copy(
                    src_ref=part_ref.at[4 * q3 + i],
                    dst_ref=rr_ref.at[target],
                    send_sem=send_sems.at[1],
                    recv_sem=recv_sems.at[1],
                    device_id=me + far + subset(to_group[1:], mask),
                    device_id_type=LOGICAL,
                ).start()

            if mask or h == 0:
                send()
            else:
                rr_ref[target] = part

    def first_half():
        pltpu.make_async_copy(xr_ref, xr_ref, recv_sems.at[0]).wait()
        lax.fori_loop(0, 8, split, 0)
        half(0)

    late_levels(coef_ref, box, top, order, w_ref, p_ref, c_ref, v_ref, g_ref, first_half)
    half(1)
    fetch_tail.wait()
    for i in range(3):
        sum_ref[128 * i + 96 : 128 * i + 128, :] = jnp.zeros((32, 128), BF16)
    last_weights(coef_ref, target, tail_ref, h_ref)
    pltpu.make_async_copy(rr_ref.at[0:7], rr_ref.at[0:7], recv_sems.at[1]).wait()

    def add(i, _):
        rows = pl.ds(pl.multiple_of(16 * i, 16), 16)
        total = rr_ref[0, rows, :]
        for k in range(1, 8):
            total = total + rr_ref[k, rows, :]
        high = total.astype(BF16)
        sum_ref[rows, :] = high
        sum_ref[pl.ds(pl.multiple_of(128 + 16 * i, 16), 16), :] = high
        sum_ref[pl.ds(pl.multiple_of(256 + 16 * i, 16), 16), :] = (total - high.astype(F32)).astype(BF16)
        return 0

    lax.fori_loop(0, 6, add, 0)

    home = zh + 2 * yl + 4 * yh + 8 * xl + 16 * xh + 32 * zl
    own = core == classes[2]
    row = pl.multiple_of((classes[0] + 2 * classes[1]) * 8, 8)
    here = out_ref.at[pl.ds(row, 8), pl.ds(pl.multiple_of(block * 128, 128), 128)]
    turns = flips((zh, yl, xl, yh, xh, zl), (1, 2, 8, 4, 16, 32))

    def deliver(high):
        pltpu.make_async_remote_copy(
            src_ref=tile_ref.at[high],
            dst_ref=here,
            send_sem=send_sems.at[2],
            recv_sem=recv_sems.at[2],
            device_id=2 * high + classes[2],
            device_id_type=LOGICAL,
        ).start()

    early = (0, 8)
    lost = (63 - home, home + subset(turns, 62))
    instead = [jnp.where(lost[n] == early[1 - n], lost[1 - n], lost[n]) for n in range(2)]

    def settle(high):
        return jnp.where(high == early[0], instead[0], jnp.where(high == early[1], instead[1], high))

    for quarter in range(4):
        rows = slice(128 * quarter, 128 * quarter + 128)
        tiles = jnp.dot(h_ref[rows, :], sum_ref[...], preferred_element_type=F32)
        tile_ref[16 * quarter : 16 * quarter + 16] = tiles.reshape(16, 8, 128)
        if quarter == 0:
            for high in early:
                pl.when(jnp.logical_or(home != high, jnp.logical_not(own)))(functools.partial(deliver, high))
    for mask in range(61, 0, -1):
        deliver(settle(home + subset(turns, mask)))
    moved = jnp.logical_or(home == early[0], home == early[1])
    pl.when(jnp.logical_or(moved, jnp.logical_not(own)))(lambda: deliver(settle(home)))

    @pl.when(own)
    def _():
        pltpu.make_async_copy(tile_ref.at[home], here, recv_sems.at[2]).start()

    pltpu.make_async_copy(xr_ref.at[0:15], xr_ref.at[0:15], send_sems.at[0]).wait()
    pltpu.make_async_copy(part_ref.at[0:7], part_ref.at[0:7], send_sems.at[1]).wait()

    @pl.when(own)
    def _():
        pltpu.make_async_copy(tile_ref.at[0:63], tile_ref.at[0:63], send_sems.at[2]).wait()

    @pl.when(jnp.logical_not(own))
    def _():
        pltpu.make_async_copy(tile_ref, tile_ref, send_sems.at[2]).wait()

    pltpu.make_async_copy(out_ref, out_ref, recv_sems.at[2]).wait()


def shards(traces, phase_coef):
    return pl.pallas_call(
        kernel,
        out_shape=jax.ShapeDtypeStruct((32, 2048), F32),
        in_specs=[
            pl.BlockSpec(memory_space=pl.ANY),
            pl.BlockSpec(memory_space=pl.ANY),
            pl.BlockSpec(memory_space=pl.ANY),
        ],
        out_specs=pl.BlockSpec(memory_space=pl.ANY),
        scratch_shapes=[
            pltpu.SMEM((2, 4), F32),
            pltpu.VMEM((6, 64, 128), F32),
            pltpu.VMEM((5, 36, 8, 128), F32),
            pltpu.VMEM((5, 6, 8, 128), F32),
            pltpu.VMEM((5, 8, 128), F32),
            pltpu.VMEM((3, 12, 4, 8, 128), F32),
            pltpu.VMEM((1536, 512), BF16),
            pltpu.VMEM((512, 384), BF16),
            pltpu.VMEM((16, 32, 128), F32),
            pltpu.VMEM((512, 256), BF16),
            pltpu.VMEM((768, 256), F32),
            pltpu.VMEM((8, 96, 128), F32),
            pltpu.VMEM((8, 96, 128), F32),
            pltpu.VMEM((384, 128), BF16),
            pltpu.VMEM((64, 8, 128), F32),
            pltpu.SemaphoreType.DMA((3,)),
            pltpu.SemaphoreType.DMA((5,)),
        ],
        compiler_params=pltpu.CompilerParams(
            collective_id=0, has_side_effects=True, vmem_limit_bytes=60 * 2**20
        ),
    )(traces, phase_coef, jnp.asarray(tail_table()))


def solution(mesh):
    placed = (P(("gx", "gy"), None), P())
    return jax.shard_map(
        shards, mesh=mesh, in_specs=placed, out_specs=P(("gx", "gy"), None), check_vma=False
    )
```

```python
import functools

import jax
import jax.numpy as jnp
import numpy as np
from jax import lax
from jax.experimental import pallas as pl
from jax.experimental.pallas import tpu as pltpu
from jax.sharding import PartitionSpec as P

ORDER = 6
LOGICAL = pl.DeviceIdType.LOGICAL
F32 = jnp.float32
BF16 = jnp.bfloat16
AMP = 64.0

NODES = 0.5 * np.cos(np.pi * (2.0 * np.arange(ORDER) + 1.0) / (2.0 * ORDER))


def lagrange(points):
    points = np.asarray(points)[..., None, None]
    same = np.eye(ORDER, dtype=bool)
    spread = np.where(same, 1.0, NODES[:, None] - NODES[None, :])
    return np.where(same, 1.0, (points - NODES[None, :]) / spread).prod(-1)


CENTRE = lagrange(0.0)
HALVES = np.stack([((side - 0.5) + NODES) * 0.5 for side in (0, 1)])
TABLE = lagrange(HALVES)
WEIGHT = np.transpose(TABLE, (0, 2, 1))


def tail_table():
    out = np.zeros((ORDER, 64, 128))
    for high in range(64):
        total = np.eye(ORDER)
        for place in range(6):
            total = TABLE[(high >> place) & 1] @ total
        out[:, high, :96] = np.repeat(CENTRE[:, None] * total, 16, axis=1)
    return out.astype(np.float32)


def fit(function, terms):
    u = 0.125 + 0.125 * np.cos(np.pi * (np.arange(200) + 0.5) / 200)
    poly = np.polynomial.chebyshev.Chebyshev.fit(u, function(np.sqrt(u)), terms - 1, domain=[0, 0.25])
    return [float(c) for c in poly.convert(kind=np.polynomial.Polynomial).coef]


SIN = fit(lambda r: np.sin(np.pi * r) / r, 5)
SIN2 = [2.0 * c for c in fit(lambda r: np.sin(np.pi * r) / r, 4)]
COS = fit(lambda r: np.cos(np.pi * r), 5)
COS4 = fit(lambda r: np.cos(np.pi * r), 4)


def horner(coefs, u):
    total = coefs[-1]
    for c in coefs[-2::-1]:
        total = total * u + c
    return total


def turn(c):
    r = c - jnp.floor(c + 0.5)
    u = r * r
    twice = r * horner(SIN2, u)
    half_cos = horner(COS4, u)
    return 1.0 - (0.5 * twice) * twice, twice * half_cos


def turn_cos(c):
    r = c - jnp.floor(c + 0.5)
    twice = r * horner(SIN2, r * r)
    return 1.0 - (0.5 * twice) * twice


def half_turn(y):
    r = 0.5 - y
    u = r * r
    return r * horner(SIN, u), horner(COS, u)


def bend_value(coef, row, y):
    cosine = (0.5 - y) * horner(SIN, (0.5 - y) * (0.5 - y))
    c0, c1, c2, c3 = (coef[row, m] for m in range(4))
    return (c0 - c2) + cosine * ((c1 - 3.0 * c3) + cosine * (2.0 * c2 + cosine * (4.0 * c3)))


def bend_terms(coef, size):
    e1, e2, e3 = (coef[0, m] * float(-2.0 * AMP * np.sin(np.pi * m * size / 2.0)) for m in (1, 2, 3))
    return e1 - e3, 2.0 * e2, 4.0 * e3


def bend_step(terms, middle):
    cosine, sine = half_turn(middle)
    return sine * (terms[0] + cosine * (terms[1] + cosine * terms[2]))


def apply_real(weights, values):
    out = []
    for t in range(ORDER):
        total = weights[t][0] * values[0]
        for s in range(1, ORDER):
            total = total + weights[t][s] * values[s]
        out.append(total)
    return out


def iota(axis):
    return lax.broadcasted_iota(jnp.int32, (8, 128), axis)


def asf(value):
    return value.astype(F32)


def div(a, b):
    return lax.div(a, jnp.int32(b))


def rem(a, b):
    return lax.rem(a, jnp.int32(b))


def subset(deltas, mask):
    total = None
    for k, delta in enumerate(deltas):
        if (mask >> k) & 1:
            total = delta if total is None else total + delta
    return 0 if total is None else total


def abs_flip(bit, turned):
    return 1 - bit if turned else bit


def flips(bits, weights):
    return [weight * (1 - 2 * bit) for bit, weight in zip(bits, weights)]


def lane_parts(classes, core):
    lane = iota(1)
    place = lane >> 4
    x, y, z = (
        (2 * c + e + core) & 3 for c, e in zip(classes, (place >> 2, (place >> 1) & 1, place & 1))
    )
    return (z >> 1) + 2 * y + 8 * x + 32 * (z & 1), lane & 15


def early_levels(coef, box, top, w_ref, p_ref, v_ref):
    sub = iota(0)
    bits = [asf(sub & 1), asf((sub >> 1) & 1), asf(sub >> 2)]
    sign = [2.0 * bit - 1.0 for bit in bits]
    x0 = jnp.full((8, 128), 0.5, F32)
    x1 = x0 + sign[0] * 0.25
    x2 = x1 + sign[1] * 0.125
    word4 = asf(box * 16 + top)
    steps = [
        bend_step(bend_terms(coef, 2.0 ** -(level + 1)), x + sign[level - 1] * 2.0 ** -(level + 2))
        for level, x in ((1, x0), (2, x1), (3, x2))
    ]
    p0_mid = coef[0, 0] - coef[0, 2]

    def turned(values, angles):
        pairs = [(a * c - b * d, a * d + b * c) for (a, b), (c, d) in zip(values, angles)]
        return [a for a, _ in pairs], [b for _, b in pairs]

    linear2 = 2.0 * asf(top & 1) + 0.5
    linear3 = asf(top & 3) + 0.5
    third = [turn(sign[2] * ((linear3 + float(NODES[s])) * 0.25 + steps[2] * p_ref[0, s])) for s in range(ORDER)]
    constants = [[float(WEIGHT[0][t][s]) for s in range(ORDER)] for t in range(ORDER)]

    def by_side(side, values):
        mirror = jnp.broadcast_to(side, (8, 128)) == 1
        picked = [jnp.where(mirror, values[5 - s], values[s]) for s in range(ORDER)]
        out = apply_real(constants, picked)
        return [jnp.where(mirror, out[5 - t], out[t]) for t in range(ORDER)]

    def body(group, _):
        j0, j1 = rem(group, 2), div(group, 2)
        j0f, j1f, groupf = asf(j0), asf(j1), asf(group)
        word = word4 * 4.0 + groupf
        start = 0.5 * (j0f + 0.5) + AMP * p0_mid * bend_value(coef, 1, (word + 0.5) * 2.0**-12)
        real, imag = [], []
        for s in range(ORDER):
            node = float(NODES[s])
            p1 = bend_value(coef, 1, (word + (0.5 + node)) * 2.0**-12)
            c, d = turn(start + sign[0] * ((groupf + (0.5 + node)) * 0.25 + steps[0] * p1))
            real.append(c * float(CENTRE[s]))
            imag.append(d * float(CENTRE[s]))
        values = list(zip(by_side(j0, real), by_side(j0, imag)))
        word = word4 * 2.0 + j1f
        angles = []
        for s in range(ORDER):
            node = float(NODES[s])
            p1 = bend_value(coef, 1, (word + (0.5 + node)) * 2.0**-11)
            angles.append(turn(sign[1] * (((linear2 + j1f) + node) * 0.25 + steps[1] * p1)))
        values = list(zip(*(by_side(j1, part) for part in turned(values, angles))))
        weights = [[w_ref[0, ORDER * t + s] for s in range(ORDER)] for t in range(ORDER)]
        for c, part in enumerate(turned(values, third)):
            for t, value in enumerate(apply_real(weights, part)):
                v_ref[0, 2 * t + c, group] = value
        return 0

    lax.fori_loop(0, 4, body, 0)


def late_setup(coef, box, top, w_ref, p_ref, c_ref):
    full = box * 16 + top

    def body(i, scale):
        word = full >> i
        pick = (word & 1) == 1
        for t in range(ORDER):
            for s in range(ORDER):
                w_ref[i, ORDER * t + s] = jnp.where(pick, float(WEIGHT[1][t][s]), float(WEIGHT[0][t][s]))
        for s in range(ORDER):
            p_ref[i, s] = bend_value(coef, 1, (asf(word) + float(0.5 + NODES[s])) * scale)
        return scale * 2.0

    lax.fori_loop(0, 5, body, jnp.float32(2.0**-10))
    turn_of = top & 7

    def by_lane(values):
        out = jnp.full((8, 128), float(values[ORDER - 1]), F32)
        for t in range(ORDER - 1):
            out = jnp.where(turn_of == t, float(values[t]), out)
        return out

    e1, e2, e3 = (coef[0, m] * by_lane(-2.0 * AMP * np.sin(np.pi * m * NODES / 128.0)) for m in (1, 2, 3))
    node = by_lane(NODES)
    c_ref[0] = node
    c_ref[1] = e1 - e3
    c_ref[2] = 2.0 * e2
    c_ref[3] = 4.0 * e3
    c_ref[4] = node * (asf(box) + 0.5)


def spread(value, t):
    return jnp.take_along_axis(value, (iota(1) & 120) + t, axis=1)


def late_levels(coef, box, top, order, w_ref, p_ref, c_ref, v_ref, g_ref, between):
    sub = iota(0)
    x3 = asf(4 * (sub & 1) + (sub & 2) + (sub >> 2)) * 0.125 + 0.0625
    full = box * 16 + top
    terms = [bend_terms(coef, 2.0 ** -(level + 1)) for level in (4, 5, 6)]

    def sign_of(bit):
        return (2 * bit - 1).astype(F32)

    def turns(i, level_terms, shift, parent, sign):
        steps = bend_step(level_terms, parent + sign * shift)
        linear = asf((full >> i) & 3) + 0.5
        return [turn(sign * ((linear + float(NODES[s])) * 0.25 + steps * p_ref[i, s])) for s in range(ORDER)]

    def level_step(level, q3, q4):
        first = level == 4
        i = level - 3
        parent = x3 + jnp.where(first, 0.0, sign_of(q3) * 2.0**-5)
        sign = jnp.where(first, sign_of(q3), sign_of(q4))
        level_terms = [jnp.where(first, a, b) for a, b in zip(terms[0], terms[1])]
        real, imag = [], []
        for s, (c, d) in enumerate(turns(i, level_terms, jnp.where(first, 2.0**-6, 2.0**-7), parent, sign)):
            a, b = v_ref[i - 1, 2 * s], v_ref[i - 1, 2 * s + 1]
            real.append(a * c - b * d)
            imag.append(a * d + b * c)
        weights = [[w_ref[i, ORDER * t + s] for s in range(ORDER)] for t in range(ORDER)]
        for c, values in enumerate((real, imag)):
            for t, value in enumerate(apply_real(weights, values)):
                v_ref[i, 2 * t + c] = value

    def last_step(parent, bit, place):
        sign = sign_of(bit)
        middle = parent + sign * 2.0**-7 + c_ref[0] * (1.0 / 128.0)
        steps = bend_step((c_ref[1], c_ref[2], c_ref[3]), middle)
        switch = [turn((c_ref[4] + c_ref[0] * float(NODES[u])) + steps * p_ref[4, u]) for u in range(ORDER)]
        merged = []
        for s, (c, d) in enumerate(turns(3, terms[2], 2.0**-8, parent, sign)):
            a = b = None
            for u in range(ORDER):
                weight = w_ref[3, ORDER * u + s]
                a = switch[u][0] * weight if a is None else a + switch[u][0] * weight
                b = switch[u][1] * weight if b is None else b + switch[u][1] * weight
            merged.append((a * c - b * d, a * d + b * c))
        parts = [v_ref[2, 2 * s] + v_ref[2, 2 * s + 1] for s in range(ORDER)]
        for t in range(ORDER):
            k1 = k2 = k3 = None
            for s in range(ORDER):
                c, d = spread(merged[s][0], t), spread(merged[s][1], t)
                m1, m2, m3 = parts[s] * c, v_ref[2, 2 * s] * (d - c), v_ref[2, 2 * s + 1] * (c + d)
                k1 = m1 if k1 is None else k1 + m1
                k2 = m2 if k2 is None else k2 + m2
                k3 = m3 if k3 is None else k3 + m3
            real, imag = k1 - k3, k1 + k2
            rows = pl.ds(pl.multiple_of(place * 192 + 16 * t, 16), 16)
            rows_low = pl.ds(pl.multiple_of(place * 192 + 96 + 16 * t, 16), 16)
            for j in range(4):
                both = jnp.concatenate([real[j], imag[j]], axis=0)
                high = both.astype(BF16)
                g_ref[rows, 128 * j : 128 * (j + 1)] = high
                g_ref[rows_low, 128 * j : 128 * (j + 1)] = (both - high.astype(F32)).astype(BF16)

    def over(n, _):
        @pl.when(n >= 3)
        def _():
            between(n - 3)

        @pl.when(n < 4)
        def _():
            q3, q4 = order(div(n, 2)), rem(n, 2)

            def levels(level, _):
                level_step(level, q3, q4)
                return 0

            lax.fori_loop(4 + q4, 6, levels, 0)
            x5 = x3 + (sign_of(q3) * 2.0**-5 + sign_of(q4) * 2.0**-6)

            def over5(q5, _):
                last_step(x5, q5, 4 * q3 + q4 + 2 * q5)
                return 0

            lax.fori_loop(0, 2, over5, 0)

        return 0

    lax.fori_loop(0, 5, over, 0)


def last_weights(coef, group, tail_ref, h_ref):
    sub, lane = iota(0), iota(1)
    own = lane & 7
    same = sub == own
    box6 = 32 * (own & 1) + 8 * (own & 2) + 2 * (own & 4)
    box6 = box6 + (4 * rem(group, 2) + 2 * rem(div(group, 2), 2) + div(group, 4))
    inner = 32 * (sub & 1) + 8 * (sub & 2) + 2 * (sub & 4)
    base = box6 * 64 + inner
    quarter = 0.25 * asf((lane >> 3) & 1)
    p1_mid = coef[1, 0] - coef[1, 2]

    def rows_of(r):
        centre = (asf(base + (4 * rem(r, 2) + 2 * rem(div(r, 2), 2) + div(r, 4))) + 0.5) * 2.0**-12
        total = None
        for t in range(ORDER):
            node = float(NODES[t])
            steps = bend_step(bend_terms(coef, node / 4096.0), centre + node / 8192.0)
            term = turn_cos((quarter - 0.5 * node) - steps * p1_mid)
            term = term * tail_ref[t, pl.ds(pl.multiple_of(8 * r, 8), 8), :]
            total = term if total is None else total + term
        return total

    def body(r, _):
        total = rows_of(r)
        for k in range(0, 8, 2):
            both = jnp.concatenate(
                [jnp.where(same, jnp.broadcast_to(total[k + n : k + n + 1], (8, 128)), 0.0) for n in range(2)], axis=0
            )
            high = both.astype(BF16)
            rows = pl.ds(pl.multiple_of(64 * r + 8 * k, 16), 16)
            h_ref[rows, 0:128] = high
            h_ref[rows, 128:256] = (both - high.astype(F32)).astype(BF16)
            h_ref[rows, 256:384] = high
        return 0

    lax.fori_loop(0, 8, body, 0)


def kernel(
    x_ref,
    coef_hbm,
    tail_hbm,
    out_ref,
    coef_ref,
    tail_ref,
    w_ref,
    p_ref,
    c_ref,
    v_ref,
    g_ref,
    h_ref,
    xr_ref,
    xs_ref,
    wide_ref,
    part_ref,
    rr_ref,
    sum_ref,
    tile_ref,
    send_sems,
    recv_sems,
):
    fetch_coef = pltpu.make_async_copy(coef_hbm, coef_ref, recv_sems.at[3])
    fetch_tail = pltpu.make_async_copy(tail_hbm, tail_ref, recv_sems.at[4])
    fetch_coef.start()
    fetch_tail.start()
    gx, gy = lax.axis_index("gx"), lax.axis_index("gy")
    core = rem(gy, 2)
    zl, xs = div(gx, 4), rem(gx, 4)
    xh, xl = div(xs, 2), rem(xs, 2)
    yh, yl, zh = div(gy, 8), rem(div(gy, 4), 2), rem(div(gy, 2), 2)
    me = gx * 16 + gy
    highs, lows = (xh, yh, zh), (xl, yl, zl)
    unlike = [h + l - 2 * h * l for h, l in zip(highs, lows)]
    to_a = [16 * (1 - 2 * xl), 4 * (1 - 2 * yl), 64 * (1 - 2 * zl)]
    to_b = [16 * (3 - 2 * xs), 4 * (3 - 2 * (2 * yh + yl)), 2 * (1 - 2 * zh) + 64 * (1 - 2 * zl)]
    to_class = [a + core * (b - a) for a, b in zip(to_a, to_b)]
    to_group = [b + core * (a - b) for a, b in zip(to_a, to_b)]
    to_core = 1 - 2 * core
    class_a, class_b = highs, [1 - d for d in unlike]
    place_a, place_b = lows, [1 - l for l in lows]
    group_a, group_b = [1 - d for d in unlike], [1 - h for h in highs]

    def mine(for_a, for_b):
        return [a + core * (b - a) for a, b in zip(for_a, for_b)]

    def others(for_a, for_b):
        return [b + core * (a - b) for a, b in zip(for_a, for_b)]

    def number(values):
        return values[0] + 2 * values[1] + 4 * values[2]

    classes, groups = mine(class_a, class_b), mine(group_a, group_b)
    target = number(classes)
    block = number(groups) + 8 * core

    barrier = pltpu.get_barrier_semaphore()
    for mask in range(1, 16):
        source = me + subset(to_class + [to_core], mask)
        pl.semaphore_signal(barrier, inc=1, device_id=source, device_id_type=LOGICAL)
    for mask in range(1, 8):
        pl.semaphore_signal(barrier, inc=1, device_id=me + subset(to_group, mask), device_id_type=LOGICAL)
    box, top = lane_parts(classes, core)
    fetch_coef.wait()
    late_setup(coef_ref, box, top, w_ref, p_ref, c_ref)
    pl.semaphore_wait(barrier, 22)

    def columns(m):
        return x_ref.at[:, pl.ds(pl.multiple_of(m * 128, 128), 128)]

    own_slot = 2 * number(mine(place_a, place_b)[::-1]) + core
    other_slot = 2 * number(others(place_a, place_b)[::-1]) + core
    other_groups = others(group_a, group_b)
    other_block = number(other_groups) + 8 * (1 - core)
    for mask in range(7, -1, -1):
        routes = [(other_block, other_groups, other_slot, me + to_core + subset(to_group, mask))]
        if mask:
            routes.append((block, groups, own_slot, me + subset(to_class, mask)))
        for first, group_bits, slot, device in routes:
            pltpu.make_async_remote_copy(
                src_ref=columns(first + subset(flips(group_bits, (1, 2, 4)), mask)),
                dst_ref=xr_ref.at[slot],
                send_sem=send_sems.at[0],
                recv_sem=recv_sems.at[0],
                device_id=device,
                device_id_type=LOGICAL,
            ).start()
    pltpu.make_async_copy(columns(block), xr_ref.at[own_slot], recv_sems.at[0]).start()
    early_levels(coef_ref, box, top, w_ref, p_ref, v_ref)

    def order(h):
        return classes[0] + (1 - h) * (1 - 2 * classes[0])

    def split(i, _):
        for j in range(4):
            piece = jnp.concatenate([xr_ref[2 * i + s, pl.ds(j, 8, stride=4), :] for s in range(2)], axis=0)
            high = piece.astype(BF16)
            rows = pl.ds(pl.multiple_of(128 * j + 16 * i, 16), 16)
            xs_ref[rows, 0:128] = high
            xs_ref[rows, 128:256] = (piece - high.astype(F32)).astype(BF16)
        return 0

    def half(h):
        @pl.when(h == 0)
        def _():
            pltpu.make_async_copy(xr_ref, xr_ref, recv_sems.at[0]).wait()
            lax.fori_loop(0, 8, split, 0)

        q3 = order(h)
        rows = pl.ds(pl.multiple_of(q3 * 768, 16), 768)
        wide_ref[...] = jnp.dot(g_ref[rows, :], xs_ref[...], preferred_element_type=F32)

        far = (1 - h) * to_group[0]
        for mask in range(3, -1, -1):
            i = classes[1] + 2 * classes[2] + subset(flips(classes[1:], (1, 2)), mask)
            high = pl.ds(pl.multiple_of(i * 192, 8), 96)
            low = pl.ds(pl.multiple_of(i * 192 + 96, 8), 96)
            part = wide_ref[high, 0:128] + (wide_ref[high, 128:256] + wide_ref[low, 0:128])

            def send():
                part_ref[4 * q3 + i] = part
                pltpu.make_async_remote_copy(
                    src_ref=part_ref.at[4 * q3 + i],
                    dst_ref=rr_ref.at[target],
                    send_sem=send_sems.at[1],
                    recv_sem=recv_sems.at[1],
                    device_id=me + far + subset(to_group[1:], mask),
                    device_id_type=LOGICAL,
                ).start()

            if mask:
                send()
            else:
                pl.when(h == 0)(send)

                @pl.when(h == 1)
                def _():
                    rr_ref[target] = part

    late_levels(coef_ref, box, top, order, w_ref, p_ref, c_ref, v_ref, g_ref, half)
    fetch_tail.wait()
    for i in range(3):
        sum_ref[128 * i + 96 : 128 * i + 128, :] = jnp.zeros((32, 128), BF16)
    last_weights(coef_ref, target, tail_ref, h_ref)
    pltpu.make_async_copy(rr_ref.at[0:7], rr_ref.at[0:7], recv_sems.at[1]).wait()

    def add(i, _):
        rows = pl.ds(pl.multiple_of(16 * i, 16), 16)
        total = rr_ref[0, rows, :]
        for k in range(1, 8):
            total = total + rr_ref[k, rows, :]
        high = total.astype(BF16)
        sum_ref[rows, :] = high
        sum_ref[pl.ds(pl.multiple_of(128 + 16 * i, 16), 16), :] = high
        sum_ref[pl.ds(pl.multiple_of(256 + 16 * i, 16), 16), :] = (total - high.astype(F32)).astype(BF16)
        return 0

    lax.fori_loop(0, 6, add, 0)

    home = zh + 2 * yl + 4 * yh + 8 * xl + 16 * xh + 32 * zl
    own = core == classes[2]
    row = pl.multiple_of((classes[0] + 2 * classes[1]) * 8, 8)
    here = out_ref.at[pl.ds(row, 8), pl.ds(pl.multiple_of(block * 128, 128), 128)]
    turns = flips((zh, yl, xl, yh, xh, zl), (1, 2, 8, 4, 16, 32))

    def deliver(high):
        pltpu.make_async_remote_copy(
            src_ref=tile_ref.at[high],
            dst_ref=here,
            send_sem=send_sems.at[2],
            recv_sem=recv_sems.at[2],
            device_id=2 * high + classes[2],
            device_id_type=LOGICAL,
        ).start()

    early = (0, 8)
    lost = (63 - home, home + subset(turns, 62))
    instead = [jnp.where(lost[n] == early[1 - n], lost[1 - n], lost[n]) for n in range(2)]

    def settle(high):
        return jnp.where(high == early[0], instead[0], jnp.where(high == early[1], instead[1], high))

    def make(quarter, _):
        rows = pl.ds(pl.multiple_of(128 * quarter, 16), 128)
        tiles = jnp.dot(h_ref[rows, :], sum_ref[...], preferred_element_type=F32)
        tile_ref[pl.ds(16 * quarter, 16)] = tiles.reshape(16, 8, 128)

        @pl.when(quarter == 0)
        def _():
            for high in early:
                pl.when(jnp.logical_or(home != high, jnp.logical_not(own)))(functools.partial(deliver, high))

        return 0

    lax.fori_loop(0, 4, make, 0)
    moved = jnp.logical_or(home == early[0], home == early[1])
    last = jnp.logical_or(moved, jnp.logical_not(own))

    def deliver_some(step, _):
        same_x, same_z = rem(step, 2), div(step, 2)
        first = home + (1 - same_x) * turns[4] + (1 - same_z) * turns[5]

        def send(mask):
            deliver(settle(first + subset(turns, mask)))

        @pl.when(step > 0)
        def _():
            send(15)
            send(14)

        for mask in range(13, 0, -1):
            send(mask)

        pl.when(jnp.logical_or(step < 3, last))(lambda: send(0))
        return 0

    lax.fori_loop(0, 4, deliver_some, 0)

    @pl.when(own)
    def _():
        pltpu.make_async_copy(tile_ref.at[home], here, recv_sems.at[2]).start()

    pltpu.make_async_copy(xr_ref.at[0:15], xr_ref.at[0:15], send_sems.at[0]).wait()
    pltpu.make_async_copy(part_ref.at[0:7], part_ref.at[0:7], send_sems.at[1]).wait()

    @pl.when(own)
    def _():
        pltpu.make_async_copy(tile_ref.at[0:63], tile_ref.at[0:63], send_sems.at[2]).wait()

    @pl.when(jnp.logical_not(own))
    def _():
        pltpu.make_async_copy(tile_ref, tile_ref, send_sems.at[2]).wait()

    pltpu.make_async_copy(out_ref, out_ref, recv_sems.at[2]).wait()


def shards(traces, phase_coef):
    return pl.pallas_call(
        kernel,
        out_shape=jax.ShapeDtypeStruct((32, 2048), F32),
        in_specs=[
            pl.BlockSpec(memory_space=pl.ANY),
            pl.BlockSpec(memory_space=pl.ANY),
            pl.BlockSpec(memory_space=pl.ANY),
        ],
        out_specs=pl.BlockSpec(memory_space=pl.ANY),
        scratch_shapes=[
            pltpu.SMEM((2, 4), F32),
            pltpu.VMEM((6, 64, 128), F32),
            pltpu.VMEM((5, 36, 8, 128), F32),
            pltpu.VMEM((5, 6, 8, 128), F32),
            pltpu.VMEM((5, 8, 128), F32),
            pltpu.VMEM((3, 12, 4, 8, 128), F32),
            pltpu.VMEM((1536, 512), BF16),
            pltpu.VMEM((512, 384), BF16),
            pltpu.VMEM((16, 32, 128), F32),
            pltpu.VMEM((512, 256), BF16),
            pltpu.VMEM((768, 256), F32),
            pltpu.VMEM((8, 96, 128), F32),
            pltpu.VMEM((8, 96, 128), F32),
            pltpu.VMEM((384, 128), BF16),
            pltpu.VMEM((64, 8, 128), F32),
            pltpu.SemaphoreType.DMA((3,)),
            pltpu.SemaphoreType.DMA((5,)),
        ],
        compiler_params=pltpu.CompilerParams(
            collective_id=0, has_side_effects=True, vmem_limit_bytes=60 * 2**20
        ),
    )(traces, phase_coef, jnp.asarray(tail_table()))


def solution(mesh):
    placed = (P(("gx", "gy"), None), P())
    return jax.shard_map(
        shards, mesh=mesh, in_specs=placed, out_specs=P(("gx", "gy"), None), check_vma=False
    )
```

```python
import functools

import jax
import jax.numpy as jnp
import numpy as np
from jax import lax
from jax.experimental import pallas as pl
from jax.experimental.pallas import tpu as pltpu
from jax.sharding import PartitionSpec as P

ORDER = 6
LOGICAL = pl.DeviceIdType.LOGICAL
F32 = jnp.float32
BF16 = jnp.bfloat16
AMP = 64.0

NODES = 0.5 * np.cos(np.pi * (2.0 * np.arange(ORDER) + 1.0) / (2.0 * ORDER))


def lagrange(points):
    points = np.asarray(points)[..., None, None]
    same = np.eye(ORDER, dtype=bool)
    spread = np.where(same, 1.0, NODES[:, None] - NODES[None, :])
    return np.where(same, 1.0, (points - NODES[None, :]) / spread).prod(-1)


CENTRE = lagrange(0.0)
HALVES = np.stack([((side - 0.5) + NODES) * 0.5 for side in (0, 1)])
TABLE = lagrange(HALVES)
WEIGHT = np.transpose(TABLE, (0, 2, 1))


def tail_table():
    out = np.zeros((ORDER, 64, 128))
    for high in range(64):
        total = np.eye(ORDER)
        for place in range(6):
            total = TABLE[(high >> place) & 1] @ total
        out[:, high, :96] = np.repeat(CENTRE[:, None] * total, 16, axis=1)
    return out.astype(np.float32)


def fit(function, terms):
    u = 0.125 + 0.125 * np.cos(np.pi * (np.arange(200) + 0.5) / 200)
    poly = np.polynomial.chebyshev.Chebyshev.fit(u, function(np.sqrt(u)), terms - 1, domain=[0, 0.25])
    return [float(c) for c in poly.convert(kind=np.polynomial.Polynomial).coef]


SIN = fit(lambda r: np.sin(np.pi * r) / r, 5)
SIN2 = [2.0 * c for c in fit(lambda r: np.sin(np.pi * r) / r, 4)]
COS = fit(lambda r: np.cos(np.pi * r), 5)
COS4 = fit(lambda r: np.cos(np.pi * r), 4)


def horner(coefs, u):
    total = coefs[-1]
    for c in coefs[-2::-1]:
        total = total * u + c
    return total


def turn(c):
    r = c - jnp.floor(c + 0.5)
    u = r * r
    twice = r * horner(SIN2, u)
    half_cos = horner(COS4, u)
    return 1.0 - (0.5 * twice) * twice, twice * half_cos


def turn_cos(c):
    r = c - jnp.floor(c + 0.5)
    twice = r * horner(SIN2, r * r)
    return 1.0 - (0.5 * twice) * twice


def half_turn(y):
    r = 0.5 - y
    u = r * r
    return r * horner(SIN, u), horner(COS, u)


def bend_value(coef, row, y):
    cosine = (0.5 - y) * horner(SIN, (0.5 - y) * (0.5 - y))
    c0, c1, c2, c3 = (coef[row, m] for m in range(4))
    return (c0 - c2) + cosine * ((c1 - 3.0 * c3) + cosine * (2.0 * c2 + cosine * (4.0 * c3)))


def bend_terms(coef, size):
    e1, e2, e3 = (coef[0, m] * float(-2.0 * AMP * np.sin(np.pi * m * size / 2.0)) for m in (1, 2, 3))
    return e1 - e3, 2.0 * e2, 4.0 * e3


def bend_step(terms, middle):
    cosine, sine = half_turn(middle)
    return sine * (terms[0] + cosine * (terms[1] + cosine * terms[2]))


def apply_real(weights, values):
    out = []
    for t in range(ORDER):
        total = weights[t][0] * values[0]
        for s in range(1, ORDER):
            total = total + weights[t][s] * values[s]
        out.append(total)
    return out


def iota(axis):
    return lax.broadcasted_iota(jnp.int32, (8, 128), axis)


def asf(value):
    return value.astype(F32)


def div(a, b):
    return lax.div(a, jnp.int32(b))


def rem(a, b):
    return lax.rem(a, jnp.int32(b))


def subset(deltas, mask):
    total = None
    for k, delta in enumerate(deltas):
        if (mask >> k) & 1:
            total = delta if total is None else total + delta
    return 0 if total is None else total


def abs_flip(bit, turned):
    return 1 - bit if turned else bit


def flips(bits, weights):
    return [weight * (1 - 2 * bit) for bit, weight in zip(bits, weights)]


def lane_parts(classes, core):
    lane = iota(1)
    place = lane >> 4
    x, y, z = (
        2 * c + e + core * (e - c) for c, e in zip(classes, (place >> 2, (place >> 1) & 1, place & 1))
    )
    return (z >> 1) + 2 * y + 8 * x + 32 * (z & 1), lane & 15


def early_levels(coef, box, top, w_ref, p_ref, v_ref):
    sub = iota(0)
    bits = [asf(sub & 1), asf((sub >> 1) & 1), asf(sub >> 2)]
    sign = [2.0 * bit - 1.0 for bit in bits]
    x0 = jnp.full((8, 128), 0.5, F32)
    x1 = x0 + sign[0] * 0.25
    x2 = x1 + sign[1] * 0.125
    word4 = asf(box * 16 + top)
    steps = [
        bend_step(bend_terms(coef, 2.0 ** -(level + 1)), x + sign[level - 1] * 2.0 ** -(level + 2))
        for level, x in ((1, x0), (2, x1), (3, x2))
    ]
    p0_mid = coef[0, 0] - coef[0, 2]

    def turned(values, angles):
        pairs = [(a * c - b * d, a * d + b * c) for (a, b), (c, d) in zip(values, angles)]
        return [a for a, _ in pairs], [b for _, b in pairs]

    linear2 = 2.0 * asf(top & 1) + 0.5
    linear3 = asf(top & 3) + 0.5
    third = [turn(sign[2] * ((linear3 + float(NODES[s])) * 0.25 + steps[2] * p_ref[0, s])) for s in range(ORDER)]
    constants = [[float(WEIGHT[0][t][s]) for s in range(ORDER)] for t in range(ORDER)]

    def by_side(side, values):
        mirror = jnp.broadcast_to(side, (8, 128)) == 1
        picked = [jnp.where(mirror, values[5 - s], values[s]) for s in range(ORDER)]
        out = apply_real(constants, picked)
        return [jnp.where(mirror, out[5 - t], out[t]) for t in range(ORDER)]

    def body(group, _):
        j0, j1 = rem(group, 2), div(group, 2)
        j0f, j1f, groupf = asf(j0), asf(j1), asf(group)
        word = word4 * 4.0 + groupf
        start = 0.5 * (j0f + 0.5) + AMP * p0_mid * bend_value(coef, 1, (word + 0.5) * 2.0**-12)
        real, imag = [], []
        for s in range(ORDER):
            node = float(NODES[s])
            p1 = bend_value(coef, 1, (word + (0.5 + node)) * 2.0**-12)
            c, d = turn(start + sign[0] * ((groupf + (0.5 + node)) * 0.25 + steps[0] * p1))
            real.append(c * float(CENTRE[s]))
            imag.append(d * float(CENTRE[s]))
        values = list(zip(by_side(j0, real), by_side(j0, imag)))
        word = word4 * 2.0 + j1f
        angles = []
        for s in range(ORDER):
            node = float(NODES[s])
            p1 = bend_value(coef, 1, (word + (0.5 + node)) * 2.0**-11)
            angles.append(turn(sign[1] * (((linear2 + j1f) + node) * 0.25 + steps[1] * p1)))
        values = list(zip(*(by_side(j1, part) for part in turned(values, angles))))
        weights = [[w_ref[0, ORDER * t + s] for s in range(ORDER)] for t in range(ORDER)]
        for c, part in enumerate(turned(values, third)):
            for t, value in enumerate(apply_real(weights, part)):
                v_ref[0, 2 * t + c, group] = value
        return 0

    lax.fori_loop(0, 4, body, 0)


def late_setup(coef, box, top, w_ref, p_ref, c_ref):
    full = box * 16 + top

    def body(i, scale):
        word = full >> i
        pick = (word & 1) == 1
        for t in range(ORDER):
            for s in range(ORDER):
                w_ref[i, ORDER * t + s] = jnp.where(pick, float(WEIGHT[1][t][s]), float(WEIGHT[0][t][s]))
        for s in range(ORDER):
            p_ref[i, s] = bend_value(coef, 1, (asf(word) + float(0.5 + NODES[s])) * scale)
        return scale * 2.0

    lax.fori_loop(0, 5, body, jnp.float32(2.0**-10))
    turn_of = top & 7

    def by_lane(values):
        out = jnp.full((8, 128), float(values[ORDER - 1]), F32)
        for t in range(ORDER - 1):
            out = jnp.where(turn_of == t, float(values[t]), out)
        return out

    e1, e2, e3 = (coef[0, m] * by_lane(-2.0 * AMP * np.sin(np.pi * m * NODES / 128.0)) for m in (1, 2, 3))
    node = by_lane(NODES)
    c_ref[0] = node
    c_ref[1] = e1 - e3
    c_ref[2] = 2.0 * e2
    c_ref[3] = 4.0 * e3
    c_ref[4] = node * (asf(box) + 0.5)


def spread(value, t):
    return jnp.take_along_axis(value, (iota(1) & 120) + t, axis=1)


def late_levels(coef, box, top, order, w_ref, p_ref, c_ref, v_ref, g_ref, between):
    sub = iota(0)
    x3 = asf(4 * (sub & 1) + (sub & 2) + (sub >> 2)) * 0.125 + 0.0625
    full = box * 16 + top
    terms = [bend_terms(coef, 2.0 ** -(level + 1)) for level in (4, 5, 6)]

    def sign_of(bit):
        return (2 * bit - 1).astype(F32)

    def turns(i, level_terms, shift, parent, sign):
        steps = bend_step(level_terms, parent + sign * shift)
        linear = asf((full >> i) & 3) + 0.5
        return [turn(sign * ((linear + float(NODES[s])) * 0.25 + steps * p_ref[i, s])) for s in range(ORDER)]

    def level_step(level, q3, q4):
        first = level == 4
        i = level - 3
        parent = x3 + jnp.where(first, 0.0, sign_of(q3) * 2.0**-5)
        sign = jnp.where(first, sign_of(q3), sign_of(q4))
        level_terms = [jnp.where(first, a, b) for a, b in zip(terms[0], terms[1])]
        real, imag = [], []
        for s, (c, d) in enumerate(turns(i, level_terms, jnp.where(first, 2.0**-6, 2.0**-7), parent, sign)):
            a, b = v_ref[i - 1, 2 * s], v_ref[i - 1, 2 * s + 1]
            real.append(a * c - b * d)
            imag.append(a * d + b * c)
        weights = [[w_ref[i, ORDER * t + s] for s in range(ORDER)] for t in range(ORDER)]
        for c, values in enumerate((real, imag)):
            for t, value in enumerate(apply_real(weights, values)):
                v_ref[i, 2 * t + c] = value

    def last_step(parent, bit, place):
        sign = sign_of(bit)
        middle = parent + sign * 2.0**-7 + c_ref[0] * (1.0 / 128.0)
        steps = bend_step((c_ref[1], c_ref[2], c_ref[3]), middle)
        switch = [turn((c_ref[4] + c_ref[0] * float(NODES[u])) + steps * p_ref[4, u]) for u in range(ORDER)]
        merged = []
        for s, (c, d) in enumerate(turns(3, terms[2], 2.0**-8, parent, sign)):
            a = b = None
            for u in range(ORDER):
                weight = w_ref[3, ORDER * u + s]
                a = switch[u][0] * weight if a is None else a + switch[u][0] * weight
                b = switch[u][1] * weight if b is None else b + switch[u][1] * weight
            merged.append((a * c - b * d, a * d + b * c))
        parts = [v_ref[2, 2 * s] + v_ref[2, 2 * s + 1] for s in range(ORDER)]
        for t in range(ORDER):
            k1 = k2 = k3 = None
            for s in range(ORDER):
                c, d = spread(merged[s][0], t), spread(merged[s][1], t)
                m1, m2, m3 = parts[s] * c, v_ref[2, 2 * s] * (d - c), v_ref[2, 2 * s + 1] * (c + d)
                k1 = m1 if k1 is None else k1 + m1
                k2 = m2 if k2 is None else k2 + m2
                k3 = m3 if k3 is None else k3 + m3
            real, imag = k1 - k3, k1 + k2
            rows = pl.ds(pl.multiple_of(place * 192 + 16 * t, 16), 16)
            rows_low = pl.ds(pl.multiple_of(place * 192 + 96 + 16 * t, 16), 16)
            for j in range(4):
                both = jnp.concatenate([real[j], imag[j]], axis=0)
                high = both.astype(BF16)
                g_ref[rows, 128 * j : 128 * (j + 1)] = high
                g_ref[rows_low, 128 * j : 128 * (j + 1)] = (both - high.astype(F32)).astype(BF16)

    def over(n, _):
        @pl.when(n >= 3)
        def _():
            between(n - 3)

        @pl.when(n < 4)
        def _():
            q3, q4 = order(div(n, 2)), rem(n, 2)

            def levels(level, _):
                level_step(level, q3, q4)
                return 0

            lax.fori_loop(4 + q4, 6, levels, 0)
            x5 = x3 + (sign_of(q3) * 2.0**-5 + sign_of(q4) * 2.0**-6)

            def over5(q5, _):
                last_step(x5, q5, 4 * q3 + q4 + 2 * q5)
                return 0

            lax.fori_loop(0, 2, over5, 0)

        return 0

    lax.fori_loop(0, 5, over, 0)


def last_weights(coef, group, tail_ref, h_ref):
    sub, lane = iota(0), iota(1)
    own = lane & 7
    same = sub == own
    box6 = 32 * (own & 1) + 8 * (own & 2) + 2 * (own & 4)
    box6 = box6 + (4 * rem(group, 2) + 2 * rem(div(group, 2), 2) + div(group, 4))
    inner = 32 * (sub & 1) + 8 * (sub & 2) + 2 * (sub & 4)
    base = box6 * 64 + inner
    quarter = 0.25 * asf((lane >> 3) & 1)
    p1_mid = coef[1, 0] - coef[1, 2]

    def rows_of(r):
        centre = (asf(base + (4 * rem(r, 2) + 2 * rem(div(r, 2), 2) + div(r, 4))) + 0.5) * 2.0**-12
        total = None
        for t in range(ORDER):
            node = float(NODES[t])
            steps = bend_step(bend_terms(coef, node / 4096.0), centre + node / 8192.0)
            term = turn_cos((quarter - 0.5 * node) - steps * p1_mid)
            term = term * tail_ref[t, pl.ds(pl.multiple_of(8 * r, 8), 8), :]
            total = term if total is None else total + term
        return total

    def body(r, _):
        total = rows_of(r)
        for k in range(0, 8, 2):
            both = jnp.concatenate(
                [jnp.where(same, jnp.broadcast_to(total[k + n : k + n + 1], (8, 128)), 0.0) for n in range(2)], axis=0
            )
            high = both.astype(BF16)
            rows = pl.ds(pl.multiple_of(64 * r + 8 * k, 16), 16)
            h_ref[rows, 0:128] = high
            h_ref[rows, 128:256] = (both - high.astype(F32)).astype(BF16)
            h_ref[rows, 256:384] = high
        return 0

    lax.fori_loop(0, 8, body, 0)


def kernel(
    x_ref,
    coef_hbm,
    tail_hbm,
    out_ref,
    coef_ref,
    tail_ref,
    w_ref,
    p_ref,
    c_ref,
    v_ref,
    g_ref,
    h_ref,
    xr_ref,
    xs_ref,
    wide_ref,
    part_ref,
    rr_ref,
    sum_ref,
    tile_ref,
    send_sems,
    recv_sems,
):
    fetch_coef = pltpu.make_async_copy(coef_hbm, coef_ref, recv_sems.at[3])
    fetch_tail = pltpu.make_async_copy(tail_hbm, tail_ref, recv_sems.at[4])
    fetch_coef.start()
    fetch_tail.start()
    gx, gy = lax.axis_index("gx"), lax.axis_index("gy")
    core = rem(gy, 2)
    zl, xs = div(gx, 4), rem(gx, 4)
    xh, xl = div(xs, 2), rem(xs, 2)
    yh, yl, zh = div(gy, 8), rem(div(gy, 4), 2), rem(div(gy, 2), 2)
    me = gx * 16 + gy
    highs, lows = (xh, yh, zh), (xl, yl, zl)
    to_a = [16 * (1 - 2 * xl), 4 * (1 - 2 * yl), 64 * (1 - 2 * zl)]
    to_b = [32 * (1 - 2 * xh), 8 * (1 - 2 * yh), 2 * (1 - 2 * zh)]
    to_class = [a + core * (b - a) for a, b in zip(to_a, to_b)]
    to_group = [b + core * (a - b) for a, b in zip(to_a, to_b)]
    to_core = 1 - 2 * core
    class_a, class_b = highs, lows
    place_a, place_b = lows, highs
    group_a, group_b = lows, highs

    def mine(for_a, for_b):
        return [a + core * (b - a) for a, b in zip(for_a, for_b)]

    def others(for_a, for_b):
        return [b + core * (a - b) for a, b in zip(for_a, for_b)]

    def number(values):
        return values[0] + 2 * values[1] + 4 * values[2]

    classes, groups = mine(class_a, class_b), mine(group_a, group_b)
    target = number(classes)
    block = number(groups) + 8 * core

    barrier = pltpu.get_barrier_semaphore()
    for mask in range(1, 16):
        source = me + subset(to_class + [to_core], mask)
        pl.semaphore_signal(barrier, inc=1, device_id=source, device_id_type=LOGICAL)
    for mask in range(1, 8):
        pl.semaphore_signal(barrier, inc=1, device_id=me + subset(to_group, mask), device_id_type=LOGICAL)
    box, top = lane_parts(classes, core)
    fetch_coef.wait()
    late_setup(coef_ref, box, top, w_ref, p_ref, c_ref)
    pl.semaphore_wait(barrier, 22)

    def columns(m):
        return x_ref.at[:, pl.ds(pl.multiple_of(m * 128, 128), 128)]

    own_slot = 2 * number(mine(place_a, place_b)[::-1]) + core
    other_slot = 2 * number(others(place_a, place_b)[::-1]) + core
    other_groups = others(group_a, group_b)
    other_block = number(other_groups) + 8 * (1 - core)
    for mask in range(7, -1, -1):
        routes = [(other_block, other_groups, other_slot, me + to_core + subset(to_group, mask))]
        if mask:
            routes.append((block, groups, own_slot, me + subset(to_class, mask)))
        for first, group_bits, slot, device in routes:
            pltpu.make_async_remote_copy(
                src_ref=columns(first + subset(flips(group_bits, (1, 2, 4)), mask)),
                dst_ref=xr_ref.at[slot],
                send_sem=send_sems.at[0],
                recv_sem=recv_sems.at[0],
                device_id=device,
                device_id_type=LOGICAL,
            ).start()
    pltpu.make_async_copy(columns(block), xr_ref.at[own_slot], recv_sems.at[0]).start()
    early_levels(coef_ref, box, top, w_ref, p_ref, v_ref)

    def order(h):
        return classes[0] + (1 - h) * (1 - 2 * classes[0])

    def split(i, _):
        for j in range(4):
            piece = jnp.concatenate([xr_ref[2 * i + s, pl.ds(j, 8, stride=4), :] for s in range(2)], axis=0)
            high = piece.astype(BF16)
            rows = pl.ds(pl.multiple_of(128 * j + 16 * i, 16), 16)
            xs_ref[rows, 0:128] = high
            xs_ref[rows, 128:256] = (piece - high.astype(F32)).astype(BF16)
        return 0

    def half(h):
        @pl.when(h == 0)
        def _():
            pltpu.make_async_copy(xr_ref, xr_ref, recv_sems.at[0]).wait()
            lax.fori_loop(0, 8, split, 0)

        q3 = order(h)
        rows = pl.ds(pl.multiple_of(q3 * 768, 16), 768)
        wide_ref[...] = jnp.dot(g_ref[rows, :], xs_ref[...], preferred_element_type=F32)

        far = (1 - h) * to_group[0]
        for mask in range(3, -1, -1):
            i = classes[1] + 2 * classes[2] + subset(flips(classes[1:], (1, 2)), mask)
            high = pl.ds(pl.multiple_of(i * 192, 8), 96)
            low = pl.ds(pl.multiple_of(i * 192 + 96, 8), 96)
            part = wide_ref[high, 0:128] + (wide_ref[high, 128:256] + wide_ref[low, 0:128])

            def send():
                part_ref[4 * q3 + i] = part
                pltpu.make_async_remote_copy(
                    src_ref=part_ref.at[4 * q3 + i],
                    dst_ref=rr_ref.at[target],
                    send_sem=send_sems.at[1],
                    recv_sem=recv_sems.at[1],
                    device_id=me + far + subset(to_group[1:], mask),
                    device_id_type=LOGICAL,
                ).start()

            if mask:
                send()
            else:
                pl.when(h == 0)(send)

                @pl.when(h == 1)
                def _():
                    rr_ref[target] = part

    late_levels(coef_ref, box, top, order, w_ref, p_ref, c_ref, v_ref, g_ref, half)
    fetch_tail.wait()
    for i in range(3):
        sum_ref[128 * i + 96 : 128 * i + 128, :] = jnp.zeros((32, 128), BF16)
    last_weights(coef_ref, target, tail_ref, h_ref)
    pltpu.make_async_copy(rr_ref.at[0:7], rr_ref.at[0:7], recv_sems.at[1]).wait()

    def add(i, _):
        rows = pl.ds(pl.multiple_of(16 * i, 16), 16)
        total = rr_ref[0, rows, :]
        for k in range(1, 8):
            total = total + rr_ref[k, rows, :]
        high = total.astype(BF16)
        sum_ref[rows, :] = high
        sum_ref[pl.ds(pl.multiple_of(128 + 16 * i, 16), 16), :] = high
        sum_ref[pl.ds(pl.multiple_of(256 + 16 * i, 16), 16), :] = (total - high.astype(F32)).astype(BF16)
        return 0

    lax.fori_loop(0, 6, add, 0)

    home = zh + 2 * yl + 4 * yh + 8 * xl + 16 * xh + 32 * zl
    own = core == classes[2]
    row = pl.multiple_of((classes[0] + 2 * classes[1]) * 8, 8)
    here = out_ref.at[pl.ds(row, 8), pl.ds(pl.multiple_of(block * 128, 128), 128)]
    turns = flips((zh, yl, xl, yh, xh, zl), (1, 2, 8, 4, 16, 32))

    def deliver(high):
        pltpu.make_async_remote_copy(
            src_ref=tile_ref.at[high],
            dst_ref=here,
            send_sem=send_sems.at[2],
            recv_sem=recv_sems.at[2],
            device_id=2 * high + classes[2],
            device_id_type=LOGICAL,
        ).start()

    early = (0, 8)
    lost = (63 - home, home + subset(turns, 62))
    instead = [jnp.where(lost[n] == early[1 - n], lost[1 - n], lost[n]) for n in range(2)]

    def settle(high):
        return jnp.where(high == early[0], instead[0], jnp.where(high == early[1], instead[1], high))

    def make(quarter, _):
        rows = pl.ds(pl.multiple_of(128 * quarter, 16), 128)
        tiles = jnp.dot(h_ref[rows, :], sum_ref[...], preferred_element_type=F32)
        tile_ref[pl.ds(16 * quarter, 16)] = tiles.reshape(16, 8, 128)

        @pl.when(quarter == 0)
        def _():
            for high in early:
                pl.when(jnp.logical_or(home != high, jnp.logical_not(own)))(functools.partial(deliver, high))

        return 0

    lax.fori_loop(0, 4, make, 0)
    moved = jnp.logical_or(home == early[0], home == early[1])
    last = jnp.logical_or(moved, jnp.logical_not(own))

    def deliver_some(step, _):
        same_x, same_z = rem(step, 2), div(step, 2)
        first = home + (1 - same_x) * turns[4] + (1 - same_z) * turns[5]

        def send(mask):
            deliver(settle(first + subset(turns, mask)))

        @pl.when(step > 0)
        def _():
            send(15)
            send(14)

        for mask in range(13, 0, -1):
            send(mask)

        pl.when(jnp.logical_or(step < 3, last))(lambda: send(0))
        return 0

    lax.fori_loop(0, 4, deliver_some, 0)

    @pl.when(own)
    def _():
        pltpu.make_async_copy(tile_ref.at[home], here, recv_sems.at[2]).start()

    pltpu.make_async_copy(xr_ref.at[0:15], xr_ref.at[0:15], send_sems.at[0]).wait()
    pltpu.make_async_copy(part_ref.at[0:7], part_ref.at[0:7], send_sems.at[1]).wait()

    @pl.when(own)
    def _():
        pltpu.make_async_copy(tile_ref.at[0:63], tile_ref.at[0:63], send_sems.at[2]).wait()

    @pl.when(jnp.logical_not(own))
    def _():
        pltpu.make_async_copy(tile_ref, tile_ref, send_sems.at[2]).wait()

    pltpu.make_async_copy(out_ref, out_ref, recv_sems.at[2]).wait()


def shards(traces, phase_coef):
    return pl.pallas_call(
        kernel,
        out_shape=jax.ShapeDtypeStruct((32, 2048), F32),
        in_specs=[
            pl.BlockSpec(memory_space=pl.ANY),
            pl.BlockSpec(memory_space=pl.ANY),
            pl.BlockSpec(memory_space=pl.ANY),
        ],
        out_specs=pl.BlockSpec(memory_space=pl.ANY),
        scratch_shapes=[
            pltpu.SMEM((2, 4), F32),
            pltpu.VMEM((6, 64, 128), F32),
            pltpu.VMEM((5, 36, 8, 128), F32),
            pltpu.VMEM((5, 6, 8, 128), F32),
            pltpu.VMEM((5, 8, 128), F32),
            pltpu.VMEM((3, 12, 4, 8, 128), F32),
            pltpu.VMEM((1536, 512), BF16),
            pltpu.VMEM((512, 384), BF16),
            pltpu.VMEM((16, 32, 128), F32),
            pltpu.VMEM((512, 256), BF16),
            pltpu.VMEM((768, 256), F32),
            pltpu.VMEM((8, 96, 128), F32),
            pltpu.VMEM((8, 96, 128), F32),
            pltpu.VMEM((384, 128), BF16),
            pltpu.VMEM((64, 8, 128), F32),
            pltpu.SemaphoreType.DMA((3,)),
            pltpu.SemaphoreType.DMA((5,)),
        ],
        compiler_params=pltpu.CompilerParams(
            collective_id=0, has_side_effects=True, vmem_limit_bytes=60 * 2**20
        ),
    )(traces, phase_coef, jnp.asarray(tail_table()))


def solution(mesh):
    placed = (P(("gx", "gy"), None), P())
    return jax.shard_map(
        shards, mesh=mesh, in_specs=placed, out_specs=P(("gx", "gy"), None), check_vma=False
    )
```

```python
import functools

import jax
import jax.numpy as jnp
import numpy as np
from jax import lax
from jax.experimental import pallas as pl
from jax.experimental.pallas import tpu as pltpu
from jax.sharding import PartitionSpec as P

ORDER = 6
LOGICAL = pl.DeviceIdType.LOGICAL
F32 = jnp.float32
BF16 = jnp.bfloat16
AMP = 64.0

NODES = 0.5 * np.cos(np.pi * (2.0 * np.arange(ORDER) + 1.0) / (2.0 * ORDER))


def lagrange(points):
    points = np.asarray(points)[..., None, None]
    same = np.eye(ORDER, dtype=bool)
    spread = np.where(same, 1.0, NODES[:, None] - NODES[None, :])
    return np.where(same, 1.0, (points - NODES[None, :]) / spread).prod(-1)


CENTRE = lagrange(0.0)
HALVES = np.stack([((side - 0.5) + NODES) * 0.5 for side in (0, 1)])
TABLE = lagrange(HALVES)
WEIGHT = np.transpose(TABLE, (0, 2, 1))


def tail_table():
    out = np.zeros((ORDER, 64, 128))
    for high in range(64):
        total = np.eye(ORDER)
        for place in range(6):
            total = TABLE[(high >> place) & 1] @ total
        out[:, high, :96] = np.repeat(CENTRE[:, None] * total, 16, axis=1)
    return out.astype(np.float32)


def fit(function, terms):
    u = 0.125 + 0.125 * np.cos(np.pi * (np.arange(200) + 0.5) / 200)
    poly = np.polynomial.chebyshev.Chebyshev.fit(u, function(np.sqrt(u)), terms - 1, domain=[0, 0.25])
    return [float(c) for c in poly.convert(kind=np.polynomial.Polynomial).coef]


SIN = fit(lambda r: np.sin(np.pi * r) / r, 5)
SIN2 = [2.0 * c for c in fit(lambda r: np.sin(np.pi * r) / r, 4)]
COS = fit(lambda r: np.cos(np.pi * r), 5)
COS4 = fit(lambda r: np.cos(np.pi * r), 4)


def horner(coefs, u):
    total = coefs[-1]
    for c in coefs[-2::-1]:
        total = total * u + c
    return total


def turn(c):
    r = c - jnp.floor(c + 0.5)
    u = r * r
    twice = r * horner(SIN2, u)
    half_cos = horner(COS4, u)
    return 1.0 - (0.5 * twice) * twice, twice * half_cos


def turn_cos(c):
    r = c - jnp.floor(c + 0.5)
    twice = r * horner(SIN2, r * r)
    return 1.0 - (0.5 * twice) * twice


def half_turn(y):
    r = 0.5 - y
    u = r * r
    return r * horner(SIN, u), horner(COS, u)


def bend_value(coef, row, y):
    cosine = (0.5 - y) * horner(SIN, (0.5 - y) * (0.5 - y))
    c0, c1, c2, c3 = (coef[row, m] for m in range(4))
    return (c0 - c2) + cosine * ((c1 - 3.0 * c3) + cosine * (2.0 * c2 + cosine * (4.0 * c3)))


def bend_terms(coef, size):
    e1, e2, e3 = (coef[0, m] * float(-2.0 * AMP * np.sin(np.pi * m * size / 2.0)) for m in (1, 2, 3))
    return e1 - e3, 2.0 * e2, 4.0 * e3


def bend_step(terms, middle):
    cosine, sine = half_turn(middle)
    return sine * (terms[0] + cosine * (terms[1] + cosine * terms[2]))


def apply_real(weights, values):
    out = []
    for t in range(ORDER):
        total = weights[t][0] * values[0]
        for s in range(1, ORDER):
            total = total + weights[t][s] * values[s]
        out.append(total)
    return out


def iota(axis):
    return lax.broadcasted_iota(jnp.int32, (8, 128), axis)


def asf(value):
    return value.astype(F32)


def div(a, b):
    return lax.div(a, jnp.int32(b))


def rem(a, b):
    return lax.rem(a, jnp.int32(b))


def subset(deltas, mask):
    total = None
    for k, delta in enumerate(deltas):
        if (mask >> k) & 1:
            total = delta if total is None else total + delta
    return 0 if total is None else total


def abs_flip(bit, turned):
    return 1 - bit if turned else bit


def flips(bits, weights):
    return [weight * (1 - 2 * bit) for bit, weight in zip(bits, weights)]


def lane_parts(classes, core):
    lane = iota(1)
    place = lane >> 4
    x, y, z = (
        (2 * c + e + core) & 3 for c, e in zip(classes, (place >> 2, (place >> 1) & 1, place & 1))
    )
    return (z >> 1) + 2 * y + 8 * x + 32 * (z & 1), lane & 15


def early_levels(coef, box, top, w_ref, p_ref, v_ref):
    sub = iota(0)
    bits = [asf(sub & 1), asf((sub >> 1) & 1), asf(sub >> 2)]
    sign = [2.0 * bit - 1.0 for bit in bits]
    x0 = jnp.full((8, 128), 0.5, F32)
    x1 = x0 + sign[0] * 0.25
    x2 = x1 + sign[1] * 0.125
    word4 = asf(box * 16 + top)
    steps = [
        bend_step(bend_terms(coef, 2.0 ** -(level + 1)), x + sign[level - 1] * 2.0 ** -(level + 2))
        for level, x in ((1, x0), (2, x1), (3, x2))
    ]
    p0_mid = coef[0, 0] - coef[0, 2]

    def turned(values, angles):
        pairs = [(a * c - b * d, a * d + b * c) for (a, b), (c, d) in zip(values, angles)]
        return [a for a, _ in pairs], [b for _, b in pairs]

    linear2 = 2.0 * asf(top & 1) + 0.5
    linear3 = asf(top & 3) + 0.5
    third = [turn(sign[2] * ((linear3 + float(NODES[s])) * 0.25 + steps[2] * p_ref[0, s])) for s in range(ORDER)]
    constants = [[float(WEIGHT[0][t][s]) for s in range(ORDER)] for t in range(ORDER)]

    def by_side(side, values):
        mirror = jnp.broadcast_to(side, (8, 128)) == 1
        picked = [jnp.where(mirror, values[5 - s], values[s]) for s in range(ORDER)]
        out = apply_real(constants, picked)
        return [jnp.where(mirror, out[5 - t], out[t]) for t in range(ORDER)]

    def body(group, _):
        j0, j1 = rem(group, 2), div(group, 2)
        j0f, j1f, groupf = asf(j0), asf(j1), asf(group)
        word = word4 * 4.0 + groupf
        start = 0.5 * (j0f + 0.5) + AMP * p0_mid * bend_value(coef, 1, (word + 0.5) * 2.0**-12)
        real, imag = [], []
        for s in range(ORDER):
            node = float(NODES[s])
            p1 = bend_value(coef, 1, (word + (0.5 + node)) * 2.0**-12)
            c, d = turn(start + sign[0] * ((groupf + (0.5 + node)) * 0.25 + steps[0] * p1))
            real.append(c * float(CENTRE[s]))
            imag.append(d * float(CENTRE[s]))
        values = list(zip(by_side(j0, real), by_side(j0, imag)))
        word = word4 * 2.0 + j1f
        angles = []
        for s in range(ORDER):
            node = float(NODES[s])
            p1 = bend_value(coef, 1, (word + (0.5 + node)) * 2.0**-11)
            angles.append(turn(sign[1] * (((linear2 + j1f) + node) * 0.25 + steps[1] * p1)))
        values = list(zip(*(by_side(j1, part) for part in turned(values, angles))))
        weights = [[w_ref[0, ORDER * t + s] for s in range(ORDER)] for t in range(ORDER)]
        for c, part in enumerate(turned(values, third)):
            for t, value in enumerate(apply_real(weights, part)):
                v_ref[0, 2 * t + c, group] = value
        return 0

    lax.fori_loop(0, 4, body, 0)


def late_setup(coef, box, top, w_ref, p_ref, c_ref):
    full = box * 16 + top

    def body(i, scale):
        word = full >> i
        pick = (word & 1) == 1
        for t in range(ORDER):
            for s in range(ORDER):
                w_ref[i, ORDER * t + s] = jnp.where(pick, float(WEIGHT[1][t][s]), float(WEIGHT[0][t][s]))
        for s in range(ORDER):
            p_ref[i, s] = bend_value(coef, 1, (asf(word) + float(0.5 + NODES[s])) * scale)
        return scale * 2.0

    lax.fori_loop(0, 5, body, jnp.float32(2.0**-10))
    turn_of = top & 7

    def by_lane(values):
        out = jnp.full((8, 128), float(values[ORDER - 1]), F32)
        for t in range(ORDER - 1):
            out = jnp.where(turn_of == t, float(values[t]), out)
        return out

    e1, e2, e3 = (coef[0, m] * by_lane(-2.0 * AMP * np.sin(np.pi * m * NODES / 128.0)) for m in (1, 2, 3))
    node = by_lane(NODES)
    c_ref[0] = node
    c_ref[1] = e1 - e3
    c_ref[2] = 2.0 * e2
    c_ref[3] = 4.0 * e3
    c_ref[4] = node * (asf(box) + 0.5)


def spread(value, t):
    return jnp.take_along_axis(value, (iota(1) & 120) + t, axis=1)


def late_levels(coef, box, top, order, w_ref, p_ref, c_ref, v_ref, g_ref, between):
    sub = iota(0)
    x3 = asf(4 * (sub & 1) + (sub & 2) + (sub >> 2)) * 0.125 + 0.0625
    full = box * 16 + top
    terms = [bend_terms(coef, 2.0 ** -(level + 1)) for level in (4, 5, 6)]

    def sign_of(bit):
        return (2 * bit - 1).astype(F32)

    def turns(i, level_terms, shift, parent, sign):
        steps = bend_step(level_terms, parent + sign * shift)
        linear = asf((full >> i) & 3) + 0.5
        return [turn(sign * ((linear + float(NODES[s])) * 0.25 + steps * p_ref[i, s])) for s in range(ORDER)]

    def level_step(level, q3, q4):
        first = level == 4
        i = level - 3
        parent = x3 + jnp.where(first, 0.0, sign_of(q3) * 2.0**-5)
        sign = jnp.where(first, sign_of(q3), sign_of(q4))
        level_terms = [jnp.where(first, a, b) for a, b in zip(terms[0], terms[1])]
        real, imag = [], []
        for s, (c, d) in enumerate(turns(i, level_terms, jnp.where(first, 2.0**-6, 2.0**-7), parent, sign)):
            a, b = v_ref[i - 1, 2 * s], v_ref[i - 1, 2 * s + 1]
            real.append(a * c - b * d)
            imag.append(a * d + b * c)
        weights = [[w_ref[i, ORDER * t + s] for s in range(ORDER)] for t in range(ORDER)]
        for c, values in enumerate((real, imag)):
            for t, value in enumerate(apply_real(weights, values)):
                v_ref[i, 2 * t + c] = value

    def last_step(parent, bit, place):
        sign = sign_of(bit)
        middle = parent + sign * 2.0**-7 + c_ref[0] * (1.0 / 128.0)
        steps = bend_step((c_ref[1], c_ref[2], c_ref[3]), middle)
        switch = [turn((c_ref[4] + c_ref[0] * float(NODES[u])) + steps * p_ref[4, u]) for u in range(ORDER)]
        merged = []
        for s, (c, d) in enumerate(turns(3, terms[2], 2.0**-8, parent, sign)):
            a = b = None
            for u in range(ORDER):
                weight = w_ref[3, ORDER * u + s]
                a = switch[u][0] * weight if a is None else a + switch[u][0] * weight
                b = switch[u][1] * weight if b is None else b + switch[u][1] * weight
            merged.append((a * c - b * d, a * d + b * c))
        parts = [v_ref[2, 2 * s] + v_ref[2, 2 * s + 1] for s in range(ORDER)]
        for t in range(ORDER):
            k1 = k2 = k3 = None
            for s in range(ORDER):
                c, d = spread(merged[s][0], t), spread(merged[s][1], t)
                m1, m2, m3 = parts[s] * c, v_ref[2, 2 * s] * (d - c), v_ref[2, 2 * s + 1] * (c + d)
                k1 = m1 if k1 is None else k1 + m1
                k2 = m2 if k2 is None else k2 + m2
                k3 = m3 if k3 is None else k3 + m3
            real, imag = k1 - k3, k1 + k2
            rows = pl.ds(pl.multiple_of(place * 192 + 16 * t, 16), 16)
            rows_low = pl.ds(pl.multiple_of(place * 192 + 96 + 16 * t, 16), 16)
            for j in range(4):
                both = jnp.concatenate([real[j], imag[j]], axis=0)
                high = both.astype(BF16)
                g_ref[rows, 128 * j : 128 * (j + 1)] = high
                g_ref[rows_low, 128 * j : 128 * (j + 1)] = (both - high.astype(F32)).astype(BF16)

    def over(n, _):
        @pl.when(n >= 3)
        def _():
            between(n - 3)

        @pl.when(n < 4)
        def _():
            q3, q4 = order(div(n, 2)), rem(n, 2)

            def levels(level, _):
                level_step(level, q3, q4)
                return 0

            lax.fori_loop(4 + q4, 6, levels, 0)
            x5 = x3 + (sign_of(q3) * 2.0**-5 + sign_of(q4) * 2.0**-6)

            def over5(q5, _):
                last_step(x5, q5, 4 * q3 + q4 + 2 * q5)
                return 0

            lax.fori_loop(0, 2, over5, 0)

        return 0

    lax.fori_loop(0, 5, over, 0)


def last_weights(coef, group, tail_ref, h_ref):
    sub, lane = iota(0), iota(1)
    own = lane & 7
    same = sub == own
    box6 = 32 * (own & 1) + 8 * (own & 2) + 2 * (own & 4)
    box6 = box6 + (4 * rem(group, 2) + 2 * rem(div(group, 2), 2) + div(group, 4))
    inner = 32 * (sub & 1) + 8 * (sub & 2) + 2 * (sub & 4)
    base = box6 * 64 + inner
    quarter = 0.25 * asf((lane >> 3) & 1)
    p1_mid = coef[1, 0] - coef[1, 2]

    def rows_of(r):
        centre = (asf(base + (4 * rem(r, 2) + 2 * rem(div(r, 2), 2) + div(r, 4))) + 0.5) * 2.0**-12
        total = None
        for t in range(ORDER):
            node = float(NODES[t])
            steps = bend_step(bend_terms(coef, node / 4096.0), centre + node / 8192.0)
            term = turn_cos((quarter - 0.5 * node) - steps * p1_mid)
            term = term * tail_ref[t, pl.ds(pl.multiple_of(8 * r, 8), 8), :]
            total = term if total is None else total + term
        return total

    def body(r, _):
        total = rows_of(r)
        for k in range(0, 8, 2):
            both = jnp.concatenate(
                [jnp.where(same, jnp.broadcast_to(total[k + n : k + n + 1], (8, 128)), 0.0) for n in range(2)], axis=0
            )
            high = both.astype(BF16)
            rows = pl.ds(pl.multiple_of(64 * r + 8 * k, 16), 16)
            h_ref[rows, 0:128] = high
            h_ref[rows, 128:256] = (both - high.astype(F32)).astype(BF16)
            h_ref[rows, 256:384] = high
        return 0

    lax.fori_loop(0, 8, body, 0)


def kernel(
    x_ref,
    coef_hbm,
    tail_hbm,
    out_ref,
    coef_ref,
    tail_ref,
    w_ref,
    p_ref,
    c_ref,
    v_ref,
    g_ref,
    h_ref,
    xr_ref,
    xs_ref,
    wide_ref,
    part_ref,
    rr_ref,
    sum_ref,
    tile_ref,
    send_sems,
    recv_sems,
):
    fetch_coef = pltpu.make_async_copy(coef_hbm, coef_ref, recv_sems.at[3])
    fetch_tail = pltpu.make_async_copy(tail_hbm, tail_ref, recv_sems.at[4])
    fetch_coef.start()
    fetch_tail.start()
    gx, gy = lax.axis_index("gx"), lax.axis_index("gy")
    core = rem(gy, 2)
    zl, xs = div(gx, 4), rem(gx, 4)
    xh, xl = div(xs, 2), rem(xs, 2)
    yh, yl, zh = div(gy, 8), rem(div(gy, 4), 2), rem(div(gy, 2), 2)
    me = gx * 16 + gy
    highs, lows = (xh, yh, zh), (xl, yl, zl)
    unlike = [h + l - 2 * h * l for h, l in zip(highs, lows)]
    to_a = [16 * (1 - 2 * xl), 4 * (1 - 2 * yl), 64 * (1 - 2 * zl)]
    to_b = [16 * (3 - 2 * xs), 4 * (3 - 2 * (2 * yh + yl)), 2 * (1 - 2 * zh) + 64 * (1 - 2 * zl)]
    to_class = [a + core * (b - a) for a, b in zip(to_a, to_b)]
    to_group = [b + core * (a - b) for a, b in zip(to_a, to_b)]
    to_core = 1 - 2 * core
    class_a, class_b = highs, [1 - d for d in unlike]
    place_a, place_b = lows, [1 - l for l in lows]
    group_a, group_b = [1 - d for d in unlike], [1 - h for h in highs]

    def mine(for_a, for_b):
        return [a + core * (b - a) for a, b in zip(for_a, for_b)]

    def others(for_a, for_b):
        return [b + core * (a - b) for a, b in zip(for_a, for_b)]

    def number(values):
        return values[0] + 2 * values[1] + 4 * values[2]

    classes, groups = mine(class_a, class_b), mine(group_a, group_b)
    target = number(classes)
    block = number(groups) + 8 * core

    barrier = pltpu.get_barrier_semaphore()
    for mask in range(1, 16):
        source = me + subset(to_class + [to_core], mask)
        pl.semaphore_signal(barrier, inc=1, device_id=source, device_id_type=LOGICAL)
    for mask in range(1, 8):
        pl.semaphore_signal(barrier, inc=1, device_id=me + subset(to_group, mask), device_id_type=LOGICAL)
    box, top = lane_parts(classes, core)
    fetch_coef.wait()
    late_setup(coef_ref, box, top, w_ref, p_ref, c_ref)
    pl.semaphore_wait(barrier, 22)

    def columns(m):
        return x_ref.at[:, pl.ds(pl.multiple_of(m * 128, 128), 128)]

    own_slot = 2 * number(mine(place_a, place_b)[::-1]) + core
    other_slot = 2 * number(others(place_a, place_b)[::-1]) + core
    other_groups = others(group_a, group_b)
    other_block = number(other_groups) + 8 * (1 - core)
    for mask in range(7, -1, -1):
        routes = [(other_block, other_groups, other_slot, me + to_core + subset(to_group, mask))]
        if mask:
            routes.append((block, groups, own_slot, me + subset(to_class, mask)))
        for first, group_bits, slot, device in routes:
            pltpu.make_async_remote_copy(
                src_ref=columns(first + subset(flips(group_bits, (1, 2, 4)), mask)),
                dst_ref=xr_ref.at[slot],
                send_sem=send_sems.at[0],
                recv_sem=recv_sems.at[0],
                device_id=device,
                device_id_type=LOGICAL,
            ).start()
    pltpu.make_async_copy(columns(block), xr_ref.at[own_slot], recv_sems.at[0]).start()
    early_levels(coef_ref, box, top, w_ref, p_ref, v_ref)

    def order(h):
        return classes[0] + (1 - h) * (1 - 2 * classes[0])

    def split(i, _):
        for j in range(4):
            piece = jnp.concatenate([xr_ref[2 * i + s, pl.ds(j, 8, stride=4), :] for s in range(2)], axis=0)
            high = piece.astype(BF16)
            rows = pl.ds(pl.multiple_of(128 * j + 16 * i, 16), 16)
            xs_ref[rows, 0:128] = high
            xs_ref[rows, 128:256] = (piece - high.astype(F32)).astype(BF16)
        return 0

    def half(h):
        @pl.when(h == 0)
        def _():
            pltpu.make_async_copy(xr_ref, xr_ref, recv_sems.at[0]).wait()
            lax.fori_loop(0, 8, split, 0)

        q3 = order(h)
        rows = pl.ds(pl.multiple_of(q3 * 768, 16), 768)
        wide_ref[...] = jnp.dot(g_ref[rows, :], xs_ref[...], preferred_element_type=F32)

        far = (1 - h) * to_group[0]
        for mask in range(3, -1, -1):
            i = classes[1] + 2 * classes[2] + subset(flips(classes[1:], (1, 2)), mask)
            high = pl.ds(pl.multiple_of(i * 192, 8), 96)
            low = pl.ds(pl.multiple_of(i * 192 + 96, 8), 96)
            part = wide_ref[high, 0:128] + (wide_ref[high, 128:256] + wide_ref[low, 0:128])

            def send():
                part_ref[4 * q3 + i] = part
                pltpu.make_async_remote_copy(
                    src_ref=part_ref.at[4 * q3 + i],
                    dst_ref=rr_ref.at[target],
                    send_sem=send_sems.at[1],
                    recv_sem=recv_sems.at[1],
                    device_id=me + far + subset(to_group[1:], mask),
                    device_id_type=LOGICAL,
                ).start()

            if mask:
                send()
            else:
                pl.when(h == 0)(send)

                @pl.when(h == 1)
                def _():
                    rr_ref[target] = part

    late_levels(coef_ref, box, top, order, w_ref, p_ref, c_ref, v_ref, g_ref, half)
    fetch_tail.wait()
    for i in range(3):
        sum_ref[128 * i + 96 : 128 * i + 128, :] = jnp.zeros((32, 128), BF16)
    last_weights(coef_ref, target, tail_ref, h_ref)
    pltpu.make_async_copy(rr_ref.at[0:7], rr_ref.at[0:7], recv_sems.at[1]).wait()

    def add(i, _):
        rows = pl.ds(pl.multiple_of(16 * i, 16), 16)
        total = rr_ref[0, rows, :]
        for k in range(1, 8):
            total = total + rr_ref[k, rows, :]
        high = total.astype(BF16)
        sum_ref[rows, :] = high
        sum_ref[pl.ds(pl.multiple_of(128 + 16 * i, 16), 16), :] = high
        sum_ref[pl.ds(pl.multiple_of(256 + 16 * i, 16), 16), :] = (total - high.astype(F32)).astype(BF16)
        return 0

    lax.fori_loop(0, 6, add, 0)

    home = zh + 2 * yl + 4 * yh + 8 * xl + 16 * xh + 32 * zl
    own = core == classes[2]
    row = pl.multiple_of((classes[0] + 2 * classes[1]) * 8, 8)
    here = out_ref.at[pl.ds(row, 8), pl.ds(pl.multiple_of(block * 128, 128), 128)]
    turns = flips((zh, xl, xh, yh, yl, zl), (1, 8, 16, 4, 2, 32))

    def deliver(high):
        pltpu.make_async_remote_copy(
            src_ref=tile_ref.at[high],
            dst_ref=here,
            send_sem=send_sems.at[2],
            recv_sem=recv_sems.at[2],
            device_id=2 * high + classes[2],
            device_id_type=LOGICAL,
        ).start()

    early = (0, 8)
    lost = (63 - home, home + subset(turns, 48))
    instead = [jnp.where(lost[n] == early[1 - n], lost[1 - n], lost[n]) for n in range(2)]

    def settle(high):
        return jnp.where(high == early[0], instead[0], jnp.where(high == early[1], instead[1], high))

    def make(quarter, _):
        rows = pl.ds(pl.multiple_of(128 * quarter, 16), 128)
        tiles = jnp.dot(h_ref[rows, :], sum_ref[...], preferred_element_type=F32)
        tile_ref[pl.ds(16 * quarter, 16)] = tiles.reshape(16, 8, 128)

        @pl.when(quarter == 0)
        def _():
            for high in early:
                pl.when(jnp.logical_or(home != high, jnp.logical_not(own)))(functools.partial(deliver, high))

        return 0

    lax.fori_loop(0, 4, make, 0)
    moved = jnp.logical_or(home == early[0], home == early[1])
    last = jnp.logical_or(moved, jnp.logical_not(own))

    def deliver_some(step, _):
        same_y, same_z = rem(step, 2), div(step, 2)
        first = home + (1 - same_y) * turns[4] + (1 - same_z) * turns[5]

        def send(mask):
            deliver(settle(first + subset(turns, mask)))

        pl.when(step > 0)(lambda: send(15))
        pl.when(jnp.logical_and(step > 0, jnp.logical_or(step < 3, last)))(lambda: send(0))
        for mask in (14, 1, 13, 2, 12, 3, 11, 4, 10, 5, 9, 6, 8, 7):
            send(mask)
        return 0

    lax.fori_loop(0, 4, deliver_some, 0)

    @pl.when(own)
    def _():
        pltpu.make_async_copy(tile_ref.at[home], here, recv_sems.at[2]).start()

    pltpu.make_async_copy(xr_ref.at[0:15], xr_ref.at[0:15], send_sems.at[0]).wait()
    pltpu.make_async_copy(part_ref.at[0:7], part_ref.at[0:7], send_sems.at[1]).wait()

    @pl.when(own)
    def _():
        pltpu.make_async_copy(tile_ref.at[0:63], tile_ref.at[0:63], send_sems.at[2]).wait()

    @pl.when(jnp.logical_not(own))
    def _():
        pltpu.make_async_copy(tile_ref, tile_ref, send_sems.at[2]).wait()

    pltpu.make_async_copy(out_ref, out_ref, recv_sems.at[2]).wait()


def shards(traces, phase_coef):
    return pl.pallas_call(
        kernel,
        out_shape=jax.ShapeDtypeStruct((32, 2048), F32),
        in_specs=[
            pl.BlockSpec(memory_space=pl.ANY),
            pl.BlockSpec(memory_space=pl.ANY),
            pl.BlockSpec(memory_space=pl.ANY),
        ],
        out_specs=pl.BlockSpec(memory_space=pl.ANY),
        scratch_shapes=[
            pltpu.SMEM((2, 4), F32),
            pltpu.VMEM((6, 64, 128), F32),
            pltpu.VMEM((5, 36, 8, 128), F32),
            pltpu.VMEM((5, 6, 8, 128), F32),
            pltpu.VMEM((5, 8, 128), F32),
            pltpu.VMEM((3, 12, 4, 8, 128), F32),
            pltpu.VMEM((1536, 512), BF16),
            pltpu.VMEM((512, 384), BF16),
            pltpu.VMEM((16, 32, 128), F32),
            pltpu.VMEM((512, 256), BF16),
            pltpu.VMEM((768, 256), F32),
            pltpu.VMEM((8, 96, 128), F32),
            pltpu.VMEM((8, 96, 128), F32),
            pltpu.VMEM((384, 128), BF16),
            pltpu.VMEM((64, 8, 128), F32),
            pltpu.SemaphoreType.DMA((3,)),
            pltpu.SemaphoreType.DMA((5,)),
        ],
        compiler_params=pltpu.CompilerParams(
            collective_id=0, has_side_effects=True, vmem_limit_bytes=60 * 2**20
        ),
    )(traces, phase_coef, jnp.asarray(tail_table()))


def solution(mesh):
    placed = (P(("gx", "gy"), None), P())
    return jax.shard_map(
        shards, mesh=mesh, in_specs=placed, out_specs=P(("gx", "gy"), None), check_vma=False
    )
```

```python
import functools

import jax
import jax.numpy as jnp
import numpy as np
from jax import lax
from jax.experimental import pallas as pl
from jax.experimental.pallas import tpu as pltpu
from jax.sharding import PartitionSpec as P

ORDER = 6
LOGICAL = pl.DeviceIdType.LOGICAL
F32 = jnp.float32
BF16 = jnp.bfloat16
AMP = 64.0

NODES = 0.5 * np.cos(np.pi * (2.0 * np.arange(ORDER) + 1.0) / (2.0 * ORDER))


def lagrange(points):
    points = np.asarray(points)[..., None, None]
    same = np.eye(ORDER, dtype=bool)
    spread = np.where(same, 1.0, NODES[:, None] - NODES[None, :])
    return np.where(same, 1.0, (points - NODES[None, :]) / spread).prod(-1)


CENTRE = lagrange(0.0)
HALVES = np.stack([((side - 0.5) + NODES) * 0.5 for side in (0, 1)])
TABLE = lagrange(HALVES)
WEIGHT = np.transpose(TABLE, (0, 2, 1))


def tail_table():
    out = np.zeros((ORDER, 64, 128))
    for high in range(64):
        total = np.eye(ORDER)
        for place in range(6):
            total = TABLE[(high >> place) & 1] @ total
        out[:, high, :96] = np.repeat(CENTRE[:, None] * total, 16, axis=1)
    return out.astype(np.float32)


def fit(function, terms):
    u = 0.125 + 0.125 * np.cos(np.pi * (np.arange(200) + 0.5) / 200)
    poly = np.polynomial.chebyshev.Chebyshev.fit(u, function(np.sqrt(u)), terms - 1, domain=[0, 0.25])
    return [float(c) for c in poly.convert(kind=np.polynomial.Polynomial).coef]


SIN = fit(lambda r: np.sin(np.pi * r) / r, 5)
SIN2 = [2.0 * c for c in fit(lambda r: np.sin(np.pi * r) / r, 4)]
COS = fit(lambda r: np.cos(np.pi * r), 5)
COS4 = fit(lambda r: np.cos(np.pi * r), 4)


def horner(coefs, u):
    total = coefs[-1]
    for c in coefs[-2::-1]:
        total = total * u + c
    return total


def turn(c):
    r = c - jnp.floor(c + 0.5)
    u = r * r
    twice = r * horner(SIN2, u)
    half_cos = horner(COS4, u)
    return 1.0 - (0.5 * twice) * twice, twice * half_cos


def turn_cos(c):
    r = c - jnp.floor(c + 0.5)
    twice = r * horner(SIN2, r * r)
    return 1.0 - (0.5 * twice) * twice


def half_turn(y):
    r = 0.5 - y
    u = r * r
    return r * horner(SIN, u), horner(COS, u)


def bend_value(coef, row, y):
    cosine = (0.5 - y) * horner(SIN, (0.5 - y) * (0.5 - y))
    c0, c1, c2, c3 = (coef[row, m] for m in range(4))
    return (c0 - c2) + cosine * ((c1 - 3.0 * c3) + cosine * (2.0 * c2 + cosine * (4.0 * c3)))


def bend_terms(coef, size):
    e1, e2, e3 = (coef[0, m] * float(-2.0 * AMP * np.sin(np.pi * m * size / 2.0)) for m in (1, 2, 3))
    return e1 - e3, 2.0 * e2, 4.0 * e3


def bend_step(terms, middle):
    cosine, sine = half_turn(middle)
    return sine * (terms[0] + cosine * (terms[1] + cosine * terms[2]))


def apply_real(weights, values):
    out = []
    for t in range(ORDER):
        total = weights[t][0] * values[0]
        for s in range(1, ORDER):
            total = total + weights[t][s] * values[s]
        out.append(total)
    return out


def iota(axis):
    return lax.broadcasted_iota(jnp.int32, (8, 128), axis)


def asf(value):
    return value.astype(F32)


def div(a, b):
    return lax.div(a, jnp.int32(b))


def rem(a, b):
    return lax.rem(a, jnp.int32(b))


def subset(deltas, mask):
    total = None
    for k, delta in enumerate(deltas):
        if (mask >> k) & 1:
            total = delta if total is None else total + delta
    return 0 if total is None else total


def abs_flip(bit, turned):
    return 1 - bit if turned else bit


def flips(bits, weights):
    return [weight * (1 - 2 * bit) for bit, weight in zip(bits, weights)]


def lane_parts(classes, core):
    lane = iota(1)
    place = lane >> 4
    x, y, z = (
        (2 * c + e + core) & 3 for c, e in zip(classes, (place >> 2, (place >> 1) & 1, place & 1))
    )
    return (z >> 1) + 2 * y + 8 * x + 32 * (z & 1), lane & 15


def early_levels(coef, box, top, w_ref, p_ref, v_ref):
    sub = iota(0)
    bits = [asf(sub & 1), asf((sub >> 1) & 1), asf(sub >> 2)]
    sign = [2.0 * bit - 1.0 for bit in bits]
    x0 = jnp.full((8, 128), 0.5, F32)
    x1 = x0 + sign[0] * 0.25
    x2 = x1 + sign[1] * 0.125
    word4 = asf(box * 16 + top)
    steps = [
        bend_step(bend_terms(coef, 2.0 ** -(level + 1)), x + sign[level - 1] * 2.0 ** -(level + 2))
        for level, x in ((1, x0), (2, x1), (3, x2))
    ]
    p0_mid = coef[0, 0] - coef[0, 2]

    def turned(values, angles):
        pairs = [(a * c - b * d, a * d + b * c) for (a, b), (c, d) in zip(values, angles)]
        return [a for a, _ in pairs], [b for _, b in pairs]

    linear2 = 2.0 * asf(top & 1) + 0.5
    linear3 = asf(top & 3) + 0.5
    third = [turn(sign[2] * ((linear3 + float(NODES[s])) * 0.25 + steps[2] * p_ref[0, s])) for s in range(ORDER)]
    constants = [[float(WEIGHT[0][t][s]) for s in range(ORDER)] for t in range(ORDER)]

    def by_side(side, values):
        mirror = jnp.broadcast_to(side, (8, 128)) == 1
        picked = [jnp.where(mirror, values[5 - s], values[s]) for s in range(ORDER)]
        out = apply_real(constants, picked)
        return [jnp.where(mirror, out[5 - t], out[t]) for t in range(ORDER)]

    def body(group, _):
        j0, j1 = rem(group, 2), div(group, 2)
        j0f, j1f, groupf = asf(j0), asf(j1), asf(group)
        word = word4 * 4.0 + groupf
        start = 0.5 * (j0f + 0.5) + AMP * p0_mid * bend_value(coef, 1, (word + 0.5) * 2.0**-12)
        real, imag = [], []
        for s in range(ORDER):
            node = float(NODES[s])
            p1 = bend_value(coef, 1, (word + (0.5 + node)) * 2.0**-12)
            c, d = turn(start + sign[0] * ((groupf + (0.5 + node)) * 0.25 + steps[0] * p1))
            real.append(c * float(CENTRE[s]))
            imag.append(d * float(CENTRE[s]))
        values = list(zip(by_side(j0, real), by_side(j0, imag)))
        word = word4 * 2.0 + j1f
        angles = []
        for s in range(ORDER):
            node = float(NODES[s])
            p1 = bend_value(coef, 1, (word + (0.5 + node)) * 2.0**-11)
            angles.append(turn(sign[1] * (((linear2 + j1f) + node) * 0.25 + steps[1] * p1)))
        values = list(zip(*(by_side(j1, part) for part in turned(values, angles))))
        weights = [[w_ref[0, ORDER * t + s] for s in range(ORDER)] for t in range(ORDER)]
        for c, part in enumerate(turned(values, third)):
            for t, value in enumerate(apply_real(weights, part)):
                v_ref[0, 2 * t + c, group] = value
        return 0

    lax.fori_loop(0, 4, body, 0)


def late_setup(coef, box, top, w_ref, p_ref, c_ref):
    full = box * 16 + top

    def body(i, scale):
        word = full >> i
        pick = (word & 1) == 1
        for t in range(ORDER):
            for s in range(ORDER):
                w_ref[i, ORDER * t + s] = jnp.where(pick, float(WEIGHT[1][t][s]), float(WEIGHT[0][t][s]))
        for s in range(ORDER):
            p_ref[i, s] = bend_value(coef, 1, (asf(word) + float(0.5 + NODES[s])) * scale)
        return scale * 2.0

    lax.fori_loop(0, 5, body, jnp.float32(2.0**-10))
    turn_of = top & 7

    def by_lane(values):
        out = jnp.full((8, 128), float(values[ORDER - 1]), F32)
        for t in range(ORDER - 1):
            out = jnp.where(turn_of == t, float(values[t]), out)
        return out

    e1, e2, e3 = (coef[0, m] * by_lane(-2.0 * AMP * np.sin(np.pi * m * NODES / 128.0)) for m in (1, 2, 3))
    node = by_lane(NODES)
    c_ref[0] = node
    c_ref[1] = e1 - e3
    c_ref[2] = 2.0 * e2
    c_ref[3] = 4.0 * e3
    c_ref[4] = node * (asf(box) + 0.5)


def spread(value, t):
    return jnp.take_along_axis(value, (iota(1) & 120) + t, axis=1)


def late_levels(coef, box, top, order, w_ref, p_ref, c_ref, v_ref, g_ref, between):
    sub = iota(0)
    x3 = asf(4 * (sub & 1) + (sub & 2) + (sub >> 2)) * 0.125 + 0.0625
    full = box * 16 + top
    terms = [bend_terms(coef, 2.0 ** -(level + 1)) for level in (4, 5, 6)]

    def sign_of(bit):
        return (2 * bit - 1).astype(F32)

    def turns(i, level_terms, shift, parent, sign):
        steps = bend_step(level_terms, parent + sign * shift)
        linear = asf((full >> i) & 3) + 0.5
        return [turn(sign * ((linear + float(NODES[s])) * 0.25 + steps * p_ref[i, s])) for s in range(ORDER)]

    def level_step(level, q3, q4):
        first = level == 4
        i = level - 3
        parent = x3 + jnp.where(first, 0.0, sign_of(q3) * 2.0**-5)
        sign = jnp.where(first, sign_of(q3), sign_of(q4))
        level_terms = [jnp.where(first, a, b) for a, b in zip(terms[0], terms[1])]
        real, imag = [], []
        for s, (c, d) in enumerate(turns(i, level_terms, jnp.where(first, 2.0**-6, 2.0**-7), parent, sign)):
            a, b = v_ref[i - 1, 2 * s], v_ref[i - 1, 2 * s + 1]
            real.append(a * c - b * d)
            imag.append(a * d + b * c)
        weights = [[w_ref[i, ORDER * t + s] for s in range(ORDER)] for t in range(ORDER)]
        for c, values in enumerate((real, imag)):
            for t, value in enumerate(apply_real(weights, values)):
                v_ref[i, 2 * t + c] = value

    def last_step(parent, bit, place):
        sign = sign_of(bit)
        middle = parent + sign * 2.0**-7 + c_ref[0] * (1.0 / 128.0)
        steps = bend_step((c_ref[1], c_ref[2], c_ref[3]), middle)
        switch = [turn((c_ref[4] + c_ref[0] * float(NODES[u])) + steps * p_ref[4, u]) for u in range(ORDER)]
        merged = []
        for s, (c, d) in enumerate(turns(3, terms[2], 2.0**-8, parent, sign)):
            a = b = None
            for u in range(ORDER):
                weight = w_ref[3, ORDER * u + s]
                a = switch[u][0] * weight if a is None else a + switch[u][0] * weight
                b = switch[u][1] * weight if b is None else b + switch[u][1] * weight
            merged.append((a * c - b * d, a * d + b * c))
        parts = [v_ref[2, 2 * s] + v_ref[2, 2 * s + 1] for s in range(ORDER)]
        for t in range(ORDER):
            k1 = k2 = k3 = None
            for s in range(ORDER):
                c, d = spread(merged[s][0], t), spread(merged[s][1], t)
                m1, m2, m3 = parts[s] * c, v_ref[2, 2 * s] * (d - c), v_ref[2, 2 * s + 1] * (c + d)
                k1 = m1 if k1 is None else k1 + m1
                k2 = m2 if k2 is None else k2 + m2
                k3 = m3 if k3 is None else k3 + m3
            real, imag = k1 - k3, k1 + k2
            rows = pl.ds(pl.multiple_of(place * 192 + 16 * t, 16), 16)
            rows_low = pl.ds(pl.multiple_of(place * 192 + 96 + 16 * t, 16), 16)
            for j in range(4):
                both = jnp.concatenate([real[j], imag[j]], axis=0)
                high = both.astype(BF16)
                g_ref[rows, 128 * j : 128 * (j + 1)] = high
                g_ref[rows_low, 128 * j : 128 * (j + 1)] = (both - high.astype(F32)).astype(BF16)

    def over(n, _):
        @pl.when(n >= 3)
        def _():
            between(n - 3)

        @pl.when(n < 4)
        def _():
            q3, q4 = order(div(n, 2)), rem(n, 2)

            def levels(level, _):
                level_step(level, q3, q4)
                return 0

            lax.fori_loop(4 + q4, 6, levels, 0)
            x5 = x3 + (sign_of(q3) * 2.0**-5 + sign_of(q4) * 2.0**-6)

            def over5(q5, _):
                last_step(x5, q5, 4 * q3 + q4 + 2 * q5)
                return 0

            lax.fori_loop(0, 2, over5, 0)

        return 0

    lax.fori_loop(0, 5, over, 0)


def last_weights(coef, group, tail_ref, h_ref):
    sub, lane = iota(0), iota(1)
    own = lane & 7
    same = sub == own
    box6 = 32 * (own & 1) + 8 * (own & 2) + 2 * (own & 4)
    box6 = box6 + (4 * rem(group, 2) + 2 * rem(div(group, 2), 2) + div(group, 4))
    inner = 32 * (sub & 1) + 8 * (sub & 2) + 2 * (sub & 4)
    base = box6 * 64 + inner
    quarter = 0.25 * asf((lane >> 3) & 1)
    p1_mid = coef[1, 0] - coef[1, 2]

    def rows_of(r):
        centre = (asf(base + (4 * rem(r, 2) + 2 * rem(div(r, 2), 2) + div(r, 4))) + 0.5) * 2.0**-12
        total = None
        for t in range(ORDER):
            node = float(NODES[t])
            steps = bend_step(bend_terms(coef, node / 4096.0), centre + node / 8192.0)
            term = turn_cos((quarter - 0.5 * node) - steps * p1_mid)
            term = term * tail_ref[t, pl.ds(pl.multiple_of(8 * r, 8), 8), :]
            total = term if total is None else total + term
        return total

    def body(r, _):
        total = rows_of(r)
        for k in range(0, 8, 2):
            both = jnp.concatenate(
                [jnp.where(same, jnp.broadcast_to(total[k + n : k + n + 1], (8, 128)), 0.0) for n in range(2)], axis=0
            )
            high = both.astype(BF16)
            rows = pl.ds(pl.multiple_of(64 * r + 8 * k, 16), 16)
            h_ref[rows, 0:128] = high
            h_ref[rows, 128:256] = (both - high.astype(F32)).astype(BF16)
            h_ref[rows, 256:384] = high
        return 0

    lax.fori_loop(0, 8, body, 0)


def kernel(
    x_ref,
    coef_hbm,
    tail_hbm,
    out_ref,
    coef_ref,
    tail_ref,
    w_ref,
    p_ref,
    c_ref,
    v_ref,
    g_ref,
    h_ref,
    xr_ref,
    xs_ref,
    part_ref,
    rr_ref,
    sum_ref,
    tile_ref,
    send_sems,
    recv_sems,
):
    fetch_coef = pltpu.make_async_copy(coef_hbm, coef_ref, recv_sems.at[3])
    fetch_tail = pltpu.make_async_copy(tail_hbm, tail_ref, recv_sems.at[4])
    fetch_coef.start()
    fetch_tail.start()
    gx, gy = lax.axis_index("gx"), lax.axis_index("gy")
    core = rem(gy, 2)
    zl, xs = div(gx, 4), rem(gx, 4)
    xh, xl = div(xs, 2), rem(xs, 2)
    yh, yl, zh = div(gy, 8), rem(div(gy, 4), 2), rem(div(gy, 2), 2)
    me = gx * 16 + gy
    highs, lows = (xh, yh, zh), (xl, yl, zl)
    unlike = [h + l - 2 * h * l for h, l in zip(highs, lows)]
    to_a = [16 * (1 - 2 * xl), 4 * (1 - 2 * yl), 64 * (1 - 2 * zl)]
    to_b = [16 * (3 - 2 * xs), 4 * (3 - 2 * (2 * yh + yl)), 2 * (1 - 2 * zh) + 64 * (1 - 2 * zl)]
    to_class = [a + core * (b - a) for a, b in zip(to_a, to_b)]
    to_group = [b + core * (a - b) for a, b in zip(to_a, to_b)]
    to_core = 1 - 2 * core
    class_a, class_b = highs, [1 - d for d in unlike]
    place_a, place_b = lows, [1 - l for l in lows]
    group_a, group_b = [1 - d for d in unlike], [1 - h for h in highs]

    def mine(for_a, for_b):
        return [a + core * (b - a) for a, b in zip(for_a, for_b)]

    def others(for_a, for_b):
        return [b + core * (a - b) for a, b in zip(for_a, for_b)]

    def number(values):
        return values[0] + 2 * values[1] + 4 * values[2]

    classes, groups = mine(class_a, class_b), mine(group_a, group_b)
    target = number(classes)
    block = number(groups) + 8 * core

    barrier = pltpu.get_barrier_semaphore()
    for mask in range(1, 16):
        source = me + subset(to_class + [to_core], mask)
        pl.semaphore_signal(barrier, inc=1, device_id=source, device_id_type=LOGICAL)
    for mask in range(1, 8):
        pl.semaphore_signal(barrier, inc=1, device_id=me + subset(to_group, mask), device_id_type=LOGICAL)
    box, top = lane_parts(classes, core)
    fetch_coef.wait()
    late_setup(coef_ref, box, top, w_ref, p_ref, c_ref)
    pl.semaphore_wait(barrier, 22)

    def columns(m):
        return x_ref.at[:, pl.ds(pl.multiple_of(m * 128, 128), 128)]

    own_slot = 2 * number(mine(place_a, place_b)[::-1]) + core
    other_slot = 2 * number(others(place_a, place_b)[::-1]) + core
    other_groups = others(group_a, group_b)
    other_block = number(other_groups) + 8 * (1 - core)
    for mask in range(7, -1, -1):
        routes = [(other_block, other_groups, other_slot, me + to_core + subset(to_group, mask))]
        if mask:
            routes.append((block, groups, own_slot, me + subset(to_class, mask)))
        for first, group_bits, slot, device in routes:
            pltpu.make_async_remote_copy(
                src_ref=columns(first + subset(flips(group_bits, (1, 2, 4)), mask)),
                dst_ref=xr_ref.at[slot],
                send_sem=send_sems.at[0],
                recv_sem=recv_sems.at[0],
                device_id=device,
                device_id_type=LOGICAL,
            ).start()
    pltpu.make_async_copy(columns(block), xr_ref.at[own_slot], recv_sems.at[0]).start()
    early_levels(coef_ref, box, top, w_ref, p_ref, v_ref)

    def order(h):
        return classes[0] + (1 - h) * (1 - 2 * classes[0])

    def split(i, _):
        for j in range(4):
            piece = jnp.concatenate([xr_ref[2 * i + s, pl.ds(j, 8, stride=4), :] for s in range(2)], axis=0)
            high = piece.astype(BF16)
            rows = pl.ds(pl.multiple_of(128 * j + 16 * i, 16), 16)
            xs_ref[rows, 0:128] = high
            xs_ref[rows, 128:256] = (piece - high.astype(F32)).astype(BF16)
        return 0

    def half(h):
        @pl.when(h == 0)
        def _():
            pltpu.make_async_copy(xr_ref, xr_ref, recv_sems.at[0]).wait()
            lax.fori_loop(0, 8, split, 0, unroll=4)

        q3 = order(h)
        far = (1 - h) * to_group[0]
        for mask in range(3, -1, -1):
            i = classes[1] + 2 * classes[2] + subset(flips(classes[1:], (1, 2)), mask)
            rows = pl.ds(pl.multiple_of((4 * q3 + i) * 192, 16), 192)
            wide = jnp.dot(g_ref[rows, :], xs_ref[...], preferred_element_type=F32)
            part = wide[0:96, 0:128] + (wide[0:96, 128:256] + wide[96:192, 0:128])

            def send():
                part_ref[4 * q3 + i] = part
                pltpu.make_async_remote_copy(
                    src_ref=part_ref.at[4 * q3 + i],
                    dst_ref=rr_ref.at[target],
                    send_sem=send_sems.at[1],
                    recv_sem=recv_sems.at[1],
                    device_id=me + far + subset(to_group[1:], mask),
                    device_id_type=LOGICAL,
                ).start()

            if mask:
                send()
            else:
                pl.when(h == 0)(send)

                @pl.when(h == 1)
                def _():
                    rr_ref[target] = part

    late_levels(coef_ref, box, top, order, w_ref, p_ref, c_ref, v_ref, g_ref, half)
    fetch_tail.wait()
    for i in range(3):
        sum_ref[128 * i + 96 : 128 * i + 128, :] = jnp.zeros((32, 128), BF16)
    last_weights(coef_ref, target, tail_ref, h_ref)
    pltpu.make_async_copy(rr_ref.at[0:7], rr_ref.at[0:7], recv_sems.at[1]).wait()

    def add(i, _):
        rows = pl.ds(pl.multiple_of(16 * i, 16), 16)
        total = rr_ref[0, rows, :]
        for k in range(1, 8):
            total = total + rr_ref[k, rows, :]
        high = total.astype(BF16)
        sum_ref[rows, :] = high
        sum_ref[pl.ds(pl.multiple_of(128 + 16 * i, 16), 16), :] = high
        sum_ref[pl.ds(pl.multiple_of(256 + 16 * i, 16), 16), :] = (total - high.astype(F32)).astype(BF16)
        return 0

    lax.fori_loop(0, 6, add, 0, unroll=True)

    home = zh + 2 * yl + 4 * yh + 8 * xl + 16 * xh + 32 * zl
    own = core == classes[2]
    row = pl.multiple_of((classes[0] + 2 * classes[1]) * 8, 8)
    here = out_ref.at[pl.ds(row, 8), pl.ds(pl.multiple_of(block * 128, 128), 128)]
    turns = flips((zh, xl, xh, yh, yl, zl), (1, 8, 16, 4, 2, 32))

    def deliver(high):
        pltpu.make_async_remote_copy(
            src_ref=tile_ref.at[high],
            dst_ref=here,
            send_sem=send_sems.at[2],
            recv_sem=recv_sems.at[2],
            device_id=2 * high + classes[2],
            device_id_type=LOGICAL,
        ).start()

    early = (0, 8)
    lost = (63 - home, home + subset(turns, 48))
    instead = [jnp.where(lost[n] == early[1 - n], lost[1 - n], lost[n]) for n in range(2)]

    def settle(high):
        return jnp.where(high == early[0], instead[0], jnp.where(high == early[1], instead[1], high))

    tile_ref[...] = jnp.dot(h_ref[...], sum_ref[...], preferred_element_type=F32).reshape(64, 8, 128)
    for high in early:
        pl.when(jnp.logical_or(home != high, jnp.logical_not(own)))(functools.partial(deliver, high))
    moved = jnp.logical_or(home == early[0], home == early[1])
    last = jnp.logical_or(moved, jnp.logical_not(own))

    def deliver_some(step, _):
        same_y, same_z = rem(step, 2), div(step, 2)
        first = home + (1 - same_y) * turns[4] + (1 - same_z) * turns[5]

        def send(mask):
            deliver(settle(first + subset(turns, mask)))

        pl.when(step > 0)(lambda: send(15))
        pl.when(jnp.logical_and(step > 0, jnp.logical_or(step < 3, last)))(lambda: send(0))
        for mask in (14, 1, 13, 2, 12, 3, 11, 4, 10, 5, 9, 6, 8, 7):
            send(mask)
        return 0

    lax.fori_loop(0, 4, deliver_some, 0)

    @pl.when(own)
    def _():
        pltpu.make_async_copy(tile_ref.at[home], here, recv_sems.at[2]).start()

    pltpu.make_async_copy(xr_ref.at[0:15], xr_ref.at[0:15], send_sems.at[0]).wait()
    pltpu.make_async_copy(part_ref.at[0:7], part_ref.at[0:7], send_sems.at[1]).wait()

    @pl.when(own)
    def _():
        pltpu.make_async_copy(tile_ref.at[0:63], tile_ref.at[0:63], send_sems.at[2]).wait()

    @pl.when(jnp.logical_not(own))
    def _():
        pltpu.make_async_copy(tile_ref, tile_ref, send_sems.at[2]).wait()

    pltpu.make_async_copy(out_ref, out_ref, recv_sems.at[2]).wait()


def shards(traces, phase_coef):
    return pl.pallas_call(
        kernel,
        out_shape=jax.ShapeDtypeStruct((32, 2048), F32),
        in_specs=[
            pl.BlockSpec(memory_space=pl.ANY),
            pl.BlockSpec(memory_space=pl.ANY),
            pl.BlockSpec(memory_space=pl.ANY),
        ],
        out_specs=pl.BlockSpec(memory_space=pl.ANY),
        scratch_shapes=[
            pltpu.SMEM((2, 4), F32),
            pltpu.VMEM((6, 64, 128), F32),
            pltpu.VMEM((5, 36, 8, 128), F32),
            pltpu.VMEM((5, 6, 8, 128), F32),
            pltpu.VMEM((5, 8, 128), F32),
            pltpu.VMEM((3, 12, 4, 8, 128), F32),
            pltpu.VMEM((1536, 512), BF16),
            pltpu.VMEM((512, 384), BF16),
            pltpu.VMEM((16, 32, 128), F32),
            pltpu.VMEM((512, 256), BF16),
            pltpu.VMEM((8, 96, 128), F32),
            pltpu.VMEM((8, 96, 128), F32),
            pltpu.VMEM((384, 128), BF16),
            pltpu.VMEM((64, 8, 128), F32),
            pltpu.SemaphoreType.DMA((3,)),
            pltpu.SemaphoreType.DMA((5,)),
        ],
        compiler_params=pltpu.CompilerParams(
            collective_id=0, has_side_effects=True, vmem_limit_bytes=60 * 2**20
        ),
    )(traces, phase_coef, jnp.asarray(tail_table()))


def solution(mesh):
    placed = (P(("gx", "gy"), None), P())
    return jax.shard_map(
        shards, mesh=mesh, in_specs=placed, out_specs=P(("gx", "gy"), None), check_vma=False
    )
```

```python
import functools

import jax
import jax.numpy as jnp
import numpy as np
from jax import lax
from jax.experimental import pallas as pl
from jax.experimental.pallas import tpu as pltpu
from jax.sharding import PartitionSpec as P

ORDER = 6
LOGICAL = pl.DeviceIdType.LOGICAL
F32 = jnp.float32
BF16 = jnp.bfloat16
AMP = 64.0

NODES = 0.5 * np.cos(np.pi * (2.0 * np.arange(ORDER) + 1.0) / (2.0 * ORDER))


def lagrange(points):
    points = np.asarray(points)[..., None, None]
    same = np.eye(ORDER, dtype=bool)
    spread = np.where(same, 1.0, NODES[:, None] - NODES[None, :])
    return np.where(same, 1.0, (points - NODES[None, :]) / spread).prod(-1)


CENTRE = lagrange(0.0)
HALVES = np.stack([((side - 0.5) + NODES) * 0.5 for side in (0, 1)])
TABLE = lagrange(HALVES)
WEIGHT = np.transpose(TABLE, (0, 2, 1))


def tail_table():
    out = np.zeros((ORDER, 64, 128))
    for high in range(64):
        total = np.eye(ORDER)
        for place in range(6):
            total = TABLE[(high >> place) & 1] @ total
        out[:, high, :96] = np.repeat(CENTRE[:, None] * total, 16, axis=1)
    return out.astype(np.float32)


def fit(function, terms):
    u = 0.125 + 0.125 * np.cos(np.pi * (np.arange(200) + 0.5) / 200)
    poly = np.polynomial.chebyshev.Chebyshev.fit(u, function(np.sqrt(u)), terms - 1, domain=[0, 0.25])
    return [float(c) for c in poly.convert(kind=np.polynomial.Polynomial).coef]


SIN = fit(lambda r: np.sin(np.pi * r) / r, 5)
SIN2 = [2.0 * c for c in fit(lambda r: np.sin(np.pi * r) / r, 4)]
COS = fit(lambda r: np.cos(np.pi * r), 5)
COS4 = fit(lambda r: np.cos(np.pi * r), 4)


def horner(coefs, u):
    total = coefs[-1]
    for c in coefs[-2::-1]:
        total = total * u + c
    return total


def turn(c):
    r = c - jnp.floor(c + 0.5)
    u = r * r
    twice = r * horner(SIN2, u)
    half_cos = horner(COS4, u)
    return 1.0 - (0.5 * twice) * twice, twice * half_cos


def turn_cos(c):
    r = c - jnp.floor(c + 0.5)
    twice = r * horner(SIN2, r * r)
    return 1.0 - (0.5 * twice) * twice


def half_turn(y):
    r = 0.5 - y
    u = r * r
    return r * horner(SIN, u), horner(COS, u)


def bend_value(coef, row, y):
    cosine = (0.5 - y) * horner(SIN, (0.5 - y) * (0.5 - y))
    c0, c1, c2, c3 = (coef[row, m] for m in range(4))
    return (c0 - c2) + cosine * ((c1 - 3.0 * c3) + cosine * (2.0 * c2 + cosine * (4.0 * c3)))


def bend_terms(coef, size):
    e1, e2, e3 = (coef[0, m] * float(-2.0 * AMP * np.sin(np.pi * m * size / 2.0)) for m in (1, 2, 3))
    return e1 - e3, 2.0 * e2, 4.0 * e3


def bend_step(terms, middle):
    cosine, sine = half_turn(middle)
    return sine * (terms[0] + cosine * (terms[1] + cosine * terms[2]))


def apply_real(weights, values):
    out = []
    for t in range(ORDER):
        total = weights[t][0] * values[0]
        for s in range(1, ORDER):
            total = total + weights[t][s] * values[s]
        out.append(total)
    return out


def iota(axis):
    return lax.broadcasted_iota(jnp.int32, (8, 128), axis)


def asf(value):
    return value.astype(F32)


def div(a, b):
    return lax.div(a, jnp.int32(b))


def rem(a, b):
    return lax.rem(a, jnp.int32(b))


def subset(deltas, mask):
    total = None
    for k, delta in enumerate(deltas):
        if (mask >> k) & 1:
            total = delta if total is None else total + delta
    return 0 if total is None else total


def abs_flip(bit, turned):
    return 1 - bit if turned else bit


def flips(bits, weights):
    return [weight * (1 - 2 * bit) for bit, weight in zip(bits, weights)]


def lane_parts(classes, core):
    lane = iota(1)
    place = lane >> 4
    x, y, z = (
        (2 * c + e + core) & 3 for c, e in zip(classes, (place >> 2, (place >> 1) & 1, place & 1))
    )
    return (z >> 1) + 2 * y + 8 * x + 32 * (z & 1), lane & 15


def early_levels(coef, box, top, w_ref, p_ref, v_ref):
    sub = iota(0)
    bits = [asf(sub & 1), asf((sub >> 1) & 1), asf(sub >> 2)]
    sign = [2.0 * bit - 1.0 for bit in bits]
    x0 = jnp.full((8, 128), 0.5, F32)
    x1 = x0 + sign[0] * 0.25
    x2 = x1 + sign[1] * 0.125
    word4 = asf(box * 16 + top)
    steps = [
        bend_step(bend_terms(coef, 2.0 ** -(level + 1)), x + sign[level - 1] * 2.0 ** -(level + 2))
        for level, x in ((1, x0), (2, x1), (3, x2))
    ]
    p0_mid = coef[0, 0] - coef[0, 2]

    def turned(values, angles):
        pairs = [(a * c - b * d, a * d + b * c) for (a, b), (c, d) in zip(values, angles)]
        return [a for a, _ in pairs], [b for _, b in pairs]

    linear2 = 2.0 * asf(top & 1) + 0.5
    linear3 = asf(top & 3) + 0.5
    third = [turn(sign[2] * ((linear3 + float(NODES[s])) * 0.25 + steps[2] * p_ref[0, s])) for s in range(ORDER)]
    constants = [[float(WEIGHT[0][t][s]) for s in range(ORDER)] for t in range(ORDER)]

    def by_side(side, values):
        mirror = jnp.broadcast_to(side, (8, 128)) == 1
        picked = [jnp.where(mirror, values[5 - s], values[s]) for s in range(ORDER)]
        out = apply_real(constants, picked)
        return [jnp.where(mirror, out[5 - t], out[t]) for t in range(ORDER)]

    def body(group, _):
        j0, j1 = rem(group, 2), div(group, 2)
        j0f, j1f, groupf = asf(j0), asf(j1), asf(group)
        word = word4 * 4.0 + groupf
        start = 0.5 * (j0f + 0.5) + AMP * p0_mid * bend_value(coef, 1, (word + 0.5) * 2.0**-12)
        real, imag = [], []
        for s in range(ORDER):
            node = float(NODES[s])
            p1 = bend_value(coef, 1, (word + (0.5 + node)) * 2.0**-12)
            c, d = turn(start + sign[0] * ((groupf + (0.5 + node)) * 0.25 + steps[0] * p1))
            real.append(c * float(CENTRE[s]))
            imag.append(d * float(CENTRE[s]))
        values = list(zip(by_side(j0, real), by_side(j0, imag)))
        word = word4 * 2.0 + j1f
        angles = []
        for s in range(ORDER):
            node = float(NODES[s])
            p1 = bend_value(coef, 1, (word + (0.5 + node)) * 2.0**-11)
            angles.append(turn(sign[1] * (((linear2 + j1f) + node) * 0.25 + steps[1] * p1)))
        values = list(zip(*(by_side(j1, part) for part in turned(values, angles))))
        weights = [[w_ref[0, ORDER * t + s] for s in range(ORDER)] for t in range(ORDER)]
        for c, part in enumerate(turned(values, third)):
            for t, value in enumerate(apply_real(weights, part)):
                v_ref[0, 2 * t + c, group] = value
        return 0

    lax.fori_loop(0, 4, body, 0)


def late_setup(coef, box, top, w_ref, p_ref, c_ref):
    full = box * 16 + top

    def body(i, scale):
        word = full >> i
        pick = (word & 1) == 1
        for t in range(ORDER):
            for s in range(ORDER):
                w_ref[i, ORDER * t + s] = jnp.where(pick, float(WEIGHT[1][t][s]), float(WEIGHT[0][t][s]))
        for s in range(ORDER):
            p_ref[i, s] = bend_value(coef, 1, (asf(word) + float(0.5 + NODES[s])) * scale)
        return scale * 2.0

    lax.fori_loop(0, 5, body, jnp.float32(2.0**-10))
    turn_of = top & 7

    def by_lane(values):
        out = jnp.full((8, 128), float(values[ORDER - 1]), F32)
        for t in range(ORDER - 1):
            out = jnp.where(turn_of == t, float(values[t]), out)
        return out

    e1, e2, e3 = (coef[0, m] * by_lane(-2.0 * AMP * np.sin(np.pi * m * NODES / 128.0)) for m in (1, 2, 3))
    node = by_lane(NODES)
    c_ref[0] = node
    c_ref[1] = e1 - e3
    c_ref[2] = 2.0 * e2
    c_ref[3] = 4.0 * e3
    c_ref[4] = node * (asf(box) + 0.5)


def spread(value, t):
    return jnp.take_along_axis(value, (iota(1) & 120) + t, axis=1)


def late_levels(coef, box, top, order, w_ref, p_ref, c_ref, v_ref, g_ref, between):
    sub = iota(0)
    x3 = asf(4 * (sub & 1) + (sub & 2) + (sub >> 2)) * 0.125 + 0.0625
    full = box * 16 + top
    terms = [bend_terms(coef, 2.0 ** -(level + 1)) for level in (4, 5, 6)]

    def sign_of(bit):
        return (2 * bit - 1).astype(F32)

    def turns(i, level_terms, shift, parent, sign):
        steps = bend_step(level_terms, parent + sign * shift)
        linear = asf((full >> i) & 3) + 0.5
        return [turn(sign * ((linear + float(NODES[s])) * 0.25 + steps * p_ref[i, s])) for s in range(ORDER)]

    def level_step(level, q3, q4):
        first = level == 4
        i = level - 3
        parent = x3 + jnp.where(first, 0.0, sign_of(q3) * 2.0**-5)
        sign = jnp.where(first, sign_of(q3), sign_of(q4))
        level_terms = [jnp.where(first, a, b) for a, b in zip(terms[0], terms[1])]
        real, imag = [], []
        for s, (c, d) in enumerate(turns(i, level_terms, jnp.where(first, 2.0**-6, 2.0**-7), parent, sign)):
            a, b = v_ref[i - 1, 2 * s], v_ref[i - 1, 2 * s + 1]
            real.append(a * c - b * d)
            imag.append(a * d + b * c)
        weights = [[w_ref[i, ORDER * t + s] for s in range(ORDER)] for t in range(ORDER)]
        for c, values in enumerate((real, imag)):
            for t, value in enumerate(apply_real(weights, values)):
                v_ref[i, 2 * t + c] = value

    def last_step(parent, bit, place):
        sign = sign_of(bit)
        middle = parent + sign * 2.0**-7 + c_ref[0] * (1.0 / 128.0)
        steps = bend_step((c_ref[1], c_ref[2], c_ref[3]), middle)
        switch = [turn((c_ref[4] + c_ref[0] * float(NODES[u])) + steps * p_ref[4, u]) for u in range(ORDER)]
        merged = []
        for s, (c, d) in enumerate(turns(3, terms[2], 2.0**-8, parent, sign)):
            a = b = None
            for u in range(ORDER):
                weight = w_ref[3, ORDER * u + s]
                a = switch[u][0] * weight if a is None else a + switch[u][0] * weight
                b = switch[u][1] * weight if b is None else b + switch[u][1] * weight
            merged.append((a * c - b * d, a * d + b * c))
        parts = [v_ref[2, 2 * s] + v_ref[2, 2 * s + 1] for s in range(ORDER)]
        for t in range(ORDER):
            k1 = k2 = k3 = None
            for s in range(ORDER):
                c, d = spread(merged[s][0], t), spread(merged[s][1], t)
                m1, m2, m3 = parts[s] * c, v_ref[2, 2 * s] * (d - c), v_ref[2, 2 * s + 1] * (c + d)
                k1 = m1 if k1 is None else k1 + m1
                k2 = m2 if k2 is None else k2 + m2
                k3 = m3 if k3 is None else k3 + m3
            real, imag = k1 - k3, k1 + k2
            rows = pl.ds(pl.multiple_of(place * 192 + 16 * t, 16), 16)
            rows_low = pl.ds(pl.multiple_of(place * 192 + 96 + 16 * t, 16), 16)
            for j in range(4):
                both = jnp.concatenate([real[j], imag[j]], axis=0)
                high = both.astype(BF16)
                g_ref[rows, 128 * j : 128 * (j + 1)] = high
                g_ref[rows_low, 128 * j : 128 * (j + 1)] = (both - high.astype(F32)).astype(BF16)

    def over(n, _):
        @pl.when(n >= 4)
        def _():
            between(n - 4)

        @pl.when(n < 4)
        def _():
            q3, q4 = order(div(n, 2)), rem(n, 2)

            def levels(level, _):
                level_step(level, q3, q4)
                return 0

            lax.fori_loop(4 + q4, 6, levels, 0)
            x5 = x3 + (sign_of(q3) * 2.0**-5 + sign_of(q4) * 2.0**-6)

            def over5(q5, _):
                last_step(x5, q5, 4 * q3 + q4 + 2 * q5)
                return 0

            lax.fori_loop(0, 2, over5, 0)

        return 0

    lax.fori_loop(0, 6, over, 0)


def last_weights(coef, group, tail_ref, h_ref):
    sub, lane = iota(0), iota(1)
    own = lane & 7
    same = sub == own
    box6 = 32 * (own & 1) + 8 * (own & 2) + 2 * (own & 4)
    box6 = box6 + (4 * rem(group, 2) + 2 * rem(div(group, 2), 2) + div(group, 4))
    inner = 32 * (sub & 1) + 8 * (sub & 2) + 2 * (sub & 4)
    base = box6 * 64 + inner
    quarter = 0.25 * asf((lane >> 3) & 1)
    p1_mid = coef[1, 0] - coef[1, 2]

    def rows_of(r):
        centre = (asf(base + (4 * rem(r, 2) + 2 * rem(div(r, 2), 2) + div(r, 4))) + 0.5) * 2.0**-12
        total = None
        for t in range(ORDER):
            node = float(NODES[t])
            steps = bend_step(bend_terms(coef, node / 4096.0), centre + node / 8192.0)
            term = turn_cos((quarter - 0.5 * node) - steps * p1_mid)
            term = term * tail_ref[t, pl.ds(pl.multiple_of(8 * r, 8), 8), :]
            total = term if total is None else total + term
        return total

    def body(r, _):
        total = rows_of(r)
        for k in range(0, 8, 2):
            both = jnp.concatenate(
                [jnp.where(same, jnp.broadcast_to(total[k + n : k + n + 1], (8, 128)), 0.0) for n in range(2)], axis=0
            )
            high = both.astype(BF16)
            rows = pl.ds(pl.multiple_of(64 * r + 8 * k, 16), 16)
            h_ref[rows, 0:128] = high
            h_ref[rows, 128:256] = (both - high.astype(F32)).astype(BF16)
            h_ref[rows, 256:384] = high
        return 0

    lax.fori_loop(0, 8, body, 0)


def kernel(
    x_ref,
    coef_hbm,
    tail_hbm,
    out_ref,
    coef_ref,
    tail_ref,
    w_ref,
    p_ref,
    c_ref,
    v_ref,
    g_ref,
    h_ref,
    xr_ref,
    xs_ref,
    part_ref,
    rr_ref,
    sum_ref,
    tile_ref,
    send_sems,
    recv_sems,
):
    fetch_coef = pltpu.make_async_copy(coef_hbm, coef_ref, recv_sems.at[3])
    fetch_tail = pltpu.make_async_copy(tail_hbm, tail_ref, recv_sems.at[4])
    fetch_coef.start()
    fetch_tail.start()
    gx, gy = lax.axis_index("gx"), lax.axis_index("gy")
    core = rem(gy, 2)
    zl, xs = div(gx, 4), rem(gx, 4)
    xh, xl = div(xs, 2), rem(xs, 2)
    yh, yl, zh = div(gy, 8), rem(div(gy, 4), 2), rem(div(gy, 2), 2)
    me = gx * 16 + gy
    highs, lows = (xh, yh, zh), (xl, yl, zl)
    unlike = [h + l - 2 * h * l for h, l in zip(highs, lows)]
    to_a = [16 * (1 - 2 * xl), 4 * (1 - 2 * yl), 64 * (1 - 2 * zl)]
    to_b = [16 * (3 - 2 * xs), 4 * (3 - 2 * (2 * yh + yl)), 2 * (1 - 2 * zh) + 64 * (1 - 2 * zl)]
    to_class = [a + core * (b - a) for a, b in zip(to_a, to_b)]
    to_group = [b + core * (a - b) for a, b in zip(to_a, to_b)]
    to_core = 1 - 2 * core
    class_a, class_b = highs, [1 - d for d in unlike]
    place_a, place_b = lows, [1 - l for l in lows]
    group_a, group_b = [1 - d for d in unlike], [1 - h for h in highs]

    def mine(for_a, for_b):
        return [a + core * (b - a) for a, b in zip(for_a, for_b)]

    def others(for_a, for_b):
        return [b + core * (a - b) for a, b in zip(for_a, for_b)]

    def number(values):
        return values[0] + 2 * values[1] + 4 * values[2]

    classes, groups = mine(class_a, class_b), mine(group_a, group_b)
    target = number(classes)
    block = number(groups) + 8 * core

    barrier = pltpu.get_barrier_semaphore()
    for mask in range(1, 16):
        source = me + subset(to_class + [to_core], mask)
        pl.semaphore_signal(barrier, inc=1, device_id=source, device_id_type=LOGICAL)
    for mask in range(1, 8):
        pl.semaphore_signal(barrier, inc=1, device_id=me + subset(to_group, mask), device_id_type=LOGICAL)
    box, top = lane_parts(classes, core)
    fetch_coef.wait()
    late_setup(coef_ref, box, top, w_ref, p_ref, c_ref)
    pl.semaphore_wait(barrier, 22)

    def columns(m):
        return x_ref.at[:, pl.ds(pl.multiple_of(m * 128, 128), 128)]

    own_slot = 2 * number(mine(place_a, place_b)[::-1]) + core
    other_slot = 2 * number(others(place_a, place_b)[::-1]) + core
    other_groups = others(group_a, group_b)
    other_block = number(other_groups) + 8 * (1 - core)
    for mask in range(7, -1, -1):
        routes = [(other_block, other_groups, other_slot, me + to_core + subset(to_group, mask))]
        if mask:
            routes.append((block, groups, own_slot, me + subset(to_class, mask)))
        for first, group_bits, slot, device in routes:
            pltpu.make_async_remote_copy(
                src_ref=columns(first + subset(flips(group_bits, (1, 2, 4)), mask)),
                dst_ref=xr_ref.at[slot],
                send_sem=send_sems.at[0],
                recv_sem=recv_sems.at[0],
                device_id=device,
                device_id_type=LOGICAL,
            ).start()
    pltpu.make_async_copy(columns(block), xr_ref.at[own_slot], recv_sems.at[0]).start()
    early_levels(coef_ref, box, top, w_ref, p_ref, v_ref)

    def order(h):
        return classes[0] + (1 - h) * (1 - 2 * classes[0])

    def split(i, _):
        for j in range(4):
            piece = jnp.concatenate([xr_ref[2 * i + s, pl.ds(j, 8, stride=4), :] for s in range(2)], axis=0)
            high = piece.astype(BF16)
            rows = pl.ds(pl.multiple_of(128 * j + 16 * i, 16), 16)
            xs_ref[rows, 0:128] = high
            xs_ref[rows, 128:256] = (piece - high.astype(F32)).astype(BF16)
        return 0

    def half(h):
        @pl.when(h == 0)
        def _():
            pltpu.make_async_copy(xr_ref, xr_ref, recv_sems.at[0]).wait()
            lax.fori_loop(0, 8, split, 0, unroll=4)

        q3 = order(h)
        far = (1 - h) * to_group[0]
        for mask in range(3, -1, -1):
            i = classes[1] + 2 * classes[2] + subset(flips(classes[1:], (1, 2)), mask)
            rows = pl.ds(pl.multiple_of((4 * q3 + i) * 192, 16), 192)
            wide = jnp.dot(g_ref[rows, :], xs_ref[...], preferred_element_type=F32)
            part = wide[0:96, 0:128] + (wide[0:96, 128:256] + wide[96:192, 0:128])

            def send():
                part_ref[4 * q3 + i] = part
                pltpu.make_async_remote_copy(
                    src_ref=part_ref.at[4 * q3 + i],
                    dst_ref=rr_ref.at[target],
                    send_sem=send_sems.at[1],
                    recv_sem=recv_sems.at[1],
                    device_id=me + far + subset(to_group[1:], mask),
                    device_id_type=LOGICAL,
                ).start()

            if mask:
                send()
            else:
                pl.when(h == 0)(send)

                @pl.when(h == 1)
                def _():
                    rr_ref[target] = part

    late_levels(coef_ref, box, top, order, w_ref, p_ref, c_ref, v_ref, g_ref, half)
    fetch_tail.wait()
    for i in range(3):
        sum_ref[128 * i + 96 : 128 * i + 128, :] = jnp.zeros((32, 128), BF16)
    last_weights(coef_ref, target, tail_ref, h_ref)
    pltpu.make_async_copy(rr_ref.at[0:7], rr_ref.at[0:7], recv_sems.at[1]).wait()

    def add(i, _):
        rows = pl.ds(pl.multiple_of(16 * i, 16), 16)
        total = rr_ref[0, rows, :]
        for k in range(1, 8):
            total = total + rr_ref[k, rows, :]
        high = total.astype(BF16)
        sum_ref[rows, :] = high
        sum_ref[pl.ds(pl.multiple_of(128 + 16 * i, 16), 16), :] = high
        sum_ref[pl.ds(pl.multiple_of(256 + 16 * i, 16), 16), :] = (total - high.astype(F32)).astype(BF16)
        return 0

    lax.fori_loop(0, 6, add, 0, unroll=True)

    home = zh + 2 * yl + 4 * yh + 8 * xl + 16 * xh + 32 * zl
    own = core == classes[2]
    row = pl.multiple_of((classes[0] + 2 * classes[1]) * 8, 8)
    here = out_ref.at[pl.ds(row, 8), pl.ds(pl.multiple_of(block * 128, 128), 128)]
    turns = flips((zh, xl, xh, yh, yl, zl), (1, 8, 16, 4, 2, 32))

    def deliver(high):
        pltpu.make_async_remote_copy(
            src_ref=tile_ref.at[high],
            dst_ref=here,
            send_sem=send_sems.at[2],
            recv_sem=recv_sems.at[2],
            device_id=2 * high + classes[2],
            device_id_type=LOGICAL,
        ).start()

    early = (0, 8)
    lost = (63 - home, home + subset(turns, 48))
    instead = [jnp.where(lost[n] == early[1 - n], lost[1 - n], lost[n]) for n in range(2)]

    def settle(high):
        return jnp.where(high == early[0], instead[0], jnp.where(high == early[1], instead[1], high))

    tile_ref[...] = jnp.dot(h_ref[...], sum_ref[...], preferred_element_type=F32).reshape(64, 8, 128)
    for high in early:
        pl.when(jnp.logical_or(home != high, jnp.logical_not(own)))(functools.partial(deliver, high))
    moved = jnp.logical_or(home == early[0], home == early[1])
    last = jnp.logical_or(moved, jnp.logical_not(own))

    def deliver_some(step, _):
        same_y, same_z = rem(step, 2), div(step, 2)
        first = home + (1 - same_y) * turns[4] + (1 - same_z) * turns[5]

        def send(mask):
            deliver(settle(first + subset(turns, mask)))

        pl.when(step > 0)(lambda: send(15))
        pl.when(jnp.logical_and(step > 0, jnp.logical_or(step < 3, last)))(lambda: send(0))
        for mask in (14, 1, 13, 2, 12, 3, 11, 4, 10, 5, 9, 6, 8, 7):
            send(mask)
        return 0

    lax.fori_loop(0, 4, deliver_some, 0)

    @pl.when(own)
    def _():
        pltpu.make_async_copy(tile_ref.at[home], here, recv_sems.at[2]).start()

    pltpu.make_async_copy(xr_ref.at[0:15], xr_ref.at[0:15], send_sems.at[0]).wait()
    pltpu.make_async_copy(part_ref.at[0:7], part_ref.at[0:7], send_sems.at[1]).wait()

    @pl.when(own)
    def _():
        pltpu.make_async_copy(tile_ref.at[0:63], tile_ref.at[0:63], send_sems.at[2]).wait()

    @pl.when(jnp.logical_not(own))
    def _():
        pltpu.make_async_copy(tile_ref, tile_ref, send_sems.at[2]).wait()

    pltpu.make_async_copy(out_ref, out_ref, recv_sems.at[2]).wait()


def shards(traces, phase_coef):
    return pl.pallas_call(
        kernel,
        out_shape=jax.ShapeDtypeStruct((32, 2048), F32),
        in_specs=[
            pl.BlockSpec(memory_space=pl.ANY),
            pl.BlockSpec(memory_space=pl.ANY),
            pl.BlockSpec(memory_space=pl.ANY),
        ],
        out_specs=pl.BlockSpec(memory_space=pl.ANY),
        scratch_shapes=[
            pltpu.SMEM((2, 4), F32),
            pltpu.VMEM((6, 64, 128), F32),
            pltpu.VMEM((5, 36, 8, 128), F32),
            pltpu.VMEM((5, 6, 8, 128), F32),
            pltpu.VMEM((5, 8, 128), F32),
            pltpu.VMEM((3, 12, 4, 8, 128), F32),
            pltpu.VMEM((1536, 512), BF16),
            pltpu.VMEM((512, 384), BF16),
            pltpu.VMEM((16, 32, 128), F32),
            pltpu.VMEM((512, 256), BF16),
            pltpu.VMEM((8, 96, 128), F32),
            pltpu.VMEM((8, 96, 128), F32),
            pltpu.VMEM((384, 128), BF16),
            pltpu.VMEM((64, 8, 128), F32),
            pltpu.SemaphoreType.DMA((3,)),
            pltpu.SemaphoreType.DMA((5,)),
        ],
        compiler_params=pltpu.CompilerParams(
            collective_id=0, has_side_effects=True, vmem_limit_bytes=60 * 2**20
        ),
    )(traces, phase_coef, jnp.asarray(tail_table()))


def solution(mesh):
    placed = (P(("gx", "gy"), None), P())
    return jax.shard_map(
        shards, mesh=mesh, in_specs=placed, out_specs=P(("gx", "gy"), None), check_vma=False
    )
```

```python
import functools

import jax
import jax.numpy as jnp
import numpy as np
from jax import lax
from jax.experimental import pallas as pl
from jax.experimental.pallas import tpu as pltpu
from jax.sharding import PartitionSpec as P

ORDER = 6
LOGICAL = pl.DeviceIdType.LOGICAL
F32 = jnp.float32
BF16 = jnp.bfloat16
AMP = 64.0

NODES = 0.5 * np.cos(np.pi * (2.0 * np.arange(ORDER) + 1.0) / (2.0 * ORDER))


def lagrange(points):
    points = np.asarray(points)[..., None, None]
    same = np.eye(ORDER, dtype=bool)
    spread = np.where(same, 1.0, NODES[:, None] - NODES[None, :])
    return np.where(same, 1.0, (points - NODES[None, :]) / spread).prod(-1)


CENTRE = lagrange(0.0)
HALVES = np.stack([((side - 0.5) + NODES) * 0.5 for side in (0, 1)])
TABLE = lagrange(HALVES)
WEIGHT = np.transpose(TABLE, (0, 2, 1))


def tail_table():
    out = np.zeros((ORDER, 64, 128))
    for high in range(64):
        total = np.eye(ORDER)
        for place in range(6):
            total = TABLE[(high >> place) & 1] @ total
        out[:, high, :96] = np.repeat(CENTRE[:, None] * total, 16, axis=1)
    return out.astype(np.float32)


def fit(function, terms):
    u = 0.125 + 0.125 * np.cos(np.pi * (np.arange(200) + 0.5) / 200)
    poly = np.polynomial.chebyshev.Chebyshev.fit(u, function(np.sqrt(u)), terms - 1, domain=[0, 0.25])
    return [float(c) for c in poly.convert(kind=np.polynomial.Polynomial).coef]


SIN = fit(lambda r: np.sin(np.pi * r) / r, 5)
SIN2 = [2.0 * c for c in fit(lambda r: np.sin(np.pi * r) / r, 4)]
COS = fit(lambda r: np.cos(np.pi * r), 5)
COS4 = fit(lambda r: np.cos(np.pi * r), 4)


def horner(coefs, u):
    total = coefs[-1]
    for c in coefs[-2::-1]:
        total = total * u + c
    return total


def turn(c):
    r = c - jnp.floor(c + 0.5)
    u = r * r
    twice = r * horner(SIN2, u)
    half_cos = horner(COS4, u)
    return 1.0 - (0.5 * twice) * twice, twice * half_cos


def turn_cos(c):
    r = c - jnp.floor(c + 0.5)
    twice = r * horner(SIN2, r * r)
    return 1.0 - (0.5 * twice) * twice


def half_turn(y):
    r = 0.5 - y
    u = r * r
    return r * horner(SIN, u), horner(COS, u)


def bend_value(coef, row, y):
    cosine = (0.5 - y) * horner(SIN, (0.5 - y) * (0.5 - y))
    c0, c1, c2, c3 = (coef[row, m] for m in range(4))
    return (c0 - c2) + cosine * ((c1 - 3.0 * c3) + cosine * (2.0 * c2 + cosine * (4.0 * c3)))


def bend_terms(coef, size):
    e1, e2, e3 = (coef[0, m] * float(-2.0 * AMP * np.sin(np.pi * m * size / 2.0)) for m in (1, 2, 3))
    return e1 - e3, 2.0 * e2, 4.0 * e3


def bend_step(terms, middle):
    cosine, sine = half_turn(middle)
    return sine * (terms[0] + cosine * (terms[1] + cosine * terms[2]))


def apply_real(weights, values):
    out = []
    for t in range(ORDER):
        total = weights[t][0] * values[0]
        for s in range(1, ORDER):
            total = total + weights[t][s] * values[s]
        out.append(total)
    return out


def iota(axis):
    return lax.broadcasted_iota(jnp.int32, (8, 128), axis)


def asf(value):
    return value.astype(F32)


def div(a, b):
    return lax.div(a, jnp.int32(b))


def rem(a, b):
    return lax.rem(a, jnp.int32(b))


def subset(deltas, mask):
    total = None
    for k, delta in enumerate(deltas):
        if (mask >> k) & 1:
            total = delta if total is None else total + delta
    return 0 if total is None else total


def abs_flip(bit, turned):
    return 1 - bit if turned else bit


def flips(bits, weights):
    return [weight * (1 - 2 * bit) for bit, weight in zip(bits, weights)]


def lane_parts(classes, core):
    lane = iota(1)
    place = lane >> 4
    x, y, z = (
        (2 * c + e + core) & 3 for c, e in zip(classes, (place >> 2, (place >> 1) & 1, place & 1))
    )
    return (z >> 1) + 2 * y + 8 * x + 32 * (z & 1), lane & 15


def early_levels(coef, box, top, w_ref, p_ref, v_ref):
    sub = iota(0)
    bits = [asf(sub & 1), asf((sub >> 1) & 1), asf(sub >> 2)]
    sign = [2.0 * bit - 1.0 for bit in bits]
    x0 = jnp.full((8, 128), 0.5, F32)
    x1 = x0 + sign[0] * 0.25
    x2 = x1 + sign[1] * 0.125
    word4 = asf(box * 16 + top)
    steps = [
        bend_step(bend_terms(coef, 2.0 ** -(level + 1)), x + sign[level - 1] * 2.0 ** -(level + 2))
        for level, x in ((1, x0), (2, x1), (3, x2))
    ]
    p0_mid = coef[0, 0] - coef[0, 2]

    def turned(values, angles):
        pairs = [(a * c - b * d, a * d + b * c) for (a, b), (c, d) in zip(values, angles)]
        return [a for a, _ in pairs], [b for _, b in pairs]

    linear2 = 2.0 * asf(top & 1) + 0.5
    linear3 = asf(top & 3) + 0.5
    third = [turn(sign[2] * ((linear3 + float(NODES[s])) * 0.25 + steps[2] * p_ref[0, s])) for s in range(ORDER)]
    constants = [[float(WEIGHT[0][t][s]) for s in range(ORDER)] for t in range(ORDER)]

    def by_side(side, values):
        mirror = jnp.broadcast_to(side, (8, 128)) == 1
        picked = [jnp.where(mirror, values[5 - s], values[s]) for s in range(ORDER)]
        out = apply_real(constants, picked)
        return [jnp.where(mirror, out[5 - t], out[t]) for t in range(ORDER)]

    def body(group, _):
        j0, j1 = rem(group, 2), div(group, 2)
        j0f, j1f, groupf = asf(j0), asf(j1), asf(group)
        word = word4 * 4.0 + groupf
        start = 0.5 * (j0f + 0.5) + AMP * p0_mid * bend_value(coef, 1, (word + 0.5) * 2.0**-12)
        real, imag = [], []
        for s in range(ORDER):
            node = float(NODES[s])
            p1 = bend_value(coef, 1, (word + (0.5 + node)) * 2.0**-12)
            c, d = turn(start + sign[0] * ((groupf + (0.5 + node)) * 0.25 + steps[0] * p1))
            real.append(c * float(CENTRE[s]))
            imag.append(d * float(CENTRE[s]))
        values = list(zip(by_side(j0, real), by_side(j0, imag)))
        word = word4 * 2.0 + j1f
        angles = []
        for s in range(ORDER):
            node = float(NODES[s])
            p1 = bend_value(coef, 1, (word + (0.5 + node)) * 2.0**-11)
            angles.append(turn(sign[1] * (((linear2 + j1f) + node) * 0.25 + steps[1] * p1)))
        values = list(zip(*(by_side(j1, part) for part in turned(values, angles))))
        weights = [[w_ref[0, ORDER * t + s] for s in range(ORDER)] for t in range(ORDER)]
        for c, part in enumerate(turned(values, third)):
            for t, value in enumerate(apply_real(weights, part)):
                v_ref[0, 2 * t + c, group] = value
        return 0

    lax.fori_loop(0, 4, body, 0)


def late_setup(coef, box, top, w_ref, p_ref, c_ref):
    full = box * 16 + top

    def body(i, scale):
        word = full >> i
        pick = (word & 1) == 1
        for t in range(ORDER):
            for s in range(ORDER):
                w_ref[i, ORDER * t + s] = jnp.where(pick, float(WEIGHT[1][t][s]), float(WEIGHT[0][t][s]))
        for s in range(ORDER):
            p_ref[i, s] = bend_value(coef, 1, (asf(word) + float(0.5 + NODES[s])) * scale)
        return scale * 2.0

    lax.fori_loop(0, 5, body, jnp.float32(2.0**-10))
    turn_of = top & 7

    def by_lane(values):
        out = jnp.full((8, 128), float(values[ORDER - 1]), F32)
        for t in range(ORDER - 1):
            out = jnp.where(turn_of == t, float(values[t]), out)
        return out

    e1, e2, e3 = (coef[0, m] * by_lane(-2.0 * AMP * np.sin(np.pi * m * NODES / 128.0)) for m in (1, 2, 3))
    node = by_lane(NODES)
    c_ref[0] = node
    c_ref[1] = e1 - e3
    c_ref[2] = 2.0 * e2
    c_ref[3] = 4.0 * e3
    c_ref[4] = node * (asf(box) + 0.5)


def spread(value, t):
    return jnp.take_along_axis(value, (iota(1) & 120) + t, axis=1)


def late_levels(coef, box, top, order, w_ref, p_ref, c_ref, v_ref, g_ref, between):
    sub = iota(0)
    x3 = asf(4 * (sub & 1) + (sub & 2) + (sub >> 2)) * 0.125 + 0.0625
    full = box * 16 + top
    terms = [bend_terms(coef, 2.0 ** -(level + 1)) for level in (4, 5, 6)]

    def sign_of(bit):
        return (2 * bit - 1).astype(F32)

    def turns(i, level_terms, shift, parent, sign):
        steps = bend_step(level_terms, parent + sign * shift)
        linear = asf((full >> i) & 3) + 0.5
        return [turn(sign * ((linear + float(NODES[s])) * 0.25 + steps * p_ref[i, s])) for s in range(ORDER)]

    def level_step(level, q3, q4):
        first = level == 4
        i = level - 3
        parent = x3 + jnp.where(first, 0.0, sign_of(q3) * 2.0**-5)
        sign = jnp.where(first, sign_of(q3), sign_of(q4))
        level_terms = [jnp.where(first, a, b) for a, b in zip(terms[0], terms[1])]
        real, imag = [], []
        for s, (c, d) in enumerate(turns(i, level_terms, jnp.where(first, 2.0**-6, 2.0**-7), parent, sign)):
            a, b = v_ref[i - 1, 2 * s], v_ref[i - 1, 2 * s + 1]
            real.append(a * c - b * d)
            imag.append(a * d + b * c)
        weights = [[w_ref[i, ORDER * t + s] for s in range(ORDER)] for t in range(ORDER)]
        for c, values in enumerate((real, imag)):
            for t, value in enumerate(apply_real(weights, values)):
                v_ref[i, 2 * t + c] = value

    def last_step(parent, bit, place):
        sign = sign_of(bit)
        middle = parent + sign * 2.0**-7 + c_ref[0] * (1.0 / 128.0)
        steps = bend_step((c_ref[1], c_ref[2], c_ref[3]), middle)
        switch = [turn((c_ref[4] + c_ref[0] * float(NODES[u])) + steps * p_ref[4, u]) for u in range(ORDER)]
        merged = []
        for s, (c, d) in enumerate(turns(3, terms[2], 2.0**-8, parent, sign)):
            a = b = None
            for u in range(ORDER):
                weight = w_ref[3, ORDER * u + s]
                a = switch[u][0] * weight if a is None else a + switch[u][0] * weight
                b = switch[u][1] * weight if b is None else b + switch[u][1] * weight
            merged.append((a * c - b * d, a * d + b * c))
        parts = [v_ref[2, 2 * s] + v_ref[2, 2 * s + 1] for s in range(ORDER)]
        for t in range(ORDER):
            k1 = k2 = k3 = None
            for s in range(ORDER):
                c, d = spread(merged[s][0], t), spread(merged[s][1], t)
                m1, m2, m3 = parts[s] * c, v_ref[2, 2 * s] * (d - c), v_ref[2, 2 * s + 1] * (c + d)
                k1 = m1 if k1 is None else k1 + m1
                k2 = m2 if k2 is None else k2 + m2
                k3 = m3 if k3 is None else k3 + m3
            real, imag = k1 - k3, k1 + k2
            rows = pl.ds(pl.multiple_of(place * 192 + 16 * t, 16), 16)
            rows_low = pl.ds(pl.multiple_of(place * 192 + 96 + 16 * t, 16), 16)
            for j in range(4):
                both = jnp.concatenate([real[j], imag[j]], axis=0)
                high = both.astype(BF16)
                g_ref[rows, 128 * j : 128 * (j + 1)] = high
                g_ref[rows_low, 128 * j : 128 * (j + 1)] = (both - high.astype(F32)).astype(BF16)

    def over(n, _):
        @pl.when(n >= 4)
        def _():
            between(n - 4)

        @pl.when(n < 4)
        def _():
            q3, q4 = order(div(n, 2)), rem(n, 2)

            def levels(level, _):
                level_step(level, q3, q4)
                return 0

            lax.fori_loop(4 + q4, 6, levels, 0)
            x5 = x3 + (sign_of(q3) * 2.0**-5 + sign_of(q4) * 2.0**-6)

            def over5(q5, _):
                last_step(x5, q5, 4 * q3 + q4 + 2 * q5)
                return 0

            lax.fori_loop(0, 2, over5, 0)

        return 0

    lax.fori_loop(0, 6, over, 0)


def last_weights(coef, group, tail_ref, h_ref):
    sub, lane = iota(0), iota(1)
    own = lane & 7
    same = sub == own
    box6 = 32 * (own & 1) + 8 * (own & 2) + 2 * (own & 4)
    box6 = box6 + (4 * rem(group, 2) + 2 * rem(div(group, 2), 2) + div(group, 4))
    inner = 32 * (sub & 1) + 8 * (sub & 2) + 2 * (sub & 4)
    base = box6 * 64 + inner
    quarter = 0.25 * asf((lane >> 3) & 1)
    p1_mid = coef[1, 0] - coef[1, 2]

    def rows_of(r):
        centre = (asf(base + (4 * rem(r, 2) + 2 * rem(div(r, 2), 2) + div(r, 4))) + 0.5) * 2.0**-12
        total = None
        for t in range(ORDER):
            node = float(NODES[t])
            steps = bend_step(bend_terms(coef, node / 4096.0), centre + node / 8192.0)
            term = turn_cos((quarter - 0.5 * node) - steps * p1_mid)
            term = term * tail_ref[t, pl.ds(pl.multiple_of(8 * r, 8), 8), :]
            total = term if total is None else total + term
        return total

    def body(r, _):
        total = rows_of(r)
        for k in range(0, 8, 2):
            both = jnp.concatenate(
                [jnp.where(same, jnp.broadcast_to(total[k + n : k + n + 1], (8, 128)), 0.0) for n in range(2)], axis=0
            )
            high = both.astype(BF16)
            rows = pl.ds(pl.multiple_of(64 * r + 8 * k, 16), 16)
            h_ref[rows, 0:128] = high
            h_ref[rows, 128:256] = (both - high.astype(F32)).astype(BF16)
            h_ref[rows, 256:384] = high
        return 0

    lax.fori_loop(0, 8, body, 0)


def kernel(
    x_ref,
    coef_hbm,
    tail_hbm,
    out_ref,
    coef_ref,
    tail_ref,
    w_ref,
    p_ref,
    c_ref,
    v_ref,
    g_ref,
    h_ref,
    xr_ref,
    xs_ref,
    part_ref,
    rr_ref,
    sum_ref,
    tile_ref,
    send_sems,
    recv_sems,
):
    fetch_coef = pltpu.make_async_copy(coef_hbm, coef_ref, recv_sems.at[3])
    fetch_tail = pltpu.make_async_copy(tail_hbm, tail_ref, recv_sems.at[4])
    fetch_coef.start()
    fetch_tail.start()
    gx, gy = lax.axis_index("gx"), lax.axis_index("gy")
    core = rem(gy, 2)
    zl, xs = div(gx, 4), rem(gx, 4)
    xh, xl = div(xs, 2), rem(xs, 2)
    yh, yl, zh = div(gy, 8), rem(div(gy, 4), 2), rem(div(gy, 2), 2)
    me = gx * 16 + gy
    highs, lows = (xh, yh, zh), (xl, yl, zl)
    unlike = [h + l - 2 * h * l for h, l in zip(highs, lows)]
    to_a = [16 * (1 - 2 * xl), 4 * (1 - 2 * yl), 64 * (1 - 2 * zl)]
    to_b = [16 * (3 - 2 * xs), 4 * (3 - 2 * (2 * yh + yl)), 2 * (1 - 2 * zh) + 64 * (1 - 2 * zl)]
    to_class = [a + core * (b - a) for a, b in zip(to_a, to_b)]
    to_group = [b + core * (a - b) for a, b in zip(to_a, to_b)]
    to_core = 1 - 2 * core
    class_a, class_b = highs, [1 - d for d in unlike]
    place_a, place_b = lows, [1 - l for l in lows]
    group_a, group_b = [1 - d for d in unlike], [1 - h for h in highs]

    def mine(for_a, for_b):
        return [a + core * (b - a) for a, b in zip(for_a, for_b)]

    def others(for_a, for_b):
        return [b + core * (a - b) for a, b in zip(for_a, for_b)]

    def number(values):
        return values[0] + 2 * values[1] + 4 * values[2]

    classes, groups = mine(class_a, class_b), mine(group_a, group_b)
    target = number(classes)
    block = number(groups) + 8 * core

    barrier = pltpu.get_barrier_semaphore()
    for mask in range(1, 16):
        source = me + subset(to_class + [to_core], mask)
        pl.semaphore_signal(barrier, inc=1, device_id=source, device_id_type=LOGICAL)
    for mask in range(1, 8):
        pl.semaphore_signal(barrier, inc=1, device_id=me + subset(to_group, mask), device_id_type=LOGICAL)
    pl.semaphore_wait(barrier, 22)

    def columns(m):
        return x_ref.at[:, pl.ds(pl.multiple_of(m * 128, 128), 128)]

    own_slot = 2 * number(mine(place_a, place_b)[::-1]) + core
    other_slot = 2 * number(others(place_a, place_b)[::-1]) + core
    other_groups = others(group_a, group_b)
    other_block = number(other_groups) + 8 * (1 - core)
    for mask in range(7, -1, -1):
        routes = [(other_block, other_groups, other_slot, me + to_core + subset(to_group, mask))]
        if mask:
            routes.append((block, groups, own_slot, me + subset(to_class, mask)))
        for first, group_bits, slot, device in routes:
            pltpu.make_async_remote_copy(
                src_ref=columns(first + subset(flips(group_bits, (1, 2, 4)), mask)),
                dst_ref=xr_ref.at[slot],
                send_sem=send_sems.at[0],
                recv_sem=recv_sems.at[0],
                device_id=device,
                device_id_type=LOGICAL,
            ).start()
    pltpu.make_async_copy(columns(block), xr_ref.at[own_slot], recv_sems.at[0]).start()
    box, top = lane_parts(classes, core)
    fetch_coef.wait()
    late_setup(coef_ref, box, top, w_ref, p_ref, c_ref)
    early_levels(coef_ref, box, top, w_ref, p_ref, v_ref)

    def order(h):
        return classes[0] + (1 - h) * (1 - 2 * classes[0])

    def split(i, _):
        for j in range(4):
            piece = jnp.concatenate([xr_ref[2 * i + s, pl.ds(j, 8, stride=4), :] for s in range(2)], axis=0)
            high = piece.astype(BF16)
            rows = pl.ds(pl.multiple_of(128 * j + 16 * i, 16), 16)
            xs_ref[rows, 0:128] = high
            xs_ref[rows, 128:256] = (piece - high.astype(F32)).astype(BF16)
        return 0

    def half(h):
        @pl.when(h == 0)
        def _():
            pltpu.make_async_copy(xr_ref, xr_ref, recv_sems.at[0]).wait()
            lax.fori_loop(0, 8, split, 0, unroll=4)

        q3 = order(h)
        far = (1 - h) * to_group[0]
        for mask in range(3, -1, -1):
            i = classes[1] + 2 * classes[2] + subset(flips(classes[1:], (1, 2)), mask)
            rows = pl.ds(pl.multiple_of((4 * q3 + i) * 192, 16), 192)
            wide = jnp.dot(g_ref[rows, :], xs_ref[...], preferred_element_type=F32)
            part = wide[0:96, 0:128] + (wide[0:96, 128:256] + wide[96:192, 0:128])

            def send():
                part_ref[4 * q3 + i] = part
                pltpu.make_async_remote_copy(
                    src_ref=part_ref.at[4 * q3 + i],
                    dst_ref=rr_ref.at[target],
                    send_sem=send_sems.at[1],
                    recv_sem=recv_sems.at[1],
                    device_id=me + far + subset(to_group[1:], mask),
                    device_id_type=LOGICAL,
                ).start()

            if mask:
                send()
            else:
                pl.when(h == 0)(send)

                @pl.when(h == 1)
                def _():
                    rr_ref[target] = part

    late_levels(coef_ref, box, top, order, w_ref, p_ref, c_ref, v_ref, g_ref, half)
    fetch_tail.wait()
    for i in range(3):
        sum_ref[128 * i + 96 : 128 * i + 128, :] = jnp.zeros((32, 128), BF16)
    last_weights(coef_ref, target, tail_ref, h_ref)
    pltpu.make_async_copy(rr_ref.at[0:7], rr_ref.at[0:7], recv_sems.at[1]).wait()

    def add(i, _):
        rows = pl.ds(pl.multiple_of(16 * i, 16), 16)
        total = rr_ref[0, rows, :]
        for k in range(1, 8):
            total = total + rr_ref[k, rows, :]
        high = total.astype(BF16)
        sum_ref[rows, :] = high
        sum_ref[pl.ds(pl.multiple_of(128 + 16 * i, 16), 16), :] = high
        sum_ref[pl.ds(pl.multiple_of(256 + 16 * i, 16), 16), :] = (total - high.astype(F32)).astype(BF16)
        return 0

    lax.fori_loop(0, 6, add, 0, unroll=True)

    home = zh + 2 * yl + 4 * yh + 8 * xl + 16 * xh + 32 * zl
    own = core == classes[2]
    row = pl.multiple_of((classes[0] + 2 * classes[1]) * 8, 8)
    here = out_ref.at[pl.ds(row, 8), pl.ds(pl.multiple_of(block * 128, 128), 128)]
    turns = flips((zh, xl, xh, yh, yl, zl), (1, 8, 16, 4, 2, 32))

    def deliver(high):
        pltpu.make_async_remote_copy(
            src_ref=tile_ref.at[high],
            dst_ref=here,
            send_sem=send_sems.at[2],
            recv_sem=recv_sems.at[2],
            device_id=2 * high + classes[2],
            device_id_type=LOGICAL,
        ).start()

    early = (0, 8)
    lost = (63 - home, home + subset(turns, 48))
    instead = [jnp.where(lost[n] == early[1 - n], lost[1 - n], lost[n]) for n in range(2)]

    def settle(high):
        return jnp.where(high == early[0], instead[0], jnp.where(high == early[1], instead[1], high))

    tile_ref[...] = jnp.dot(h_ref[...], sum_ref[...], preferred_element_type=F32).reshape(64, 8, 128)
    for high in early:
        pl.when(jnp.logical_or(home != high, jnp.logical_not(own)))(functools.partial(deliver, high))
    moved = jnp.logical_or(home == early[0], home == early[1])
    last = jnp.logical_or(moved, jnp.logical_not(own))

    def deliver_some(step, _):
        same_y, same_z = rem(step, 2), div(step, 2)
        first = home + (1 - same_y) * turns[4] + (1 - same_z) * turns[5]

        def send(mask):
            deliver(settle(first + subset(turns, mask)))

        pl.when(step > 0)(lambda: send(15))
        pl.when(jnp.logical_and(step > 0, jnp.logical_or(step < 3, last)))(lambda: send(0))
        for mask in (14, 1, 13, 2, 12, 3, 11, 4, 10, 5, 9, 6, 8, 7):
            send(mask)
        return 0

    lax.fori_loop(0, 4, deliver_some, 0)

    @pl.when(own)
    def _():
        pltpu.make_async_copy(tile_ref.at[home], here, recv_sems.at[2]).start()

    pltpu.make_async_copy(xr_ref.at[0:15], xr_ref.at[0:15], send_sems.at[0]).wait()
    pltpu.make_async_copy(part_ref.at[0:7], part_ref.at[0:7], send_sems.at[1]).wait()

    @pl.when(own)
    def _():
        pltpu.make_async_copy(tile_ref.at[0:63], tile_ref.at[0:63], send_sems.at[2]).wait()

    @pl.when(jnp.logical_not(own))
    def _():
        pltpu.make_async_copy(tile_ref, tile_ref, send_sems.at[2]).wait()

    pltpu.make_async_copy(out_ref, out_ref, recv_sems.at[2]).wait()


def shards(traces, phase_coef):
    return pl.pallas_call(
        kernel,
        out_shape=jax.ShapeDtypeStruct((32, 2048), F32),
        in_specs=[
            pl.BlockSpec(memory_space=pl.ANY),
            pl.BlockSpec(memory_space=pl.ANY),
            pl.BlockSpec(memory_space=pl.ANY),
        ],
        out_specs=pl.BlockSpec(memory_space=pl.ANY),
        scratch_shapes=[
            pltpu.SMEM((2, 4), F32),
            pltpu.VMEM((6, 64, 128), F32),
            pltpu.VMEM((5, 36, 8, 128), F32),
            pltpu.VMEM((5, 6, 8, 128), F32),
            pltpu.VMEM((5, 8, 128), F32),
            pltpu.VMEM((3, 12, 4, 8, 128), F32),
            pltpu.VMEM((1536, 512), BF16),
            pltpu.VMEM((512, 384), BF16),
            pltpu.VMEM((16, 32, 128), F32),
            pltpu.VMEM((512, 256), BF16),
            pltpu.VMEM((8, 96, 128), F32),
            pltpu.VMEM((8, 96, 128), F32),
            pltpu.VMEM((384, 128), BF16),
            pltpu.VMEM((64, 8, 128), F32),
            pltpu.SemaphoreType.DMA((3,)),
            pltpu.SemaphoreType.DMA((5,)),
        ],
        compiler_params=pltpu.CompilerParams(
            collective_id=0, has_side_effects=True, vmem_limit_bytes=60 * 2**20
        ),
    )(traces, phase_coef, jnp.asarray(tail_table()))


def solution(mesh):
    placed = (P(("gx", "gy"), None), P())
    return jax.shard_map(
        shards, mesh=mesh, in_specs=placed, out_specs=P(("gx", "gy"), None), check_vma=False
    )
```

```python
import functools

import jax
import jax.numpy as jnp
import numpy as np
from jax import lax
from jax.experimental import pallas as pl
from jax.experimental.pallas import tpu as pltpu
from jax.sharding import PartitionSpec as P

ORDER = 6
LOGICAL = pl.DeviceIdType.LOGICAL
F32 = jnp.float32
BF16 = jnp.bfloat16
AMP = 64.0

NODES = 0.5 * np.cos(np.pi * (2.0 * np.arange(ORDER) + 1.0) / (2.0 * ORDER))


def lagrange(points):
    points = np.asarray(points)[..., None, None]
    same = np.eye(ORDER, dtype=bool)
    spread = np.where(same, 1.0, NODES[:, None] - NODES[None, :])
    return np.where(same, 1.0, (points - NODES[None, :]) / spread).prod(-1)


CENTRE = lagrange(0.0)
HALVES = np.stack([((side - 0.5) + NODES) * 0.5 for side in (0, 1)])
TABLE = lagrange(HALVES)
WEIGHT = np.transpose(TABLE, (0, 2, 1))


def tail_table():
    out = np.zeros((ORDER, 64, 128))
    for high in range(64):
        total = np.eye(ORDER)
        for place in range(6):
            total = TABLE[(high >> place) & 1] @ total
        out[:, high, :96] = np.repeat(CENTRE[:, None] * total, 16, axis=1)
    return out.astype(np.float32)


def fit(function, terms):
    u = 0.125 + 0.125 * np.cos(np.pi * (np.arange(200) + 0.5) / 200)
    poly = np.polynomial.chebyshev.Chebyshev.fit(u, function(np.sqrt(u)), terms - 1, domain=[0, 0.25])
    return [float(c) for c in poly.convert(kind=np.polynomial.Polynomial).coef]


SIN = fit(lambda r: np.sin(np.pi * r) / r, 5)
SIN2 = [2.0 * c for c in fit(lambda r: np.sin(np.pi * r) / r, 4)]
COS = fit(lambda r: np.cos(np.pi * r), 5)
COS4 = fit(lambda r: np.cos(np.pi * r), 4)


def horner(coefs, u):
    total = coefs[-1]
    for c in coefs[-2::-1]:
        total = total * u + c
    return total


def turn(c):
    r = c - jnp.floor(c + 0.5)
    u = r * r
    twice = r * horner(SIN2, u)
    half_cos = horner(COS4, u)
    return 1.0 - (0.5 * twice) * twice, twice * half_cos


def turn_cos(c):
    r = c - jnp.floor(c + 0.5)
    twice = r * horner(SIN2, r * r)
    return 1.0 - (0.5 * twice) * twice


def half_turn(y):
    r = 0.5 - y
    u = r * r
    return r * horner(SIN, u), horner(COS, u)


def bend_value(coef, row, y):
    cosine = (0.5 - y) * horner(SIN, (0.5 - y) * (0.5 - y))
    c0, c1, c2, c3 = (coef[row, m] for m in range(4))
    return (c0 - c2) + cosine * ((c1 - 3.0 * c3) + cosine * (2.0 * c2 + cosine * (4.0 * c3)))


def bend_terms(coef, size):
    e1, e2, e3 = (coef[0, m] * float(-2.0 * AMP * np.sin(np.pi * m * size / 2.0)) for m in (1, 2, 3))
    return e1 - e3, 2.0 * e2, 4.0 * e3


def bend_step(terms, middle):
    cosine, sine = half_turn(middle)
    return sine * (terms[0] + cosine * (terms[1] + cosine * terms[2]))


def apply_real(weights, values):
    out = []
    for t in range(ORDER):
        total = weights[t][0] * values[0]
        for s in range(1, ORDER):
            total = total + weights[t][s] * values[s]
        out.append(total)
    return out


def iota(axis):
    return lax.broadcasted_iota(jnp.int32, (8, 128), axis)


def asf(value):
    return value.astype(F32)


def div(a, b):
    return lax.div(a, jnp.int32(b))


def rem(a, b):
    return lax.rem(a, jnp.int32(b))


def subset(deltas, mask):
    total = None
    for k, delta in enumerate(deltas):
        if (mask >> k) & 1:
            total = delta if total is None else total + delta
    return 0 if total is None else total


def abs_flip(bit, turned):
    return 1 - bit if turned else bit


def flips(bits, weights):
    return [weight * (1 - 2 * bit) for bit, weight in zip(bits, weights)]


def lane_parts(classes, core):
    lane = iota(1)
    place = lane >> 4
    x, y, z = (
        (2 * c + e + core) & 3 for c, e in zip(classes, (place >> 2, (place >> 1) & 1, place & 1))
    )
    return (z >> 1) + 2 * y + 8 * x + 32 * (z & 1), lane & 15


def early_levels(coef, box, top, w_ref, p_ref, v_ref):
    sub = iota(0)
    bits = [asf(sub & 1), asf((sub >> 1) & 1), asf(sub >> 2)]
    sign = [2.0 * bit - 1.0 for bit in bits]
    x0 = jnp.full((8, 128), 0.5, F32)
    x1 = x0 + sign[0] * 0.25
    x2 = x1 + sign[1] * 0.125
    word4 = asf(box * 16 + top)
    steps = [
        bend_step(bend_terms(coef, 2.0 ** -(level + 1)), x + sign[level - 1] * 2.0 ** -(level + 2))
        for level, x in ((1, x0), (2, x1), (3, x2))
    ]
    p0_mid = coef[0, 0] - coef[0, 2]

    def turned(values, angles):
        pairs = [(a * c - b * d, a * d + b * c) for (a, b), (c, d) in zip(values, angles)]
        return [a for a, _ in pairs], [b for _, b in pairs]

    linear2 = 2.0 * asf(top & 1) + 0.5
    linear3 = asf(top & 3) + 0.5
    third = [turn(sign[2] * ((linear3 + float(NODES[s])) * 0.25 + steps[2] * p_ref[0, s])) for s in range(ORDER)]
    constants = [[float(WEIGHT[0][t][s]) for s in range(ORDER)] for t in range(ORDER)]

    def by_side(side, values):
        mirror = jnp.broadcast_to(side, (8, 128)) == 1
        picked = [jnp.where(mirror, values[5 - s], values[s]) for s in range(ORDER)]
        out = apply_real(constants, picked)
        return [jnp.where(mirror, out[5 - t], out[t]) for t in range(ORDER)]

    def body(group, _):
        j0, j1 = rem(group, 2), div(group, 2)
        j0f, j1f, groupf = asf(j0), asf(j1), asf(group)
        word = word4 * 4.0 + groupf
        start = 0.5 * (j0f + 0.5) + AMP * p0_mid * bend_value(coef, 1, (word + 0.5) * 2.0**-12)
        real, imag = [], []
        for s in range(ORDER):
            node = float(NODES[s])
            p1 = bend_value(coef, 1, (word + (0.5 + node)) * 2.0**-12)
            c, d = turn(start + sign[0] * ((groupf + (0.5 + node)) * 0.25 + steps[0] * p1))
            real.append(c * float(CENTRE[s]))
            imag.append(d * float(CENTRE[s]))
        values = list(zip(by_side(j0, real), by_side(j0, imag)))
        word = word4 * 2.0 + j1f
        angles = []
        for s in range(ORDER):
            node = float(NODES[s])
            p1 = bend_value(coef, 1, (word + (0.5 + node)) * 2.0**-11)
            angles.append(turn(sign[1] * (((linear2 + j1f) + node) * 0.25 + steps[1] * p1)))
        values = list(zip(*(by_side(j1, part) for part in turned(values, angles))))
        weights = [[w_ref[0, ORDER * t + s] for s in range(ORDER)] for t in range(ORDER)]
        for c, part in enumerate(turned(values, third)):
            for t, value in enumerate(apply_real(weights, part)):
                v_ref[0, 2 * t + c, group] = value
        return 0

    lax.fori_loop(0, 4, body, 0)


def late_setup(coef, box, top, w_ref, p_ref, c_ref):
    full = box * 16 + top

    def body(i, scale):
        word = full >> i
        pick = (word & 1) == 1
        for t in range(ORDER):
            for s in range(ORDER):
                w_ref[i, ORDER * t + s] = jnp.where(pick, float(WEIGHT[1][t][s]), float(WEIGHT[0][t][s]))
        for s in range(ORDER):
            p_ref[i, s] = bend_value(coef, 1, (asf(word) + float(0.5 + NODES[s])) * scale)
        return scale * 2.0

    lax.fori_loop(0, 5, body, jnp.float32(2.0**-10))
    turn_of = top & 7

    def by_lane(values):
        out = jnp.full((8, 128), float(values[ORDER - 1]), F32)
        for t in range(ORDER - 1):
            out = jnp.where(turn_of == t, float(values[t]), out)
        return out

    e1, e2, e3 = (coef[0, m] * by_lane(-2.0 * AMP * np.sin(np.pi * m * NODES / 128.0)) for m in (1, 2, 3))
    node = by_lane(NODES)
    c_ref[0] = node
    c_ref[1] = e1 - e3
    c_ref[2] = 2.0 * e2
    c_ref[3] = 4.0 * e3
    c_ref[4] = node * (asf(box) + 0.5)


def spread(value, t):
    return jnp.take_along_axis(value, (iota(1) & 120) + t, axis=1)


def late_levels(coef, box, top, order, w_ref, p_ref, c_ref, v_ref, g_ref, between):
    sub = iota(0)
    x3 = asf(4 * (sub & 1) + (sub & 2) + (sub >> 2)) * 0.125 + 0.0625
    full = box * 16 + top
    terms = [bend_terms(coef, 2.0 ** -(level + 1)) for level in (4, 5, 6)]

    def sign_of(bit):
        return (2 * bit - 1).astype(F32)

    def turns(i, level_terms, shift, parent, sign):
        steps = bend_step(level_terms, parent + sign * shift)
        linear = asf((full >> i) & 3) + 0.5
        return [turn(sign * ((linear + float(NODES[s])) * 0.25 + steps * p_ref[i, s])) for s in range(ORDER)]

    def level_step(level, q3, q4):
        first = level == 4
        i = level - 3
        parent = x3 + jnp.where(first, 0.0, sign_of(q3) * 2.0**-5)
        sign = jnp.where(first, sign_of(q3), sign_of(q4))
        level_terms = [jnp.where(first, a, b) for a, b in zip(terms[0], terms[1])]
        real, imag = [], []
        for s, (c, d) in enumerate(turns(i, level_terms, jnp.where(first, 2.0**-6, 2.0**-7), parent, sign)):
            a, b = v_ref[i - 1, 2 * s], v_ref[i - 1, 2 * s + 1]
            real.append(a * c - b * d)
            imag.append(a * d + b * c)
        weights = [[w_ref[i, ORDER * t + s] for s in range(ORDER)] for t in range(ORDER)]
        for c, values in enumerate((real, imag)):
            for t, value in enumerate(apply_real(weights, values)):
                v_ref[i, 2 * t + c] = value

    def last_step(parent, bit, place):
        sign = sign_of(bit)
        middle = parent + sign * 2.0**-7 + c_ref[0] * (1.0 / 128.0)
        steps = bend_step((c_ref[1], c_ref[2], c_ref[3]), middle)
        switch = [turn((c_ref[4] + c_ref[0] * float(NODES[u])) + steps * p_ref[4, u]) for u in range(ORDER)]
        merged = []
        for s, (c, d) in enumerate(turns(3, terms[2], 2.0**-8, parent, sign)):
            a = b = None
            for u in range(ORDER):
                weight = w_ref[3, ORDER * u + s]
                a = switch[u][0] * weight if a is None else a + switch[u][0] * weight
                b = switch[u][1] * weight if b is None else b + switch[u][1] * weight
            merged.append((a * c - b * d, a * d + b * c))
        parts = [v_ref[2, 2 * s] + v_ref[2, 2 * s + 1] for s in range(ORDER)]
        for t in range(ORDER):
            k1 = k2 = k3 = None
            for s in range(ORDER):
                c, d = spread(merged[s][0], t), spread(merged[s][1], t)
                m1, m2, m3 = parts[s] * c, v_ref[2, 2 * s] * (d - c), v_ref[2, 2 * s + 1] * (c + d)
                k1 = m1 if k1 is None else k1 + m1
                k2 = m2 if k2 is None else k2 + m2
                k3 = m3 if k3 is None else k3 + m3
            real, imag = k1 - k3, k1 + k2
            rows = pl.ds(pl.multiple_of(place * 192 + 16 * t, 16), 16)
            rows_low = pl.ds(pl.multiple_of(place * 192 + 96 + 16 * t, 16), 16)
            for j in range(4):
                both = jnp.concatenate([real[j], imag[j]], axis=0)
                high = both.astype(BF16)
                g_ref[rows, 128 * j : 128 * (j + 1)] = high
                g_ref[rows_low, 128 * j : 128 * (j + 1)] = (both - high.astype(F32)).astype(BF16)

    def over(n, _):
        @pl.when(n >= 4)
        def _():
            between(n - 4)

        @pl.when(n < 4)
        def _():
            q3, q4 = order(div(n, 2)), rem(n, 2)

            def levels(level, _):
                level_step(level, q3, q4)
                return 0

            lax.fori_loop(4 + q4, 6, levels, 0)
            x5 = x3 + (sign_of(q3) * 2.0**-5 + sign_of(q4) * 2.0**-6)

            def over5(q5, _):
                last_step(x5, q5, 4 * q3 + q4 + 2 * q5)
                return 0

            lax.fori_loop(0, 2, over5, 0)

        return 0

    lax.fori_loop(0, 6, over, 0)


def last_weights(coef, group, tail_ref, h_ref):
    sub, lane = iota(0), iota(1)
    own = lane & 7
    same = sub == own
    box6 = 32 * (own & 1) + 8 * (own & 2) + 2 * (own & 4)
    box6 = box6 + (4 * rem(group, 2) + 2 * rem(div(group, 2), 2) + div(group, 4))
    inner = 32 * (sub & 1) + 8 * (sub & 2) + 2 * (sub & 4)
    base = box6 * 64 + inner
    quarter = 0.25 * asf((lane >> 3) & 1)
    p1_mid = coef[1, 0] - coef[1, 2]

    def rows_of(r):
        centre = (asf(base + (4 * rem(r, 2) + 2 * rem(div(r, 2), 2) + div(r, 4))) + 0.5) * 2.0**-12
        total = None
        for t in range(ORDER):
            node = float(NODES[t])
            steps = bend_step(bend_terms(coef, node / 4096.0), centre + node / 8192.0)
            term = turn_cos((quarter - 0.5 * node) - steps * p1_mid)
            term = term * tail_ref[t, pl.ds(pl.multiple_of(8 * r, 8), 8), :]
            total = term if total is None else total + term
        return total

    def body(r, _):
        total = rows_of(r)
        for k in range(0, 8, 2):
            both = jnp.concatenate(
                [jnp.where(same, jnp.broadcast_to(total[k + n : k + n + 1], (8, 128)), 0.0) for n in range(2)], axis=0
            )
            high = both.astype(BF16)
            rows = pl.ds(pl.multiple_of(64 * r + 8 * k, 16), 16)
            h_ref[rows, 0:128] = high
            h_ref[rows, 128:256] = (both - high.astype(F32)).astype(BF16)
            h_ref[rows, 256:384] = high
        return 0

    lax.fori_loop(0, 8, body, 0)


def kernel(
    x_ref,
    coef_hbm,
    tail_hbm,
    out_ref,
    coef_ref,
    tail_ref,
    w_ref,
    p_ref,
    c_ref,
    v_ref,
    g_ref,
    h_ref,
    xr_ref,
    xs_ref,
    part_ref,
    rr_ref,
    sum_ref,
    tile_ref,
    send_sems,
    recv_sems,
):
    fetch_coef = pltpu.make_async_copy(coef_hbm, coef_ref, recv_sems.at[3])
    fetch_tail = pltpu.make_async_copy(tail_hbm, tail_ref, recv_sems.at[4])
    fetch_coef.start()
    fetch_tail.start()
    gx, gy = lax.axis_index("gx"), lax.axis_index("gy")
    core = rem(gy, 2)
    zl, xs = div(gx, 4), rem(gx, 4)
    xh, xl = div(xs, 2), rem(xs, 2)
    yh, yl, zh = div(gy, 8), rem(div(gy, 4), 2), rem(div(gy, 2), 2)
    me = gx * 16 + gy
    highs, lows = (xh, yh, zh), (xl, yl, zl)
    unlike = [h + l - 2 * h * l for h, l in zip(highs, lows)]
    to_a = [16 * (1 - 2 * xl), 4 * (1 - 2 * yl), 64 * (1 - 2 * zl)]
    to_b = [16 * (3 - 2 * xs), 4 * (3 - 2 * (2 * yh + yl)), 2 * (1 - 2 * zh) + 64 * (1 - 2 * zl)]
    to_class = [a + core * (b - a) for a, b in zip(to_a, to_b)]
    to_group = [b + core * (a - b) for a, b in zip(to_a, to_b)]
    to_core = 1 - 2 * core
    class_a, class_b = highs, [1 - d for d in unlike]
    place_a, place_b = lows, [1 - l for l in lows]
    group_a, group_b = [1 - d for d in unlike], [1 - h for h in highs]

    def mine(for_a, for_b):
        return [a + core * (b - a) for a, b in zip(for_a, for_b)]

    def others(for_a, for_b):
        return [b + core * (a - b) for a, b in zip(for_a, for_b)]

    def number(values):
        return values[0] + 2 * values[1] + 4 * values[2]

    classes, groups = mine(class_a, class_b), mine(group_a, group_b)
    target = number(classes)
    block = number(groups) + 8 * core

    barrier = pltpu.get_barrier_semaphore()
    for mask in range(1, 16):
        source = me + subset(to_class + [to_core], mask)
        pl.semaphore_signal(barrier, inc=1, device_id=source, device_id_type=LOGICAL)
    for mask in range(1, 8):
        pl.semaphore_signal(barrier, inc=1, device_id=me + subset(to_group, mask), device_id_type=LOGICAL)
    box, top = lane_parts(classes, core)
    fetch_coef.wait()
    late_setup(coef_ref, box, top, w_ref, p_ref, c_ref)
    pl.semaphore_wait(barrier, 22)

    def columns(m):
        return x_ref.at[:, pl.ds(pl.multiple_of(m * 128, 128), 128)]

    own_slot = 2 * number(mine(place_a, place_b)[::-1]) + core
    other_slot = 2 * number(others(place_a, place_b)[::-1]) + core
    other_groups = others(group_a, group_b)
    other_block = number(other_groups) + 8 * (1 - core)
    for mask in range(7, -1, -1):
        routes = [(other_block, other_groups, other_slot, me + to_core + subset(to_group, mask))]
        if mask:
            routes.append((block, groups, own_slot, me + subset(to_class, mask)))
        for first, group_bits, slot, device in routes:
            pltpu.make_async_remote_copy(
                src_ref=columns(first + subset(flips(group_bits, (1, 2, 4)), mask)),
                dst_ref=xr_ref.at[slot],
                send_sem=send_sems.at[0],
                recv_sem=recv_sems.at[0],
                device_id=device,
                device_id_type=LOGICAL,
            ).start()
    pltpu.make_async_copy(columns(block), xr_ref.at[own_slot], recv_sems.at[0]).start()
    early_levels(coef_ref, box, top, w_ref, p_ref, v_ref)

    def order(h):
        return classes[0] + (1 - h) * (1 - 2 * classes[0])

    def split(i, _):
        for j in range(4):
            piece = jnp.concatenate([xr_ref[2 * i + s, pl.ds(j, 8, stride=4), :] for s in range(2)], axis=0)
            high = piece.astype(BF16)
            rows = pl.ds(pl.multiple_of(128 * j + 16 * i, 16), 16)
            xs_ref[rows, 0:128] = high
            xs_ref[rows, 128:256] = (piece - high.astype(F32)).astype(BF16)
        return 0

    def half(h):
        @pl.when(h == 0)
        def _():
            pltpu.make_async_copy(xr_ref, xr_ref, recv_sems.at[0]).wait()
            lax.fori_loop(0, 8, split, 0, unroll=4)

        q3 = order(h)
        far = (1 - h) * to_group[0]
        for mask in range(3, -1, -1):
            i = classes[1] + 2 * classes[2] + subset(flips(classes[1:], (1, 2)), mask)
            rows = pl.ds(pl.multiple_of((4 * q3 + i) * 192, 16), 192)
            wide = jnp.dot(g_ref[rows, :], xs_ref[...], preferred_element_type=F32)
            part = wide[0:96, 0:128] + (wide[0:96, 128:256] + wide[96:192, 0:128])

            def send():
                part_ref[4 * q3 + i] = part
                pltpu.make_async_remote_copy(
                    src_ref=part_ref.at[4 * q3 + i],
                    dst_ref=rr_ref.at[target],
                    send_sem=send_sems.at[1],
                    recv_sem=recv_sems.at[1],
                    device_id=me + far + subset(to_group[1:], mask),
                    device_id_type=LOGICAL,
                ).start()

            if mask:
                send()
            else:
                pl.when(h == 0)(send)

                @pl.when(h == 1)
                def _():
                    rr_ref[target] = part

    late_levels(coef_ref, box, top, order, w_ref, p_ref, c_ref, v_ref, g_ref, half)
    fetch_tail.wait()
    for i in range(3):
        sum_ref[128 * i + 96 : 128 * i + 128, :] = jnp.zeros((32, 128), BF16)
    last_weights(coef_ref, target, tail_ref, h_ref)
    pltpu.make_async_copy(rr_ref.at[0:7], rr_ref.at[0:7], recv_sems.at[1]).wait()

    def add(i, _):
        rows = pl.ds(pl.multiple_of(16 * i, 16), 16)
        total = rr_ref[0, rows, :]
        for k in range(1, 8):
            total = total + rr_ref[k, rows, :]
        high = total.astype(BF16)
        sum_ref[rows, :] = high
        sum_ref[pl.ds(pl.multiple_of(128 + 16 * i, 16), 16), :] = high
        sum_ref[pl.ds(pl.multiple_of(256 + 16 * i, 16), 16), :] = (total - high.astype(F32)).astype(BF16)
        return 0

    lax.fori_loop(0, 6, add, 0, unroll=True)

    home = zh + 2 * yl + 4 * yh + 8 * xl + 16 * xh + 32 * zl
    own = core == classes[2]
    row = pl.multiple_of((classes[0] + 2 * classes[1]) * 8, 8)
    here = out_ref.at[pl.ds(row, 8), pl.ds(pl.multiple_of(block * 128, 128), 128)]
    turns = flips((zh, xl, xh, yh, yl, zl), (1, 8, 16, 4, 2, 32))

    def deliver(high):
        pltpu.make_async_remote_copy(
            src_ref=tile_ref.at[high],
            dst_ref=here,
            send_sem=send_sems.at[2],
            recv_sem=recv_sems.at[2],
            device_id=2 * high + classes[2],
            device_id_type=LOGICAL,
        ).start()

    early = (0, 8)
    lost = (63 - home, home + subset(turns, 48))
    instead = [jnp.where(lost[n] == early[1 - n], lost[1 - n], lost[n]) for n in range(2)]

    def settle(high):
        return jnp.where(high == early[0], instead[0], jnp.where(high == early[1], instead[1], high))

    def make(start, end):
        tiles = jnp.dot(h_ref[8 * start : 8 * end, :], sum_ref[...], preferred_element_type=F32)
        tile_ref[start:end] = tiles.reshape(end - start, 8, 128)

    make(0, 16)
    for high in early:
        pl.when(jnp.logical_or(home != high, jnp.logical_not(own)))(functools.partial(deliver, high))
    make(16, 64)
    moved = jnp.logical_or(home == early[0], home == early[1])
    last = jnp.logical_or(moved, jnp.logical_not(own))

    def deliver_some(step, _):
        same_y, same_z = rem(step, 2), div(step, 2)
        first = home + (1 - same_y) * turns[4] + (1 - same_z) * turns[5]

        def send(mask):
            deliver(settle(first + subset(turns, mask)))

        pl.when(step > 0)(lambda: send(15))
        pl.when(jnp.logical_and(step > 0, jnp.logical_or(step < 3, last)))(lambda: send(0))
        for mask in (14, 1, 13, 2, 12, 3, 11, 4, 10, 5, 9, 6, 8, 7):
            send(mask)
        return 0

    lax.fori_loop(0, 4, deliver_some, 0)

    @pl.when(own)
    def _():
        pltpu.make_async_copy(tile_ref.at[home], here, recv_sems.at[2]).start()

    pltpu.make_async_copy(xr_ref.at[0:15], xr_ref.at[0:15], send_sems.at[0]).wait()
    pltpu.make_async_copy(part_ref.at[0:7], part_ref.at[0:7], send_sems.at[1]).wait()

    @pl.when(own)
    def _():
        pltpu.make_async_copy(tile_ref.at[0:63], tile_ref.at[0:63], send_sems.at[2]).wait()

    @pl.when(jnp.logical_not(own))
    def _():
        pltpu.make_async_copy(tile_ref, tile_ref, send_sems.at[2]).wait()

    pltpu.make_async_copy(out_ref, out_ref, recv_sems.at[2]).wait()


def shards(traces, phase_coef):
    return pl.pallas_call(
        kernel,
        out_shape=jax.ShapeDtypeStruct((32, 2048), F32),
        in_specs=[
            pl.BlockSpec(memory_space=pl.ANY),
            pl.BlockSpec(memory_space=pl.ANY),
            pl.BlockSpec(memory_space=pl.ANY),
        ],
        out_specs=pl.BlockSpec(memory_space=pl.ANY),
        scratch_shapes=[
            pltpu.SMEM((2, 4), F32),
            pltpu.VMEM((6, 64, 128), F32),
            pltpu.VMEM((5, 36, 8, 128), F32),
            pltpu.VMEM((5, 6, 8, 128), F32),
            pltpu.VMEM((5, 8, 128), F32),
            pltpu.VMEM((3, 12, 4, 8, 128), F32),
            pltpu.VMEM((1536, 512), BF16),
            pltpu.VMEM((512, 384), BF16),
            pltpu.VMEM((16, 32, 128), F32),
            pltpu.VMEM((512, 256), BF16),
            pltpu.VMEM((8, 96, 128), F32),
            pltpu.VMEM((8, 96, 128), F32),
            pltpu.VMEM((384, 128), BF16),
            pltpu.VMEM((64, 8, 128), F32),
            pltpu.SemaphoreType.DMA((3,)),
            pltpu.SemaphoreType.DMA((5,)),
        ],
        compiler_params=pltpu.CompilerParams(
            collective_id=0, has_side_effects=True, vmem_limit_bytes=60 * 2**20
        ),
    )(traces, phase_coef, jnp.asarray(tail_table()))


def solution(mesh):
    placed = (P(("gx", "gy"), None), P())
    return jax.shard_map(
        shards, mesh=mesh, in_specs=placed, out_specs=P(("gx", "gy"), None), check_vma=False
    )
```

```python
import functools

import jax
import jax.numpy as jnp
import numpy as np
from jax import lax
from jax.experimental import pallas as pl
from jax.experimental.pallas import tpu as pltpu
from jax.sharding import PartitionSpec as P

ORDER = 6
LOGICAL = pl.DeviceIdType.LOGICAL
F32 = jnp.float32
BF16 = jnp.bfloat16
AMP = 64.0

NODES = 0.5 * np.cos(np.pi * (2.0 * np.arange(ORDER) + 1.0) / (2.0 * ORDER))


def lagrange(points):
    points = np.asarray(points)[..., None, None]
    same = np.eye(ORDER, dtype=bool)
    spread = np.where(same, 1.0, NODES[:, None] - NODES[None, :])
    return np.where(same, 1.0, (points - NODES[None, :]) / spread).prod(-1)


CENTRE = lagrange(0.0)
HALVES = np.stack([((side - 0.5) + NODES) * 0.5 for side in (0, 1)])
TABLE = lagrange(HALVES)
WEIGHT = np.transpose(TABLE, (0, 2, 1))


def tail_table():
    out = np.zeros((ORDER, 64, 128))
    for high in range(64):
        total = np.eye(ORDER)
        for place in range(6):
            total = TABLE[(high >> place) & 1] @ total
        out[:, high, :96] = np.repeat(CENTRE[:, None] * total, 16, axis=1)
    return out.astype(np.float32)


def fit(function, terms):
    u = 0.125 + 0.125 * np.cos(np.pi * (np.arange(200) + 0.5) / 200)
    poly = np.polynomial.chebyshev.Chebyshev.fit(u, function(np.sqrt(u)), terms - 1, domain=[0, 0.25])
    return [float(c) for c in poly.convert(kind=np.polynomial.Polynomial).coef]


SIN = fit(lambda r: np.sin(np.pi * r) / r, 5)
SIN2 = [2.0 * c for c in fit(lambda r: np.sin(np.pi * r) / r, 4)]
COS = fit(lambda r: np.cos(np.pi * r), 5)
COS4 = fit(lambda r: np.cos(np.pi * r), 4)


def horner(coefs, u):
    total = coefs[-1]
    for c in coefs[-2::-1]:
        total = total * u + c
    return total


def turn(c):
    r = c - jnp.floor(c + 0.5)
    u = r * r
    twice = r * horner(SIN2, u)
    half_cos = horner(COS4, u)
    return 1.0 - (0.5 * twice) * twice, twice * half_cos


def turn_cos(c):
    r = c - jnp.floor(c + 0.5)
    twice = r * horner(SIN2, r * r)
    return 1.0 - (0.5 * twice) * twice


def half_turn(y):
    r = 0.5 - y
    u = r * r
    return r * horner(SIN, u), horner(COS, u)


def bend_value(coef, row, y):
    cosine = (0.5 - y) * horner(SIN, (0.5 - y) * (0.5 - y))
    c0, c1, c2, c3 = (coef[row, m] for m in range(4))
    return (c0 - c2) + cosine * ((c1 - 3.0 * c3) + cosine * (2.0 * c2 + cosine * (4.0 * c3)))


def bend_terms(coef, size):
    e1, e2, e3 = (coef[0, m] * float(-2.0 * AMP * np.sin(np.pi * m * size / 2.0)) for m in (1, 2, 3))
    return e1 - e3, 2.0 * e2, 4.0 * e3


def bend_step(terms, middle):
    cosine, sine = half_turn(middle)
    return sine * (terms[0] + cosine * (terms[1] + cosine * terms[2]))


def apply_real(weights, values):
    out = []
    for t in range(ORDER):
        total = weights[t][0] * values[0]
        for s in range(1, ORDER):
            total = total + weights[t][s] * values[s]
        out.append(total)
    return out


def iota(axis):
    return lax.broadcasted_iota(jnp.int32, (8, 128), axis)


def asf(value):
    return value.astype(F32)


def div(a, b):
    return lax.div(a, jnp.int32(b))


def rem(a, b):
    return lax.rem(a, jnp.int32(b))


def subset(deltas, mask):
    total = None
    for k, delta in enumerate(deltas):
        if (mask >> k) & 1:
            total = delta if total is None else total + delta
    return 0 if total is None else total


def abs_flip(bit, turned):
    return 1 - bit if turned else bit


def flips(bits, weights):
    return [weight * (1 - 2 * bit) for bit, weight in zip(bits, weights)]


def lane_parts(classes, core):
    lane = iota(1)
    place = lane >> 4
    x, y, z = (
        (2 * c + e + core) & 3 for c, e in zip(classes, (place >> 2, (place >> 1) & 1, place & 1))
    )
    return (z >> 1) + 2 * y + 8 * x + 32 * (z & 1), lane & 15


def early_levels(coef, box, top, w_ref, p_ref, v_ref):
    sub = iota(0)
    bits = [asf(sub & 1), asf((sub >> 1) & 1), asf(sub >> 2)]
    sign = [2.0 * bit - 1.0 for bit in bits]
    x0 = jnp.full((8, 128), 0.5, F32)
    x1 = x0 + sign[0] * 0.25
    x2 = x1 + sign[1] * 0.125
    word4 = asf(box * 16 + top)
    steps = [
        bend_step(bend_terms(coef, 2.0 ** -(level + 1)), x + sign[level - 1] * 2.0 ** -(level + 2))
        for level, x in ((1, x0), (2, x1), (3, x2))
    ]
    p0_mid = coef[0, 0] - coef[0, 2]

    def turned(values, angles):
        pairs = [(a * c - b * d, a * d + b * c) for (a, b), (c, d) in zip(values, angles)]
        return [a for a, _ in pairs], [b for _, b in pairs]

    linear2 = 2.0 * asf(top & 1) + 0.5
    linear3 = asf(top & 3) + 0.5
    third = [turn(sign[2] * ((linear3 + float(NODES[s])) * 0.25 + steps[2] * p_ref[0, s])) for s in range(ORDER)]
    constants = [[float(WEIGHT[0][t][s]) for s in range(ORDER)] for t in range(ORDER)]

    def by_side(side, values):
        mirror = jnp.broadcast_to(side, (8, 128)) == 1
        picked = [jnp.where(mirror, values[5 - s], values[s]) for s in range(ORDER)]
        out = apply_real(constants, picked)
        return [jnp.where(mirror, out[5 - t], out[t]) for t in range(ORDER)]

    def body(group, _):
        j0, j1 = rem(group, 2), div(group, 2)
        j0f, j1f, groupf = asf(j0), asf(j1), asf(group)
        word = word4 * 4.0 + groupf
        start = 0.5 * (j0f + 0.5) + AMP * p0_mid * bend_value(coef, 1, (word + 0.5) * 2.0**-12)
        real, imag = [], []
        for s in range(ORDER):
            node = float(NODES[s])
            p1 = bend_value(coef, 1, (word + (0.5 + node)) * 2.0**-12)
            c, d = turn(start + sign[0] * ((groupf + (0.5 + node)) * 0.25 + steps[0] * p1))
            real.append(c * float(CENTRE[s]))
            imag.append(d * float(CENTRE[s]))
        values = list(zip(by_side(j0, real), by_side(j0, imag)))
        word = word4 * 2.0 + j1f
        angles = []
        for s in range(ORDER):
            node = float(NODES[s])
            p1 = bend_value(coef, 1, (word + (0.5 + node)) * 2.0**-11)
            angles.append(turn(sign[1] * (((linear2 + j1f) + node) * 0.25 + steps[1] * p1)))
        values = list(zip(*(by_side(j1, part) for part in turned(values, angles))))
        weights = [[w_ref[0, ORDER * t + s] for s in range(ORDER)] for t in range(ORDER)]
        for c, part in enumerate(turned(values, third)):
            for t, value in enumerate(apply_real(weights, part)):
                v_ref[0, 2 * t + c, group] = value
        return 0

    lax.fori_loop(0, 4, body, 0)


def late_setup(coef, box, top, w_ref, p_ref, c_ref):
    full = box * 16 + top

    def body(i, scale):
        word = full >> i
        pick = (word & 1) == 1
        for t in range(ORDER):
            for s in range(ORDER):
                w_ref[i, ORDER * t + s] = jnp.where(pick, float(WEIGHT[1][t][s]), float(WEIGHT[0][t][s]))
        for s in range(ORDER):
            p_ref[i, s] = bend_value(coef, 1, (asf(word) + float(0.5 + NODES[s])) * scale)
        return scale * 2.0

    lax.fori_loop(0, 5, body, jnp.float32(2.0**-10))
    turn_of = top & 7

    def by_lane(values):
        out = jnp.full((8, 128), float(values[ORDER - 1]), F32)
        for t in range(ORDER - 1):
            out = jnp.where(turn_of == t, float(values[t]), out)
        return out

    e1, e2, e3 = (coef[0, m] * by_lane(-2.0 * AMP * np.sin(np.pi * m * NODES / 128.0)) for m in (1, 2, 3))
    node = by_lane(NODES)
    c_ref[0] = node
    c_ref[1] = e1 - e3
    c_ref[2] = 2.0 * e2
    c_ref[3] = 4.0 * e3
    c_ref[4] = node * (asf(box) + 0.5)


def spread(value, t):
    return jnp.take_along_axis(value, (iota(1) & 120) + t, axis=1)


def late_levels(coef, box, top, order, w_ref, p_ref, c_ref, v_ref, g_ref, between):
    sub = iota(0)
    x3 = asf(4 * (sub & 1) + (sub & 2) + (sub >> 2)) * 0.125 + 0.0625
    full = box * 16 + top
    terms = [bend_terms(coef, 2.0 ** -(level + 1)) for level in (4, 5, 6)]

    def sign_of(bit):
        return (2 * bit - 1).astype(F32)

    def turns(i, level_terms, shift, parent, sign):
        steps = bend_step(level_terms, parent + sign * shift)
        linear = asf((full >> i) & 3) + 0.5
        return [turn(sign * ((linear + float(NODES[s])) * 0.25 + steps * p_ref[i, s])) for s in range(ORDER)]

    def level_step(level, q3, q4):
        first = level == 4
        i = level - 3
        parent = x3 + jnp.where(first, 0.0, sign_of(q3) * 2.0**-5)
        sign = jnp.where(first, sign_of(q3), sign_of(q4))
        level_terms = [jnp.where(first, a, b) for a, b in zip(terms[0], terms[1])]
        real, imag = [], []
        for s, (c, d) in enumerate(turns(i, level_terms, jnp.where(first, 2.0**-6, 2.0**-7), parent, sign)):
            a, b = v_ref[i - 1, 2 * s], v_ref[i - 1, 2 * s + 1]
            real.append(a * c - b * d)
            imag.append(a * d + b * c)
        weights = [[w_ref[i, ORDER * t + s] for s in range(ORDER)] for t in range(ORDER)]
        for c, values in enumerate((real, imag)):
            for t, value in enumerate(apply_real(weights, values)):
                v_ref[i, 2 * t + c] = value

    def last_step(parent, bit, place):
        sign = sign_of(bit)
        middle = parent + sign * 2.0**-7 + c_ref[0] * (1.0 / 128.0)
        steps = bend_step((c_ref[1], c_ref[2], c_ref[3]), middle)
        switch = [turn((c_ref[4] + c_ref[0] * float(NODES[u])) + steps * p_ref[4, u]) for u in range(ORDER)]
        merged = []
        for s, (c, d) in enumerate(turns(3, terms[2], 2.0**-8, parent, sign)):
            a = b = None
            for u in range(ORDER):
                weight = w_ref[3, ORDER * u + s]
                a = switch[u][0] * weight if a is None else a + switch[u][0] * weight
                b = switch[u][1] * weight if b is None else b + switch[u][1] * weight
            merged.append((a * c - b * d, a * d + b * c))
        parts = [v_ref[2, 2 * s] + v_ref[2, 2 * s + 1] for s in range(ORDER)]
        for t in range(ORDER):
            k1 = k2 = k3 = None
            for s in range(ORDER):
                c, d = spread(merged[s][0], t), spread(merged[s][1], t)
                m1, m2, m3 = parts[s] * c, v_ref[2, 2 * s] * (d - c), v_ref[2, 2 * s + 1] * (c + d)
                k1 = m1 if k1 is None else k1 + m1
                k2 = m2 if k2 is None else k2 + m2
                k3 = m3 if k3 is None else k3 + m3
            real, imag = k1 - k3, k1 + k2
            rows = pl.ds(pl.multiple_of(place * 192 + 16 * t, 16), 16)
            rows_low = pl.ds(pl.multiple_of(place * 192 + 96 + 16 * t, 16), 16)
            for j in range(4):
                both = jnp.concatenate([real[j], imag[j]], axis=0)
                high = both.astype(BF16)
                g_ref[rows, 128 * j : 128 * (j + 1)] = high
                g_ref[rows_low, 128 * j : 128 * (j + 1)] = (both - high.astype(F32)).astype(BF16)

    def over(n, _):
        @pl.when(n >= 4)
        def _():
            between(n - 4)

        @pl.when(n < 4)
        def _():
            q3, q4 = order(div(n, 2)), rem(n, 2)

            def levels(level, _):
                level_step(level, q3, q4)
                return 0

            lax.fori_loop(4 + q4, 6, levels, 0)
            x5 = x3 + (sign_of(q3) * 2.0**-5 + sign_of(q4) * 2.0**-6)

            def over5(q5, _):
                last_step(x5, q5, 4 * q3 + q4 + 2 * q5)
                return 0

            lax.fori_loop(0, 2, over5, 0)

        return 0

    lax.fori_loop(0, 6, over, 0)


def last_weights(coef, group, tail_ref, h_ref):
    sub, lane = iota(0), iota(1)
    own = lane & 7
    same = sub == own
    box6 = 32 * (own & 1) + 8 * (own & 2) + 2 * (own & 4)
    box6 = box6 + (4 * rem(group, 2) + 2 * rem(div(group, 2), 2) + div(group, 4))
    inner = 32 * (sub & 1) + 8 * (sub & 2) + 2 * (sub & 4)
    base = box6 * 64 + inner
    quarter = 0.25 * asf((lane >> 3) & 1)
    p1_mid = coef[1, 0] - coef[1, 2]

    def rows_of(r):
        centre = (asf(base + (4 * rem(r, 2) + 2 * rem(div(r, 2), 2) + div(r, 4))) + 0.5) * 2.0**-12
        total = None
        for t in range(ORDER):
            node = float(NODES[t])
            steps = bend_step(bend_terms(coef, node / 4096.0), centre + node / 8192.0)
            term = turn_cos((quarter - 0.5 * node) - steps * p1_mid)
            term = term * tail_ref[t, pl.ds(pl.multiple_of(8 * r, 8), 8), :]
            total = term if total is None else total + term
        return total

    def body(r, _):
        total = rows_of(r)
        for k in range(0, 8, 2):
            both = jnp.concatenate(
                [jnp.where(same, jnp.broadcast_to(total[k + n : k + n + 1], (8, 128)), 0.0) for n in range(2)], axis=0
            )
            high = both.astype(BF16)
            rows = pl.ds(pl.multiple_of(64 * r + 8 * k, 16), 16)
            h_ref[rows, 0:128] = high
            h_ref[rows, 128:256] = (both - high.astype(F32)).astype(BF16)
            h_ref[rows, 256:384] = high
        return 0

    lax.fori_loop(0, 8, body, 0)


def kernel(
    x_ref,
    coef_hbm,
    tail_hbm,
    out_ref,
    coef_ref,
    tail_ref,
    w_ref,
    p_ref,
    c_ref,
    v_ref,
    g_ref,
    h_ref,
    xr_ref,
    xs_ref,
    part_ref,
    rr_ref,
    sum_ref,
    tile_ref,
    send_sems,
    recv_sems,
):
    fetch_coef = pltpu.make_async_copy(coef_hbm, coef_ref, recv_sems.at[3])
    fetch_tail = pltpu.make_async_copy(tail_hbm, tail_ref, recv_sems.at[4])
    gx, gy = lax.axis_index("gx"), lax.axis_index("gy")
    core = rem(gy, 2)
    zl, xs = div(gx, 4), rem(gx, 4)
    xh, xl = div(xs, 2), rem(xs, 2)
    yh, yl, zh = div(gy, 8), rem(div(gy, 4), 2), rem(div(gy, 2), 2)
    me = gx * 16 + gy
    highs, lows = (xh, yh, zh), (xl, yl, zl)
    unlike = [h + l - 2 * h * l for h, l in zip(highs, lows)]
    to_a = [16 * (1 - 2 * xl), 4 * (1 - 2 * yl), 64 * (1 - 2 * zl)]
    to_b = [16 * (3 - 2 * xs), 4 * (3 - 2 * (2 * yh + yl)), 2 * (1 - 2 * zh) + 64 * (1 - 2 * zl)]
    to_class = [a + core * (b - a) for a, b in zip(to_a, to_b)]
    to_group = [b + core * (a - b) for a, b in zip(to_a, to_b)]
    to_core = 1 - 2 * core
    class_a, class_b = highs, [1 - d for d in unlike]
    place_a, place_b = lows, [1 - l for l in lows]
    group_a, group_b = [1 - d for d in unlike], [1 - h for h in highs]

    def mine(for_a, for_b):
        return [a + core * (b - a) for a, b in zip(for_a, for_b)]

    def others(for_a, for_b):
        return [b + core * (a - b) for a, b in zip(for_a, for_b)]

    def number(values):
        return values[0] + 2 * values[1] + 4 * values[2]

    classes, groups = mine(class_a, class_b), mine(group_a, group_b)
    target = number(classes)
    block = number(groups) + 8 * core

    barrier = pltpu.get_barrier_semaphore()
    for mask in range(1, 16):
        source = me + subset(to_class + [to_core], mask)
        pl.semaphore_signal(barrier, inc=1, device_id=source, device_id_type=LOGICAL)
    for mask in range(1, 8):
        pl.semaphore_signal(barrier, inc=1, device_id=me + subset(to_group, mask), device_id_type=LOGICAL)
    fetch_coef.start()
    fetch_tail.start()
    pl.semaphore_wait(barrier, 22)

    def columns(m):
        return x_ref.at[:, pl.ds(pl.multiple_of(m * 128, 128), 128)]

    own_slot = 2 * number(mine(place_a, place_b)[::-1]) + core
    other_slot = 2 * number(others(place_a, place_b)[::-1]) + core
    other_groups = others(group_a, group_b)
    other_block = number(other_groups) + 8 * (1 - core)
    for mask in range(7, -1, -1):
        routes = [(other_block, other_groups, other_slot, me + to_core + subset(to_group, mask))]
        if mask:
            routes.append((block, groups, own_slot, me + subset(to_class, mask)))
        for first, group_bits, slot, device in routes:
            pltpu.make_async_remote_copy(
                src_ref=columns(first + subset(flips(group_bits, (1, 2, 4)), mask)),
                dst_ref=xr_ref.at[slot],
                send_sem=send_sems.at[0],
                recv_sem=recv_sems.at[0],
                device_id=device,
                device_id_type=LOGICAL,
            ).start()
    pltpu.make_async_copy(columns(block), xr_ref.at[own_slot], recv_sems.at[0]).start()
    box, top = lane_parts(classes, core)
    fetch_coef.wait()
    late_setup(coef_ref, box, top, w_ref, p_ref, c_ref)
    early_levels(coef_ref, box, top, w_ref, p_ref, v_ref)

    def order(h):
        return classes[0] + (1 - h) * (1 - 2 * classes[0])

    def split(i, _):
        for j in range(4):
            piece = jnp.concatenate([xr_ref[2 * i + s, pl.ds(j, 8, stride=4), :] for s in range(2)], axis=0)
            high = piece.astype(BF16)
            rows = pl.ds(pl.multiple_of(128 * j + 16 * i, 16), 16)
            xs_ref[rows, 0:128] = high
            xs_ref[rows, 128:256] = (piece - high.astype(F32)).astype(BF16)
        return 0

    def half(h):
        @pl.when(h == 0)
        def _():
            pltpu.make_async_copy(xr_ref, xr_ref, recv_sems.at[0]).wait()
            lax.fori_loop(0, 8, split, 0, unroll=4)

        q3 = order(h)
        far = (1 - h) * to_group[0]
        for mask in range(3, -1, -1):
            i = classes[1] + 2 * classes[2] + subset(flips(classes[1:], (1, 2)), mask)
            rows = pl.ds(pl.multiple_of((4 * q3 + i) * 192, 16), 192)
            wide = jnp.dot(g_ref[rows, :], xs_ref[...], preferred_element_type=F32)
            part = wide[0:96, 0:128] + (wide[0:96, 128:256] + wide[96:192, 0:128])

            def send():
                part_ref[4 * q3 + i] = part
                pltpu.make_async_remote_copy(
                    src_ref=part_ref.at[4 * q3 + i],
                    dst_ref=rr_ref.at[target],
                    send_sem=send_sems.at[1],
                    recv_sem=recv_sems.at[1],
                    device_id=me + far + subset(to_group[1:], mask),
                    device_id_type=LOGICAL,
                ).start()

            if mask:
                send()
            else:
                pl.when(h == 0)(send)

                @pl.when(h == 1)
                def _():
                    rr_ref[target] = part

    late_levels(coef_ref, box, top, order, w_ref, p_ref, c_ref, v_ref, g_ref, half)
    fetch_tail.wait()
    for i in range(3):
        sum_ref[128 * i + 96 : 128 * i + 128, :] = jnp.zeros((32, 128), BF16)
    last_weights(coef_ref, target, tail_ref, h_ref)
    pltpu.make_async_copy(rr_ref.at[0:7], rr_ref.at[0:7], recv_sems.at[1]).wait()

    def add(i, _):
        rows = pl.ds(pl.multiple_of(16 * i, 16), 16)
        total = rr_ref[0, rows, :]
        for k in range(1, 8):
            total = total + rr_ref[k, rows, :]
        high = total.astype(BF16)
        sum_ref[rows, :] = high
        sum_ref[pl.ds(pl.multiple_of(128 + 16 * i, 16), 16), :] = high
        sum_ref[pl.ds(pl.multiple_of(256 + 16 * i, 16), 16), :] = (total - high.astype(F32)).astype(BF16)
        return 0

    lax.fori_loop(0, 6, add, 0, unroll=True)

    home = zh + 2 * yl + 4 * yh + 8 * xl + 16 * xh + 32 * zl
    own = core == classes[2]
    row = pl.multiple_of((classes[0] + 2 * classes[1]) * 8, 8)
    here = out_ref.at[pl.ds(row, 8), pl.ds(pl.multiple_of(block * 128, 128), 128)]
    turns = flips((zh, xl, xh, yh, yl, zl), (1, 8, 16, 4, 2, 32))

    def deliver(high):
        pltpu.make_async_remote_copy(
            src_ref=tile_ref.at[high],
            dst_ref=here,
            send_sem=send_sems.at[2],
            recv_sem=recv_sems.at[2],
            device_id=2 * high + classes[2],
            device_id_type=LOGICAL,
        ).start()

    early = (0, 8)
    lost = (63 - home, home + subset(turns, 48))
    instead = [jnp.where(lost[n] == early[1 - n], lost[1 - n], lost[n]) for n in range(2)]

    def settle(high):
        return jnp.where(high == early[0], instead[0], jnp.where(high == early[1], instead[1], high))

    def make(start, end):
        tiles = jnp.dot(h_ref[8 * start : 8 * end, :], sum_ref[...], preferred_element_type=F32)
        tile_ref[start:end] = tiles.reshape(end - start, 8, 128)

    make(0, 16)
    for high in early:
        pl.when(jnp.logical_or(home != high, jnp.logical_not(own)))(functools.partial(deliver, high))
    make(16, 64)
    moved = jnp.logical_or(home == early[0], home == early[1])
    last = jnp.logical_or(moved, jnp.logical_not(own))

    def deliver_some(step, _):
        same_y, same_z = rem(step, 2), div(step, 2)
        first = home + (1 - same_y) * turns[4] + (1 - same_z) * turns[5]

        def send(mask):
            deliver(settle(first + subset(turns, mask)))

        pl.when(step > 0)(lambda: send(15))
        pl.when(jnp.logical_and(step > 0, jnp.logical_or(step < 3, last)))(lambda: send(0))
        for mask in (14, 1, 13, 2, 12, 3, 11, 4, 10, 5, 9, 6, 8, 7):
            send(mask)
        return 0

    lax.fori_loop(0, 4, deliver_some, 0)

    @pl.when(own)
    def _():
        pltpu.make_async_copy(tile_ref.at[home], here, recv_sems.at[2]).start()

    pltpu.make_async_copy(xr_ref.at[0:15], xr_ref.at[0:15], send_sems.at[0]).wait()
    pltpu.make_async_copy(part_ref.at[0:7], part_ref.at[0:7], send_sems.at[1]).wait()

    @pl.when(own)
    def _():
        pltpu.make_async_copy(tile_ref.at[0:63], tile_ref.at[0:63], send_sems.at[2]).wait()

    @pl.when(jnp.logical_not(own))
    def _():
        pltpu.make_async_copy(tile_ref, tile_ref, send_sems.at[2]).wait()

    pltpu.make_async_copy(out_ref, out_ref, recv_sems.at[2]).wait()


def shards(traces, phase_coef):
    return pl.pallas_call(
        kernel,
        out_shape=jax.ShapeDtypeStruct((32, 2048), F32),
        in_specs=[
            pl.BlockSpec(memory_space=pl.ANY),
            pl.BlockSpec(memory_space=pl.ANY),
            pl.BlockSpec(memory_space=pl.ANY),
        ],
        out_specs=pl.BlockSpec(memory_space=pl.ANY),
        scratch_shapes=[
            pltpu.SMEM((2, 4), F32),
            pltpu.VMEM((6, 64, 128), F32),
            pltpu.VMEM((5, 36, 8, 128), F32),
            pltpu.VMEM((5, 6, 8, 128), F32),
            pltpu.VMEM((5, 8, 128), F32),
            pltpu.VMEM((3, 12, 4, 8, 128), F32),
            pltpu.VMEM((1536, 512), BF16),
            pltpu.VMEM((512, 384), BF16),
            pltpu.VMEM((16, 32, 128), F32),
            pltpu.VMEM((512, 256), BF16),
            pltpu.VMEM((8, 96, 128), F32),
            pltpu.VMEM((8, 96, 128), F32),
            pltpu.VMEM((384, 128), BF16),
            pltpu.VMEM((64, 8, 128), F32),
            pltpu.SemaphoreType.DMA((3,)),
            pltpu.SemaphoreType.DMA((5,)),
        ],
        compiler_params=pltpu.CompilerParams(
            collective_id=0, has_side_effects=True, vmem_limit_bytes=60 * 2**20
        ),
    )(traces, phase_coef, jnp.asarray(tail_table()))


def solution(mesh):
    placed = (P(("gx", "gy"), None), P())
    return jax.shard_map(
        shards, mesh=mesh, in_specs=placed, out_specs=P(("gx", "gy"), None), check_vma=False
    )
```

```python
import functools

import jax
import jax.numpy as jnp
import numpy as np
from jax import lax
from jax.experimental import pallas as pl
from jax.experimental.pallas import tpu as pltpu
from jax.sharding import PartitionSpec as P

ORDER = 6
LOGICAL = pl.DeviceIdType.LOGICAL
F32 = jnp.float32
BF16 = jnp.bfloat16
AMP = 64.0

NODES = 0.5 * np.cos(np.pi * (2.0 * np.arange(ORDER) + 1.0) / (2.0 * ORDER))


def lagrange(points):
    points = np.asarray(points)[..., None, None]
    same = np.eye(ORDER, dtype=bool)
    spread = np.where(same, 1.0, NODES[:, None] - NODES[None, :])
    return np.where(same, 1.0, (points - NODES[None, :]) / spread).prod(-1)


CENTRE = lagrange(0.0)
HALVES = np.stack([((side - 0.5) + NODES) * 0.5 for side in (0, 1)])
TABLE = lagrange(HALVES)
WEIGHT = np.transpose(TABLE, (0, 2, 1))


def tail_table():
    out = np.zeros((ORDER, 64, 128))
    for high in range(64):
        total = np.eye(ORDER)
        for place in range(6):
            total = TABLE[(high >> place) & 1] @ total
        out[:, high, :96] = np.repeat(CENTRE[:, None] * total, 16, axis=1)
    return out.astype(np.float32)


def fit(function, terms):
    u = 0.125 + 0.125 * np.cos(np.pi * (np.arange(200) + 0.5) / 200)
    poly = np.polynomial.chebyshev.Chebyshev.fit(u, function(np.sqrt(u)), terms - 1, domain=[0, 0.25])
    return [float(c) for c in poly.convert(kind=np.polynomial.Polynomial).coef]


SIN = fit(lambda r: np.sin(np.pi * r) / r, 5)
SIN2 = [2.0 * c for c in fit(lambda r: np.sin(np.pi * r) / r, 4)]
COS = fit(lambda r: np.cos(np.pi * r), 5)
COS4 = fit(lambda r: np.cos(np.pi * r), 4)


def horner(coefs, u):
    total = coefs[-1]
    for c in coefs[-2::-1]:
        total = total * u + c
    return total


def turn(c):
    r = c - jnp.floor(c + 0.5)
    u = r * r
    twice = r * horner(SIN2, u)
    half_cos = horner(COS4, u)
    return 1.0 - (0.5 * twice) * twice, twice * half_cos


def turn_cos(c):
    r = c - jnp.floor(c + 0.5)
    twice = r * horner(SIN2, r * r)
    return 1.0 - (0.5 * twice) * twice


def half_turn(y):
    r = 0.5 - y
    u = r * r
    return r * horner(SIN, u), horner(COS, u)


def bend_value(coef, row, y):
    cosine = (0.5 - y) * horner(SIN, (0.5 - y) * (0.5 - y))
    c0, c1, c2, c3 = (coef[row, m] for m in range(4))
    return (c0 - c2) + cosine * ((c1 - 3.0 * c3) + cosine * (2.0 * c2 + cosine * (4.0 * c3)))


def bend_terms(coef, size):
    e1, e2, e3 = (coef[0, m] * float(-2.0 * AMP * np.sin(np.pi * m * size / 2.0)) for m in (1, 2, 3))
    return e1 - e3, 2.0 * e2, 4.0 * e3


def bend_step(terms, middle):
    cosine, sine = half_turn(middle)
    return sine * (terms[0] + cosine * (terms[1] + cosine * terms[2]))


def apply_real(weights, values):
    out = []
    for t in range(ORDER):
        total = weights[t][0] * values[0]
        for s in range(1, ORDER):
            total = total + weights[t][s] * values[s]
        out.append(total)
    return out


def iota(axis):
    return lax.broadcasted_iota(jnp.int32, (8, 128), axis)


def asf(value):
    return value.astype(F32)


def div(a, b):
    return lax.div(a, jnp.int32(b))


def rem(a, b):
    return lax.rem(a, jnp.int32(b))


def subset(deltas, mask):
    total = None
    for k, delta in enumerate(deltas):
        if (mask >> k) & 1:
            total = delta if total is None else total + delta
    return 0 if total is None else total


def abs_flip(bit, turned):
    return 1 - bit if turned else bit


def flips(bits, weights):
    return [weight * (1 - 2 * bit) for bit, weight in zip(bits, weights)]


def lane_parts(classes, core):
    lane = iota(1)
    place = lane >> 4
    x, y, z = (
        (2 * c + e + core) & 3 for c, e in zip(classes, (place >> 2, (place >> 1) & 1, place & 1))
    )
    return (z >> 1) + 2 * y + 8 * x + 32 * (z & 1), lane & 15


def early_levels(coef, box, top, w_ref, p_ref, v_ref):
    sub = iota(0)
    bits = [asf(sub & 1), asf((sub >> 1) & 1), asf(sub >> 2)]
    sign = [2.0 * bit - 1.0 for bit in bits]
    x0 = jnp.full((8, 128), 0.5, F32)
    x1 = x0 + sign[0] * 0.25
    x2 = x1 + sign[1] * 0.125
    word4 = asf(box * 16 + top)
    steps = [
        bend_step(bend_terms(coef, 2.0 ** -(level + 1)), x + sign[level - 1] * 2.0 ** -(level + 2))
        for level, x in ((1, x0), (2, x1), (3, x2))
    ]
    p0_mid = coef[0, 0] - coef[0, 2]

    def turned(values, angles):
        pairs = [(a * c - b * d, a * d + b * c) for (a, b), (c, d) in zip(values, angles)]
        return [a for a, _ in pairs], [b for _, b in pairs]

    linear2 = 2.0 * asf(top & 1) + 0.5
    linear3 = asf(top & 3) + 0.5
    third = [turn(sign[2] * ((linear3 + float(NODES[s])) * 0.25 + steps[2] * p_ref[0, s])) for s in range(ORDER)]
    constants = [[float(WEIGHT[0][t][s]) for s in range(ORDER)] for t in range(ORDER)]

    def by_side(side, values):
        mirror = jnp.broadcast_to(side, (8, 128)) == 1
        picked = [jnp.where(mirror, values[5 - s], values[s]) for s in range(ORDER)]
        out = apply_real(constants, picked)
        return [jnp.where(mirror, out[5 - t], out[t]) for t in range(ORDER)]

    def body(group, _):
        j0, j1 = rem(group, 2), div(group, 2)
        j0f, j1f, groupf = asf(j0), asf(j1), asf(group)
        word = word4 * 4.0 + groupf
        start = 0.5 * (j0f + 0.5) + AMP * p0_mid * bend_value(coef, 1, (word + 0.5) * 2.0**-12)
        real, imag = [], []
        for s in range(ORDER):
            node = float(NODES[s])
            p1 = bend_value(coef, 1, (word + (0.5 + node)) * 2.0**-12)
            c, d = turn(start + sign[0] * ((groupf + (0.5 + node)) * 0.25 + steps[0] * p1))
            real.append(c * float(CENTRE[s]))
            imag.append(d * float(CENTRE[s]))
        values = list(zip(by_side(j0, real), by_side(j0, imag)))
        word = word4 * 2.0 + j1f
        angles = []
        for s in range(ORDER):
            node = float(NODES[s])
            p1 = bend_value(coef, 1, (word + (0.5 + node)) * 2.0**-11)
            angles.append(turn(sign[1] * (((linear2 + j1f) + node) * 0.25 + steps[1] * p1)))
        values = list(zip(*(by_side(j1, part) for part in turned(values, angles))))
        weights = [[w_ref[0, ORDER * t + s] for s in range(ORDER)] for t in range(ORDER)]
        for c, part in enumerate(turned(values, third)):
            for t, value in enumerate(apply_real(weights, part)):
                v_ref[0, 2 * t + c, group] = value
        return 0

    lax.fori_loop(0, 4, body, 0)


def late_setup(coef, box, top, w_ref, p_ref, c_ref):
    full = box * 16 + top

    def body(i, scale):
        word = full >> i
        pick = (word & 1) == 1
        for t in range(ORDER):
            for s in range(ORDER):
                w_ref[i, ORDER * t + s] = jnp.where(pick, float(WEIGHT[1][t][s]), float(WEIGHT[0][t][s]))
        for s in range(ORDER):
            p_ref[i, s] = bend_value(coef, 1, (asf(word) + float(0.5 + NODES[s])) * scale)
        return scale * 2.0

    lax.fori_loop(0, 5, body, jnp.float32(2.0**-10))
    turn_of = top & 7

    def by_lane(values):
        out = jnp.full((8, 128), float(values[ORDER - 1]), F32)
        for t in range(ORDER - 1):
            out = jnp.where(turn_of == t, float(values[t]), out)
        return out

    e1, e2, e3 = (coef[0, m] * by_lane(-2.0 * AMP * np.sin(np.pi * m * NODES / 128.0)) for m in (1, 2, 3))
    node = by_lane(NODES)
    c_ref[0] = node
    c_ref[1] = e1 - e3
    c_ref[2] = 2.0 * e2
    c_ref[3] = 4.0 * e3
    c_ref[4] = node * (asf(box) + 0.5)


def spread(value, t):
    return jnp.take_along_axis(value, (iota(1) & 120) + t, axis=1)


def late_levels(coef, box, top, order, w_ref, p_ref, c_ref, v_ref, g_ref, between):
    sub = iota(0)
    x3 = asf(4 * (sub & 1) + (sub & 2) + (sub >> 2)) * 0.125 + 0.0625
    full = box * 16 + top
    terms = [bend_terms(coef, 2.0 ** -(level + 1)) for level in (4, 5, 6)]

    def sign_of(bit):
        return (2 * bit - 1).astype(F32)

    def turns(i, level_terms, shift, parent, sign):
        steps = bend_step(level_terms, parent + sign * shift)
        linear = asf((full >> i) & 3) + 0.5
        return [turn(sign * ((linear + float(NODES[s])) * 0.25 + steps * p_ref[i, s])) for s in range(ORDER)]

    def level_step(level, q3, q4):
        first = level == 4
        i = level - 3
        parent = x3 + jnp.where(first, 0.0, sign_of(q3) * 2.0**-5)
        sign = jnp.where(first, sign_of(q3), sign_of(q4))
        level_terms = [jnp.where(first, a, b) for a, b in zip(terms[0], terms[1])]
        real, imag = [], []
        for s, (c, d) in enumerate(turns(i, level_terms, jnp.where(first, 2.0**-6, 2.0**-7), parent, sign)):
            a, b = v_ref[i - 1, 2 * s], v_ref[i - 1, 2 * s + 1]
            real.append(a * c - b * d)
            imag.append(a * d + b * c)
        weights = [[w_ref[i, ORDER * t + s] for s in range(ORDER)] for t in range(ORDER)]
        for c, values in enumerate((real, imag)):
            for t, value in enumerate(apply_real(weights, values)):
                v_ref[i, 2 * t + c] = value

    def last_step(parent, bit, place):
        sign = sign_of(bit)
        middle = parent + sign * 2.0**-7 + c_ref[0] * (1.0 / 128.0)
        steps = bend_step((c_ref[1], c_ref[2], c_ref[3]), middle)
        switch = [turn((c_ref[4] + c_ref[0] * float(NODES[u])) + steps * p_ref[4, u]) for u in range(ORDER)]
        merged = []
        for s, (c, d) in enumerate(turns(3, terms[2], 2.0**-8, parent, sign)):
            a = b = None
            for u in range(ORDER):
                weight = w_ref[3, ORDER * u + s]
                a = switch[u][0] * weight if a is None else a + switch[u][0] * weight
                b = switch[u][1] * weight if b is None else b + switch[u][1] * weight
            merged.append((a * c - b * d, a * d + b * c))
        parts = [v_ref[2, 2 * s] + v_ref[2, 2 * s + 1] for s in range(ORDER)]
        for t in range(ORDER):
            k1 = k2 = k3 = None
            for s in range(ORDER):
                c, d = spread(merged[s][0], t), spread(merged[s][1], t)
                m1, m2, m3 = parts[s] * c, v_ref[2, 2 * s] * (d - c), v_ref[2, 2 * s + 1] * (c + d)
                k1 = m1 if k1 is None else k1 + m1
                k2 = m2 if k2 is None else k2 + m2
                k3 = m3 if k3 is None else k3 + m3
            real, imag = k1 - k3, k1 + k2
            rows = pl.ds(pl.multiple_of(place * 192 + 16 * t, 16), 16)
            rows_low = pl.ds(pl.multiple_of(place * 192 + 96 + 16 * t, 16), 16)
            for j in range(4):
                both = jnp.concatenate([real[j], imag[j]], axis=0)
                high = both.astype(BF16)
                g_ref[rows, 128 * j : 128 * (j + 1)] = high
                g_ref[rows_low, 128 * j : 128 * (j + 1)] = (both - high.astype(F32)).astype(BF16)

    def over(n, _):
        @pl.when(n >= 4)
        def _():
            between(n - 4)

        @pl.when(n < 4)
        def _():
            q3, q4 = order(div(n, 2)), rem(n, 2)

            def levels(level, _):
                level_step(level, q3, q4)
                return 0

            lax.fori_loop(4 + q4, 6, levels, 0)
            x5 = x3 + (sign_of(q3) * 2.0**-5 + sign_of(q4) * 2.0**-6)

            def over5(q5, _):
                last_step(x5, q5, 4 * q3 + q4 + 2 * q5)
                return 0

            lax.fori_loop(0, 2, over5, 0)

        return 0

    lax.fori_loop(0, 6, over, 0)


def last_weights(coef, group, tail_ref, h_ref):
    sub, lane = iota(0), iota(1)
    own = lane & 7
    same = sub == own
    box6 = 32 * (own & 1) + 8 * (own & 2) + 2 * (own & 4)
    box6 = box6 + (4 * rem(group, 2) + 2 * rem(div(group, 2), 2) + div(group, 4))
    inner = 32 * (sub & 1) + 8 * (sub & 2) + 2 * (sub & 4)
    base = box6 * 64 + inner
    quarter = 0.25 * asf((lane >> 3) & 1)
    p1_mid = coef[1, 0] - coef[1, 2]

    def rows_of(r):
        centre = (asf(base + (4 * rem(r, 2) + 2 * rem(div(r, 2), 2) + div(r, 4))) + 0.5) * 2.0**-12
        total = None
        for t in range(ORDER):
            node = float(NODES[t])
            steps = bend_step(bend_terms(coef, node / 4096.0), centre + node / 8192.0)
            term = turn_cos((quarter - 0.5 * node) - steps * p1_mid)
            term = term * tail_ref[t, pl.ds(pl.multiple_of(8 * r, 8), 8), :]
            total = term if total is None else total + term
        return total

    def body(r, _):
        total = rows_of(r)
        for k in range(0, 8, 2):
            both = jnp.concatenate(
                [jnp.where(same, jnp.broadcast_to(total[k + n : k + n + 1], (8, 128)), 0.0) for n in range(2)], axis=0
            )
            high = both.astype(BF16)
            rows = pl.ds(pl.multiple_of(64 * r + 8 * k, 16), 16)
            h_ref[rows, 0:128] = high
            h_ref[rows, 128:256] = (both - high.astype(F32)).astype(BF16)
            h_ref[rows, 256:384] = high
        return 0

    lax.fori_loop(0, 8, body, 0)


def kernel(
    x_ref,
    coef_hbm,
    tail_hbm,
    out_ref,
    coef_ref,
    tail_ref,
    w_ref,
    p_ref,
    c_ref,
    v_ref,
    g_ref,
    h_ref,
    xr_ref,
    xs_ref,
    part_ref,
    rr_ref,
    sum_ref,
    tile_ref,
    send_sems,
    recv_sems,
):
    fetch_coef = pltpu.make_async_copy(coef_hbm, coef_ref, recv_sems.at[3])
    fetch_tail = pltpu.make_async_copy(tail_hbm, tail_ref, recv_sems.at[4])
    fetch_coef.start()
    fetch_tail.start()
    gx, gy = lax.axis_index("gx"), lax.axis_index("gy")
    core = rem(gy, 2)
    zl, xs = div(gx, 4), rem(gx, 4)
    xh, xl = div(xs, 2), rem(xs, 2)
    yh, yl, zh = div(gy, 8), rem(div(gy, 4), 2), rem(div(gy, 2), 2)
    me = gx * 16 + gy
    highs, lows = (xh, yh, zh), (xl, yl, zl)
    unlike = [h + l - 2 * h * l for h, l in zip(highs, lows)]
    to_a = [16 * (1 - 2 * xl), 4 * (1 - 2 * yl), 64 * (1 - 2 * zl)]
    to_b = [16 * (3 - 2 * xs), 4 * (3 - 2 * (2 * yh + yl)), 2 * (1 - 2 * zh) + 64 * (1 - 2 * zl)]
    to_class = [a + core * (b - a) for a, b in zip(to_a, to_b)]
    to_group = [b + core * (a - b) for a, b in zip(to_a, to_b)]
    to_core = 1 - 2 * core
    class_a, class_b = highs, [1 - d for d in unlike]
    place_a, place_b = lows, [1 - l for l in lows]
    group_a, group_b = [1 - d for d in unlike], [1 - h for h in highs]

    def mine(for_a, for_b):
        return [a + core * (b - a) for a, b in zip(for_a, for_b)]

    def others(for_a, for_b):
        return [b + core * (a - b) for a, b in zip(for_a, for_b)]

    def number(values):
        return values[0] + 2 * values[1] + 4 * values[2]

    classes, groups = mine(class_a, class_b), mine(group_a, group_b)
    target = number(classes)
    block = number(groups) + 8 * core

    barrier = pltpu.get_barrier_semaphore()
    for mask in range(1, 16):
        source = me + subset(to_class + [to_core], mask)
        pl.semaphore_signal(barrier, inc=1, device_id=source, device_id_type=LOGICAL)
    for mask in range(1, 8):
        pl.semaphore_signal(barrier, inc=1, device_id=me + subset(to_group, mask), device_id_type=LOGICAL)
    box, top = lane_parts(classes, core)
    fetch_coef.wait()
    late_setup(coef_ref, box, top, w_ref, p_ref, c_ref)
    early_levels(coef_ref, box, top, w_ref, p_ref, v_ref)
    pl.semaphore_wait(barrier, 22)

    def columns(m):
        return x_ref.at[:, pl.ds(pl.multiple_of(m * 128, 128), 128)]

    own_slot = 2 * number(mine(place_a, place_b)[::-1]) + core
    other_slot = 2 * number(others(place_a, place_b)[::-1]) + core
    other_groups = others(group_a, group_b)
    other_block = number(other_groups) + 8 * (1 - core)
    for mask in range(7, -1, -1):
        routes = [(other_block, other_groups, other_slot, me + to_core + subset(to_group, mask))]
        if mask:
            routes.append((block, groups, own_slot, me + subset(to_class, mask)))
        for first, group_bits, slot, device in routes:
            pltpu.make_async_remote_copy(
                src_ref=columns(first + subset(flips(group_bits, (1, 2, 4)), mask)),
                dst_ref=xr_ref.at[slot],
                send_sem=send_sems.at[0],
                recv_sem=recv_sems.at[0],
                device_id=device,
                device_id_type=LOGICAL,
            ).start()
    pltpu.make_async_copy(columns(block), xr_ref.at[own_slot], recv_sems.at[0]).start()

    def order(h):
        return classes[0] + (1 - h) * (1 - 2 * classes[0])

    def split(i, _):
        for j in range(4):
            piece = jnp.concatenate([xr_ref[2 * i + s, pl.ds(j, 8, stride=4), :] for s in range(2)], axis=0)
            high = piece.astype(BF16)
            rows = pl.ds(pl.multiple_of(128 * j + 16 * i, 16), 16)
            xs_ref[rows, 0:128] = high
            xs_ref[rows, 128:256] = (piece - high.astype(F32)).astype(BF16)
        return 0

    def half(h):
        @pl.when(h == 0)
        def _():
            pltpu.make_async_copy(xr_ref, xr_ref, recv_sems.at[0]).wait()
            lax.fori_loop(0, 8, split, 0, unroll=4)

        q3 = order(h)
        far = (1 - h) * to_group[0]
        for mask in range(3, -1, -1):
            i = classes[1] + 2 * classes[2] + subset(flips(classes[1:], (1, 2)), mask)
            rows = pl.ds(pl.multiple_of((4 * q3 + i) * 192, 16), 192)
            wide = jnp.dot(g_ref[rows, :], xs_ref[...], preferred_element_type=F32)
            part = wide[0:96, 0:128] + (wide[0:96, 128:256] + wide[96:192, 0:128])

            def send():
                part_ref[4 * q3 + i] = part
                pltpu.make_async_remote_copy(
                    src_ref=part_ref.at[4 * q3 + i],
                    dst_ref=rr_ref.at[target],
                    send_sem=send_sems.at[1],
                    recv_sem=recv_sems.at[1],
                    device_id=me + far + subset(to_group[1:], mask),
                    device_id_type=LOGICAL,
                ).start()

            if mask:
                send()
            else:
                pl.when(h == 0)(send)

                @pl.when(h == 1)
                def _():
                    rr_ref[target] = part

    late_levels(coef_ref, box, top, order, w_ref, p_ref, c_ref, v_ref, g_ref, half)
    fetch_tail.wait()
    for i in range(3):
        sum_ref[128 * i + 96 : 128 * i + 128, :] = jnp.zeros((32, 128), BF16)
    last_weights(coef_ref, target, tail_ref, h_ref)
    pltpu.make_async_copy(rr_ref.at[0:7], rr_ref.at[0:7], recv_sems.at[1]).wait()

    def add(i, _):
        rows = pl.ds(pl.multiple_of(16 * i, 16), 16)
        total = rr_ref[0, rows, :]
        for k in range(1, 8):
            total = total + rr_ref[k, rows, :]
        high = total.astype(BF16)
        sum_ref[rows, :] = high
        sum_ref[pl.ds(pl.multiple_of(128 + 16 * i, 16), 16), :] = high
        sum_ref[pl.ds(pl.multiple_of(256 + 16 * i, 16), 16), :] = (total - high.astype(F32)).astype(BF16)
        return 0

    lax.fori_loop(0, 6, add, 0, unroll=True)

    home = zh + 2 * yl + 4 * yh + 8 * xl + 16 * xh + 32 * zl
    own = core == classes[2]
    row = pl.multiple_of((classes[0] + 2 * classes[1]) * 8, 8)
    here = out_ref.at[pl.ds(row, 8), pl.ds(pl.multiple_of(block * 128, 128), 128)]
    turns = flips((zh, xl, xh, yh, yl, zl), (1, 8, 16, 4, 2, 32))

    def deliver(high):
        pltpu.make_async_remote_copy(
            src_ref=tile_ref.at[high],
            dst_ref=here,
            send_sem=send_sems.at[2],
            recv_sem=recv_sems.at[2],
            device_id=2 * high + classes[2],
            device_id_type=LOGICAL,
        ).start()

    early = (0, 8)
    lost = (63 - home, home + subset(turns, 48))
    instead = [jnp.where(lost[n] == early[1 - n], lost[1 - n], lost[n]) for n in range(2)]

    def settle(high):
        return jnp.where(high == early[0], instead[0], jnp.where(high == early[1], instead[1], high))

    def make(start, end):
        tiles = jnp.dot(h_ref[8 * start : 8 * end, :], sum_ref[...], preferred_element_type=F32)
        tile_ref[start:end] = tiles.reshape(end - start, 8, 128)

    make(0, 16)
    for high in early:
        pl.when(jnp.logical_or(home != high, jnp.logical_not(own)))(functools.partial(deliver, high))
    make(16, 64)
    moved = jnp.logical_or(home == early[0], home == early[1])
    last = jnp.logical_or(moved, jnp.logical_not(own))

    def deliver_some(step, _):
        same_y, same_z = rem(step, 2), div(step, 2)
        first = home + (1 - same_y) * turns[4] + (1 - same_z) * turns[5]

        def send(mask):
            deliver(settle(first + subset(turns, mask)))

        pl.when(step > 0)(lambda: send(15))
        pl.when(jnp.logical_and(step > 0, jnp.logical_or(step < 3, last)))(lambda: send(0))
        for mask in (14, 1, 13, 2, 12, 3, 11, 4, 10, 5, 9, 6, 8, 7):
            send(mask)
        return 0

    lax.fori_loop(0, 4, deliver_some, 0)

    @pl.when(own)
    def _():
        pltpu.make_async_copy(tile_ref.at[home], here, recv_sems.at[2]).start()

    pltpu.make_async_copy(xr_ref.at[0:15], xr_ref.at[0:15], send_sems.at[0]).wait()
    pltpu.make_async_copy(part_ref.at[0:7], part_ref.at[0:7], send_sems.at[1]).wait()

    @pl.when(own)
    def _():
        pltpu.make_async_copy(tile_ref.at[0:63], tile_ref.at[0:63], send_sems.at[2]).wait()

    @pl.when(jnp.logical_not(own))
    def _():
        pltpu.make_async_copy(tile_ref, tile_ref, send_sems.at[2]).wait()

    pltpu.make_async_copy(out_ref, out_ref, recv_sems.at[2]).wait()


def shards(traces, phase_coef):
    return pl.pallas_call(
        kernel,
        out_shape=jax.ShapeDtypeStruct((32, 2048), F32),
        in_specs=[
            pl.BlockSpec(memory_space=pl.ANY),
            pl.BlockSpec(memory_space=pl.ANY),
            pl.BlockSpec(memory_space=pl.ANY),
        ],
        out_specs=pl.BlockSpec(memory_space=pl.ANY),
        scratch_shapes=[
            pltpu.SMEM((2, 4), F32),
            pltpu.VMEM((6, 64, 128), F32),
            pltpu.VMEM((5, 36, 8, 128), F32),
            pltpu.VMEM((5, 6, 8, 128), F32),
            pltpu.VMEM((5, 8, 128), F32),
            pltpu.VMEM((3, 12, 4, 8, 128), F32),
            pltpu.VMEM((1536, 512), BF16),
            pltpu.VMEM((512, 384), BF16),
            pltpu.VMEM((16, 32, 128), F32),
            pltpu.VMEM((512, 256), BF16),
            pltpu.VMEM((8, 96, 128), F32),
            pltpu.VMEM((8, 96, 128), F32),
            pltpu.VMEM((384, 128), BF16),
            pltpu.VMEM((64, 8, 128), F32),
            pltpu.SemaphoreType.DMA((3,)),
            pltpu.SemaphoreType.DMA((5,)),
        ],
        compiler_params=pltpu.CompilerParams(
            collective_id=0, has_side_effects=True, vmem_limit_bytes=60 * 2**20
        ),
    )(traces, phase_coef, jnp.asarray(tail_table()))


def solution(mesh):
    placed = (P(("gx", "gy"), None), P())
    return jax.shard_map(
        shards, mesh=mesh, in_specs=placed, out_specs=P(("gx", "gy"), None), check_vma=False
    )
```
